32 devices in a mesh: row: 2 (over x), col: 16 (over z, y, core).
Axes of the slice: x: 2, y: 2, z: 4, core: 2. Of those that a mesh axis runs over, the one named last changes fastest.
Arguments:
- left_features: bfloat16 [8, 1024, 320], P('row', 'col'), may hold values from -6 to 6
- right_features: bfloat16 [8, 1024, 320], P('row', 'col'), may hold values from -6 to 6
- conv_weight: bfloat16 [3, 3, 3, 40, 32], replicated, may hold values from -0.1875 to 0.1875
- cotangent: bfloat16 [24, 8, 1024, 32], P(None, 'row', 'col'), may hold values from -6 to 6
Outputs:
- cost_output: bfloat16 [24, 8, 1024, 32], P(None, 'row', 'col')
- weight_grad: float32 [3, 3, 3, 40, 32], replicated
- left_grad: bfloat16 [8, 1024, 320], P('row', 'col')
- right_grad: bfloat16 [8, 1024, 320], P('row', 'col')
The draws below stay inside these ranges and needn't reach their ends.
All inputs are finite; a program needn't handle non-finite values.
Results may differ from the reference program's by a relative error of at most 0.0049.
Values may be sent and summed in bfloat16 or wider, within the bound.
No kernel may reach another device: no remote copies, remote signals or barrier semaphores. Data moves between devices by JAX's collectives and lax.ppermute only.
A program may use at most 128 MiB of HBM per device.

```python
import math
import jax
import jax.numpy as jnp
from jax import lax

C = 320
G = 40
F = 32
DISP = 24
STEP = 4
H = 8
W = 1024


def shard_levels(key, extent, pieces, smallest, top_value):
    def one(dim, shards_of):
        draws = jax.random.uniform(jax.random.fold_in(jax.random.fold_in(key, 6), dim), (shards_of,), jnp.float32, smallest / len(pieces), top_value / len(pieces))
        return jnp.repeat(jnp.exp(draws), extent[dim] // shards_of).reshape((-1,) + (1,) * (len(extent) - dim - 1))

    loudness = one(*pieces[0])
    for cut in pieces[1:]:
        loudness = loudness * one(*cut)
    return loudness


def noise(key, extent, deviation, reach, cuts=(), held_as=jnp.bfloat16):
    gain = shard_levels(key, extent, cuts, -0.22, 0.18) if cuts else 1.0
    result = jax.random.normal(key, extent, jnp.float32) * deviation * gain
    return jnp.minimum(jnp.maximum(result, -reach), reach).astype(held_as)


def setup_inputs(seed: int = 0) -> dict:
    arg_keys = jax.random.split(jax.random.key(seed), 5)
    return {
        "left_features": noise(arg_keys[0], (H, W, C), 1.0, 6.0, ((0, 2), (1, 16))),
        "right_features": noise(arg_keys[1], (H, W, C), 1.0, 6.0, ((0, 2), (1, 16))),
        "conv_weight": noise(arg_keys[2], (3, 3, 3, G, F), (27 * G) ** -0.5, 0.1875),
        "cotangent": noise(arg_keys[3], (DISP, H, W, F), 1.0, 6.0, ((1, 2), (2, 16))),
    }


DIMS = ('NDHWC', 'DHWIO', 'NDHWC')

def conv_volume(volume, kernel):
    return lax.conv_general_dilated(volume[None], kernel, (1, 1, 1), ((1, 1), (1, 1), (1, 1)), dimension_numbers=DIMS, precision=lax.Precision.HIGHEST)[0]

def reference(left_features, right_features, conv_weight, cotangent):
    image_height, image_width, channels = left_features.shape
    groups = conv_weight.shape[3]
    group_size = channels // groups
    left_f = left_features.astype(jnp.float32).reshape(image_height, image_width, groups, group_size)
    right_f = right_features.astype(jnp.float32)
    planes = []
    for disp_index in range(DISP):
        offset = STEP * disp_index
        shifted = jnp.pad(right_f, ((0, 0), (offset, 0), (0, 0)))[:, :image_width]
        shifted = shifted.reshape(image_height, image_width, groups, group_size)
        planes.append(lax.optimization_barrier(jnp.sum(left_f * shifted, axis=3)) / group_size)
    volume = lax.optimization_barrier(jnp.stack(planes).astype(jnp.bfloat16)).astype(jnp.float32)
    output, pullback = jax.vjp(conv_volume, volume, conv_weight.astype(jnp.float32))
    grad_volume, grad_kernel = pullback(cotangent.astype(jnp.float32))
    grad_volume = lax.optimization_barrier(grad_volume.astype(jnp.bfloat16)).astype(jnp.float32)
    weight_grad = grad_kernel / math.sqrt(DISP * image_height * image_width)
    left_accum = jnp.zeros((image_height, image_width, groups, group_size), jnp.float32)
    right_accum = jnp.zeros((image_height, image_width, channels), jnp.float32)
    for disp_index in range(DISP):
        offset = STEP * disp_index
        shifted = jnp.pad(right_f, ((0, 0), (offset, 0), (0, 0)))[:, :image_width]
        shifted = shifted.reshape(image_height, image_width, groups, group_size)
        left_accum = left_accum + grad_volume[disp_index][..., None] * shifted
        contrib = (grad_volume[disp_index][..., None] * left_f).reshape(image_height, image_width, channels)
        right_accum = right_accum + jnp.pad(contrib, ((0, 0), (0, offset), (0, 0)))[:, offset:]
    left_grad = (left_accum / group_size).reshape(image_height, image_width, channels).astype(jnp.bfloat16)
    right_grad = (right_accum / group_size).astype(jnp.bfloat16)
    return (output.astype(jnp.bfloat16), weight_grad, left_grad, right_grad)
```

```python
import functools
import math

import jax
import jax.numpy as jnp
from jax import lax
from jax.experimental import pallas as pl
from jax.experimental.pallas import tpu as pltpu
from jax.sharding import PartitionSpec as P

DISP = 24
STEP = 4
SLOT = 64
PAD = 8
F32 = jnp.float32
BF16 = jnp.bfloat16
VMEM = pl.BlockSpec(memory_space=pltpu.VMEM)
LIMIT = 40 * 1024 * 1024


def params():
    return pltpu.CompilerParams(vmem_limit_bytes=LIMIT)


def lanes(shape):
    return lax.broadcasted_iota(jnp.int32, shape, len(shape) - 1)


def channel_table(channels, group_size, flip):
    shape = (group_size * SLOT, channels) if flip else (channels, group_size * SLOT)
    c = lax.broadcasted_iota(jnp.int32, shape, 1 if flip else 0)
    j = lax.broadcasted_iota(jnp.int32, shape, 0 if flip else 1)
    hit = (lax.rem(c, group_size) == lax.div(j, SLOT)) & (lax.div(c, group_size) == lax.rem(j, SLOT))
    return jnp.where(hit, 1.0, 0.0).astype(BF16)


def dot(a, b):
    return jnp.dot(a, b, preferred_element_type=F32)


def pack_kernel(ends, left, right, ct, r1, r2, c1, ctl, *rest):
    n = len(ends)
    row_refs, lo_refs, hi_refs = rest[:n], rest[n : 2 * n], rest[2 * n : 3 * n]
    ctf, rowf = rest[3 * n :]
    disp, rows, cols, feat = ct.shape
    for h in range(rows):
        r1[h * cols : (h + 1) * cols] = right[h]
        r2[h * (cols // 2) : (h + 1) * (cols // 2)] = right[h, cols // 2 :]
    for d in range(disp):
        block = jnp.concatenate([ct[d, h].astype(F32) for h in range(rows)], axis=1)
        ctf[d * cols : (d + 1) * cols] = block
        ctl[d] = block.astype(BF16)
    width = rows * feat
    for ref, base, col in ((r1, rows * cols, cols - 1), (c1, 0, 0)):
        ref[base : base + 32] = jnp.zeros((32, ref.shape[1]), BF16)
        ref[base : base + disp, 0:width] = ctf[pl.ds(col, disp, stride=cols), :].astype(BF16)
        edge = [left[h, col : col + 1].astype(F32) for h in range(rows)]
        edge += [right[h, col : col + 1].astype(F32) for h in range(rows)]
        ref[base + disp : base + 32] = jnp.concatenate(edge, axis=0).astype(BF16)
    per = 128 // feat
    for end, row_ref, lo_ref, hi_ref in zip(ends, row_refs, lo_refs, hi_refs):
        h = end()
        for q in range(disp // per):
            rowf[q * cols : (q + 1) * cols] = jnp.concatenate(
                [ct[q * per + i, h].astype(F32) for i in range(per)], axis=1
            )
        row_ref[...] = rowf[...].astype(BF16)
        for ref, col in ((lo_ref, 0), (hi_ref, cols - 1)):
            ref[...] = jnp.zeros(ref.shape, BF16)
            ref[0 : disp // per] = rowf[pl.ds(col, disp // per, stride=cols), :].astype(BF16)


def volume_kernel(ends, group_size, left, right, r1, r2, c1, vsh, fl, fr, fr4, *rest):
    pays, vbuf = rest[: len(ends)], rest[len(ends)]
    rows, cols, channels = left.shape
    disp = vsh.shape[0] - 2
    reach = fr.shape[1] - cols - PAD
    table = channel_table(channels, group_size, False)
    wide = group_size * SLOT

    def spread(x):
        return dot(x, table)

    base = rows * cols
    edge_l = spread(r1[base : base + 32])
    edge_r = spread(c1[...])
    far = spread(r2[...])
    near = spread(r1[0:base])
    own = spread(right[...].reshape(base, channels))
    own_l = spread(left[...].reshape(base, channels))
    half = cols // 2
    for h in range(rows):
        fl[h, 0:PAD] = jnp.zeros((PAD, wide), F32)
        fl[h, PAD + cols :] = jnp.zeros((PAD, wide), F32)
        fl[h, PAD - 1 : PAD] = edge_l[disp + h : disp + h + 1]
        fl[h, PAD : PAD + cols] = own_l[h * cols : (h + 1) * cols]
        fl[h, PAD + cols : PAD + cols + 1] = edge_r[disp + h : disp + h + 1]
        for ref, off in ((fr, 0), (fr4, STEP)):
            start = reach - cols - half + off
            ref[h, 0:start] = jnp.zeros((start, wide), F32)
            ref[h, start : start + half] = far[h * half : (h + 1) * half]
            ref[h, start + half : start + half + cols] = near[h * cols : (h + 1) * cols]
            ref[h, start + half + cols : start + half + 2 * cols] = own[h * cols : (h + 1) * cols]
            tail = ref.shape[1] - (start + half + 2 * cols)
            ref[h, start + half + 2 * cols :] = jnp.zeros((tail, wide), F32)
            ref[h, start + half + 2 * cols : start + half + 2 * cols + 1] = edge_r[
                disp + rows + h : disp + rows + h + 1
            ]
    vsh[0] = jnp.zeros(vsh.shape[1:], BF16)
    vsh[disp + 1] = jnp.zeros(vsh.shape[1:], BF16)
    total = cols + 2 * PAD
    block = 16
    low = lanes((block, 128)) < SLOT
    scale = 1.0 / group_size

    def pair(dd, _):
        for odd in range(2):
            band = fr4 if odd else fr
            for b in range(total // block):
                at = pl.multiple_of(reach - PAD + b * block - 2 * STEP * dd, 8)
                sums = []
                for h in range(rows):
                    prod = fl[h, b * block : (b + 1) * block] * band[h, pl.ds(at, block)]
                    acc = prod[:, 0:128]
                    for j in range(1, wide // 128):
                        acc = acc + prod[:, 128 * j : 128 * (j + 1)]
                    sums.append((acc + pltpu.roll(acc, SLOT, 1)) * scale)
                for p in range(rows // 2):
                    vbuf[odd, b * block : (b + 1) * block, 128 * p : 128 * (p + 1)] = jnp.where(
                        low, sums[2 * p], sums[2 * p + 1]
                    )
            for e in range(3):
                vsh[2 * dd + odd + 1, :, 256 * e : 256 * (e + 1)] = vbuf[
                    odd, PAD - 1 + e : PAD - 1 + e + cols
                ].astype(BF16)
        big = lanes((total, 128)) < SLOT
        for end, pay in zip(ends, pays):
            h = end()
            if isinstance(h, int):
                lane = 128 * (h // 2)
                halves = [vbuf[o, :, lane : lane + 128] for o in range(2)]
                if h % 2 == 0:
                    halves[1] = pltpu.roll(halves[1], SLOT, 1)
                else:
                    halves[0] = pltpu.roll(halves[0], SLOT, 1)
                out = jnp.where(big, halves[0], halves[1])
            else:
                first = jnp.where(big, vbuf[0, :, 0:128], pltpu.roll(vbuf[1, :, 0:128], SLOT, 1))
                last = jnp.where(
                    big, pltpu.roll(vbuf[0, :, 128:256], SLOT, 1), vbuf[1, :, 128:256]
                )
                out = jnp.where(h == 0, first, last)
            pay[dd] = out.astype(BF16)
        return 0

    lax.fori_loop(0, disp // 2, pair, 0)


def weight_kernel(
    masks, groups, vsh, ctl, r1, c1, top, bot, tl, bl, tr, br, pay, ctsh, vt, buf, edges
):
    disp, cols, width = ctl.shape
    rows, feat = vsh.shape[2] // 3 // SLOT, 32
    per = 128 // feat
    mtop, mbot = masks()
    first = lanes((8, 128))
    base = r1.shape[0] - 32
    for side, (main, at, t, b) in enumerate(((r1, base, tl, bl), (c1, 0, tr, br))):
        edges[2 * side] = main[at : at + disp, 0:128].astype(F32)
        tv = t[0:8].astype(F32) * mtop
        bv = b[0:8].astype(F32) * mbot
        for i in range(per):
            a = tv if i == 0 else pltpu.roll(tv, 128 - feat * i, 1)
            z = pltpu.roll(bv, (128 + feat - feat * i) % 128, 1) if i != 1 else bv
            val = jnp.where(first < feat, a, jnp.where(first < 2 * feat, z, 0.0))
            edges[2 * side + 1, pl.ds(i, disp // per, stride=per)] = val[0 : disp // per]
    ctsh[0] = jnp.zeros(ctsh.shape[1:], BF16)
    ctsh[disp + 1] = jnp.zeros(ctsh.shape[1:], BF16)
    lane = lanes((cols, 128))

    def fill(q, _):
        t = top[pl.ds(pl.multiple_of(q * cols, cols), cols)].astype(F32) * mtop
        z = bot[pl.ds(pl.multiple_of(q * cols, cols), cols)].astype(F32) * mbot
        for i in range(per):
            d = q * per + i
            a = t if i == 0 else pltpu.roll(t, 128 - feat * i, 1)
            y = z if i == 1 else pltpu.roll(z, (128 + feat - feat * i) % 128, 1)
            buf[i, PAD : PAD + cols, 0:128] = ctl[d].astype(F32)
            buf[i, PAD : PAD + cols, 128:256] = jnp.where(
                lane < feat, a, jnp.where(lane < 2 * feat, y, 0.0)
            )
            for part in range(2):
                at = slice(128 * part, 128 * (part + 1))
                buf[i, PAD - 1 : PAD, at] = edges[part, pl.ds(d, 1)]
                buf[i, PAD + cols : PAD + cols + 1, at] = edges[2 + part, pl.ds(d, 1)]
            for e in range(3):
                ctsh[d + 1, :, 256 * e : 256 * (e + 1)] = buf[
                    i, PAD - 1 + e : PAD - 1 + e + cols
                ].astype(BF16)
        return 0

    lax.fori_loop(0, disp // per, fill, 0)
    step = 256 // cols
    for q in range(disp // step):
        v = vsh[1 + q * step : 1 + (q + 1) * step, :, 256:512].reshape(256, 256)
        vt[:, 256 * q : 256 * (q + 1)] = v.T
    keep = lanes((groups, 128))

    def taps(a, _):
        for e in range(3):
            ct_block = ctsh[pl.ds(a, disp), :, 256 * e : 256 * (e + 1)].reshape(disp * cols, 256)
            full = dot(vt[...], ct_block)
            out = None
            for h in range(rows):
                x = full[SLOT * h : SLOT * h + groups, 0:128]
                y = full[SLOT * h : SLOT * h + groups, 128:256]
                if h == 0:
                    term = jnp.where(keep < feat, y, pltpu.roll(x, feat, 1))
                else:
                    term = x if h == 1 else pltpu.roll(x, 128 - feat * (h - 1), 1)
                    if h == rows - 1:
                        term = jnp.where(keep < 2 * feat, term, pltpu.roll(y, feat, 1))
                out = term if out is None else out + term
            pay[a, groups * e : groups * (e + 1)] = jnp.where(keep < 3 * feat, out, 0.0).astype(BF16)
        return 0

    lax.fori_loop(0, 3, taps, 0)


def feature_kernel(group_size, ctsh, w2, fl, fr, fr4, lg, rg0, rg1, rg2, gv, accl, accr):
    disp = ctsh.shape[0] - 2
    rows, cols, channels = lg.shape
    reach = fr.shape[1] - cols - PAD
    wide = group_size * SLOT
    step = 256 // cols
    low = lanes((256, 128)) < SLOT
    scale = 1.0 / group_size
    for h in range(rows):
        gv[h, :, 0:PAD] = jnp.zeros((disp, PAD, 128), F32)
        gv[h, :, PAD + cols :] = jnp.zeros((disp, PAD, 128), F32)

    def conv(q, _):
        acc = None
        for a in range(3):
            block = ctsh[pl.ds(q * step + a, step)].reshape(256, ctsh.shape[2])
            part = dot(block, w2[a])
            acc = part if acc is None else acc + part
        g = acc.astype(BF16).astype(F32) * scale
        for p in range(rows // 2):
            x = g[:, 128 * p : 128 * (p + 1)]
            r = pltpu.roll(x, SLOT, 1)
            for o in range(2):
                y = jnp.where(low, r, x) if o else jnp.where(low, x, r)
                gv[2 * p + o, pl.ds(q * step, step), PAD : PAD + cols] = y.reshape(step, cols, 128)
        return 0

    lax.fori_loop(0, disp // step, conv, 0)

    def left_block(i, _):
        h = lax.div(i, cols // 8)
        w = pl.multiple_of(lax.rem(i, cols // 8) * 8, 8)
        accs = [jnp.zeros((8, 128), F32) for _ in range(wide // 128)]
        for d in range(disp):
            band = fr4 if d % 2 else fr
            at = pl.multiple_of(w + reach - 2 * STEP * (d // 2), 8)
            g = gv[h, d, pl.ds(w + PAD, 8)]
            for j in range(wide // 128):
                accs[j] = accs[j] + g * band[h, pl.ds(at, 8), 128 * j : 128 * (j + 1)]
        for j in range(wide // 128):
            accl[h, pl.ds(w, 8), 128 * j : 128 * (j + 1)] = accs[j]
        return 0

    lax.fori_loop(0, rows * (cols // 8), left_block, 0)
    back = accr.shape[1] - cols

    def right_row(h, _):
        for u in range(-back, cols, 8):
            accs = [jnp.zeros((8, 128), F32) for _ in range(wide // 128)]
            for d in range(disp):
                w = u + STEP * d
                if w <= -8 or w >= cols:
                    continue
                g = gv[h, d, w + PAD : w + PAD + 8]
                for j in range(wide // 128):
                    accs[j] = accs[j] + g * fl[h, w + PAD : w + PAD + 8, 128 * j : 128 * (j + 1)]
            for j in range(wide // 128):
                accr[h, u + back : u + back + 8, 128 * j : 128 * (j + 1)] = accs[j]
        return 0

    lax.fori_loop(0, rows, right_row, 0)
    table = channel_table(channels, group_size, True)
    half = cols // 2
    for h in range(rows):
        lg[h] = dot(accl[h].astype(BF16), table).astype(BF16)
        whole = dot(accr[h].astype(BF16), table).astype(BF16)
        rg2[h] = whole[back - cols - half : back - cols]
        rg1[h] = whole[back - cols : back]
        rg0[h] = whole[back:]


def conv_kernel(masks, vsh, top, bot, wc, wh, out, halo, buf):
    disp, rows, cols, feat = out.shape
    mtop, mbot = masks()
    total = top.shape[1]
    low = lanes((total, 128)) < SLOT
    halo[0] = jnp.zeros(halo.shape[1:], BF16)
    halo[disp + 1] = jnp.zeros(halo.shape[1:], BF16)

    def fill(dd, _):
        t = top[dd].astype(F32) * mtop
        b = bot[dd].astype(F32) * mbot
        buf[0] = jnp.where(low, t, pltpu.roll(b, SLOT, 1))
        buf[1] = jnp.where(low, pltpu.roll(t, SLOT, 1), b)
        for o in range(2):
            for e in range(3):
                halo[2 * dd + o + 1, :, 128 * e : 128 * (e + 1)] = buf[
                    o, PAD - 1 + e : PAD - 1 + e + cols
                ].astype(BF16)
        return 0

    lax.fori_loop(0, disp // 2, fill, 0)
    step = 256 // cols

    def conv(q, _):
        acc = None
        for a in range(3):
            main = vsh[pl.ds(q * step + a, step)].reshape(256, vsh.shape[2])
            side = halo[pl.ds(q * step + a, step)].reshape(256, halo.shape[2])
            part = dot(main, wc[a]) + dot(side, wh[a])
            acc = part if acc is None else acc + part
        for i in range(step):
            for h in range(rows):
                out[q * step + i, h] = acc[
                    i * cols : (i + 1) * cols, feat * h : feat * (h + 1)
                ].astype(BF16)
        return 0

    lax.fori_loop(0, disp // step, conv, 0)


def finish_weight_kernel(scale, one, two, out):
    _, _, _, groups, feat = out.shape
    for a in range(3):
        for e in range(3):
            at = groups * e
            x = (one[a, at : at + groups].astype(F32) + two[a, at : at + groups].astype(F32)) * scale
            for b in range(3):
                out[2 - a, 2 - b, 2 - e] = x[:, feat * b : feat * (b + 1)]


def finish_right_kernel(own, near, far, out):
    rows, cols, channels = out.shape
    half = cols // 2
    for h in range(rows):
        total = own[h].astype(F32) + near[h].astype(F32)
        out[h, 0:half] = total[0:half].astype(BF16)
        out[h, half:] = (total[half:] + far[h].astype(F32)).astype(BF16)


def call(kernel, outs, scratch, *args):
    return pl.pallas_call(
        kernel,
        out_shape=[jax.ShapeDtypeStruct(s, t) for s, t in outs],
        in_specs=[VMEM] * len(args),
        out_specs=[VMEM] * len(outs),
        scratch_shapes=scratch,
        compiler_params=params(),
    )(*args)


def col_shift(block, distance):
    n = lax.axis_size("col")
    route = [(i - distance, i) for i in range(n) if 0 <= i - distance < n]
    return lax.ppermute(block, "col", route)


def grid_shift(block, down, distance):
    rows, n = lax.axis_size("row"), lax.axis_size("col")
    route = []
    for r in range(rows):
        for c in range(n):
            if 0 <= r - down < rows and 0 <= c - distance < n:
                route.append(((r - down) * n + c - distance, r * n + c))
    return lax.ppermute(block, ("row", "col"), route)


def grid_swap(block, distance):
    n = lax.axis_size("col")
    route = [
        ((1 - r) * n + c - distance, r * n + c)
        for r in range(2)
        for c in range(n)
        if 0 <= c - distance < n
    ]
    return lax.ppermute(block, ("row", "col"), route)


def halos(pays, distance):
    if lax.axis_size("row") == 2:
        got = grid_swap(pays[0], distance)
        return got, got
    return grid_shift(pays[0], 1, distance), grid_shift(pays[1], -1, distance)


def banded(conv_weight, rows):
    _, _, _, groups, _ = conv_weight.shape
    padded = jnp.pad(conv_weight, ((0, 0), (rows - 1, rows - 1), (0, 0), (0, SLOT - groups), (0, 0)))
    stack = [padded[:, rows - 1 - h : 2 * rows + 1 - h] for h in range(rows)]
    return jnp.stack(stack, axis=4).transpose(0, 2, 1, 3, 4, 5)


def on_device(left_features, right_features, conv_weight, cotangent):
    rows, cols, channels = left_features.shape
    disp, feat = cotangent.shape[0], cotangent.shape[3]
    groups = conv_weight.shape[3]
    group_size = channels // groups
    wide = group_size * SLOT
    n_row, n_col = lax.axis_size("row"), lax.axis_size("col")
    per = 128 // feat

    if n_row == 2:
        ends = [lambda: (rows - 1) * (1 - lax.axis_index("row"))]
    else:
        ends = [lambda: rows - 1, lambda: 0]
    n = len(ends)

    def masks():
        at = lax.axis_index("row")
        return (
            jnp.where(at > 0, 1.0, 0.0).astype(F32),
            jnp.where(at < n_row - 1, 1.0, 0.0).astype(F32),
        )

    packed = call(
        functools.partial(pack_kernel, ends),
        [
            ((rows * cols + 32, channels), BF16),
            ((rows * cols // 2, channels), BF16),
            ((32, channels), BF16),
            ((disp, cols, rows * feat), BF16),
        ]
        + [((disp // per * cols, 128), BF16)] * n
        + [((16, 128), BF16)] * (2 * n),
        [pltpu.VMEM((disp * cols, rows * feat), F32), pltpu.VMEM((disp // per * cols, 128), F32)],
        left_features,
        right_features,
        cotangent,
    )
    r1, r2, c1, ctl = packed[:4]
    row_pay, lo_pay, hi_pay = packed[4 : 4 + n], packed[4 + n : 4 + 2 * n], packed[4 + 2 * n :]
    r1 = col_shift(r1, 1)
    top, bot = halos(row_pay, 0)
    r2 = col_shift(r2, 2)
    c1 = col_shift(c1, -1)
    tl, bl = halos(hi_pay, 1)
    tr, br = halos(lo_pay, -1)

    six = banded(conv_weight, rows)
    wc = six[:, :, 1 : rows + 1].reshape(3, 3 * rows * SLOT, rows * feat)
    wh = jnp.concatenate([six[:, :, :1], six[:, :, rows + 1 :]], axis=2)
    wh = wh.reshape(3, 3 * 2 * SLOT, rows * feat)
    back = banded(conv_weight[::-1, ::-1, ::-1], rows)
    back = jnp.concatenate([back[:, :, 1 : rows + 1], back[:, :, :1], back[:, :, rows + 1 :]], axis=2)
    back = back.transpose(0, 1, 2, 5, 4, 3).reshape(3, 3, (rows + 2) * feat, rows * SLOT)
    w2 = jnp.pad(back, ((0, 0), (0, 0), (0, 256 - (rows + 2) * feat), (0, 0)))
    w2 = w2.reshape(3, 3 * 256, rows * SLOT)

    band = 104 + cols + PAD
    volume = call(
        functools.partial(volume_kernel, ends, group_size),
        [
            ((disp + 2, cols, 3 * rows * SLOT), BF16),
            ((rows, cols + 2 * PAD, wide), F32),
            ((rows, band, wide), F32),
            ((rows, band, wide), F32),
        ]
        + [((disp // 2, cols + 2 * PAD, 128), BF16)] * n,
        [pltpu.VMEM((2, cols + 2 * PAD, rows * SLOT), F32)],
        left_features,
        right_features,
        r1,
        r2,
        c1,
    )
    vsh, fl, fr, fr4 = volume[:4]
    vtop, vbot = halos(volume[4:], 0)

    part, ctsh = call(
        functools.partial(weight_kernel, masks, groups),
        [((3, 3 * groups, 128), BF16), ((disp + 2, cols, 3 * 256), BF16)],
        [
            pltpu.VMEM((rows * SLOT, disp * cols), BF16),
            pltpu.VMEM((per, cols + 2 * PAD, 256), F32),
            pltpu.VMEM((4, disp, 128), F32),
        ],
        vsh, ctl, r1, c1, top, bot, tl, bl, tr, br,
    )

    hops = []
    for axis, size in (("col", n_col), ("row", n_row)):
        bit = 1
        while bit < size:
            hops.append((axis, [(i, i ^ bit) for i in range(size)]))
            bit *= 2
    for step, (axis, route) in enumerate(hops):
        other = lax.ppermute(part, axis, route)
        if step < len(hops) - 1:
            part = (part.astype(F32) + other.astype(F32)).astype(BF16)
    cells = disp * rows * n_row * cols * n_col

    lg, rg0, rg1, rg2 = call(
        functools.partial(feature_kernel, group_size),
        [
            ((rows, cols, channels), BF16),
            ((rows, cols, channels), BF16),
            ((rows, cols, channels), BF16),
            ((rows, cols // 2, channels), BF16),
        ],
        [
            pltpu.VMEM((rows, disp, cols + 2 * PAD, 128), F32),
            pltpu.VMEM((rows, cols, wide), F32),
            pltpu.VMEM((rows, cols + cols + cols // 2, wide), F32),
        ],
        ctsh, w2, fl, fr, fr4,
    )
    rg1 = col_shift(rg1, -1)
    rg2 = col_shift(rg2, -2)

    (output,) = call(
        functools.partial(conv_kernel, masks),
        [((disp, rows, cols, feat), BF16)],
        [
            pltpu.VMEM((disp + 2, cols, 3 * 2 * SLOT), BF16),
            pltpu.VMEM((2, cols + 2 * PAD, 128), F32),
        ],
        vsh, vtop, vbot, wc, wh,
    )
    (right_grad,) = call(
        finish_right_kernel, [((rows, cols, channels), BF16)], [], rg0, rg1, rg2
    )
    (weight_grad,) = call(
        functools.partial(finish_weight_kernel, 1.0 / math.sqrt(cells)),
        [(conv_weight.shape, F32)],
        [],
        part,
        other,
    )
    return (output, weight_grad, lg, right_grad)


def solution(mesh):
    in_specs = (P("row", "col", None), P("row", "col", None), P(), P(None, "row", "col", None))
    out_specs = (P(None, "row", "col", None), P(), P("row", "col", None), P("row", "col", None))
    return jax.shard_map(
        on_device, mesh=mesh, in_specs=in_specs, out_specs=out_specs, check_vma=False
    )
```

```python
import functools
import math

import jax
import jax.numpy as jnp
from jax import lax
from jax.experimental import pallas as pl
from jax.experimental.pallas import tpu as pltpu
from jax.sharding import PartitionSpec as P

DISP = 24
STEP = 4
SLOT = 64
PAD = 8
F32 = jnp.float32
BF16 = jnp.bfloat16
VMEM = pl.BlockSpec(memory_space=pltpu.VMEM)
LIMIT = 16 * 1024 * 1024


def params():
    return pltpu.CompilerParams(vmem_limit_bytes=LIMIT)


def lanes(shape):
    return lax.broadcasted_iota(jnp.int32, shape, len(shape) - 1)


def channel_table(channels, group_size, flip, value=1.0):
    shape = (group_size * SLOT, channels) if flip else (channels, group_size * SLOT)
    c = lax.broadcasted_iota(jnp.int32, shape, 1 if flip else 0)
    j = lax.broadcasted_iota(jnp.int32, shape, 0 if flip else 1)
    hit = c == (j & (SLOT - 1)) * group_size + (j >> (SLOT.bit_length() - 1))
    return jnp.where(hit, value, 0.0).astype(BF16)


def dot(a, b):
    return jnp.dot(a, b, preferred_element_type=F32)


def dot_nt(a, b):
    return lax.dot_general(a, b, (((1,), (1,)), ((), ())), preferred_element_type=F32)


def pack_kernel(ends, left, right, ct, r1, r2, c1, ctl, *rest):
    n = len(ends)
    row_refs, lo_refs, hi_refs = rest[:n], rest[n : 2 * n], rest[2 * n : 3 * n]
    ctf, rowf = rest[3 * n :]
    disp, rows, feat, cols = ct.shape
    for h in range(rows):
        r1[h * cols : (h + 1) * cols] = right[h]
        r2[h * (cols // 2) : (h + 1) * (cols // 2)] = right[h, cols // 2 :]
    for d in range(disp):
        block = ct[d].reshape(rows * feat, cols).astype(F32).T
        ctf[d * cols : (d + 1) * cols] = block
        ctl[d] = block.astype(BF16)
    width = rows * feat
    for ref, base, col in ((r1, rows * cols, cols - 1), (c1, 0, 0)):
        ref[base : base + 32] = jnp.zeros((32, ref.shape[1]), BF16)
        ref[base : base + disp, 0:width] = ctf[pl.ds(col, disp, stride=cols), :].astype(BF16)
        edge = [left[h, col : col + 1].astype(F32) for h in range(rows)]
        edge += [right[h, col : col + 1].astype(F32) for h in range(rows)]
        ref[base + disp : base + 32] = jnp.concatenate(edge, axis=0).astype(BF16)
    per = 128 // feat
    for end, row_ref, lo_ref, hi_ref in zip(ends, row_refs, lo_refs, hi_refs):
        h = end()
        for q in range(disp // per):
            rowf[q * cols : (q + 1) * cols] = jnp.concatenate(
                [ct[q * per + i, h].astype(F32) for i in range(per)], axis=0
            ).T
        row_ref[...] = rowf[...].astype(BF16)
        for ref, col in ((lo_ref, 0), (hi_ref, cols - 1)):
            ref[...] = jnp.zeros(ref.shape, BF16)
            ref[0 : disp // per] = rowf[pl.ds(col, disp // per, stride=cols), :].astype(BF16)


def volume_kernel(ends, group_size, left, right, r1, r2, c1, vsh, fl, fr, fr4, *rest):
    pays, vbuf = rest[: len(ends)], rest[len(ends)]
    rows, cols, channels = left.shape
    disp = vsh.shape[0] - 2
    reach = fr.shape[1] - cols - PAD
    table = channel_table(channels, group_size, False)
    wide = group_size * SLOT

    def spread(x):
        return dot(x, table)

    base = rows * cols
    edge_r = spread(c1[...])
    far = spread(r2[...])
    near = spread(r1[0:base])
    own = spread(right[...].reshape(base, channels))
    scaled = channel_table(channels, group_size, False, 1.0 / group_size)
    own_l = dot(left[...].reshape(base, channels), scaled)
    edge_ll = dot(r1[base : base + 32], scaled)
    edge_lr = dot(c1[...], scaled)
    half = cols // 2
    for h in range(rows):
        fl[h, 0:PAD] = jnp.zeros((PAD, wide), F32)
        fl[h, PAD + cols :] = jnp.zeros((PAD, wide), F32)
        fl[h, PAD - 1 : PAD] = edge_ll[disp + h : disp + h + 1]
        fl[h, PAD : PAD + cols] = own_l[h * cols : (h + 1) * cols]
        fl[h, PAD + cols : PAD + cols + 1] = edge_lr[disp + h : disp + h + 1]
        for ref, off in ((fr, 0), (fr4, STEP)):
            start = reach - cols - half + off
            ref[h, 0:start] = jnp.zeros((start, wide), F32)
            ref[h, start : start + half] = far[h * half : (h + 1) * half]
            ref[h, start + half : start + half + cols] = near[h * cols : (h + 1) * cols]
            ref[h, start + half + cols : start + half + 2 * cols] = own[h * cols : (h + 1) * cols]
            tail = ref.shape[1] - (start + half + 2 * cols)
            ref[h, start + half + 2 * cols :] = jnp.zeros((tail, wide), F32)
            ref[h, start + half + 2 * cols : start + half + 2 * cols + 1] = edge_r[
                disp + rows + h : disp + rows + h + 1
            ]
    vsh[0] = jnp.zeros(vsh.shape[1:], BF16)
    vsh[disp + 1] = jnp.zeros(vsh.shape[1:], BF16)
    total = cols + 2 * PAD
    block = 16
    low = lanes((block, 128)) < SLOT
    pairs = rows // 2

    def products(i, _):
        p, b = lax.rem(i, pairs), lax.div(i, pairs)
        at = pl.multiple_of(b * block, block)
        lefts = [fl[2 * p + o, pl.ds(at, block)] for o in range(2)]
        for d in range(disp):
            band = fr4 if d % 2 else fr
            start = pl.multiple_of(at + reach - PAD - 2 * STEP * (d // 2), 8)
            sums = []
            for o in range(2):
                prod = lefts[o] * band[2 * p + o, pl.ds(start, block)]
                acc = prod[:, 0:128]
                for j in range(1, wide // 128):
                    acc = acc + prod[:, 128 * j : 128 * (j + 1)]
                sums.append(acc + pltpu.roll(acc, SLOT, 1))
            vbuf[p, d, pl.ds(at, block)] = jnp.where(low, sums[0], sums[1])
        return 0

    lax.fori_loop(0, pairs * (total // block), products, 0)
    big = lanes((total, 128)) < SLOT

    def spread_taps(dd, _):
        for odd in range(2):
            d = 2 * dd + odd
            for p in range(pairs):
                for e in range(3):
                    lane = 128 * (pairs * e + p)
                    vsh[d + 1, :, lane : lane + 128] = vbuf[
                        p, d, PAD - 1 + e : PAD - 1 + e + cols
                    ].astype(BF16)
        for end, pay in zip(ends, pays):
            h = end()
            if isinstance(h, int):
                halves = [vbuf[h // 2, 2 * dd + o] for o in range(2)]
                if h % 2 == 0:
                    halves[1] = pltpu.roll(halves[1], SLOT, 1)
                else:
                    halves[0] = pltpu.roll(halves[0], SLOT, 1)
                out = jnp.where(big, halves[0], halves[1])
            else:
                last = pairs - 1
                first = jnp.where(big, vbuf[0, 2 * dd], pltpu.roll(vbuf[0, 2 * dd + 1], SLOT, 1))
                final = jnp.where(
                    big, pltpu.roll(vbuf[last, 2 * dd], SLOT, 1), vbuf[last, 2 * dd + 1]
                )
                out = jnp.where(h == 0, first, final)
            pay[dd] = out.astype(BF16)
        return 0

    lax.fori_loop(0, disp // 2, spread_taps, 0)


def weight_kernel(
    masks, groups, vsh, ctl, r1, c1, top, bot, tl, bl, tr, br, pay, ctsh, vt, buf, edges
):
    disp, cols, width = ctl.shape
    rows, feat = vsh.shape[2] // 3 // SLOT, 32
    per = 128 // feat
    mtop, mbot = masks()
    first = lanes((8, 128))
    base = r1.shape[0] - 32
    for side, (main, at, t, b) in enumerate(((r1, base, tl, bl), (c1, 0, tr, br))):
        edges[2 * side] = main[at : at + disp, 0:128].astype(F32)
        tv = t[0:8].astype(F32) * mtop
        bv = b[0:8].astype(F32) * mbot
        for i in range(per):
            a = tv if i == 0 else pltpu.roll(tv, 128 - feat * i, 1)
            z = pltpu.roll(bv, (128 + feat - feat * i) % 128, 1) if i != 1 else bv
            val = jnp.where(first < feat, a, jnp.where(first < 2 * feat, z, 0.0))
            edges[2 * side + 1, pl.ds(i, disp // per, stride=per)] = val[0 : disp // per]
    ctsh[0] = jnp.zeros(ctsh.shape[1:], BF16)
    ctsh[disp + 1] = jnp.zeros(ctsh.shape[1:], BF16)
    lane = lanes((cols, 128))

    def fill(q, _):
        t = top[pl.ds(pl.multiple_of(q * cols, cols), cols)].astype(F32) * mtop
        z = bot[pl.ds(pl.multiple_of(q * cols, cols), cols)].astype(F32) * mbot
        for i in range(per):
            d = q * per + i
            a = t if i == 0 else pltpu.roll(t, 128 - feat * i, 1)
            y = z if i == 1 else pltpu.roll(z, (128 + feat - feat * i) % 128, 1)
            buf[i, PAD : PAD + cols, 0:128] = ctl[d].astype(F32)
            buf[i, PAD : PAD + cols, 128:256] = jnp.where(
                lane < feat, a, jnp.where(lane < 2 * feat, y, 0.0)
            )
            for part in range(2):
                at = slice(128 * part, 128 * (part + 1))
                buf[i, PAD - 1 : PAD, at] = edges[part, pl.ds(d, 1)]
                buf[i, PAD + cols : PAD + cols + 1, at] = edges[2 + part, pl.ds(d, 1)]
            for e in range(3):
                ctsh[d + 1, :, 256 * e : 256 * (e + 1)] = buf[
                    i, PAD - 1 + e : PAD - 1 + e + cols
                ].astype(BF16)
        return 0

    lax.fori_loop(0, disp // per, fill, 0)
    step = 256 // cols
    for q in range(disp // step):
        v = vsh[1 + q * step : 1 + (q + 1) * step, :, 256:512].reshape(256, 256)
        vt[:, 256 * q : 256 * (q + 1)] = v.T
    keep = lanes((groups, 128))

    def taps(a, _):
        for e in range(3):
            ct_block = ctsh[pl.ds(a, disp), :, 256 * e : 256 * (e + 1)].reshape(disp * cols, 256)
            full = dot(vt[...], ct_block)
            out = None
            for h in range(rows):
                x = full[SLOT * h : SLOT * h + groups, 0:128]
                y = full[SLOT * h : SLOT * h + groups, 128:256]
                if h == 0:
                    term = jnp.where(keep < feat, y, pltpu.roll(x, feat, 1))
                else:
                    term = x if h == 1 else pltpu.roll(x, 128 - feat * (h - 1), 1)
                    if h == rows - 1:
                        term = jnp.where(keep < 2 * feat, term, pltpu.roll(y, feat, 1))
                out = term if out is None else out + term
            pay[a, groups * e : groups * (e + 1)] = jnp.where(keep < 3 * feat, out, 0.0).astype(BF16)
        return 0

    lax.fori_loop(0, 3, taps, 0)


def feature_kernel(group_size, ctsh, w2, fl, fr, fr4, lg, rg0, rg1, rg2, gv, accl, acce, acco):
    disp = ctsh.shape[0] - 2
    rows, cols, channels = lg.shape
    reach = fr.shape[1] - cols - PAD
    wide = group_size * SLOT
    step = 256 // cols
    low = lanes((256, 128)) < SLOT

    def conv(q, _):
        acc = None
        for a in range(3):
            block = ctsh[pl.ds(q * step + a, step)].reshape(256, ctsh.shape[2])
            part = dot(block, w2[a])
            acc = part if acc is None else acc + part
        g = acc.astype(BF16).astype(F32)
        for p in range(rows // 2):
            x = g[:, 128 * p : 128 * (p + 1)]
            r = pltpu.roll(x, SLOT, 1)
            for o in range(2):
                y = jnp.where(low, r, x) if o else jnp.where(low, x, r)
                gv[2 * p + o, pl.ds(q * step, step)] = y.reshape(step, cols, 128)
        return 0

    lax.fori_loop(0, disp // step, conv, 0)
    block = 16

    def left_block(i, _):
        h = lax.div(i, cols // block)
        w = pl.multiple_of(lax.rem(i, cols // block) * block, block)
        accs = [jnp.zeros((block, 128), F32) for _ in range(wide // 128)]
        for d in range(disp):
            band = fr4 if d % 2 else fr
            at = pl.multiple_of(w + reach - 2 * STEP * (d // 2), 8)
            g = gv[h, d, pl.ds(w, block)]
            for j in range(wide // 128):
                accs[j] = accs[j] + g * band[h, pl.ds(at, block), 128 * j : 128 * (j + 1)]
        for j in range(wide // 128):
            accl[h, pl.ds(w, block), 128 * j : 128 * (j + 1)] = accs[j] * (1.0 / group_size)
        return 0

    lax.fori_loop(0, rows * (cols // block), left_block, 0)
    count = cols // 8
    back = acce.shape[1] - cols
    lead = back // 8

    def right_row(h, _):
        for odd, buf in enumerate((acce, acco)):
            for k in range(lead + count):
                accs = [jnp.zeros((8, 128), F32) for _ in range(wide // 128)]
                for t in range(disp // 2):
                    b = k + t - lead
                    if b < 0 or b >= count:
                        continue
                    g = gv[h, 2 * t + odd, 8 * b : 8 * b + 8]
                    for j in range(wide // 128):
                        accs[j] = accs[j] + g * fl[
                            h, PAD + 8 * b : PAD + 8 * b + 8, 128 * j : 128 * (j + 1)
                        ]
                for j in range(wide // 128):
                    buf[h, 8 * k : 8 * k + 8, 128 * j : 128 * (j + 1)] = accs[j]
        acco[h, 8 * (lead + count) :] = jnp.zeros((8, wide), F32)
        return 0

    lax.fori_loop(0, rows, right_row, 0)
    table = channel_table(channels, group_size, True)
    half = cols // 2
    for h in range(rows):
        lg[h] = dot(accl[h].astype(BF16), table).astype(BF16)
        both = acce[h] + acco[h, STEP : STEP + back + cols]
        whole = dot(both.astype(BF16), table).astype(BF16)
        rg2[h] = whole[back - cols - half : back - cols]
        rg1[h] = whole[back - cols : back]
        rg0[h] = whole[back:]


def conv_kernel(masks, vsh, top, bot, wc, wh, out, halo, buf):
    disp, rows, feat, cols = out.shape
    mtop, mbot = masks()
    total = top.shape[1]
    low = lanes((total, 128)) < SLOT
    halo[0] = jnp.zeros(halo.shape[1:], BF16)
    halo[disp + 1] = jnp.zeros(halo.shape[1:], BF16)

    def fill(dd, _):
        t = top[dd].astype(F32) * mtop
        b = bot[dd].astype(F32) * mbot
        buf[0] = jnp.where(low, t, pltpu.roll(b, SLOT, 1))
        buf[1] = jnp.where(low, pltpu.roll(t, SLOT, 1), b)
        for o in range(2):
            for e in range(3):
                halo[2 * dd + o + 1, :, 128 * e : 128 * (e + 1)] = buf[
                    o, PAD - 1 + e : PAD - 1 + e + cols
                ].astype(BF16)
        return 0

    lax.fori_loop(0, disp // 2, fill, 0)
    step = 256 // cols

    def conv(q, _):
        acc = None
        for a in range(3):
            main = vsh[pl.ds(q * step + a, step)].reshape(256, vsh.shape[2])
            side = halo[pl.ds(q * step + a, step)].reshape(256, halo.shape[2])
            part = dot_nt(wc[a], main) + dot_nt(wh[a], side)
            acc = part if acc is None else acc + part
        acc = acc.astype(BF16)
        for i in range(step):
            out[q * step + i] = acc[:, i * cols : (i + 1) * cols].reshape(rows, feat, cols)
        return 0

    lax.fori_loop(0, disp // step, conv, 0)


def finish_kernel(scale, count, *refs):
    parts, (own, near, far, weight, right) = refs[:count], refs[count:]
    _, _, _, feat, groups = weight.shape
    for a in range(3):
        total = tree([ref[a].astype(F32) for ref in parts]) * scale
        for e in range(3):
            x = total[groups * e : groups * (e + 1)].T
            for b in range(3):
                weight[2 - a, 2 - b, 2 - e] = x[feat * b : feat * (b + 1)]
    rows, cols, channels = right.shape
    half = cols // 2
    for h in range(rows):
        total = own[h].astype(F32) + near[h].astype(F32)
        right[h, 0:half] = total[0:half].astype(BF16)
        right[h, half:] = (total[half:] + far[h].astype(F32)).astype(BF16)


def tree(terms):
    while len(terms) > 1:
        terms = [terms[i] + terms[i + 1] for i in range(0, len(terms), 2)]
    return terms[0]


def taps_kernel(taps, w2, wc, wh):
    _, _, _, feat, groups = taps.shape
    rows = wc.shape[1] // feat
    low = lanes((feat, 2 * SLOT)) < SLOT
    zero = jnp.zeros((feat, 2 * SLOT), F32)

    def wide(a, b, e):
        if not 0 <= b <= 2:
            return None
        return jnp.concatenate([taps[a, b, e].astype(F32), zero[:, groups:]], axis=1)

    def beside(x, y):
        if x is None and y is None:
            return zero.astype(BF16)
        x = zero if x is None else x
        y = zero if y is None else pltpu.roll(y, SLOT, 1)
        return jnp.where(low, x, y).astype(BF16)

    def build(a, _):
        for e in range(3):
            for h in range(rows):
                for p in range(rows // 2):
                    lane = SLOT * (rows * e + 2 * p)
                    wc[a, feat * h : feat * (h + 1), lane : lane + 2 * SLOT] = beside(
                        wide(a, 2 * p - h + 1, e), wide(a, 2 * p + 1 - h + 1, e)
                    )
                wh[a, feat * h : feat * (h + 1), 2 * SLOT * e : 2 * SLOT * (e + 1)] = beside(
                    wide(a, 0, e) if h == 0 else None, wide(a, 2, e) if h == rows - 1 else None
                )
            for slot, six in enumerate((*range(1, rows + 1), 0, rows + 1)):
                at = 256 * e + feat * slot
                for p in range(rows // 2):
                    back = [2 - (six - 2 * p - o) for o in range(2)]
                    w2[a, at : at + feat, 2 * SLOT * p : 2 * SLOT * (p + 1)] = beside(
                        wide(2 - a, back[0], 2 - e), wide(2 - a, back[1], 2 - e)
                    )
            at = 256 * e + feat * (rows + 2)
            w2[a, at : 256 * (e + 1)] = jnp.zeros((256 - feat * (rows + 2), rows * SLOT), BF16)
        return 0

    lax.fori_loop(0, 3, build, 0)


def call(kernel, outs, scratch, *args):
    return pl.pallas_call(
        kernel,
        out_shape=[jax.ShapeDtypeStruct(s, t) for s, t in outs],
        in_specs=[VMEM] * len(args),
        out_specs=[VMEM] * len(outs),
        scratch_shapes=scratch,
        compiler_params=params(),
    )(*args)


def col_shift(block, distance):
    n = lax.axis_size("col")
    route = [(i - distance, i) for i in range(n) if 0 <= i - distance < n]
    return lax.ppermute(block, "col", route)


def grid_shift(block, down, distance):
    rows, n = lax.axis_size("row"), lax.axis_size("col")
    route = []
    for r in range(rows):
        for c in range(n):
            if 0 <= r - down < rows and 0 <= c - distance < n:
                route.append(((r - down) * n + c - distance, r * n + c))
    return lax.ppermute(block, ("row", "col"), route)


def grid_swap(block, distance):
    n = lax.axis_size("col")
    route = [
        ((1 - r) * n + c - distance, r * n + c)
        for r in range(2)
        for c in range(n)
        if 0 <= c - distance < n
    ]
    return lax.ppermute(block, ("row", "col"), route)


def halos(pays, distance):
    if lax.axis_size("row") == 2:
        got = grid_swap(pays[0], distance)
        return got, got
    return grid_shift(pays[0], 1, distance), grid_shift(pays[1], -1, distance)


def stages(n_row, n_col):
    col_bits = [1 << i for i in range(n_col.bit_length() - 1)]
    row_bits = [n_col << i for i in range(n_row.bit_length() - 1)]
    assert n_col == 1 << len(col_bits) and n_row == 1 << len(row_bits)
    rest = col_bits[1:2] + row_bits + col_bits[2:]
    out = [col_bits[:1]]
    for i in range(0, len(rest), 2):
        pair = rest[i : i + 2]
        out.append(pair + [sum(pair)] if len(pair) == 2 else pair)
    return out


def on_device(left_features, right_features, conv_weight, cotangent):
    rows, cols, channels = left_features.shape
    disp, feat = cotangent.shape[0], cotangent.shape[3]
    groups = conv_weight.shape[3]
    group_size = channels // groups
    wide = group_size * SLOT
    n_row, n_col = lax.axis_size("row"), lax.axis_size("col")
    per = 128 // feat

    if n_row == 2:
        ends = [lambda: (rows - 1) * (1 - lax.axis_index("row"))]
    else:
        ends = [lambda: rows - 1, lambda: 0]
    n = len(ends)

    def masks():
        at = lax.axis_index("row")
        return (
            jnp.where(at > 0, 1.0, 0.0).astype(F32),
            jnp.where(at < n_row - 1, 1.0, 0.0).astype(F32),
        )

    packed = call(
        functools.partial(pack_kernel, ends),
        [
            ((rows * cols + 32, channels), BF16),
            ((rows * cols // 2, channels), BF16),
            ((32, channels), BF16),
            ((disp, cols, rows * feat), BF16),
        ]
        + [((disp // per * cols, 128), BF16)] * n
        + [((16, 128), BF16)] * (2 * n),
        [pltpu.VMEM((disp * cols, rows * feat), F32), pltpu.VMEM((disp // per * cols, 128), F32)],
        left_features,
        right_features,
        cotangent.transpose(0, 1, 3, 2),
    )
    r1, r2, c1, ctl = packed[:4]
    row_pay, lo_pay, hi_pay = packed[4 : 4 + n], packed[4 + n : 4 + 2 * n], packed[4 + 2 * n :]
    r1 = col_shift(r1, 1)
    top, bot = halos(row_pay, 0)
    r2 = col_shift(r2, 2)
    c1 = col_shift(c1, -1)
    tl, bl = halos(hi_pay, 1)
    tr, br = halos(lo_pay, -1)

    w2, wc, wh = call(
        taps_kernel,
        [
            ((3, 3 * 256, rows * SLOT), BF16),
            ((3, rows * feat, 3 * rows * SLOT), BF16),
            ((3, rows * feat, 3 * 2 * SLOT), BF16),
        ],
        [],
        conv_weight.transpose(0, 1, 2, 4, 3),
    )

    band = 104 + cols + PAD
    volume = call(
        functools.partial(volume_kernel, ends, group_size),
        [
            ((disp + 2, cols, 3 * rows * SLOT), BF16),
            ((rows, cols + 2 * PAD, wide), F32),
            ((rows, band, wide), F32),
            ((rows, band, wide), F32),
        ]
        + [((disp // 2, cols + 2 * PAD, 128), BF16)] * n,
        [pltpu.VMEM((rows // 2, disp, cols + 2 * PAD, 2 * SLOT), F32)],
        left_features,
        right_features,
        r1,
        r2,
        c1,
    )
    vsh, fl, fr, fr4 = volume[:4]
    vtop, vbot = halos(volume[4:], 0)

    part, ctsh = call(
        functools.partial(weight_kernel, masks, groups),
        [((3, 3 * groups, 128), BF16), ((disp + 2, cols, 3 * 256), BF16)],
        [
            pltpu.VMEM((rows * SLOT, disp * cols), BF16),
            pltpu.VMEM((per, cols + 2 * PAD, 256), F32),
            pltpu.VMEM((4, disp, 128), F32),
        ],
        vsh, ctl, r1, c1, top, bot, tl, bl, tr, br,
    )

    parts = None
    for masks_of in stages(n_row, n_col):
        if parts is not None:
            part = tree([x.astype(F32) for x in parts]).astype(BF16)
        parts = [part] + [
            lax.ppermute(part, ("row", "col"), [(i, i ^ m) for i in range(n_row * n_col)])
            for m in masks_of
        ]
    cells = disp * rows * n_row * cols * n_col

    lg, rg0, rg1, rg2 = call(
        functools.partial(feature_kernel, group_size),
        [
            ((rows, cols, channels), BF16),
            ((rows, cols, channels), BF16),
            ((rows, cols, channels), BF16),
            ((rows, cols // 2, channels), BF16),
        ],
        [
            pltpu.VMEM((rows, disp, cols, 128), F32),
            pltpu.VMEM((rows, cols, wide), F32),
            pltpu.VMEM((rows, cols + cols + cols // 2, wide), F32),
            pltpu.VMEM((rows, cols + cols + cols // 2 + 8, wide), F32),
        ],
        ctsh, w2, fl, fr, fr4,
    )
    rg1 = col_shift(rg1, -1)
    rg2 = col_shift(rg2, -2)

    (output,) = call(
        functools.partial(conv_kernel, masks),
        [((disp, rows, feat, cols), BF16)],
        [
            pltpu.VMEM((disp + 2, cols, 3 * 2 * SLOT), BF16),
            pltpu.VMEM((2, cols + 2 * PAD, 128), F32),
        ],
        vsh, vtop, vbot, wc, wh,
    )
    weight_grad, right_grad = call(
        functools.partial(finish_kernel, 1.0 / math.sqrt(cells), len(parts)),
        [((3, 3, 3, feat, groups), F32), ((rows, cols, channels), BF16)],
        [],
        *parts, rg0, rg1, rg2,
    )
    return (
        output.transpose(0, 1, 3, 2),
        weight_grad.transpose(0, 1, 2, 4, 3),
        lg,
        right_grad,
    )


def solution(mesh):
    in_specs = (P("row", "col", None), P("row", "col", None), P(), P(None, "row", "col", None))
    out_specs = (P(None, "row", "col", None), P(), P("row", "col", None), P("row", "col", None))
    return jax.shard_map(
        on_device, mesh=mesh, in_specs=in_specs, out_specs=out_specs, check_vma=False
    )
```

```python
import functools
import math

import jax
import jax.numpy as jnp
from jax import lax
from jax.experimental import pallas as pl
from jax.experimental.pallas import tpu as pltpu
from jax.sharding import PartitionSpec as P

DISP = 24
STEP = 4
SLOT = 64
PAD = 8
F32 = jnp.float32
BF16 = jnp.bfloat16
VMEM = pl.BlockSpec(memory_space=pltpu.VMEM)
LIMIT = 16 * 1024 * 1024


def lanes(shape):
    return lax.broadcasted_iota(jnp.int32, shape, len(shape) - 1)


def channel_table(channels, group_size, flip, value=1.0):
    shape = (group_size * SLOT, channels) if flip else (channels, group_size * SLOT)
    c = lax.broadcasted_iota(jnp.int32, shape, 1 if flip else 0)
    j = lax.broadcasted_iota(jnp.int32, shape, 0 if flip else 1)
    hit = c == (j & (SLOT - 1)) * group_size + (j >> (SLOT.bit_length() - 1))
    return jnp.where(hit, value, 0.0).astype(BF16)


def dot(a, b):
    return jnp.dot(a, b, preferred_element_type=F32)


def dot_nt(a, b):
    return lax.dot_general(a, b, (((1,), (1,)), ((), ())), preferred_element_type=F32)


def pack_kernel(ends, left_hbm, right_hbm, ct_hbm, r2, s1, c1, ctl, left, right, *rest):
    rims, (ctf, ct, sems) = rest[:-3], rest[-3:]
    copies = [
        pltpu.make_async_copy(src, dst, sems.at[i])
        for i, (src, dst) in enumerate(((ct_hbm, ct), (left_hbm, left), (right_hbm, right)))
    ]
    for copy in copies:
        copy.start()
    for copy in copies:
        copy.wait()
    disp, rows, feat, cols = ct.shape
    per = 128 // feat
    r2[...] = right[:, cols // 2 :]
    for end, rim in zip(ends, rims):
        h = end()
        for q in range(disp // per):
            rim[q, PAD : PAD + cols] = jnp.concatenate(
                [ct[q * per + i, h].astype(F32) for i in range(per)], axis=0
            ).T
    for d in range(disp):
        block = ct[d].reshape(rows * feat, cols).astype(F32).T
        ctf[d * cols : (d + 1) * cols] = block
        ctl[d] = block.astype(BF16)
    for ref, col in ((s1, cols - 1), (c1, 0)):
        ref[...] = jnp.zeros(ref.shape, BF16)
        ref[0:disp, 0 : rows * feat] = ctf[pl.ds(col, disp, stride=cols), :].astype(BF16)
        edge = [left[h, col : col + 1].astype(F32) for h in range(rows)]
        edge += [right[h, col : col + 1].astype(F32) for h in range(rows)]
        ref[disp:] = jnp.concatenate(edge, axis=0).astype(BF16)


def row_kernel(ends, rows, s1, c1, *rest):
    n = len(ends)
    rims, pays, (edges, buf) = rest[:n], rest[n : 2 * n], rest[2 * n :]
    count, total, _ = buf.shape
    disp = edges.shape[1]
    per, cols = disp // count, total - 2 * PAD
    feat = 128 // per
    lane = lanes((count, 128))
    for side, ref in enumerate((s1, c1)):
        edges[side] = ref[0:disp, 0:128].astype(F32)
    for end, rim, pay in zip(ends, rims, pays):
        h = end()
        buf[...] = rim[...]
        for side, at in ((0, PAD - 1), (1, PAD + cols)):
            out = jnp.zeros((count, 128), F32)
            for i in range(per):
                x = edges[side, pl.ds(i, count, stride=per)]
                first = pltpu.roll(x, feat * i, 1) if i else x
                last = pltpu.roll(x, (feat * (i - rows + 1)) % 128, 1) if i != rows - 1 else x
                x = jnp.where(h == 0, first, last)
                out = jnp.where((lane >= feat * i) & (lane < feat * (i + 1)), x, out)
            for q in range(count):
                buf[q, at : at + 1] = out[q : q + 1]
        pay[...] = buf[...].astype(BF16)


def volume_kernel(ends, group_size, left, right, r1, r2, s1, c1, vsh, fl, fr, fr4, *rest):
    pays, vbuf = rest[: len(ends)], rest[len(ends)]
    rows, cols, channels = left.shape
    disp = vsh.shape[0] - 2
    reach = fr.shape[1] - cols - PAD
    table = channel_table(channels, group_size, False)
    wide = group_size * SLOT

    def spread(x):
        return dot(x, table)

    base = rows * cols
    edge_r = spread(c1[...])
    far = spread(r2[...].reshape(base // 2, channels))
    near = spread(r1[...].reshape(base, channels))
    own = spread(right[...].reshape(base, channels))
    scaled = channel_table(channels, group_size, False, 1.0 / group_size)
    own_l = dot(left[...].reshape(base, channels), scaled)
    edge_ll = dot(s1[...], scaled)
    edge_lr = dot(c1[...], scaled)
    half = cols // 2
    for h in range(rows):
        fl[h, 0:PAD] = jnp.zeros((PAD, wide), F32)
        fl[h, PAD + cols :] = jnp.zeros((PAD, wide), F32)
        fl[h, PAD - 1 : PAD] = edge_ll[disp + h : disp + h + 1]
        fl[h, PAD : PAD + cols] = own_l[h * cols : (h + 1) * cols]
        fl[h, PAD + cols : PAD + cols + 1] = edge_lr[disp + h : disp + h + 1]
        for ref, off in ((fr, 0), (fr4, STEP)):
            start = reach - cols - half + off
            ref[h, 0:start] = jnp.zeros((start, wide), F32)
            ref[h, start : start + half] = far[h * half : (h + 1) * half]
            ref[h, start + half : start + half + cols] = near[h * cols : (h + 1) * cols]
            ref[h, start + half + cols : start + half + 2 * cols] = own[h * cols : (h + 1) * cols]
            tail = ref.shape[1] - (start + half + 2 * cols)
            ref[h, start + half + 2 * cols :] = jnp.zeros((tail, wide), F32)
            ref[h, start + half + 2 * cols : start + half + 2 * cols + 1] = edge_r[
                disp + rows + h : disp + rows + h + 1
            ]
    vsh[0] = jnp.zeros(vsh.shape[1:], BF16)
    vsh[disp + 1] = jnp.zeros(vsh.shape[1:], BF16)
    total = cols + 2 * PAD
    block = 16
    low = lanes((block, 128)) < SLOT
    pairs = rows // 2

    def products(i, _):
        p, b = lax.rem(i, pairs), lax.div(i, pairs)
        at = pl.multiple_of(b * block, block)
        lefts = [fl[2 * p + o, pl.ds(at, block)] for o in range(2)]
        for d in range(disp):
            band = fr4 if d % 2 else fr
            start = pl.multiple_of(at + reach - PAD - 2 * STEP * (d // 2), 8)
            sums = []
            for o in range(2):
                prod = lefts[o] * band[2 * p + o, pl.ds(start, block)]
                acc = prod[:, 0:128]
                for j in range(1, wide // 128):
                    acc = acc + prod[:, 128 * j : 128 * (j + 1)]
                sums.append(acc + pltpu.roll(acc, SLOT, 1))
            vbuf[p, d, pl.ds(at, block)] = jnp.where(low, sums[0], sums[1])
        return 0

    lax.fori_loop(0, pairs * (total // block), products, 0)
    big = lanes((total, 128)) < SLOT

    def spread_taps(dd, _):
        for odd in range(2):
            d = 2 * dd + odd
            for p in range(pairs):
                for e in range(3):
                    lane = 128 * (pairs * e + p)
                    vsh[d + 1, :, lane : lane + 128] = vbuf[
                        p, d, PAD - 1 + e : PAD - 1 + e + cols
                    ].astype(BF16)
        for end, pay in zip(ends, pays):
            h = end()
            if isinstance(h, int):
                halves = [vbuf[h // 2, 2 * dd + o] for o in range(2)]
                if h % 2 == 0:
                    halves[1] = pltpu.roll(halves[1], SLOT, 1)
                else:
                    halves[0] = pltpu.roll(halves[0], SLOT, 1)
                out = jnp.where(big, halves[0], halves[1])
            else:
                last = pairs - 1
                first = jnp.where(big, vbuf[0, 2 * dd], pltpu.roll(vbuf[0, 2 * dd + 1], SLOT, 1))
                final = jnp.where(
                    big, pltpu.roll(vbuf[last, 2 * dd], SLOT, 1), vbuf[last, 2 * dd + 1]
                )
                out = jnp.where(h == 0, first, final)
            pay[pl.ds(pl.multiple_of(dd * total, 16), total)] = out.astype(BF16)
        return 0

    lax.fori_loop(0, disp // 2, spread_taps, 0)


def weight_kernel(masks, groups, vsh, ctl, s1, c1, top, bot, *rest):
    rider, (pay, ctsh, vt, buf, sums) = rest[:-5], rest[-5:]
    disp, cols, width = ctl.shape
    rows, feat = vsh.shape[2] // 3 // SLOT, 32
    per = 128 // feat
    mtop, mbot = masks()
    base = 0
    for ref in rider:
        pay[base : base + ref.shape[0]] = ref[...]
        base += ref.shape[0]
    ctsh[0] = jnp.zeros(ctsh.shape[1:], BF16)
    ctsh[disp + 1] = jnp.zeros(ctsh.shape[1:], BF16)
    lane = lanes(top.shape[1:])
    edges = [ref[0:disp, 0:128].astype(F32) for ref in (s1, c1)]
    for d in range(disp):
        buf[d, PAD - 1 : PAD, 0:128] = edges[0][d : d + 1]
        buf[d, PAD + cols : PAD + cols + 1, 0:128] = edges[1][d : d + 1]

    def fill(q, _):
        t = top[q].astype(F32) * mtop
        z = bot[q].astype(F32) * mbot
        for i in range(per):
            d = q * per + i
            a = t if i == 0 else pltpu.roll(t, 128 - feat * i, 1)
            y = z if i == 1 else pltpu.roll(z, (128 + feat - feat * i) % 128, 1)
            buf[d, PAD : PAD + cols, 0:128] = ctl[d].astype(F32)
            buf[d, :, 128:256] = jnp.where(lane < feat, a, jnp.where(lane < 2 * feat, y, 0.0))
            for e in range(3):
                ctsh[d + 1, :, 256 * e : 256 * (e + 1)] = buf[
                    d, PAD - 1 + e : PAD - 1 + e + cols
                ].astype(BF16)
        return 0

    lax.fori_loop(0, disp // per, fill, 0)
    step = 256 // cols
    for q in range(disp // step):
        v = vsh[1 + q * step : 1 + (q + 1) * step, :, 256:512].reshape(256, 256)
        vt[:, 256 * q : 256 * (q + 1)] = v.T
    keep = lanes((groups, 128))
    sums[...] = jnp.zeros(sums.shape, F32)

    def taps(a, _):
        for e in range(3):
            ct_block = ctsh[pl.ds(a, disp), :, 256 * e : 256 * (e + 1)].reshape(disp * cols, 256)
            full = dot(vt[...], ct_block)
            out = None
            for h in range(rows):
                x = full[SLOT * h : SLOT * h + groups, 0:128]
                y = full[SLOT * h : SLOT * h + groups, 128:256]
                if h == 0:
                    term = jnp.where(keep < feat, y, pltpu.roll(x, feat, 1))
                else:
                    term = x if h == 1 else pltpu.roll(x, 128 - feat * (h - 1), 1)
                    if h == rows - 1:
                        term = jnp.where(keep < 2 * feat, term, pltpu.roll(y, feat, 1))
                out = term if out is None else out + term
            sums[groups * e : groups * (e + 1)] = jnp.where(keep < 3 * feat, out, 0.0)
        whole = sums[...]
        high = whole.astype(BF16)
        at = base + pl.multiple_of(a * 128, 128)
        pay[pl.ds(at, 128)] = high
        pay[pl.ds(at + 3 * 128, 128)] = (whole - high.astype(F32)).astype(BF16)
        return 0

    lax.fori_loop(0, 3, taps, 0)


def right_kernel(ctsh, w2, fl, gv, rg0, rg1, rg2, acce, acco):
    disp = ctsh.shape[0] - 2
    rows, cols, channels = rg0.shape
    wide = fl.shape[2]
    group_size = wide // SLOT
    step = 512 // cols
    low = lanes((512, 128)) < SLOT

    def conv(q, _):
        acc = None
        for a in range(3):
            block = ctsh[pl.ds(q * step + a, step)].reshape(512, ctsh.shape[2])
            part = dot(block, w2[a])
            acc = part if acc is None else acc + part
        g = acc.astype(BF16).astype(F32)
        for p in range(rows // 2):
            x = g[:, 128 * p : 128 * (p + 1)]
            r = pltpu.roll(x, SLOT, 1)
            for o in range(2):
                y = jnp.where(low, r, x) if o else jnp.where(low, x, r)
                gv[2 * p + o, pl.ds(q * step, step)] = y.reshape(step, cols, 128)
        return 0

    lax.fori_loop(0, disp // step, conv, 0)
    count = cols // 8
    back = acce.shape[1] - cols
    lead = back // 8

    def right_row(h, _):
        for odd, buf in enumerate((acce, acco)):
            for k in range(lead + count):
                accs = [jnp.zeros((8, 128), F32) for _ in range(wide // 128)]
                for t in range(disp // 2):
                    b = k + t - lead
                    if b < 0 or b >= count:
                        continue
                    g = gv[h, 2 * t + odd, 8 * b : 8 * b + 8]
                    for j in range(wide // 128):
                        accs[j] = accs[j] + g * fl[
                            h, PAD + 8 * b : PAD + 8 * b + 8, 128 * j : 128 * (j + 1)
                        ]
                for j in range(wide // 128):
                    buf[h, 8 * k : 8 * k + 8, 128 * j : 128 * (j + 1)] = accs[j]
        acco[h, 8 * (lead + count) :] = jnp.zeros((8, wide), F32)
        return 0

    lax.fori_loop(0, rows, right_row, 0)
    table = channel_table(channels, group_size, True)
    half = cols // 2
    for h in range(rows):
        both = acce[h] + acco[h, STEP : STEP + back + cols]
        whole = dot(both.astype(BF16), table).astype(BF16)
        rg2[h] = whole[back - cols - half : back - cols]
        rg1[h] = whole[back - cols : back]
        rg0[h] = whole[back:]


def left_kernel(gv, fr, fr4, lg, accl):
    rows, cols, channels = lg.shape
    disp, wide = gv.shape[1], fr.shape[2]
    group_size = wide // SLOT
    reach = fr.shape[1] - cols - PAD
    block = 16

    def left_block(i, _):
        h = lax.div(i, cols // block)
        w = pl.multiple_of(lax.rem(i, cols // block) * block, block)
        accs = [jnp.zeros((block, 128), F32) for _ in range(wide // 128)]
        for d in range(disp):
            band = fr4 if d % 2 else fr
            at = pl.multiple_of(w + reach - 2 * STEP * (d // 2), 8)
            g = gv[h, d, pl.ds(w, block)]
            for j in range(wide // 128):
                accs[j] = accs[j] + g * band[h, pl.ds(at, block), 128 * j : 128 * (j + 1)]
        for j in range(wide // 128):
            accl[h, pl.ds(w, block), 128 * j : 128 * (j + 1)] = accs[j] * (1.0 / group_size)
        return 0

    lax.fori_loop(0, rows * (cols // block), left_block, 0)
    table = channel_table(channels, group_size, True)
    for h in range(rows):
        lg[h] = dot(accl[h].astype(BF16), table).astype(BF16)


def conv_kernel(masks, vsh, top, bot, wc, wh, out, halo, buf, acc):
    disp, rows, feat, cols = out.shape
    mtop, mbot = masks()
    total = buf.shape[1]
    low = lanes((total, 128)) < SLOT

    def fill(dd, _):
        at = pl.multiple_of(dd * total, 16)
        t = top[pl.ds(at, total)].astype(F32) * mtop
        b = bot[pl.ds(at, total)].astype(F32) * mbot
        buf[2 * dd] = jnp.where(low, t, pltpu.roll(b, SLOT, 1))
        buf[2 * dd + 1] = jnp.where(low, pltpu.roll(t, SLOT, 1), b)
        for o in range(2):
            for e in range(3):
                halo[2 * dd + o, :, 128 * e : 128 * (e + 1)] = buf[
                    2 * dd + o, PAD - 1 + e : PAD - 1 + e + cols
                ].astype(BF16)
        return 0

    lax.fori_loop(0, disp // 2, fill, 0)
    acc[...] = jnp.zeros(acc.shape, F32)
    half = disp // 2
    size = rows * feat

    def conv(jj, _):
        order = [2 * jj, 2 * jj + half, 2 * jj + 1, 2 * jj + 1 + half]
        main = jnp.concatenate([vsh[1 + d] for d in order], axis=0)
        side = jnp.concatenate([halo[d] for d in order], axis=0)
        taps = dot_nt(wc[...], main) + dot_nt(wh[...], side)
        for o in range(2):
            for a in range(3):
                at = 2 * jj + o + 2 - a
                acc[at] = acc[at] + taps[size * a : size * (a + 1), 128 * o : 128 * (o + 1)]
        return 0

    lax.fori_loop(0, half // 2, conv, 0)
    left = lanes((size, 128)) < cols
    acc[half] = acc[half] + jnp.where(left, pltpu.roll(acc[0], cols, 1), 0.0)
    acc[1] = acc[1] + jnp.where(left, 0.0, pltpu.roll(acc[half + 1], cols, 1))

    def store(j, _):
        x = acc[j + 1]
        out[j] = x[:, 0:cols].astype(BF16).reshape(rows, feat, cols)
        y = pltpu.roll(x, cols, 1)
        out[j + half] = y[:, 0:cols].astype(BF16).reshape(rows, feat, cols)
        return 0

    lax.fori_loop(0, half, store, 0)


def finish_kernel(scale, count, *refs):
    parts, (own, near, far, weight, right) = refs[:count], refs[count:]
    _, _, _, feat, groups = weight.shape
    for a in range(3):
        total = tree([ref[128 * a : 128 * (a + 1)].astype(F32) for ref in parts]) * scale
        for e in range(3):
            x = total[groups * e : groups * (e + 1)].T
            for b in range(3):
                weight[2 - a, 2 - b, 2 - e] = x[feat * b : feat * (b + 1)]
    rows, cols, channels = right.shape
    half = cols // 2
    for h in range(rows):
        total = own[h].astype(F32) + near[h].astype(F32)
        right[h, 0:half] = total[0:half].astype(BF16)
        right[h, half:] = (total[half:] + far[h].astype(F32)).astype(BF16)


def join_kernel(base, own, other, out):
    rows = out.shape[0]
    terms = []
    for ref in (own, other):
        terms.append(ref[base : base + rows].astype(F32) + ref[base + rows :].astype(F32))
    out[...] = tree(terms).astype(BF16)


def sum_kernel(*refs):
    *parts, out = refs
    out[...] = tree([ref[...].astype(F32) for ref in parts]).astype(BF16)


def tree(terms):
    while len(terms) > 1:
        terms = [terms[i] + terms[i + 1] for i in range(0, len(terms), 2)]
    return terms[0]


def taps_kernel(taps, w2, wc, wh):
    _, _, _, feat, groups = taps.shape
    rows = wc.shape[0] // 3 // feat
    low = lanes((feat, 2 * SLOT)) < SLOT
    zero = jnp.zeros((feat, 2 * SLOT), F32)

    def wide(a, b, e):
        if not 0 <= b <= 2:
            return None
        return jnp.concatenate([taps[a, b, e].astype(F32), zero[:, groups:]], axis=1)

    def beside(x, y):
        if x is None and y is None:
            return zero.astype(BF16)
        x = zero if x is None else x
        y = zero if y is None else pltpu.roll(y, SLOT, 1)
        return jnp.where(low, x, y).astype(BF16)

    def build(a, _):
        def at_row(h):
            return pl.multiple_of((a * rows + h) * feat, feat)

        for e in range(3):
            for h in range(rows):
                for p in range(rows // 2):
                    lane = SLOT * (rows * e + 2 * p)
                    wc[pl.ds(at_row(h), feat), lane : lane + 2 * SLOT] = beside(
                        wide(a, 2 * p - h + 1, e), wide(a, 2 * p + 1 - h + 1, e)
                    )
                wh[pl.ds(at_row(h), feat), 2 * SLOT * e : 2 * SLOT * (e + 1)] = beside(
                    wide(a, 0, e) if h == 0 else None, wide(a, 2, e) if h == rows - 1 else None
                )
            for slot, six in enumerate((*range(1, rows + 1), 0, rows + 1)):
                at = 256 * e + feat * slot
                for p in range(rows // 2):
                    back = [2 - (six - 2 * p - o) for o in range(2)]
                    w2[a, at : at + feat, 2 * SLOT * p : 2 * SLOT * (p + 1)] = beside(
                        wide(2 - a, back[0], 2 - e), wide(2 - a, back[1], 2 - e)
                    )
            at = 256 * e + feat * (rows + 2)
            w2[a, at : 256 * (e + 1)] = jnp.zeros((256 - feat * (rows + 2), rows * SLOT), BF16)
        return 0

    lax.fori_loop(0, 3, build, 0)


TOKEN = ((8, 128), F32)


def with_token(kernel, inputs, outputs):
    def run(*refs):
        kernel(*refs[: inputs + outputs], *refs[inputs + outputs + 1 :])
        refs[inputs + outputs][...] = jnp.zeros(TOKEN[0], F32)

    return run


def call(kernel, outs, scratch, *args, after=(), token=False, specs=None):
    skip = len(after)
    if token:
        kernel = with_token(kernel, len(args), len(outs))
        outs = [*outs, TOKEN]
    return pl.pallas_call(
        lambda *refs: kernel(*refs[skip:]),
        out_shape=[jax.ShapeDtypeStruct(s, t) for s, t in outs],
        in_specs=[pl.BlockSpec(memory_space=pl.ANY)] * skip + (specs or [VMEM] * len(args)),
        out_specs=[VMEM] * len(outs),
        scratch_shapes=scratch,
        compiler_params=pltpu.CompilerParams(vmem_limit_bytes=LIMIT),
    )(*after, *args)


def col_shift(block, distance):
    n = lax.axis_size("col")
    route = [(i - distance, i) for i in range(n) if 0 <= i - distance < n]
    return lax.ppermute(block, "col", route)


def row_shift(block, distance):
    n = lax.axis_size("row")
    route = [(i - distance, i) for i in range(n) if 0 <= i - distance < n]
    return lax.ppermute(block, "row", route)


def halos(pays):
    if lax.axis_size("row") == 2:
        got = lax.ppermute(pays[0], "row", [(0, 1), (1, 0)])
        return got, got
    return row_shift(pays[0], 1), row_shift(pays[1], -1)


def stages(n_row, n_col):
    bits = [1 << i for i in range((n_row * n_col).bit_length() - 1)]
    assert n_row * n_col == 1 << len(bits) and n_col & (n_col - 1) == 0
    first = n_col if n_row > 1 else 1
    bits.remove(first)
    out = [[first]]
    for i in range(0, len(bits), 2):
        pair = bits[i : i + 2]
        out.append(pair + [sum(pair)] if len(pair) == 2 else pair)
    return out


def on_device(left_features, right_features, conv_weight, cotangent):
    rows, cols, channels = left_features.shape
    disp, feat = cotangent.shape[0], cotangent.shape[3]
    groups = conv_weight.shape[3]
    group_size = channels // groups
    wide = group_size * SLOT
    n_row, n_col = lax.axis_size("row"), lax.axis_size("col")
    per = 128 // feat

    if n_row == 2:
        ends = [lambda: (rows - 1) * (1 - lax.axis_index("row"))]
    else:
        ends = [lambda: rows - 1, lambda: 0]
    n = len(ends)

    def masks():
        at = lax.axis_index("row")
        return (
            jnp.where(at > 0, 1.0, 0.0).astype(F32),
            jnp.where(at < n_row - 1, 1.0, 0.0).astype(F32),
        )

    total = cols + 2 * PAD
    r1 = col_shift(right_features, 1)
    ct = cotangent.transpose(0, 1, 3, 2)
    r2, s1, c1, ctl, left_here, right_here, *rims = call(
        functools.partial(pack_kernel, ends),
        [
            ((rows, cols // 2, channels), BF16),
            ((disp + 2 * rows, channels), BF16),
            ((disp + 2 * rows, channels), BF16),
            ((disp, cols, rows * feat), BF16),
            ((rows, cols, channels), BF16),
            ((rows, cols, channels), BF16),
        ]
        + [((disp // per, total, 128), F32)] * n,
        [
            pltpu.VMEM((disp * cols, rows * feat), F32),
            pltpu.VMEM((disp, rows, feat, cols), BF16),
            pltpu.SemaphoreType.DMA((3,)),
        ],
        left_features,
        right_features,
        ct,
        specs=[pl.BlockSpec(memory_space=pltpu.HBM)] * 3,
    )
    s1 = col_shift(s1, 1)
    c1 = col_shift(c1, -1)
    r2 = col_shift(r2, 2)
    row_pays = call(
        functools.partial(row_kernel, ends, rows),
        [((disp // per, total, 128), BF16)] * n,
        [pltpu.VMEM((2, disp, 128), F32), pltpu.VMEM((disp // per, total, 128), F32)],
        s1,
        c1,
        *rims,
    )
    top, bot = halos(row_pays)

    w2, wc, wh = call(
        taps_kernel,
        [
            ((3, 3 * 256, rows * SLOT), BF16),
            ((3 * rows * feat, 3 * rows * SLOT), BF16),
            ((3 * rows * feat, 3 * 2 * SLOT), BF16),
        ],
        [],
        conv_weight.transpose(0, 1, 2, 4, 3),
    )

    band = 104 + cols + PAD
    volume = call(
        functools.partial(volume_kernel, ends, group_size),
        [
            ((disp + 2, cols, 3 * rows * SLOT), BF16),
            ((rows, cols + 2 * PAD, wide), F32),
            ((rows, band, wide), F32),
            ((rows, band, wide), F32),
        ]
        + [((disp // 2 * total, 128), BF16)] * n,
        [pltpu.VMEM((rows // 2, disp, cols + 2 * PAD, 2 * SLOT), F32)],
        left_here,
        right_here,
        r1,
        r2,
        s1,
        c1,
        after=[w2],
    )
    vsh, fl, fr, fr4 = volume[:4]
    riders = volume[4:] if n_row == 2 else []
    base = disp // 2 * total * len(riders)
    pay, ctsh = call(
        functools.partial(weight_kernel, masks, groups),
        [((base + 6 * 128, 128), BF16), ((disp + 2, cols, 3 * 256), BF16)],
        [
            pltpu.VMEM((rows * SLOT, disp * cols), BF16),
            pltpu.VMEM((disp, total, 256), F32),
            pltpu.VMEM((128, 128), F32),
        ],
        vsh, ctl, s1, c1, top, bot, *riders,
    )
    first, *later = stages(n_row, n_col)

    def swap(block, mask):
        route = [(i, i ^ mask) for i in range(n_row * n_col)]
        return lax.ppermute(block, ("row", "col"), route)

    met = swap(pay, first[0])
    vtop, vbot = (met, met) if riders else halos(volume[4:])

    gv, rg0, rg1, rg2 = call(
        right_kernel,
        [
            ((rows, disp, cols, 128), F32),
            ((rows, cols, channels), BF16),
            ((rows, cols, channels), BF16),
            ((rows, cols // 2, channels), BF16),
        ],
        [
            pltpu.VMEM((rows, cols + cols + cols // 2, wide), F32),
            pltpu.VMEM((rows, cols + cols + cols // 2 + 8, wide), F32),
        ],
        ctsh, w2, fl,
    )
    rg1 = col_shift(rg1, -1)
    rg2 = col_shift(rg2, -2)

    (part,) = call(
        functools.partial(join_kernel, base), [((3 * 128, 128), BF16)], [], pay, met, after=[rg0]
    )
    output, conv_done = call(
        functools.partial(conv_kernel, masks),
        [((disp, rows, feat, cols), BF16)],
        [
            pltpu.VMEM((disp, cols, 3 * 2 * SLOT), BF16),
            pltpu.VMEM((disp, total, 128), F32),
            pltpu.VMEM((disp // 2 + 2, rows * feat, 128), F32),
        ],
        vsh, vtop, vbot, wc, wh,
        after=[part],
        token=True,
    )
    after = [conv_done]
    for stage in later[:-1]:
        (part,) = call(
            sum_kernel, [(part.shape, BF16)], [], part, *[swap(part, m) for m in stage], after=after
        )
        after = []
    parts = [part] + [swap(part, m) for m in later[-1]]
    cells = disp * rows * n_row * cols * n_col

    lg, left_done = call(
        left_kernel,
        [((rows, cols, channels), BF16)],
        [pltpu.VMEM((rows, cols, wide), F32)],
        gv, fr, fr4,
        after=[part],
        token=True,
    )

    weight_grad, right_grad = call(
        functools.partial(finish_kernel, 1.0 / math.sqrt(cells), len(parts)),
        [((3, 3, 3, feat, groups), F32), ((rows, cols, channels), BF16)],
        [],
        *parts, rg0, rg1, rg2,
        after=[left_done],
    )
    return (
        output.transpose(0, 1, 3, 2),
        weight_grad.transpose(0, 1, 2, 4, 3),
        lg,
        right_grad,
    )


def solution(mesh):
    in_specs = (P("row", "col", None), P("row", "col", None), P(), P(None, "row", "col", None))
    out_specs = (P(None, "row", "col", None), P(), P("row", "col", None), P("row", "col", None))
    return jax.shard_map(
        on_device, mesh=mesh, in_specs=in_specs, out_specs=out_specs, check_vma=False
    )
```

```python
import functools
import math

import jax
import jax.numpy as jnp
from jax import lax
from jax.experimental import pallas as pl
from jax.experimental.pallas import tpu as pltpu
from jax.sharding import PartitionSpec as P

DISP = 24
STEP = 4
SLOT = 64
PAD = 8
F32 = jnp.float32
BF16 = jnp.bfloat16
VMEM = pl.BlockSpec(memory_space=pltpu.VMEM)
LIMIT = 16 * 1024 * 1024
BIG = 60 * 1024 * 1024


def lanes(shape):
    return lax.broadcasted_iota(jnp.int32, shape, len(shape) - 1)


def channel_table(channels, group_size, flip, value=1.0):
    shape = (group_size * SLOT, channels) if flip else (channels, group_size * SLOT)
    c = lax.broadcasted_iota(jnp.int32, shape, 1 if flip else 0)
    j = lax.broadcasted_iota(jnp.int32, shape, 0 if flip else 1)
    hit = c == (j & (SLOT - 1)) * group_size + (j >> (SLOT.bit_length() - 1))
    return jnp.where(hit, value, 0.0).astype(BF16)


def parity():
    return lax.rem(lax.axis_index("col"), 2)


def dot(a, b):
    return jnp.dot(a, b, preferred_element_type=F32)


def dot_nt(a, b):
    return lax.dot_general(a, b, (((1,), (1,)), ((), ())), preferred_element_type=F32)


def pack_kernel(left, right, ct, even, odd, r2, ctf):
    disp, rows, feat, cols = ct.shape
    base = rows * cols
    r2[...] = right[:, cols // 2 :]
    for h in range(rows):
        even[h * cols : (h + 1) * cols] = right[h]
        odd[h * cols : (h + 1) * cols] = right[h]
    for d in range(disp):
        ctf[d * cols : (d + 1) * cols] = ct[d].reshape(rows * feat, cols).astype(F32).T
    ends = []
    for col in (cols - 1, 0):
        block = ctf[pl.ds(col, disp, stride=cols), :]
        block = jnp.concatenate([block, jnp.zeros((disp, left.shape[2] - rows * feat), F32)], axis=1)
        edge = [left[h, col : col + 1].astype(F32) for h in range(rows)]
        edge += [right[h, col : col + 1].astype(F32) for h in range(rows)]
        ends.append(jnp.concatenate([block, *edge], axis=0))
    is_even = parity() == 0
    even[base:] = jnp.where(is_even, ends[0], ends[1]).astype(BF16)
    odd[base:] = jnp.where(is_even, ends[1], ends[0]).astype(BF16)


def layout_kernel(ends, left_in, right_in, ct, left, right, ctl, *rims):
    disp, rows, feat, cols = ct.shape
    per = 128 // feat
    left[...] = left_in[...]
    right[...] = right_in[...]
    for d in range(disp):
        ctl[d] = ct[d].reshape(rows * feat, cols).astype(F32).T.astype(BF16)
    for end, rim in zip(ends, rims):
        h = end()
        for q in range(disp // per):
            rim[q, PAD : PAD + cols] = jnp.concatenate(
                [ct[q * per + i, h].astype(F32) for i in range(per)], axis=0
            ).T


def end_columns(by_even, by_odd, base):
    x, y = by_even[base:].astype(F32), by_odd[base:].astype(F32)
    is_even = parity() == 0
    return jnp.where(is_even, y, x), jnp.where(is_even, x, y)


def row_kernel(ends, rows, by_even, by_odd, *rest):
    n = len(ends)
    rims, pays, (edges, buf) = rest[:n], rest[n : 2 * n], rest[2 * n :]
    count, total, _ = buf.shape
    disp = edges.shape[1]
    per, cols = disp // count, total - 2 * PAD
    feat = 128 // per
    lane = lanes((count, 128))
    for side, x in enumerate(end_columns(by_even, by_odd, rows * cols)):
        edges[side] = x[0:disp, 0:128]
    for end, rim, pay in zip(ends, rims, pays):
        h = end()
        buf[...] = rim[...]
        for side, at in ((0, PAD - 1), (1, PAD + cols)):
            out = jnp.zeros((count, 128), F32)
            for i in range(per):
                x = edges[side, pl.ds(i, count, stride=per)]
                first = pltpu.roll(x, feat * i, 1) if i else x
                last = pltpu.roll(x, (feat * (i - rows + 1)) % 128, 1) if i != rows - 1 else x
                x = jnp.where(h == 0, first, last)
                out = jnp.where((lane >= feat * i) & (lane < feat * (i + 1)), x, out)
            for q in range(count):
                buf[q, at : at + 1] = out[q : q + 1]
        pay[...] = buf[...].astype(BF16)


def volume_kernel(ends, group_size, left, right, by_even, by_odd, r2, vsh, fl, fr, fr4, *rest):
    pays, (vbuf, mixed, wide_buf) = rest[: len(ends)], rest[len(ends) :]
    rows, cols, channels = left.shape
    disp = vsh.shape[0] - 2
    reach = fr.shape[1] - cols - PAD
    wide = group_size * SLOT
    base, half = rows * cols, cols // 2
    is_even = parity() == 0
    mixed[0:base] = jnp.where(is_even, by_odd[0:base].astype(F32), by_even[0:base].astype(F32)).astype(
        BF16
    )
    mixed[base : 2 * base] = right[...].reshape(base, channels)
    mixed[2 * base : 3 * base] = left[...].reshape(base, channels)
    at_far, at_ends = 3 * base, 3 * base + base // 2
    mixed[at_far:at_ends] = r2[...].reshape(base // 2, channels)
    count = disp + 2 * rows
    for i, x in enumerate(end_columns(by_even, by_odd, base)):
        mixed[at_ends + i * count : at_ends + (i + 1) * count] = x.astype(BF16)
    wide_buf[...] = dot(mixed[...], channel_table(channels, group_size, False))
    scale = 1.0 / group_size
    for h in range(rows):
        fl[h, 0:PAD] = jnp.zeros((PAD, wide), F32)
        fl[h, PAD + cols :] = jnp.zeros((PAD, wide), F32)
        at = at_ends + disp + h
        fl[h, PAD - 1 : PAD] = wide_buf[at : at + 1] * scale
        fl[h, PAD : PAD + cols] = wide_buf[2 * base + h * cols : 2 * base + (h + 1) * cols] * scale
        at += count
        fl[h, PAD + cols : PAD + cols + 1] = wide_buf[at : at + 1] * scale
        for ref, off in ((fr, 0), (fr4, STEP)):
            start = reach - cols - half + off
            ref[h, 0:start] = jnp.zeros((start, wide), F32)
            ref[h, start : start + half] = wide_buf[at_far + h * half : at_far + (h + 1) * half]
            for part in range(2):
                at = part * base + h * cols
                to = start + half + part * cols
                ref[h, to : to + cols] = wide_buf[at : at + cols]
            to = start + half + 2 * cols
            ref[h, to:] = jnp.zeros((ref.shape[1] - to, wide), F32)
            at = at_ends + count + disp + rows + h
            ref[h, to : to + 1] = wide_buf[at : at + 1]
    vsh[0] = jnp.zeros(vsh.shape[1:], BF16)
    vsh[disp + 1] = jnp.zeros(vsh.shape[1:], BF16)
    total = cols + 2 * PAD
    block = 16
    low = lanes((block, 128)) < SLOT
    pairs = rows // 2

    def products(i, _):
        p, b = lax.rem(i, pairs), lax.div(i, pairs)
        at = pl.multiple_of(b * block, block)
        lefts = [fl[2 * p + o, pl.ds(at, block)] for o in range(2)]
        for d in range(disp):
            band = fr4 if d % 2 else fr
            start = pl.multiple_of(at + reach - PAD - 2 * STEP * (d // 2), 8)
            sums = []
            for o in range(2):
                prod = lefts[o] * band[2 * p + o, pl.ds(start, block)]
                acc = prod[:, 0:128]
                for j in range(1, wide // 128):
                    acc = acc + prod[:, 128 * j : 128 * (j + 1)]
                sums.append(acc + pltpu.roll(acc, SLOT, 1))
            vbuf[p, d, pl.ds(at, block)] = jnp.where(low, sums[0], sums[1])
        return 0

    lax.fori_loop(0, pairs * (total // block), products, 0)
    big = lanes((total, 128)) < SLOT

    def spread_taps(dd, _):
        for odd in range(2):
            d = 2 * dd + odd
            for p in range(pairs):
                for e in range(3):
                    lane = 128 * (pairs * e + p)
                    vsh[d + 1, :, lane : lane + 128] = vbuf[
                        p, d, PAD - 1 + e : PAD - 1 + e + cols
                    ].astype(BF16)
        for end, pay in zip(ends, pays):
            h = end()
            if isinstance(h, int):
                halves = [vbuf[h // 2, 2 * dd + o] for o in range(2)]
                if h % 2 == 0:
                    halves[1] = pltpu.roll(halves[1], SLOT, 1)
                else:
                    halves[0] = pltpu.roll(halves[0], SLOT, 1)
                out = jnp.where(big, halves[0], halves[1])
            else:
                last = pairs - 1
                first = jnp.where(big, vbuf[0, 2 * dd], pltpu.roll(vbuf[0, 2 * dd + 1], SLOT, 1))
                final = jnp.where(
                    big, pltpu.roll(vbuf[last, 2 * dd], SLOT, 1), vbuf[last, 2 * dd + 1]
                )
                out = jnp.where(h == 0, first, final)
            pay[pl.ds(pl.multiple_of(dd * total, 16), total)] = out.astype(BF16)
        return 0

    lax.fori_loop(0, disp // 2, spread_taps, 0)


def weight_kernel(masks, groups, vsh, ctl, by_even, by_odd, top, bot, keep_out, give_out, ctsh, vt, buf, sums):
    disp, cols, width = ctl.shape
    rows, feat = vsh.shape[2] // 3 // SLOT, 32
    per = 128 // feat
    mtop, mbot = masks()
    ctsh[0] = jnp.zeros(ctsh.shape[1:], BF16)
    ctsh[disp + 1] = jnp.zeros(ctsh.shape[1:], BF16)
    lane = lanes(top.shape[1:])
    edges = [x[0:disp, 0:128] for x in end_columns(by_even, by_odd, rows * cols)]
    for d in range(disp):
        buf[d, PAD - 1 : PAD, 0:128] = edges[0][d : d + 1]
        buf[d, PAD + cols : PAD + cols + 1, 0:128] = edges[1][d : d + 1]

    def fill(q, _):
        t = top[q].astype(F32) * mtop
        z = bot[q].astype(F32) * mbot
        for i in range(per):
            d = q * per + i
            a = t if i == 0 else pltpu.roll(t, 128 - feat * i, 1)
            y = z if i == 1 else pltpu.roll(z, (128 + feat - feat * i) % 128, 1)
            buf[d, PAD : PAD + cols, 0:128] = ctl[d].astype(F32)
            buf[d, :, 128:256] = jnp.where(lane < feat, a, jnp.where(lane < 2 * feat, y, 0.0))
            for e in range(3):
                ctsh[d + 1, :, 256 * e : 256 * (e + 1)] = buf[
                    d, PAD - 1 + e : PAD - 1 + e + cols
                ].astype(BF16)
        return 0

    lax.fori_loop(0, disp // per, fill, 0)
    step = 256 // cols
    for q in range(disp // step):
        v = vsh[1 + q * step : 1 + (q + 1) * step, :, 256:512].reshape(256, 256)
        vt[:, 256 * q : 256 * (q + 1)] = v.T
    keep = lanes((groups, 128))
    sums[...] = jnp.zeros(sums.shape, F32)

    def taps(a, _):
        for e in range(3):
            ct_block = ctsh[pl.ds(a, disp), :, 256 * e : 256 * (e + 1)].reshape(disp * cols, 256)
            full = dot(vt[...], ct_block)
            out = None
            for h in range(rows):
                x = full[SLOT * h : SLOT * h + groups, 0:128]
                y = full[SLOT * h : SLOT * h + groups, 128:256]
                if h == 0:
                    term = jnp.where(keep < feat, y, pltpu.roll(x, feat, 1))
                else:
                    term = x if h == 1 else pltpu.roll(x, 128 - feat * (h - 1), 1)
                    if h == rows - 1:
                        term = jnp.where(keep < 2 * feat, term, pltpu.roll(y, feat, 1))
                out = term if out is None else out + term
            at = pl.multiple_of(a * 128 + groups * e, 8)
            sums[pl.ds(at, groups)] = jnp.where(keep < 3 * feat, out, 0.0)
        return 0

    lax.fori_loop(0, 3, taps, 0)
    half = sums.shape[0] // 2
    is_even = parity() == 0
    low, high = sums[0:half], sums[half:]
    keep_out[...] = jnp.where(is_even, low, high)
    give_out[...] = jnp.where(is_even, high, low)


def right_kernel(ctsh, w2, fl, gv, rg0, rg1, rg2, acce, acco, both):
    disp = ctsh.shape[0] - 2
    rows, cols, channels = rg0.shape
    wide = fl.shape[2]
    group_size = wide // SLOT
    step = 512 // cols
    low = lanes((512, 128)) < SLOT

    def conv(q, _):
        acc = None
        for a in range(3):
            block = ctsh[pl.ds(q * step + a, step)].reshape(512, ctsh.shape[2])
            part = dot(block, w2[a])
            acc = part if acc is None else acc + part
        g = acc.astype(BF16).astype(F32)
        for p in range(rows // 2):
            x = g[:, 128 * p : 128 * (p + 1)]
            r = pltpu.roll(x, SLOT, 1)
            for o in range(2):
                y = jnp.where(low, r, x) if o else jnp.where(low, x, r)
                gv[2 * p + o, pl.ds(q * step, step)] = y.reshape(step, cols, 128)
        return 0

    lax.fori_loop(0, disp // step, conv, 0)
    count = cols // 8
    back = acce.shape[1] - cols
    lead = back // 8

    def right_row(h, _):
        for odd, buf in enumerate((acce, acco)):
            for k in range(lead + count):
                accs = [jnp.zeros((8, 128), F32) for _ in range(wide // 128)]
                for t in range(disp // 2):
                    b = k + t - lead
                    if b < 0 or b >= count:
                        continue
                    g = gv[h, 2 * t + odd, 8 * b : 8 * b + 8]
                    for j in range(wide // 128):
                        accs[j] = accs[j] + g * fl[
                            h, PAD + 8 * b : PAD + 8 * b + 8, 128 * j : 128 * (j + 1)
                        ]
                for j in range(wide // 128):
                    buf[h, 8 * k : 8 * k + 8, 128 * j : 128 * (j + 1)] = accs[j]
        acco[h, 8 * (lead + count) :] = jnp.zeros((8, wide), F32)
        return 0

    lax.fori_loop(0, rows, right_row, 0)
    size = back + cols
    for h in range(rows):
        both[h * size : (h + 1) * size] = (acce[h] + acco[h, STEP : STEP + size]).astype(BF16)
    whole = dot(both[...], channel_table(channels, group_size, True)).astype(BF16)
    half = cols // 2
    for h in range(rows):
        at = h * size + back
        rg2[h] = whole[at - cols - half : at - cols]
        rg1[h] = whole[at - cols : at]
        rg0[h] = whole[at : at + cols]


def left_kernel(gv, fr, fr4, lg, accl):
    rows, cols, channels = lg.shape
    disp, wide = gv.shape[1], fr.shape[2]
    group_size = wide // SLOT
    reach = fr.shape[1] - cols - PAD
    block = 16

    def left_block(i, _):
        h = lax.div(i, cols // block)
        w = pl.multiple_of(lax.rem(i, cols // block) * block, block)
        accs = [jnp.zeros((block, 128), F32) for _ in range(wide // 128)]
        for d in range(disp):
            band = fr4 if d % 2 else fr
            at = pl.multiple_of(w + reach - 2 * STEP * (d // 2), 8)
            g = gv[h, d, pl.ds(w, block)]
            for j in range(wide // 128):
                accs[j] = accs[j] + g * band[h, pl.ds(at, block), 128 * j : 128 * (j + 1)]
        for j in range(wide // 128):
            accl[h, pl.ds(w, block), 128 * j : 128 * (j + 1)] = accs[j] * (1.0 / group_size)
        return 0

    lax.fori_loop(0, rows * (cols // block), left_block, 0)
    whole = accl[...].reshape(rows * cols, wide).astype(BF16)
    out = dot(whole, channel_table(channels, group_size, True)).astype(BF16)
    lg[...] = out.reshape(rows, cols, channels)


def combine_kernel(got, rg2, out):
    cols = out.shape[1]
    half = cols // 2
    part = jnp.where(parity() == 0, 0.0, got[...].astype(F32))
    out[:, 0:half] = part[:, 0:half].astype(BF16)
    out[:, half:] = (part[:, half:] + rg2[...].astype(F32)).astype(BF16)


def conv_kernel(masks, vsh, top, bot, wc, out, halo, buf, acc):
    disp, rows, feat, cols = out.shape
    mtop, mbot = masks()
    total = buf.shape[1]
    low = lanes((total, 128)) < SLOT

    def fill(dd, _):
        at = pl.multiple_of(dd * total, 16)
        t = top[pl.ds(at, total)].astype(F32) * mtop
        b = bot[pl.ds(at, total)].astype(F32) * mbot
        buf[2 * dd] = jnp.where(low, t, pltpu.roll(b, SLOT, 1))
        buf[2 * dd + 1] = jnp.where(low, pltpu.roll(t, SLOT, 1), b)
        for o in range(2):
            for e in range(3):
                halo[2 * dd + o, :, 128 * e : 128 * (e + 1)] = buf[
                    2 * dd + o, PAD - 1 + e : PAD - 1 + e + cols
                ].astype(BF16)
        return 0

    lax.fori_loop(0, disp // 2, fill, 0)
    acc[...] = jnp.zeros(acc.shape, F32)
    step, size, depth = 512 // cols, rows * feat, vsh.shape[2]

    def conv(q, _):
        main = vsh[pl.ds(q * step + 1, step)].reshape(512, depth)
        side = halo[pl.ds(q * step, step)].reshape(512, halo.shape[2])
        taps = dot(main, wc[0:depth]) + dot(side, wc[depth:])
        for a in range(3):
            at = pl.ds(q * step + 2 - a, step)
            acc[at] = acc[at] + taps[:, size * a : size * (a + 1)].reshape(step, cols, size)
        return 0

    lax.fori_loop(0, disp // step, conv, 0)

    def store(j, _):
        x = acc[pl.ds(2 * j + 1, 2)].reshape(2 * cols, size).T
        out[2 * j] = x[:, 0:cols].astype(BF16).reshape(rows, feat, cols)
        y = pltpu.roll(x, cols, 1)
        out[2 * j + 1] = y[:, 0:cols].astype(BF16).reshape(rows, feat, cols)
        return 0

    lax.fori_loop(0, disp // 2, store, 0)


def finish_kernel(scale, mine, other, own, near, far, weight, right):
    _, _, _, feat, groups = weight.shape
    is_even = parity() == 0
    x, y = mine[...] * scale, other[...] * scale
    total = jnp.concatenate([jnp.where(is_even, x, y), jnp.where(is_even, y, x)], axis=0)
    for a in range(3):
        for e in range(3):
            at = 128 * a + groups * e
            block = total[at : at + groups].T
            for b in range(3):
                weight[2 - a, 2 - b, 2 - e] = block[feat * b : feat * (b + 1)]
    beside = jnp.where(is_even, near[...].astype(F32), 0.0)
    right[...] = (own[...].astype(F32) + beside + far[...].astype(F32)).astype(BF16)


def sum_kernel(*refs):
    *parts, out = refs
    out[...] = tree([ref[...].astype(F32) for ref in parts]).astype(out.dtype)


def tree(terms):
    while len(terms) > 1:
        terms = [terms[i] + terms[i + 1] for i in range(0, len(terms), 2)]
    return terms[0]


def taps_kernel(taps, w2, wc, turned):
    _, _, _, feat, groups = taps.shape
    rows = wc.shape[1] // 3 // feat
    depth = 3 * rows * SLOT
    low = lanes((feat, 2 * SLOT)) < SLOT
    zero = jnp.zeros((feat, 2 * SLOT), F32)

    def wide(a, b, e):
        if not 0 <= b <= 2:
            return None
        return jnp.concatenate([taps[a, b, e].astype(F32), zero[:, groups:]], axis=1)

    def beside(x, y):
        if x is None and y is None:
            return zero
        x = zero if x is None else x
        y = zero if y is None else pltpu.roll(y, SLOT, 1)
        return jnp.where(low, x, y)

    def build(a, _):
        def at_row(h):
            return pl.multiple_of((a * rows + h) * feat, feat)

        for e in range(3):
            for h in range(rows):
                for p in range(rows // 2):
                    lane = SLOT * (rows * e + 2 * p)
                    turned[pl.ds(at_row(h), feat), lane : lane + 2 * SLOT] = beside(
                        wide(a, 2 * p - h + 1, e), wide(a, 2 * p + 1 - h + 1, e)
                    )
                lane = depth + 2 * SLOT * e
                turned[pl.ds(at_row(h), feat), lane : lane + 2 * SLOT] = beside(
                    wide(a, 0, e) if h == 0 else None, wide(a, 2, e) if h == rows - 1 else None
                )
            for slot, six in enumerate((*range(1, rows + 1), 0, rows + 1)):
                at = 256 * e + feat * slot
                for p in range(rows // 2):
                    back = [2 - (six - 2 * p - o) for o in range(2)]
                    w2[a, at : at + feat, 2 * SLOT * p : 2 * SLOT * (p + 1)] = beside(
                        wide(2 - a, back[0], 2 - e), wide(2 - a, back[1], 2 - e)
                    ).astype(BF16)
            at = 256 * e + feat * (rows + 2)
            w2[a, at : 256 * (e + 1)] = jnp.zeros((256 - feat * (rows + 2), rows * SLOT), BF16)
        return 0

    lax.fori_loop(0, 3, build, 0)
    for i in range(wc.shape[0] // 128):
        for j in range(wc.shape[1] // 128):
            x, y = slice(128 * i, 128 * (i + 1)), slice(128 * j, 128 * (j + 1))
            wc[x, y] = turned[y, x].T.astype(BF16)


TOKEN = ((8, 128), F32)


def with_token(kernel, inputs, outputs):
    def run(*refs):
        kernel(*refs[: inputs + outputs], *refs[inputs + outputs + 1 :])
        refs[inputs + outputs][...] = jnp.zeros(TOKEN[0], F32)

    return run


def call(kernel, outs, scratch, *args, after=(), token=False, limit=LIMIT):
    skip = len(after)
    if token:
        kernel = with_token(kernel, len(args), len(outs))
        outs = [*outs, TOKEN]
    return pl.pallas_call(
        lambda *refs: kernel(*refs[skip:]),
        out_shape=[jax.ShapeDtypeStruct(s, t) for s, t in outs],
        in_specs=[pl.BlockSpec(memory_space=pl.ANY)] * skip + [VMEM] * len(args),
        out_specs=[VMEM] * len(outs),
        scratch_shapes=scratch,
        compiler_params=pltpu.CompilerParams(vmem_limit_bytes=limit),
    )(*after, *args)


def col_shift(block, distance):
    n = lax.axis_size("col")
    route = [(i - distance, i) for i in range(n) if 0 <= i - distance < n]
    return lax.ppermute(block, "col", route)


def row_shift(block, distance):
    n = lax.axis_size("row")
    route = [(i - distance, i) for i in range(n) if 0 <= i - distance < n]
    return lax.ppermute(block, "row", route)


def halos(pays):
    if lax.axis_size("row") == 2:
        got = lax.ppermute(pays[0], "row", [(0, 1), (1, 0)])
        return got, got
    return row_shift(pays[0], 1), row_shift(pays[1], -1)


def stages(n_row, n_col):
    col_bits = [1 << i for i in range(1, n_col.bit_length() - 1)]
    row_bits = [n_col << i for i in range(n_row.bit_length() - 1)]
    assert n_col == 2 << len(col_bits) and n_row == 1 << len(row_bits)
    bits = col_bits[:1] + row_bits + col_bits[1:]
    out = []
    for i in range(0, len(bits), 2):
        pair = bits[i : i + 2]
        out.append(pair + [sum(pair)] if len(pair) == 2 else pair)
    return out


def on_device(left_features, right_features, conv_weight, cotangent):
    rows, cols, channels = left_features.shape
    disp, feat = cotangent.shape[0], cotangent.shape[3]
    groups = conv_weight.shape[3]
    group_size = channels // groups
    wide = group_size * SLOT
    n_row, n_col = lax.axis_size("row"), lax.axis_size("col")
    per = 128 // feat

    if n_row == 2:
        ends = [lambda: (rows - 1) * (1 - lax.axis_index("row"))]
    else:
        ends = [lambda: rows - 1, lambda: 0]
    n = len(ends)

    def masks():
        at = lax.axis_index("row")
        return (
            jnp.where(at > 0, 1.0, 0.0).astype(F32),
            jnp.where(at < n_row - 1, 1.0, 0.0).astype(F32),
        )

    total = cols + 2 * PAD
    count = disp + 2 * rows
    ct = cotangent.transpose(0, 1, 3, 2)

    def swap(block, mask):
        route = [(i, i ^ mask) for i in range(n_row * n_col)]
        return lax.ppermute(block, ("row", "col"), route)

    by_even, by_odd, r2 = call(
        pack_kernel,
        [
            ((rows * cols + count, channels), BF16),
            ((rows * cols + count, channels), BF16),
            ((rows, cols // 2, channels), BF16),
        ],
        [pltpu.VMEM((disp * cols, rows * feat), F32)],
        left_features,
        right_features,
        ct,
        limit=BIG,
    )
    by_odd = lax.ppermute(
        by_odd, "col", [(i, i + 1) for i in range(1, n_col - 1, 2)] + [(i + 1, i) for i in range(1, n_col - 1, 2)]
    )
    by_even = swap(by_even, 1)
    r2 = col_shift(r2, 2)
    left_here, right_here, ctl, *rims = call(
        functools.partial(layout_kernel, ends),
        [
            ((rows, cols, channels), BF16),
            ((rows, cols, channels), BF16),
            ((disp, cols, rows * feat), BF16),
        ]
        + [((disp // per, total, 128), F32)] * n,
        [],
        left_features,
        right_features,
        ct,
    )
    w2, wc = call(
        taps_kernel,
        [((3, 3 * 256, rows * SLOT), BF16), ((3 * (rows + 2) * SLOT, 3 * rows * feat), BF16)],
        [pltpu.VMEM((3 * rows * feat, 3 * (rows + 2) * SLOT), F32)],
        conv_weight.transpose(0, 1, 2, 4, 3),
    )
    row_pays = call(
        functools.partial(row_kernel, ends, rows),
        [((disp // per, total, 128), BF16)] * n,
        [pltpu.VMEM((2, disp, 128), F32), pltpu.VMEM((disp // per, total, 128), F32)],
        by_even,
        by_odd,
        *rims,
        after=[w2],
    )
    top, bot = halos(row_pays)

    band = 104 + cols + PAD
    spread_rows = 3 * rows * cols + rows * cols // 2 + 2 * count
    vsh, fl, fr, fr4, *volume_rows = call(
        functools.partial(volume_kernel, ends, group_size),
        [
            ((disp + 2, cols, 3 * rows * SLOT), BF16),
            ((rows, total, wide), F32),
            ((rows, band, wide), F32),
            ((rows, band, wide), F32),
        ]
        + [((disp // 2 * total, 128), BF16)] * n,
        [
            pltpu.VMEM((rows // 2, disp, total, 2 * SLOT), F32),
            pltpu.VMEM((spread_rows, channels), BF16),
            pltpu.VMEM((spread_rows, wide), F32),
        ],
        left_here,
        right_here,
        by_even,
        by_odd,
        r2,
        after=row_pays,
    )
    vtop, vbot = halos(volume_rows)

    keep, give, ctsh = call(
        functools.partial(weight_kernel, masks, groups),
        [((3 * 64, 128), F32), ((3 * 64, 128), F32), ((disp + 2, cols, 3 * 256), BF16)],
        [
            pltpu.VMEM((rows * SLOT, disp * cols), BF16),
            pltpu.VMEM((disp, total, 256), F32),
            pltpu.VMEM((3 * 128, 128), F32),
        ],
        vsh, ctl, by_even, by_odd, top, bot,
    )
    got = swap(give, 1)
    gv, rg0, rg1, rg2 = call(
        right_kernel,
        [
            ((rows, disp, cols, 128), F32),
            ((rows, cols, channels), BF16),
            ((rows, cols, channels), BF16),
            ((rows, cols // 2, channels), BF16),
        ],
        [
            pltpu.VMEM((rows, cols + cols + cols // 2, wide), F32),
            pltpu.VMEM((rows, cols + cols + cols // 2 + 8, wide), F32),
            pltpu.VMEM((rows * (cols + cols + cols // 2), wide), BF16),
        ],
        ctsh, w2, fl,
    )
    rg1 = swap(rg1, 1)
    (part,) = call(sum_kernel, [(keep.shape, BF16)], [], keep, got, after=[rg0])
    output, conv_done = call(
        functools.partial(conv_kernel, masks),
        [((disp, rows, feat, cols), BF16)],
        [
            pltpu.VMEM((disp, cols, 3 * 2 * SLOT), BF16),
            pltpu.VMEM((disp, total, 128), F32),
            pltpu.VMEM((disp + 2, cols, rows * feat), F32),
        ],
        vsh, vtop, vbot, wc,
        after=[part],
        token=True,
    )
    (rg2,) = call(
        combine_kernel, [((rows, cols, channels), BF16)], [], rg1, rg2, after=[conv_done]
    )
    rg2 = col_shift(rg2, -2)
    *middle, final = stages(n_row, n_col)
    order = [conv_done]
    for stage in middle:
        parts = [part] + [swap(part, m) for m in stage]
        (part,) = call(sum_kernel, [(part.shape, BF16)], [], *parts, after=order)
        order = []
    lg, left_done = call(
        left_kernel,
        [((rows, cols, channels), BF16)],
        [pltpu.VMEM((rows, cols, wide), F32)],
        gv, fr, fr4,
        after=[part],
        token=True,
    )
    parts = [part] + [swap(part, m) for m in final]
    (part,) = call(sum_kernel, [(part.shape, F32)], [], *parts, after=[left_done])
    cells = disp * rows * n_row * cols * n_col
    weight_grad, right_grad = call(
        functools.partial(finish_kernel, 1.0 / math.sqrt(cells)),
        [((3, 3, 3, feat, groups), F32), ((rows, cols, channels), BF16)],
        [],
        part, swap(part, 1), rg0, rg1, rg2,
    )
    return (
        output.transpose(0, 1, 3, 2),
        weight_grad.transpose(0, 1, 2, 4, 3),
        lg,
        right_grad,
    )


def solution(mesh):
    in_specs = (P("row", "col", None), P("row", "col", None), P(), P(None, "row", "col", None))
    out_specs = (P(None, "row", "col", None), P(), P("row", "col", None), P("row", "col", None))
    return jax.shard_map(
        on_device, mesh=mesh, in_specs=in_specs, out_specs=out_specs, check_vma=False
    )
```

```python
import functools
import math

import jax
import jax.numpy as jnp
from jax import lax
from jax.experimental import pallas as pl
from jax.experimental.pallas import tpu as pltpu
from jax.sharding import PartitionSpec as P

DISP = 24
STEP = 4
SLOT = 64
PAD = 8
F32 = jnp.float32
BF16 = jnp.bfloat16
VMEM = pl.BlockSpec(memory_space=pltpu.VMEM)
LIMIT = 16 * 1024 * 1024


def lanes(shape):
    return lax.broadcasted_iota(jnp.int32, shape, len(shape) - 1)


def channel_table(channels, group_size, flip, value=1.0):
    shape = (group_size * SLOT, channels) if flip else (channels, group_size * SLOT)
    c = lax.broadcasted_iota(jnp.int32, shape, 1 if flip else 0)
    j = lax.broadcasted_iota(jnp.int32, shape, 0 if flip else 1)
    hit = c == (j & (SLOT - 1)) * group_size + (j >> (SLOT.bit_length() - 1))
    return jnp.where(hit, value, 0.0).astype(BF16)


def parity():
    return lax.rem(lax.axis_index("col"), 2)


def dot(a, b):
    return jnp.dot(a, b, preferred_element_type=F32)


def dot_nt(a, b):
    return lax.dot_general(a, b, (((1,), (1,)), ((), ())), preferred_element_type=F32)


def pack_kernel(ends, left, right, ct, even, odd, r2, ctl, *rest):
    rims, ctf = rest[:-1], rest[-1]
    disp, rows, feat, cols = ct.shape
    base, per = rows * cols, 128 // feat
    r2[...] = right[:, cols // 2 :]
    for h in range(rows):
        even[h * cols : (h + 1) * cols] = right[h]
        odd[h * cols : (h + 1) * cols] = right[h]
    for d in range(disp):
        block = ct[d].reshape(rows * feat, cols).astype(F32).T
        ctf[d * cols : (d + 1) * cols] = block
        ctl[d] = block.astype(BF16)
    columns = []
    for col in (cols - 1, 0):
        block = ctf[pl.ds(col, disp, stride=cols), :]
        block = jnp.concatenate([block, jnp.zeros((disp, left.shape[2] - rows * feat), F32)], axis=1)
        edge = [left[h, col : col + 1].astype(F32) for h in range(rows)]
        edge += [right[h, col : col + 1].astype(F32) for h in range(rows)]
        columns.append(jnp.concatenate([block, *edge], axis=0))
    is_even = parity() == 0
    even[base:] = jnp.where(is_even, columns[0], columns[1]).astype(BF16)
    odd[base:] = jnp.where(is_even, columns[1], columns[0]).astype(BF16)
    for end, rim in zip(ends, rims):
        h = end()
        for q in range(disp // per):
            rim[q, PAD : PAD + cols] = jnp.concatenate(
                [ct[q * per + i, h].astype(F32) for i in range(per)], axis=0
            ).T


def end_columns(by_even, by_odd, base):
    x, y = by_even[base:].astype(F32), by_odd[base:].astype(F32)
    is_even = parity() == 0
    return jnp.where(is_even, y, x), jnp.where(is_even, x, y)


def row_kernel(ends, rows, by_even, by_odd, *rest):
    n = len(ends)
    rims, pays, (edges, buf) = rest[:n], rest[n : 2 * n], rest[2 * n :]
    count, total, _ = buf.shape
    disp = edges.shape[1]
    per, cols = disp // count, total - 2 * PAD
    feat = 128 // per
    lane = lanes((count, 128))
    for side, x in enumerate(end_columns(by_even, by_odd, rows * cols)):
        edges[side] = x[0:disp, 0:128]
    for end, rim, pay in zip(ends, rims, pays):
        h = end()
        buf[...] = rim[...]
        for side, at in ((0, PAD - 1), (1, PAD + cols)):
            out = jnp.zeros((count, 128), F32)
            for i in range(per):
                x = edges[side, pl.ds(i, count, stride=per)]
                first = pltpu.roll(x, feat * i, 1) if i else x
                last = pltpu.roll(x, (feat * (i - rows + 1)) % 128, 1) if i != rows - 1 else x
                x = jnp.where(h == 0, first, last)
                out = jnp.where((lane >= feat * i) & (lane < feat * (i + 1)), x, out)
            for q in range(count):
                buf[q, at : at + 1] = out[q : q + 1]
        pay[...] = buf[...].astype(BF16)


def volume_kernel(ends, group_size, left, right, by_even, by_odd, r2, vbuf, fl, fr, fr4, *rest):
    pays, (mixed, wide_buf) = rest[: len(ends)], rest[len(ends) :]
    rows, cols, channels = left.shape
    disp = vbuf.shape[1]
    reach = fr.shape[1] - cols - PAD
    wide = group_size * SLOT
    base, half = rows * cols, cols // 2
    is_even = parity() == 0
    mixed[0:base] = jnp.where(is_even, by_odd[0:base].astype(F32), by_even[0:base].astype(F32)).astype(
        BF16
    )
    mixed[base : 2 * base] = right[...].reshape(base, channels)
    mixed[2 * base : 3 * base] = left[...].reshape(base, channels)
    at_far, at_ends = 3 * base, 3 * base + base // 2
    mixed[at_far:at_ends] = r2[...].reshape(base // 2, channels)
    count = disp + 2 * rows
    for i, x in enumerate(end_columns(by_even, by_odd, base)):
        mixed[at_ends + i * count : at_ends + (i + 1) * count] = x.astype(BF16)
    wide_buf[...] = dot(mixed[...], channel_table(channels, group_size, False))
    scale = 1.0 / group_size
    for h in range(rows):
        fl[h, 0:PAD] = jnp.zeros((PAD, wide), F32)
        fl[h, PAD + cols :] = jnp.zeros((PAD, wide), F32)
        at = at_ends + disp + h
        fl[h, PAD - 1 : PAD] = wide_buf[at : at + 1] * scale
        fl[h, PAD : PAD + cols] = wide_buf[2 * base + h * cols : 2 * base + (h + 1) * cols] * scale
        at += count
        fl[h, PAD + cols : PAD + cols + 1] = wide_buf[at : at + 1] * scale
        for ref, off in ((fr, 0), (fr4, STEP)):
            start = reach - cols - half + off
            ref[h, 0:start] = jnp.zeros((start, wide), F32)
            ref[h, start : start + half] = wide_buf[at_far + h * half : at_far + (h + 1) * half]
            for part in range(2):
                at = part * base + h * cols
                to = start + half + part * cols
                ref[h, to : to + cols] = wide_buf[at : at + cols]
            to = start + half + 2 * cols
            ref[h, to:] = jnp.zeros((ref.shape[1] - to, wide), F32)
            at = at_ends + count + disp + rows + h
            ref[h, to : to + 1] = wide_buf[at : at + 1]
    total = cols + 2 * PAD
    block = 16
    low = lanes((block, 128)) < SLOT
    pairs = rows // 2

    def products(i, _):
        p, b = lax.rem(i, pairs), lax.div(i, pairs)
        at = pl.multiple_of(b * block, block)
        lefts = [fl[2 * p + o, pl.ds(at, block)] for o in range(2)]
        for d in range(disp):
            band = fr4 if d % 2 else fr
            start = pl.multiple_of(at + reach - PAD - 2 * STEP * (d // 2), 8)
            sums = []
            for o in range(2):
                prod = lefts[o] * band[2 * p + o, pl.ds(start, block)]
                acc = prod[:, 0:128]
                for j in range(1, wide // 128):
                    acc = acc + prod[:, 128 * j : 128 * (j + 1)]
                sums.append(acc + pltpu.roll(acc, SLOT, 1))
            vbuf[p, d, pl.ds(at, block)] = jnp.where(low, sums[0], sums[1])
        return 0

    lax.fori_loop(0, pairs * (total // block), products, 0)
    big = lanes((total, 128)) < SLOT

    for dd in range(disp // 2):
        for end, pay in zip(ends, pays):
            h = end()
            if isinstance(h, int):
                halves = [vbuf[h // 2, 2 * dd + o] for o in range(2)]
                if h % 2 == 0:
                    halves[1] = pltpu.roll(halves[1], SLOT, 1)
                else:
                    halves[0] = pltpu.roll(halves[0], SLOT, 1)
                out = jnp.where(big, halves[0], halves[1])
            else:
                last = pairs - 1
                first = jnp.where(big, vbuf[0, 2 * dd], pltpu.roll(vbuf[0, 2 * dd + 1], SLOT, 1))
                final = jnp.where(
                    big, pltpu.roll(vbuf[last, 2 * dd], SLOT, 1), vbuf[last, 2 * dd + 1]
                )
                out = jnp.where(h == 0, first, final)
            pay[dd * total : (dd + 1) * total] = out.astype(BF16)


def weight_kernel(masks, groups, vbuf, ctl, by_even, by_odd, top, bot, keep_out, give_out, ctsh, vt, buf, sums):
    disp, cols, width = ctl.shape
    rows, feat = 2 * vbuf.shape[0], 32
    per = 128 // feat
    mtop, mbot = masks()
    ctsh[0] = jnp.zeros(ctsh.shape[1:], BF16)
    ctsh[disp + 1] = jnp.zeros(ctsh.shape[1:], BF16)
    lane = lanes(top.shape[1:])
    edges = [x[0:disp, 0:128] for x in end_columns(by_even, by_odd, rows * cols)]
    for d in range(disp):
        buf[d, PAD - 1 : PAD, 0:128] = edges[0][d : d + 1]
        buf[d, PAD + cols : PAD + cols + 1, 0:128] = edges[1][d : d + 1]

    def fill(q, _):
        t = top[q].astype(F32) * mtop
        z = bot[q].astype(F32) * mbot
        for i in range(per):
            d = q * per + i
            a = t if i == 0 else pltpu.roll(t, 128 - feat * i, 1)
            y = z if i == 1 else pltpu.roll(z, (128 + feat - feat * i) % 128, 1)
            buf[d, PAD : PAD + cols, 0:128] = ctl[d].astype(F32)
            buf[d, :, 128:256] = jnp.where(lane < feat, a, jnp.where(lane < 2 * feat, y, 0.0))
            for e in range(3):
                ctsh[d + 1, :, 256 * e : 256 * (e + 1)] = buf[
                    d, PAD - 1 + e : PAD - 1 + e + cols
                ].astype(BF16)
        return 0

    lax.fori_loop(0, disp // per, fill, 0, unroll=True)
    step = 256 // cols
    for q in range(disp // step):
        for p in range(rows // 2):
            v = vbuf[p, q * step : (q + 1) * step, PAD : PAD + cols].reshape(256, 128).astype(BF16)
            vt[128 * p : 128 * (p + 1), 256 * q : 256 * (q + 1)] = v.T
    keep = lanes((groups, 128))
    sums[...] = jnp.zeros(sums.shape, F32)

    def taps(a, _):
        for e in range(3):
            ct_block = ctsh[pl.ds(a, disp), :, 256 * e : 256 * (e + 1)].reshape(disp * cols, 256)
            full = dot(vt[...], ct_block)
            out = None
            for h in range(rows):
                x = full[SLOT * h : SLOT * h + groups, 0:128]
                y = full[SLOT * h : SLOT * h + groups, 128:256]
                if h == 0:
                    term = jnp.where(keep < feat, y, pltpu.roll(x, feat, 1))
                else:
                    term = x if h == 1 else pltpu.roll(x, 128 - feat * (h - 1), 1)
                    if h == rows - 1:
                        term = jnp.where(keep < 2 * feat, term, pltpu.roll(y, feat, 1))
                out = term if out is None else out + term
            at = pl.multiple_of(a * 128 + groups * e, 8)
            sums[pl.ds(at, groups)] = jnp.where(keep < 3 * feat, out, 0.0)
        return 0

    lax.fori_loop(0, 3, taps, 0)
    half = sums.shape[0] // 2
    is_even = parity() == 0
    low, high = sums[0:half], sums[half:]
    keep_out[...] = jnp.where(is_even, low, high)
    give_out[...] = jnp.where(is_even, high, low)


def right_kernel(ctsh, w2, fl, gv, rg0, rg1, rg2, acce, acco, both):
    disp = ctsh.shape[0] - 2
    rows, cols, channels = rg0.shape
    wide = fl.shape[2]
    group_size = wide // SLOT
    step = 512 // cols
    low = lanes((512, 128)) < SLOT

    def conv(q, _):
        slabs = [ctsh[pl.ds(q * step + a, step)].reshape(512, ctsh.shape[2]) for a in range(3)]
        acc = dot(jnp.concatenate(slabs, axis=1), w2[...])
        g = acc.astype(BF16).astype(F32)
        for p in range(rows // 2):
            x = g[:, 128 * p : 128 * (p + 1)]
            r = pltpu.roll(x, SLOT, 1)
            for o in range(2):
                y = jnp.where(low, r, x) if o else jnp.where(low, x, r)
                gv[2 * p + o, pl.ds(q * step, step)] = y.reshape(step, cols, 128)
        return 0

    lax.fori_loop(0, disp // step, conv, 0)
    count = cols // 8
    back = acce.shape[1] - cols
    lead = back // 8

    def right_row(h, _):
        for odd, buf in enumerate((acce, acco)):
            for k in range(lead + count):
                accs = [jnp.zeros((8, 128), F32) for _ in range(wide // 128)]
                for t in range(disp // 2):
                    b = k + t - lead
                    if b < 0 or b >= count:
                        continue
                    g = gv[h, 2 * t + odd, 8 * b : 8 * b + 8]
                    for j in range(wide // 128):
                        accs[j] = accs[j] + g * fl[
                            h, PAD + 8 * b : PAD + 8 * b + 8, 128 * j : 128 * (j + 1)
                        ]
                for j in range(wide // 128):
                    buf[h, 8 * k : 8 * k + 8, 128 * j : 128 * (j + 1)] = accs[j]
        acco[h, 8 * (lead + count) :] = jnp.zeros((8, wide), F32)
        return 0

    lax.fori_loop(0, rows, right_row, 0)
    size = back + cols
    for h in range(rows):
        both[h * size : (h + 1) * size] = (acce[h] + acco[h, STEP : STEP + size]).astype(BF16)
    whole = dot(both[...], channel_table(channels, group_size, True)).astype(BF16)
    half = cols // 2
    for h in range(rows):
        at = h * size + back
        rg2[h] = whole[at - cols - half : at - cols]
        rg1[h] = whole[at - cols : at]
        rg0[h] = whole[at : at + cols]


def left_kernel(gv, fr, fr4, lg, accl):
    rows, cols, channels = lg.shape
    disp, wide = gv.shape[1], fr.shape[2]
    group_size = wide // SLOT
    reach = fr.shape[1] - cols - PAD
    block = 16

    def left_block(i, _):
        h = lax.div(i, cols // block)
        w = pl.multiple_of(lax.rem(i, cols // block) * block, block)
        accs = [jnp.zeros((block, 128), F32) for _ in range(wide // 128)]
        for d in range(disp):
            band = fr4 if d % 2 else fr
            at = pl.multiple_of(w + reach - 2 * STEP * (d // 2), 8)
            g = gv[h, d, pl.ds(w, block)]
            for j in range(wide // 128):
                accs[j] = accs[j] + g * band[h, pl.ds(at, block), 128 * j : 128 * (j + 1)]
        for j in range(wide // 128):
            accl[h, pl.ds(w, block), 128 * j : 128 * (j + 1)] = accs[j] * (1.0 / group_size)
        return 0

    lax.fori_loop(0, rows * (cols // block), left_block, 0)
    whole = accl[...].reshape(rows * cols, wide).astype(BF16)
    out = dot(whole, channel_table(channels, group_size, True)).astype(BF16)
    lg[...] = out.reshape(rows, cols, channels)


def combine_kernel(got, rg2, out):
    cols = out.shape[1]
    half = cols // 2
    part = jnp.where(parity() == 0, 0.0, got[...].astype(F32))
    out[:, 0:half] = part[:, 0:half].astype(BF16)
    out[:, half:] = (part[:, half:] + rg2[...].astype(F32)).astype(BF16)


def halo_lanes(groups):
    first = SLOT - groups
    assert groups - first <= first
    return (groups, SLOT, groups), (SLOT + groups, SLOT + 2 * groups - first, SLOT + groups - first)


def place_halo(base, row, groups, offset, lane):
    for start, end, shift in halo_lanes(groups):
        moved = pltpu.roll(row, (shift - offset) % 128, 1)
        base = jnp.where((lane >= start) & (lane < end), moved, base)
    return base


def conv_kernel(masks, groups, vbuf, top, bot, wc, out, taps, buf):
    disp, rows, feat, cols = out.shape
    total = buf.shape[2]
    lane = lanes((total, 128))
    zeros = jnp.zeros((cols, taps.shape[3]), BF16)
    taps[0, 0] = zeros
    taps[disp // 2, 1] = zeros
    halos_of = [(ref, mask) for ref, mask in zip((top, bot), masks())]
    for dd in range(disp // 2):
        for p, (ref, mask) in enumerate(halos_of):
            row = ref[dd * total : (dd + 1) * total].astype(F32) * mask
            for o in range(2):
                d = 2 * dd + o
                buf[p, d] = place_halo(vbuf[p, d], row, groups, SLOT * o, lane)
                for e in range(3):
                    at = 256 * e + 128 * p
                    taps[(d + 1) // 2, (d + 1) % 2, :, at : at + 128] = buf[
                        p, d, PAD - 1 + e : PAD - 1 + e + cols
                    ].astype(BF16)
    step = 6

    def conv(q, _):
        slabs = [
            taps[pl.ds(q * step + s // 2, step), s % 2].reshape(step * cols, taps.shape[3])
            for s in range(4)
        ]
        acc = dot(jnp.concatenate(slabs, axis=1), wc[...])
        for j in range(step):
            both = acc[j * cols : (j + 1) * cols].T.astype(BF16)
            for o in range(2):
                block = both[rows * feat * o : rows * feat * (o + 1)]
                out[2 * (q * step + j) + o] = block.reshape(rows, feat, cols)
        return 0

    lax.fori_loop(0, disp // 2 // step, conv, 0)


def finish_kernel(scale, mine, other, own, near, far, weight, right):
    _, _, _, feat, groups = weight.shape
    is_even = parity() == 0
    x, y = mine[...] * scale, other[...] * scale
    total = jnp.concatenate([jnp.where(is_even, x, y), jnp.where(is_even, y, x)], axis=0)
    for a in range(3):
        for e in range(3):
            at = 128 * a + groups * e
            block = total[at : at + groups].T
            for b in range(3):
                weight[2 - a, 2 - b, 2 - e] = block[feat * b : feat * (b + 1)]
    beside = jnp.where(is_even, near[...].astype(F32), 0.0)
    right[...] = (own[...].astype(F32) + beside + far[...].astype(F32)).astype(BF16)


def sum_kernel(*refs):
    *parts, out = refs
    out[...] = tree([ref[...].astype(F32) for ref in parts]).astype(out.dtype)


def tree(terms):
    while len(terms) > 1:
        terms = [terms[i] + terms[i + 1] for i in range(0, len(terms), 2)]
    return terms[0]


def taps_kernel(taps, w2, wc, turned):
    _, _, _, feat, groups = taps.shape
    rows = wc.shape[1] // 2 // feat
    lane_of = lanes((feat, 2 * SLOT))
    low = lanes((feat, 2 * SLOT)) < SLOT
    zero = jnp.zeros((feat, 2 * SLOT), F32)

    def wide(a, b, e):
        if not 0 <= b <= 2:
            return None
        return jnp.concatenate([taps[a, b, e].astype(F32), zero[:, groups:]], axis=1)

    def beside(x, y):
        if x is None and y is None:
            return zero
        x = zero if x is None else x
        y = zero if y is None else pltpu.roll(y, SLOT, 1)
        return jnp.where(low, x, y)

    def build(a, _):
        def at_row(h):
            return pl.multiple_of((a * rows + h) * feat, feat)

        def at_tap(row):
            return pl.multiple_of(a * 3 * 256 + row, feat)

        for e in range(3):
            for h in range(rows):
                for p in range(rows // 2):
                    lane = SLOT * (rows * e + 2 * p)
                    block = beside(wide(a, 2 * p - h + 1, e), wide(a, 2 * p + 1 - h + 1, e))
                    if h == 0 and p == 0:
                        block = place_halo(block, wide(a, 0, e), groups, 0, lane_of)
                    if h == rows - 1 and p == rows // 2 - 1:
                        block = place_halo(block, wide(a, 2, e), groups, 0, lane_of)
                    turned[pl.ds(at_row(h), feat), lane : lane + 2 * SLOT] = block
            for slot, six in enumerate((*range(1, rows + 1), 0, rows + 1)):
                at = 256 * e + feat * slot
                for p in range(rows // 2):
                    back = [2 - (six - 2 * p - o) for o in range(2)]
                    w2[pl.ds(at_tap(at), feat), 2 * SLOT * p : 2 * SLOT * (p + 1)] = beside(
                        wide(2 - a, back[0], 2 - e), wide(2 - a, back[1], 2 - e)
                    ).astype(BF16)
            at = 256 * e + feat * (rows + 2)
            size = 256 - feat * (rows + 2)
            w2[pl.ds(at_tap(at), size)] = jnp.zeros((size, rows * SLOT), BF16)
        return 0

    lax.fori_loop(0, 3, build, 0)
    depth, size = turned.shape[1], rows * feat
    for a in range(3):
        for i in range(depth // 128):
            x = turned[size * a : size * (a + 1), 128 * i : 128 * (i + 1)].T.astype(BF16)
            for o in range(2):
                at = depth * (a + o) + 128 * i
                wc[at : at + 128, size * o : size * (o + 1)] = x
    for o in range(2):
        at = depth * 3 * (1 - o)
        wc[at : at + depth, size * o : size * (o + 1)] = jnp.zeros((depth, size), BF16)


TOKEN = ((8, 128), F32)


def with_token(kernel, inputs, outputs):
    def run(*refs):
        kernel(*refs[: inputs + outputs], *refs[inputs + outputs + 1 :])
        refs[inputs + outputs][...] = jnp.zeros(TOKEN[0], F32)

    return run


def call(kernel, outs, scratch, *args, after=(), token=False):
    skip = len(after)
    if token:
        kernel = with_token(kernel, len(args), len(outs))
        outs = [*outs, TOKEN]
    return pl.pallas_call(
        lambda *refs: kernel(*refs[skip:]),
        out_shape=[jax.ShapeDtypeStruct(s, t) for s, t in outs],
        in_specs=[pl.BlockSpec(memory_space=pl.ANY)] * skip + [VMEM] * len(args),
        out_specs=[VMEM] * len(outs),
        scratch_shapes=scratch,
        compiler_params=pltpu.CompilerParams(vmem_limit_bytes=LIMIT),
    )(*after, *args)


def col_shift(block, distance):
    n = lax.axis_size("col")
    route = [(i - distance, i) for i in range(n) if 0 <= i - distance < n]
    return lax.ppermute(block, "col", route)


def row_shift(block, distance):
    n = lax.axis_size("row")
    route = [(i - distance, i) for i in range(n) if 0 <= i - distance < n]
    return lax.ppermute(block, "row", route)


def halos(pays):
    if lax.axis_size("row") == 2:
        got = lax.ppermute(pays[0], "row", [(0, 1), (1, 0)])
        return got, got
    return row_shift(pays[0], 1), row_shift(pays[1], -1)


def stages(n_row, n_col):
    col_bits = [1 << i for i in range(1, n_col.bit_length() - 1)]
    row_bits = [n_col << i for i in range(n_row.bit_length() - 1)]
    assert n_col == 2 << len(col_bits) and n_row == 1 << len(row_bits)
    bits = col_bits[:1] + row_bits + col_bits[1:]
    out = []
    for i in range(0, len(bits), 2):
        pair = bits[i : i + 2]
        out.append(pair + [sum(pair)] if len(pair) == 2 else pair)
    return out


def on_device(left_features, right_features, conv_weight, cotangent):
    rows, cols, channels = left_features.shape
    disp, feat = cotangent.shape[0], cotangent.shape[3]
    groups = conv_weight.shape[3]
    group_size = channels // groups
    wide = group_size * SLOT
    n_row, n_col = lax.axis_size("row"), lax.axis_size("col")
    per = 128 // feat

    if n_row == 2:
        ends = [lambda: (rows - 1) * (1 - lax.axis_index("row"))]
    else:
        ends = [lambda: rows - 1, lambda: 0]
    n = len(ends)

    def masks():
        at = lax.axis_index("row")
        return (
            jnp.where(at > 0, 1.0, 0.0).astype(F32),
            jnp.where(at < n_row - 1, 1.0, 0.0).astype(F32),
        )

    total = cols + 2 * PAD
    count = disp + 2 * rows
    ct = cotangent.transpose(0, 1, 3, 2)

    def swap(block, mask):
        route = [(i, i ^ mask) for i in range(n_row * n_col)]
        return lax.ppermute(block, ("row", "col"), route)

    by_even, by_odd, r2, ctl, *rims = call(
        functools.partial(pack_kernel, ends),
        [
            ((rows * cols + count, channels), BF16),
            ((rows * cols + count, channels), BF16),
            ((rows, cols // 2, channels), BF16),
            ((disp, cols, rows * feat), BF16),
        ]
        + [((disp // per, total, 128), F32)] * n,
        [pltpu.VMEM((disp * cols, rows * feat), F32)],
        left_features,
        right_features,
        ct,
    )
    by_odd = lax.ppermute(
        by_odd, "col", [(i, i + 1) for i in range(1, n_col - 1, 2)] + [(i + 1, i) for i in range(1, n_col - 1, 2)]
    )
    by_even = swap(by_even, 1)
    r2 = col_shift(r2, 2)
    w2, wc = call(
        taps_kernel,
        [((9 * 256, rows * SLOT), BF16), ((4 * 3 * rows * SLOT, 2 * rows * feat), BF16)],
        [pltpu.VMEM((3 * rows * feat, 3 * rows * SLOT), F32)],
        conv_weight.transpose(0, 1, 2, 4, 3),
    )
    row_pays = call(
        functools.partial(row_kernel, ends, rows),
        [((disp // per, total, 128), BF16)] * n,
        [pltpu.VMEM((2, disp, 128), F32), pltpu.VMEM((disp // per, total, 128), F32)],
        by_even,
        by_odd,
        *rims,
        after=[w2],
    )
    top, bot = halos(row_pays)

    band = 104 + cols + PAD
    spread_rows = 3 * rows * cols + rows * cols // 2 + 2 * count
    vbuf, fl, fr, fr4, *volume_rows = call(
        functools.partial(volume_kernel, ends, group_size),
        [
            ((rows // 2, disp, total, 2 * SLOT), F32),
            ((rows, total, wide), F32),
            ((rows, band, wide), F32),
            ((rows, band, wide), F32),
        ]
        + [((disp // 2 * total, 128), BF16)] * n,
        [
            pltpu.VMEM((spread_rows, channels), BF16),
            pltpu.VMEM((spread_rows, wide), F32),
        ],
        left_features,
        right_features,
        by_even,
        by_odd,
        r2,
        after=row_pays,
    )
    vtop, vbot = halos(volume_rows)

    keep, give, ctsh = call(
        functools.partial(weight_kernel, masks, groups),
        [((3 * 64, 128), F32), ((3 * 64, 128), F32), ((disp + 2, cols, 3 * 256), BF16)],
        [
            pltpu.VMEM((rows * SLOT, disp * cols), BF16),
            pltpu.VMEM((disp, total, 256), F32),
            pltpu.VMEM((3 * 128, 128), F32),
        ],
        vbuf, ctl, by_even, by_odd, top, bot,
    )
    got = swap(give, 1)
    gv, rg0, rg1, rg2 = call(
        right_kernel,
        [
            ((rows, disp, cols, 128), F32),
            ((rows, cols, channels), BF16),
            ((rows, cols, channels), BF16),
            ((rows, cols // 2, channels), BF16),
        ],
        [
            pltpu.VMEM((rows, cols + cols + cols // 2, wide), F32),
            pltpu.VMEM((rows, cols + cols + cols // 2 + 8, wide), F32),
            pltpu.VMEM((rows * (cols + cols + cols // 2), wide), BF16),
        ],
        ctsh, w2, fl,
    )
    rg1 = swap(rg1, 1)
    (part,) = call(sum_kernel, [(keep.shape, BF16)], [], keep, got, after=[rg0])
    output, conv_done = call(
        functools.partial(conv_kernel, masks, groups),
        [((disp, rows, feat, cols), BF16)],
        [
            pltpu.VMEM((disp // 2 + 1, 2, cols, 3 * rows * SLOT), BF16),
            pltpu.VMEM((rows // 2, disp, total, 128), F32),
        ],
        vbuf, vtop, vbot, wc,
        after=[part],
        token=True,
    )
    (rg2,) = call(
        combine_kernel, [((rows, cols, channels), BF16)], [], rg1, rg2, after=[conv_done]
    )
    rg2 = col_shift(rg2, -2)
    *middle, final = stages(n_row, n_col)
    order = [conv_done]
    for stage in middle:
        parts = [part] + [swap(part, m) for m in stage]
        (part,) = call(sum_kernel, [(part.shape, BF16)], [], *parts, after=order)
        order = []
    lg, left_done = call(
        left_kernel,
        [((rows, cols, channels), BF16)],
        [pltpu.VMEM((rows, cols, wide), F32)],
        gv, fr, fr4,
        after=[part],
        token=True,
    )
    parts = [part] + [swap(part, m) for m in final]
    (part,) = call(sum_kernel, [(part.shape, F32)], [], *parts, after=[left_done])
    cells = disp * rows * n_row * cols * n_col
    weight_grad, right_grad = call(
        functools.partial(finish_kernel, 1.0 / math.sqrt(cells)),
        [((3, 3, 3, feat, groups), F32), ((rows, cols, channels), BF16)],
        [],
        part, swap(part, 1), rg0, rg1, rg2,
    )
    return (
        output.transpose(0, 1, 3, 2),
        weight_grad.transpose(0, 1, 2, 4, 3),
        lg,
        right_grad,
    )


def solution(mesh):
    in_specs = (P("row", "col", None), P("row", "col", None), P(), P(None, "row", "col", None))
    out_specs = (P(None, "row", "col", None), P(), P("row", "col", None), P("row", "col", None))
    return jax.shard_map(
        on_device, mesh=mesh, in_specs=in_specs, out_specs=out_specs, check_vma=False
    )
```

```python
import functools
import math

import jax
import jax.numpy as jnp
from jax import lax
from jax.experimental import pallas as pl
from jax.experimental.pallas import tpu as pltpu
from jax.sharding import PartitionSpec as P

DISP = 24
STEP = 4
SLOT = 64
PAD = 8
F32 = jnp.float32
BF16 = jnp.bfloat16
VMEM = pl.BlockSpec(memory_space=pltpu.VMEM)
LIMIT = 16 * 1024 * 1024


def lanes(shape):
    return lax.broadcasted_iota(jnp.int32, shape, len(shape) - 1)


def channel_table(channels, group_size, flip, value=1.0):
    shape = (group_size * SLOT, channels) if flip else (channels, group_size * SLOT)
    c = lax.broadcasted_iota(jnp.int32, shape, 1 if flip else 0)
    j = lax.broadcasted_iota(jnp.int32, shape, 0 if flip else 1)
    hit = c == (j & (SLOT - 1)) * group_size + (j >> (SLOT.bit_length() - 1))
    return jnp.where(hit, value, 0.0).astype(BF16)


def parity():
    return lax.rem(lax.axis_index("col"), 2)


def dot(a, b):
    return jnp.dot(a, b, preferred_element_type=F32)


def dot_nt(a, b):
    return lax.dot_general(a, b, (((1,), (1,)), ((), ())), preferred_element_type=F32)


def pack_kernel(ends, left, right, ct, even, odd, ctl, *rest):
    rims, ctf = rest[:-1], rest[-1]
    disp, rows, feat, cols = ct.shape
    per = 128 // feat
    for d in range(disp):
        block = ct[d].reshape(rows * feat, cols).astype(F32).T
        ctf[d * cols : (d + 1) * cols] = block
        ctl[d] = block.astype(BF16)
    columns = []
    for col in (cols - 1, 0):
        block = ctf[pl.ds(col, disp, stride=cols), :]
        block = jnp.concatenate([block, jnp.zeros((disp, left.shape[2] - rows * feat), F32)], axis=1)
        edge = [left[h, col : col + 1].astype(F32) for h in range(rows)]
        edge += [right[h, col : col + 1].astype(F32) for h in range(rows)]
        columns.append(jnp.concatenate([block, *edge], axis=0))
    is_even = parity() == 0
    even[...] = jnp.where(is_even, columns[0], columns[1]).astype(BF16)
    odd[...] = jnp.where(is_even, columns[1], columns[0]).astype(BF16)
    for end, rim in zip(ends, rims):
        h = end()
        for q in range(disp // per):
            rim[q, PAD : PAD + cols] = jnp.concatenate(
                [ct[q * per + i, h].astype(F32) for i in range(per)], axis=0
            ).T


def pass_kernel(own, got, out):
    out[...] = jnp.where(parity() == 0, own[...].astype(F32), got[...].astype(F32)).astype(BF16)


def end_columns(by_even, by_odd):
    x, y = by_even[...].astype(F32), by_odd[...].astype(F32)
    is_even = parity() == 0
    return jnp.where(is_even, y, x), jnp.where(is_even, x, y)


def row_kernel(ends, rows, by_even, by_odd, *rest):
    n = len(ends)
    rims, pays, (edges, buf) = rest[:n], rest[n : 2 * n], rest[2 * n :]
    count, total, _ = buf.shape
    disp = edges.shape[1]
    per, cols = disp // count, total - 2 * PAD
    feat = 128 // per
    lane = lanes((count, 128))
    for side, x in enumerate(end_columns(by_even, by_odd)):
        edges[side] = x[0:disp, 0:128]
    for end, rim, pay in zip(ends, rims, pays):
        h = end()
        buf[...] = rim[...]
        for side, at in ((0, PAD - 1), (1, PAD + cols)):
            out = jnp.zeros((count, 128), F32)
            for i in range(per):
                x = edges[side, pl.ds(i, count, stride=per)]
                first = pltpu.roll(x, feat * i, 1) if i else x
                last = pltpu.roll(x, (feat * (i - rows + 1)) % 128, 1) if i != rows - 1 else x
                x = jnp.where(h == 0, first, last)
                out = jnp.where((lane >= feat * i) & (lane < feat * (i + 1)), x, out)
            for q in range(count):
                buf[q, at : at + 1] = out[q : q + 1]
        pay[...] = buf[...].astype(BF16)


def volume_kernel(ends, group_size, left, right, near, far, by_even, by_odd, vbuf, fl, fr, fr4, *rest):
    pays, (mixed, wide_buf) = rest[: len(ends)], rest[len(ends) :]
    rows, cols, channels = left.shape
    disp = vbuf.shape[1]
    reach = fr.shape[1] - cols - PAD
    wide = group_size * SLOT
    base, half = rows * cols, cols // 2
    mixed[0:base] = near[...].reshape(base, channels)
    mixed[base : 2 * base] = right[...].reshape(base, channels)
    mixed[2 * base : 3 * base] = left[...].reshape(base, channels)
    at_far, at_ends = 3 * base, 3 * base + base // 2
    mixed[at_far:at_ends] = far[:, half:].reshape(base // 2, channels)
    count = disp + 2 * rows
    for i, x in enumerate(end_columns(by_even, by_odd)):
        mixed[at_ends + i * count : at_ends + (i + 1) * count] = x.astype(BF16)
    wide_buf[...] = dot(mixed[...], channel_table(channels, group_size, False))
    scale = 1.0 / group_size
    for h in range(rows):
        fl[h, 0:PAD] = jnp.zeros((PAD, wide), F32)
        fl[h, PAD + cols :] = jnp.zeros((PAD, wide), F32)
        at = at_ends + disp + h
        fl[h, PAD - 1 : PAD] = wide_buf[at : at + 1] * scale
        fl[h, PAD : PAD + cols] = wide_buf[2 * base + h * cols : 2 * base + (h + 1) * cols] * scale
        at += count
        fl[h, PAD + cols : PAD + cols + 1] = wide_buf[at : at + 1] * scale
        for ref, off in ((fr, 0), (fr4, STEP)):
            start = reach - cols - half + off
            ref[h, 0:start] = jnp.zeros((start, wide), F32)
            ref[h, start : start + half] = wide_buf[at_far + h * half : at_far + (h + 1) * half]
            for part in range(2):
                at = part * base + h * cols
                to = start + half + part * cols
                ref[h, to : to + cols] = wide_buf[at : at + cols]
            to = start + half + 2 * cols
            ref[h, to:] = jnp.zeros((ref.shape[1] - to, wide), F32)
            at = at_ends + count + disp + rows + h
            ref[h, to : to + 1] = wide_buf[at : at + 1]
    total = cols + 2 * PAD
    low = lanes((8, 128)) < SLOT
    pairs, times, lots = rows // 2, disp // 2, wide // 128
    count = total // 16

    def products(i, _):
        p, at = lax.rem(i, pairs), pl.multiple_of(lax.div(i, pairs) * (8 * count), 8)
        lefts = [
            [
                [fl[2 * p + o, pl.ds(at + 8 * b, 8), 128 * j : 128 * (j + 1)] for j in range(lots)]
                for b in range(count)
            ]
            for o in range(2)
        ]
        for odd, band in enumerate((fr, fr4)):
            for r in range(1 - times, count):
                start = pl.multiple_of(at + reach - PAD + 8 * r, 8)
                here = [
                    [band[2 * p + o, pl.ds(start, 8), 128 * j : 128 * (j + 1)] for j in range(lots)]
                    for o in range(2)
                ]
                for t in range(max(0, -r), min(times, count - r)):
                    sums = []
                    for o in range(2):
                        acc = lefts[o][r + t][0] * here[o][0]
                        for j in range(1, lots):
                            acc = acc + lefts[o][r + t][j] * here[o][j]
                        sums.append(acc + pltpu.roll(acc, SLOT, 1))
                    vbuf[p, 2 * t + odd, pl.ds(at + 8 * (r + t), 8)] = jnp.where(low, *sums)
        return 0

    lax.fori_loop(0, 2 * pairs, products, 0)
    big = lanes((total, 128)) < SLOT

    for dd in range(disp // 2):
        for end, pay in zip(ends, pays):
            h = end()
            if isinstance(h, int):
                halves = [vbuf[h // 2, 2 * dd + o] for o in range(2)]
                if h % 2 == 0:
                    halves[1] = pltpu.roll(halves[1], SLOT, 1)
                else:
                    halves[0] = pltpu.roll(halves[0], SLOT, 1)
                out = jnp.where(big, halves[0], halves[1])
            else:
                last = pairs - 1
                first = jnp.where(big, vbuf[0, 2 * dd], pltpu.roll(vbuf[0, 2 * dd + 1], SLOT, 1))
                final = jnp.where(
                    big, pltpu.roll(vbuf[last, 2 * dd], SLOT, 1), vbuf[last, 2 * dd + 1]
                )
                out = jnp.where(h == 0, first, final)
            pay[dd * total : (dd + 1) * total] = out.astype(BF16)


def weight_kernel(masks, groups, vbuf, ctl, by_even, by_odd, top, bot, keep_out, give_out, ctsh, vt, buf, sums):
    disp, cols, width = ctl.shape
    rows, feat = 2 * vbuf.shape[0], 32
    per = 128 // feat
    mtop, mbot = masks()
    ctsh[0] = jnp.zeros(ctsh.shape[1:], BF16)
    ctsh[disp + 1] = jnp.zeros(ctsh.shape[1:], BF16)
    lane = lanes(top.shape[1:])
    edges = [x[0:disp, 0:128] for x in end_columns(by_even, by_odd)]
    for d in range(disp):
        buf[d, PAD - 1 : PAD, 0:128] = edges[0][d : d + 1]
        buf[d, PAD + cols : PAD + cols + 1, 0:128] = edges[1][d : d + 1]

    def fill(q, _):
        t = top[q].astype(F32) * mtop
        z = bot[q].astype(F32) * mbot
        for i in range(per):
            d = q * per + i
            a = t if i == 0 else pltpu.roll(t, 128 - feat * i, 1)
            y = z if i == 1 else pltpu.roll(z, (128 + feat - feat * i) % 128, 1)
            buf[d, PAD : PAD + cols, 0:128] = ctl[d].astype(F32)
            buf[d, :, 128:256] = jnp.where(lane < feat, a, jnp.where(lane < 2 * feat, y, 0.0))
            for e in range(3):
                ctsh[d + 1, :, 256 * e : 256 * (e + 1)] = buf[
                    d, PAD - 1 + e : PAD - 1 + e + cols
                ].astype(BF16)
        return 0

    lax.fori_loop(0, disp // per, fill, 0, unroll=True)
    step = 256 // cols
    for q in range(disp // step):
        for p in range(rows // 2):
            v = vbuf[p, q * step : (q + 1) * step, PAD : PAD + cols].reshape(256, 128).astype(BF16)
            vt[128 * p : 128 * (p + 1), 256 * q : 256 * (q + 1)] = v.T
    keep = lanes((groups, 128))
    sums[...] = jnp.zeros(sums.shape, F32)

    def taps(a, _):
        for e in range(3):
            ct_block = ctsh[pl.ds(a, disp), :, 256 * e : 256 * (e + 1)].reshape(disp * cols, 256)
            full = dot(vt[...], ct_block)
            out = None
            for h in range(rows):
                x = full[SLOT * h : SLOT * h + groups, 0:128]
                y = full[SLOT * h : SLOT * h + groups, 128:256]
                if h == 0:
                    term = jnp.where(keep < feat, y, pltpu.roll(x, feat, 1))
                else:
                    term = x if h == 1 else pltpu.roll(x, 128 - feat * (h - 1), 1)
                    if h == rows - 1:
                        term = jnp.where(keep < 2 * feat, term, pltpu.roll(y, feat, 1))
                out = term if out is None else out + term
            at = pl.multiple_of(a * 128 + groups * e, 8)
            sums[pl.ds(at, groups)] = jnp.where(keep < 3 * feat, out, 0.0)
        return 0

    lax.fori_loop(0, 3, taps, 0)
    half = sums.shape[0] // 2
    is_even = parity() == 0
    low, high = sums[0:half], sums[half:]
    keep_out[...] = jnp.where(is_even, low, high)
    give_out[...] = jnp.where(is_even, high, low)


def right_kernel(ctsh, w2, fl, gv, rg0, rg1, rg2, acce, acco, both):
    disp = ctsh.shape[0] - 2
    rows, cols, channels = rg0.shape
    wide = fl.shape[2]
    group_size = wide // SLOT
    step = 512 // cols
    low = lanes((512, 128)) < SLOT

    def conv(q, _):
        slabs = [ctsh[pl.ds(q * step + a, step)].reshape(512, ctsh.shape[2]) for a in range(3)]
        acc = dot(jnp.concatenate(slabs, axis=1), w2[...])
        g = acc.astype(BF16).astype(F32)
        for p in range(rows // 2):
            x = g[:, 128 * p : 128 * (p + 1)]
            r = pltpu.roll(x, SLOT, 1)
            for o in range(2):
                y = jnp.where(low, r, x) if o else jnp.where(low, x, r)
                gv[2 * p + o, pl.ds(q * step, step)] = y.reshape(step, cols, 128)
        return 0

    lax.fori_loop(0, disp // step, conv, 0)
    count = cols // 8
    back = acce.shape[1] - cols
    lead = back // 8

    lots = wide // 128

    def right_row(h, _):
        here = [
            [fl[h, PAD + 8 * b : PAD + 8 * b + 8, 128 * j : 128 * (j + 1)] for j in range(lots)]
            for b in range(count)
        ]
        for odd, buf in enumerate((acce, acco)):
            for k in range(lead + count):
                accs = [None] * lots
                for t in range(disp // 2):
                    b = k + t - lead
                    if b < 0 or b >= count:
                        continue
                    g = gv[h, 2 * t + odd, 8 * b : 8 * b + 8]
                    for j in range(lots):
                        term = g * here[b][j]
                        accs[j] = term if accs[j] is None else accs[j] + term
                for j in range(lots):
                    x = jnp.zeros((8, 128), F32) if accs[j] is None else accs[j]
                    buf[h, 8 * k : 8 * k + 8, 128 * j : 128 * (j + 1)] = x
        acco[h, 8 * (lead + count) :] = jnp.zeros((8, wide), F32)
        return 0

    lax.fori_loop(0, rows, right_row, 0)
    size = back + cols
    for h in range(rows):
        both[h * size : (h + 1) * size] = (acce[h] + acco[h, STEP : STEP + size]).astype(BF16)
    whole = dot(both[...], channel_table(channels, group_size, True)).astype(BF16)
    half = cols // 2
    for h in range(rows):
        at = h * size + back
        rg2[h] = whole[at - cols - half : at - cols]
        rg1[h] = whole[at - cols : at]
        rg0[h] = whole[at : at + cols]


def left_kernel(gv, fr, fr4, lg, accl):
    rows, cols, channels = lg.shape
    disp, wide = gv.shape[1], fr.shape[2]
    group_size = wide // SLOT
    reach = fr.shape[1] - cols - PAD
    count, times, lots = cols // 8, disp // 2, wide // 128

    def left_row(h, _):
        accs = [[None] * lots for _ in range(count)]
        for odd, band in enumerate((fr, fr4)):
            for r in range(1 - times, count):
                at = reach + 8 * r
                here = [band[h, at : at + 8, 128 * j : 128 * (j + 1)] for j in range(lots)]
                for t in range(max(0, -r), min(times, count - r)):
                    g = gv[h, 2 * t + odd, 8 * (r + t) : 8 * (r + t) + 8]
                    for j in range(lots):
                        term, acc = g * here[j], accs[r + t][j]
                        accs[r + t][j] = term if acc is None else acc + term
        for b in range(count):
            for j in range(lots):
                accl[h, 8 * b : 8 * b + 8, 128 * j : 128 * (j + 1)] = accs[b][j] * (1.0 / group_size)
        return 0

    lax.fori_loop(0, rows, left_row, 0)
    whole = accl[...].reshape(rows * cols, wide).astype(BF16)
    out = dot(whole, channel_table(channels, group_size, True)).astype(BF16)
    lg[...] = out.reshape(rows, cols, channels)


def combine_kernel(got, rg2, out):
    cols = out.shape[1]
    half = cols // 2
    part = jnp.where(parity() == 0, 0.0, got[...].astype(F32))
    out[:, 0:half] = part[:, 0:half].astype(BF16)
    out[:, half:] = (part[:, half:] + rg2[...].astype(F32)).astype(BF16)


def halo_lanes(groups):
    first = SLOT - groups
    assert groups - first <= first
    return (groups, SLOT, groups), (SLOT + groups, SLOT + 2 * groups - first, SLOT + groups - first)


def place_halo(base, row, groups, offset, lane):
    for start, end, shift in halo_lanes(groups):
        moved = pltpu.roll(row, (shift - offset) % 128, 1)
        base = jnp.where((lane >= start) & (lane < end), moved, base)
    return base


def conv_kernel(masks, groups, vbuf, top, bot, wc, out, taps, buf):
    disp, rows, feat, cols = out.shape
    total = buf.shape[2]
    lane = lanes((total, 128))
    zeros = jnp.zeros((cols, taps.shape[3]), BF16)
    taps[0, 0] = zeros
    taps[disp // 2, 1] = zeros
    halos_of = [(ref, mask) for ref, mask in zip((top, bot), masks())]
    for dd in range(disp // 2):
        for p, (ref, mask) in enumerate(halos_of):
            row = ref[dd * total : (dd + 1) * total].astype(F32) * mask
            for o in range(2):
                d = 2 * dd + o
                buf[p, d] = place_halo(vbuf[p, d], row, groups, SLOT * o, lane)
                for e in range(3):
                    at = 256 * e + 128 * p
                    taps[(d + 1) // 2, (d + 1) % 2, :, at : at + 128] = buf[
                        p, d, PAD - 1 + e : PAD - 1 + e + cols
                    ].astype(BF16)
    step = 6

    def conv(q, _):
        slabs = [
            taps[pl.ds(q * step + s // 2, step), s % 2].reshape(step * cols, taps.shape[3])
            for s in range(4)
        ]
        acc = dot(jnp.concatenate(slabs, axis=1), wc[...])
        for j in range(step):
            both = acc[j * cols : (j + 1) * cols].T.astype(BF16)
            for o in range(2):
                block = both[rows * feat * o : rows * feat * (o + 1)]
                out[2 * (q * step + j) + o] = block.reshape(rows, feat, cols)
        return 0

    lax.fori_loop(0, disp // 2 // step, conv, 0)


def finish_kernel(scale, mine, other, own, near, far, weight, right):
    _, _, _, feat, groups = weight.shape
    is_even = parity() == 0
    x, y = mine[...] * scale, other[...] * scale
    total = jnp.concatenate([jnp.where(is_even, x, y), jnp.where(is_even, y, x)], axis=0)
    for a in range(3):
        for e in range(3):
            at = 128 * a + groups * e
            block = total[at : at + groups].T
            for b in range(3):
                weight[2 - a, 2 - b, 2 - e] = block[feat * b : feat * (b + 1)]
    beside = jnp.where(is_even, near[...].astype(F32), 0.0)
    right[...] = (own[...].astype(F32) + beside + far[...].astype(F32)).astype(BF16)


def sum_kernel(*refs):
    *parts, out = refs
    out[...] = tree([ref[...].astype(F32) for ref in parts]).astype(out.dtype)


def tree(terms):
    while len(terms) > 1:
        terms = [terms[i] + terms[i + 1] for i in range(0, len(terms), 2)]
    return terms[0]


def taps_kernel(taps, w2, wc, turned):
    _, _, _, feat, groups = taps.shape
    rows = wc.shape[1] // 2 // feat
    lane_of = lanes((feat, 2 * SLOT))
    low = lanes((feat, 2 * SLOT)) < SLOT
    zero = jnp.zeros((feat, 2 * SLOT), F32)

    def wide(a, b, e):
        if not 0 <= b <= 2:
            return None
        return jnp.concatenate([taps[a, b, e].astype(F32), zero[:, groups:]], axis=1)

    def beside(x, y):
        if x is None and y is None:
            return zero
        x = zero if x is None else x
        y = zero if y is None else pltpu.roll(y, SLOT, 1)
        return jnp.where(low, x, y)

    def build(a, _):
        def at_row(h):
            return pl.multiple_of((a * rows + h) * feat, feat)

        def at_tap(row):
            return pl.multiple_of(a * 3 * 256 + row, feat)

        for e in range(3):
            for h in range(rows):
                for p in range(rows // 2):
                    lane = SLOT * (rows * e + 2 * p)
                    block = beside(wide(a, 2 * p - h + 1, e), wide(a, 2 * p + 1 - h + 1, e))
                    if h == 0 and p == 0:
                        block = place_halo(block, wide(a, 0, e), groups, 0, lane_of)
                    if h == rows - 1 and p == rows // 2 - 1:
                        block = place_halo(block, wide(a, 2, e), groups, 0, lane_of)
                    turned[pl.ds(at_row(h), feat), lane : lane + 2 * SLOT] = block
            for slot, six in enumerate((*range(1, rows + 1), 0, rows + 1)):
                at = 256 * e + feat * slot
                for p in range(rows // 2):
                    back = [2 - (six - 2 * p - o) for o in range(2)]
                    w2[pl.ds(at_tap(at), feat), 2 * SLOT * p : 2 * SLOT * (p + 1)] = beside(
                        wide(2 - a, back[0], 2 - e), wide(2 - a, back[1], 2 - e)
                    ).astype(BF16)
            at = 256 * e + feat * (rows + 2)
            size = 256 - feat * (rows + 2)
            w2[pl.ds(at_tap(at), size)] = jnp.zeros((size, rows * SLOT), BF16)
        return 0

    lax.fori_loop(0, 3, build, 0)
    depth, size = turned.shape[1], rows * feat
    for a in range(3):
        for i in range(depth // 128):
            x = turned[size * a : size * (a + 1), 128 * i : 128 * (i + 1)].T.astype(BF16)
            for o in range(2):
                at = depth * (a + o) + 128 * i
                wc[at : at + 128, size * o : size * (o + 1)] = x
    for o in range(2):
        at = depth * 3 * (1 - o)
        wc[at : at + depth, size * o : size * (o + 1)] = jnp.zeros((depth, size), BF16)


TOKEN = ((8, 128), F32)


def with_token(kernel, inputs, outputs):
    def run(*refs):
        kernel(*refs[: inputs + outputs], *refs[inputs + outputs + 1 :])
        refs[inputs + outputs][...] = jnp.zeros(TOKEN[0], F32)

    return run


def call(kernel, outs, scratch, *args, after=(), token=False):
    skip = len(after)
    if token:
        kernel = with_token(kernel, len(args), len(outs))
        outs = [*outs, TOKEN]
    return pl.pallas_call(
        lambda *refs: kernel(*refs[skip:]),
        out_shape=[jax.ShapeDtypeStruct(s, t) for s, t in outs],
        in_specs=[pl.BlockSpec(memory_space=pl.ANY)] * skip + [VMEM] * len(args),
        out_specs=[VMEM] * len(outs),
        scratch_shapes=scratch,
        compiler_params=pltpu.CompilerParams(vmem_limit_bytes=LIMIT),
    )(*after, *args)


def col_shift(block, distance):
    n = lax.axis_size("col")
    route = [(i - distance, i) for i in range(n) if 0 <= i - distance < n]
    return lax.ppermute(block, "col", route)


def row_shift(block, distance):
    n = lax.axis_size("row")
    route = [(i - distance, i) for i in range(n) if 0 <= i - distance < n]
    return lax.ppermute(block, "row", route)


def halos(pays):
    if lax.axis_size("row") == 2:
        got = lax.ppermute(pays[0], "row", [(0, 1), (1, 0)])
        return got, got
    return row_shift(pays[0], 1), row_shift(pays[1], -1)


def stages(n_row, n_col):
    col_bits = [1 << i for i in range(1, n_col.bit_length() - 1)]
    row_bits = [n_col << i for i in range(n_row.bit_length() - 1)]
    assert n_col == 2 << len(col_bits) and n_row == 1 << len(row_bits)
    bits = col_bits[:1] + row_bits + col_bits[1:]
    out = []
    for i in range(0, len(bits), 2):
        pair = bits[i : i + 2]
        out.append(pair + [sum(pair)] if len(pair) == 2 else pair)
    return out


def on_device(left_features, right_features, conv_weight, cotangent):
    rows, cols, channels = left_features.shape
    disp, feat = cotangent.shape[0], cotangent.shape[3]
    groups = conv_weight.shape[3]
    group_size = channels // groups
    wide = group_size * SLOT
    n_row, n_col = lax.axis_size("row"), lax.axis_size("col")
    per = 128 // feat

    if n_row == 2:
        ends = [lambda: (rows - 1) * (1 - lax.axis_index("row"))]
    else:
        ends = [lambda: rows - 1, lambda: 0]
    n = len(ends)

    def masks():
        at = lax.axis_index("row")
        return (
            jnp.where(at > 0, 1.0, 0.0).astype(F32),
            jnp.where(at < n_row - 1, 1.0, 0.0).astype(F32),
        )

    total = cols + 2 * PAD
    count = disp + 2 * rows
    ct = cotangent.transpose(0, 1, 3, 2)

    def swap(block, mask):
        route = [(i, i ^ mask) for i in range(n_row * n_col)]
        return lax.ppermute(block, ("row", "col"), route)

    far = col_shift(right_features, 2)
    by_even, by_odd, ctl, *rims = call(
        functools.partial(pack_kernel, ends),
        [
            ((count, channels), BF16),
            ((count, channels), BF16),
            ((disp, cols, rows * feat), BF16),
        ]
        + [((disp // per, total, 128), F32)] * n,
        [pltpu.VMEM((disp * cols, rows * feat), F32)],
        left_features,
        right_features,
        ct,
    )
    inner = range(1, n_col - 1, 2)
    by_even = swap(by_even, 1)
    by_odd = lax.ppermute(by_odd, "col", [(i, i + 1) for i in inner] + [(i + 1, i) for i in inner])
    w2, wc = call(
        taps_kernel,
        [((9 * 256, rows * SLOT), BF16), ((4 * 3 * rows * SLOT, 2 * rows * feat), BF16)],
        [pltpu.VMEM((3 * rows * feat, 3 * rows * SLOT), F32)],
        conv_weight.transpose(0, 1, 2, 4, 3),
    )
    row_pays = call(
        functools.partial(row_kernel, ends, rows),
        [((disp // per, total, 128), BF16)] * n,
        [pltpu.VMEM((2, disp, 128), F32), pltpu.VMEM((disp // per, total, 128), F32)],
        by_even,
        by_odd,
        *rims,
        after=[w2],
    )
    top, bot = halos(row_pays)
    (near,) = call(
        pass_kernel,
        [((rows, cols, channels), BF16)],
        [],
        right_features,
        far,
        after=row_pays,
    )
    near = swap(near, 1)

    band = 104 + cols + PAD
    spread_rows = 3 * rows * cols + rows * cols // 2 + 2 * count
    vbuf, fl, fr, fr4, *volume_rows = call(
        functools.partial(volume_kernel, ends, group_size),
        [
            ((rows // 2, disp, total, 2 * SLOT), F32),
            ((rows, total, wide), F32),
            ((rows, band, wide), F32),
            ((rows, band, wide), F32),
        ]
        + [((disp // 2 * total, 128), BF16)] * n,
        [
            pltpu.VMEM((spread_rows, channels), BF16),
            pltpu.VMEM((spread_rows, wide), F32),
        ],
        left_features,
        right_features,
        near,
        far,
        by_even,
        by_odd,
    )
    vtop, vbot = halos(volume_rows)

    keep, give, ctsh = call(
        functools.partial(weight_kernel, masks, groups),
        [((3 * 64, 128), F32), ((3 * 64, 128), F32), ((disp + 2, cols, 3 * 256), BF16)],
        [
            pltpu.VMEM((rows * SLOT, disp * cols), BF16),
            pltpu.VMEM((disp, total, 256), F32),
            pltpu.VMEM((3 * 128, 128), F32),
        ],
        vbuf, ctl, by_even, by_odd, top, bot,
    )
    got = swap(give, 1)
    gv, rg0, rg1, rg2 = call(
        right_kernel,
        [
            ((rows, disp, cols, 128), F32),
            ((rows, cols, channels), BF16),
            ((rows, cols, channels), BF16),
            ((rows, cols // 2, channels), BF16),
        ],
        [
            pltpu.VMEM((rows, cols + cols + cols // 2, wide), F32),
            pltpu.VMEM((rows, cols + cols + cols // 2 + 8, wide), F32),
            pltpu.VMEM((rows * (cols + cols + cols // 2), wide), BF16),
        ],
        ctsh, w2, fl,
    )
    rg1 = swap(rg1, 1)
    (part,) = call(sum_kernel, [(keep.shape, BF16)], [], keep, got, after=[rg0])
    output, conv_done = call(
        functools.partial(conv_kernel, masks, groups),
        [((disp, rows, feat, cols), BF16)],
        [
            pltpu.VMEM((disp // 2 + 1, 2, cols, 3 * rows * SLOT), BF16),
            pltpu.VMEM((rows // 2, disp, total, 128), F32),
        ],
        vbuf, vtop, vbot, wc,
        after=[part],
        token=True,
    )
    (rg2,) = call(
        combine_kernel, [((rows, cols, channels), BF16)], [], rg1, rg2, after=[conv_done]
    )
    rg2 = col_shift(rg2, -2)
    *middle, final = stages(n_row, n_col)
    order = [conv_done]
    for stage in middle:
        parts = [part] + [swap(part, m) for m in stage]
        (part,) = call(sum_kernel, [(part.shape, BF16)], [], *parts, after=order)
        order = []
    lg, left_done = call(
        left_kernel,
        [((rows, cols, channels), BF16)],
        [pltpu.VMEM((rows, cols, wide), F32)],
        gv, fr, fr4,
        after=[part],
        token=True,
    )
    parts = [part] + [swap(part, m) for m in final]
    (part,) = call(sum_kernel, [(part.shape, F32)], [], *parts, after=[left_done])
    cells = disp * rows * n_row * cols * n_col
    weight_grad, right_grad = call(
        functools.partial(finish_kernel, 1.0 / math.sqrt(cells)),
        [((3, 3, 3, feat, groups), F32), ((rows, cols, channels), BF16)],
        [],
        part, swap(part, 1), rg0, rg1, rg2,
    )
    return (
        output.transpose(0, 1, 3, 2),
        weight_grad.transpose(0, 1, 2, 4, 3),
        lg,
        right_grad,
    )


def solution(mesh):
    in_specs = (P("row", "col", None), P("row", "col", None), P(), P(None, "row", "col", None))
    out_specs = (P(None, "row", "col", None), P(), P("row", "col", None), P("row", "col", None))
    return jax.shard_map(
        on_device, mesh=mesh, in_specs=in_specs, out_specs=out_specs, check_vma=False
    )
```

```python
import functools
import math

import jax
import jax.numpy as jnp
from jax import lax
from jax.experimental import pallas as pl
from jax.experimental.pallas import tpu as pltpu
from jax.sharding import PartitionSpec as P

DISP = 24
STEP = 4
SLOT = 64
PAD = 8
F32 = jnp.float32
BF16 = jnp.bfloat16
VMEM = pl.BlockSpec(memory_space=pltpu.VMEM)
LIMIT = 16 * 1024 * 1024


def lanes(shape):
    return lax.broadcasted_iota(jnp.int32, shape, len(shape) - 1)


def channel_table(channels, group_size, flip, value=1.0):
    shape = (group_size * SLOT, channels) if flip else (channels, group_size * SLOT)
    c = lax.broadcasted_iota(jnp.int32, shape, 1 if flip else 0)
    j = lax.broadcasted_iota(jnp.int32, shape, 0 if flip else 1)
    hit = c == (j & (SLOT - 1)) * group_size + (j >> (SLOT.bit_length() - 1))
    return jnp.where(hit, value, 0.0).astype(BF16)


def parity():
    return lax.rem(lax.axis_index("col"), 2)


def dot(a, b):
    return jnp.dot(a, b, preferred_element_type=F32)


def dot_nt(a, b):
    return lax.dot_general(a, b, (((1,), (1,)), ((), ())), preferred_element_type=F32)


def pack_kernel(ends, left, right, ct, even, odd, ctl, *rest):
    rims, ctf = rest[:-1], rest[-1]
    disp, rows, feat, cols = ct.shape
    per = 128 // feat
    for d in range(disp):
        block = ct[d].reshape(rows * feat, cols).astype(F32).T
        ctf[d * cols : (d + 1) * cols] = block
        ctl[d] = block.astype(BF16)
    columns = []
    for col in (cols - 1, 0):
        block = ctf[pl.ds(col, disp, stride=cols), :]
        block = jnp.concatenate([block, jnp.zeros((disp, left.shape[2] - rows * feat), F32)], axis=1)
        edge = [left[h, col : col + 1].astype(F32) for h in range(rows)]
        edge += [right[h, col : col + 1].astype(F32) for h in range(rows)]
        columns.append(jnp.concatenate([block, *edge], axis=0))
    is_even = parity() == 0
    even[...] = jnp.where(is_even, columns[0], columns[1]).astype(BF16)
    odd[...] = jnp.where(is_even, columns[1], columns[0]).astype(BF16)
    for end, rim in zip(ends, rims):
        h = end()
        for q in range(disp // per):
            rim[q, PAD : PAD + cols] = jnp.concatenate(
                [ct[q * per + i, h].astype(F32) for i in range(per)], axis=0
            ).T


def pass_kernel(own, got, end, out, end_out):
    end_out[...] = end[...]
    out[...] = jnp.where(parity() == 0, own[...].astype(F32), got[...].astype(F32)).astype(BF16)


def end_columns(by_even, by_odd):
    x, y = by_even[...].astype(F32), by_odd[...].astype(F32)
    is_even = parity() == 0
    return jnp.where(is_even, y, x), jnp.where(is_even, x, y)


def row_kernel(ends, rows, by_even, by_odd, *rest):
    n = len(ends)
    rims, pays, (edges, buf) = rest[:n], rest[n : 2 * n], rest[2 * n :]
    count, total, _ = buf.shape
    disp = edges.shape[1]
    per, cols = disp // count, total - 2 * PAD
    feat = 128 // per
    lane = lanes((count, 128))
    for side, x in enumerate(end_columns(by_even, by_odd)):
        edges[side] = x[0:disp, 0:128]
    for end, rim, pay in zip(ends, rims, pays):
        h = end()
        buf[...] = rim[...]
        for side, at in ((0, PAD - 1), (1, PAD + cols)):
            out = jnp.zeros((count, 128), F32)
            for i in range(per):
                x = edges[side, pl.ds(i, count, stride=per)]
                first = pltpu.roll(x, feat * i, 1) if i else x
                last = pltpu.roll(x, (feat * (i - rows + 1)) % 128, 1) if i != rows - 1 else x
                x = jnp.where(h == 0, first, last)
                out = jnp.where((lane >= feat * i) & (lane < feat * (i + 1)), x, out)
            for q in range(count):
                buf[q, at : at + 1] = out[q : q + 1]
        pay[...] = buf[...].astype(BF16)


def volume_kernel(ends, group_size, left, right, near, far, by_even, by_odd, vbuf, fl, fr, fr4, *rest):
    pays, (mixed, wide_buf) = rest[: len(ends)], rest[len(ends) :]
    rows, cols, channels = left.shape
    disp = vbuf.shape[1]
    reach = fr.shape[1] - cols - PAD
    wide = group_size * SLOT
    base, half = rows * cols, cols // 2
    mixed[0:base] = near[...].reshape(base, channels)
    mixed[base : 2 * base] = right[...].reshape(base, channels)
    mixed[2 * base : 3 * base] = left[...].reshape(base, channels)
    at_far, at_ends = 3 * base, 3 * base + base // 2
    mixed[at_far:at_ends] = far[:, half:].reshape(base // 2, channels)
    count = disp + 2 * rows
    for i, x in enumerate(end_columns(by_even, by_odd)):
        mixed[at_ends + i * count : at_ends + (i + 1) * count] = x.astype(BF16)
    wide_buf[...] = dot(mixed[...], channel_table(channels, group_size, False))
    scale = 1.0 / group_size
    for h in range(rows):
        fl[h, 0:PAD] = jnp.zeros((PAD, wide), F32)
        fl[h, PAD + cols :] = jnp.zeros((PAD, wide), F32)
        at = at_ends + disp + h
        fl[h, PAD - 1 : PAD] = wide_buf[at : at + 1] * scale
        fl[h, PAD : PAD + cols] = wide_buf[2 * base + h * cols : 2 * base + (h + 1) * cols] * scale
        at += count
        fl[h, PAD + cols : PAD + cols + 1] = wide_buf[at : at + 1] * scale
        for ref, off in ((fr, 0), (fr4, STEP)):
            start = reach - cols - half + off
            ref[h, 0:start] = jnp.zeros((start, wide), F32)
            ref[h, start : start + half] = wide_buf[at_far + h * half : at_far + (h + 1) * half]
            for part in range(2):
                at = part * base + h * cols
                to = start + half + part * cols
                ref[h, to : to + cols] = wide_buf[at : at + cols]
            to = start + half + 2 * cols
            ref[h, to:] = jnp.zeros((ref.shape[1] - to, wide), F32)
            at = at_ends + count + disp + rows + h
            ref[h, to : to + 1] = wide_buf[at : at + 1]
    total = cols + 2 * PAD
    low = lanes((8, 128)) < SLOT
    pairs, times, lots = rows // 2, disp // 2, wide // 128
    count = total // 16

    def products(i, _):
        p, at = lax.rem(i, pairs), pl.multiple_of(lax.div(i, pairs) * (8 * count), 8)
        lefts = [
            [
                [fl[2 * p + o, pl.ds(at + 8 * b, 8), 128 * j : 128 * (j + 1)] for j in range(lots)]
                for b in range(count)
            ]
            for o in range(2)
        ]
        for odd, band in enumerate((fr, fr4)):
            for r in range(1 - times, count):
                start = pl.multiple_of(at + reach - PAD + 8 * r, 8)
                here = [
                    [band[2 * p + o, pl.ds(start, 8), 128 * j : 128 * (j + 1)] for j in range(lots)]
                    for o in range(2)
                ]
                for t in range(max(0, -r), min(times, count - r)):
                    sums = []
                    for o in range(2):
                        acc = lefts[o][r + t][0] * here[o][0]
                        for j in range(1, lots):
                            acc = acc + lefts[o][r + t][j] * here[o][j]
                        sums.append(acc + pltpu.roll(acc, SLOT, 1))
                    vbuf[p, 2 * t + odd, pl.ds(at + 8 * (r + t), 8)] = jnp.where(low, *sums)
        return 0

    lax.fori_loop(0, 2 * pairs, products, 0)
    big = lanes((total, 128)) < SLOT

    for dd in range(disp // 2):
        for end, pay in zip(ends, pays):
            h = end()
            if isinstance(h, int):
                halves = [vbuf[h // 2, 2 * dd + o] for o in range(2)]
                if h % 2 == 0:
                    halves[1] = pltpu.roll(halves[1], SLOT, 1)
                else:
                    halves[0] = pltpu.roll(halves[0], SLOT, 1)
                out = jnp.where(big, halves[0], halves[1])
            else:
                last = pairs - 1
                first = jnp.where(big, vbuf[0, 2 * dd], pltpu.roll(vbuf[0, 2 * dd + 1], SLOT, 1))
                final = jnp.where(
                    big, pltpu.roll(vbuf[last, 2 * dd], SLOT, 1), vbuf[last, 2 * dd + 1]
                )
                out = jnp.where(h == 0, first, final)
            pay[dd * total : (dd + 1) * total] = out.astype(BF16)


def weight_kernel(masks, groups, vbuf, ctl, by_even, by_odd, top, bot, keep_out, give_out, ctsh, vt, buf, sums):
    disp, cols, width = ctl.shape
    rows, feat = 2 * vbuf.shape[0], 32
    per = 128 // feat
    mtop, mbot = masks()
    ctsh[0] = jnp.zeros(ctsh.shape[1:], BF16)
    ctsh[disp + 1] = jnp.zeros(ctsh.shape[1:], BF16)
    lane = lanes(top.shape[1:])
    edges = [x[0:disp, 0:128] for x in end_columns(by_even, by_odd)]
    for d in range(disp):
        buf[d, PAD - 1 : PAD, 0:128] = edges[0][d : d + 1]
        buf[d, PAD + cols : PAD + cols + 1, 0:128] = edges[1][d : d + 1]

    def fill(q, _):
        t = top[q].astype(F32) * mtop
        z = bot[q].astype(F32) * mbot
        for i in range(per):
            d = q * per + i
            a = t if i == 0 else pltpu.roll(t, 128 - feat * i, 1)
            y = z if i == 1 else pltpu.roll(z, (128 + feat - feat * i) % 128, 1)
            buf[d, PAD : PAD + cols, 0:128] = ctl[d].astype(F32)
            buf[d, :, 128:256] = jnp.where(lane < feat, a, jnp.where(lane < 2 * feat, y, 0.0))
            for e in range(3):
                ctsh[d + 1, :, 256 * e : 256 * (e + 1)] = buf[
                    d, PAD - 1 + e : PAD - 1 + e + cols
                ].astype(BF16)
        return 0

    lax.fori_loop(0, disp // per, fill, 0, unroll=True)
    step = 256 // cols
    for q in range(disp // step):
        for p in range(rows // 2):
            v = vbuf[p, q * step : (q + 1) * step, PAD : PAD + cols].reshape(256, 128).astype(BF16)
            vt[128 * p : 128 * (p + 1), 256 * q : 256 * (q + 1)] = v.T
    keep = lanes((groups, 128))
    sums[...] = jnp.zeros(sums.shape, F32)

    def taps(a, _):
        for e in range(3):
            ct_block = ctsh[pl.ds(a, disp), :, 256 * e : 256 * (e + 1)].reshape(disp * cols, 256)
            full = dot(vt[...], ct_block)
            out = None
            for h in range(rows):
                x = full[SLOT * h : SLOT * h + groups, 0:128]
                y = full[SLOT * h : SLOT * h + groups, 128:256]
                if h == 0:
                    term = jnp.where(keep < feat, y, pltpu.roll(x, feat, 1))
                else:
                    term = x if h == 1 else pltpu.roll(x, 128 - feat * (h - 1), 1)
                    if h == rows - 1:
                        term = jnp.where(keep < 2 * feat, term, pltpu.roll(y, feat, 1))
                out = term if out is None else out + term
            at = pl.multiple_of(a * 128 + groups * e, 8)
            sums[pl.ds(at, groups)] = jnp.where(keep < 3 * feat, out, 0.0)
        return 0

    lax.fori_loop(0, 3, taps, 0)
    half = sums.shape[0] // 2
    is_even = parity() == 0
    low, high = sums[0:half], sums[half:]
    keep_out[...] = jnp.where(is_even, low, high)
    give_out[...] = jnp.where(is_even, high, low)


def right_kernel(ctsh, w2, fl, gv, rg0, rg1, rg2, acce, acco, both):
    disp = ctsh.shape[0] - 2
    rows, cols, channels = rg0.shape
    wide = fl.shape[2]
    group_size = wide // SLOT
    step = 512 // cols
    low = lanes((512, 128)) < SLOT

    def conv(q, _):
        slabs = [ctsh[pl.ds(q * step + a, step)].reshape(512, ctsh.shape[2]) for a in range(3)]
        acc = dot(jnp.concatenate(slabs, axis=1), w2[...])
        g = acc.astype(BF16).astype(F32)
        for p in range(rows // 2):
            x = g[:, 128 * p : 128 * (p + 1)]
            r = pltpu.roll(x, SLOT, 1)
            for o in range(2):
                y = jnp.where(low, r, x) if o else jnp.where(low, x, r)
                gv[2 * p + o, pl.ds(q * step, step)] = y.reshape(step, cols, 128)
        return 0

    lax.fori_loop(0, disp // step, conv, 0)
    count = cols // 8
    back = acce.shape[1] - cols
    lead = back // 8

    lots = wide // 128

    def right_row(h, _):
        here = [
            [fl[h, PAD + 8 * b : PAD + 8 * b + 8, 128 * j : 128 * (j + 1)] for j in range(lots)]
            for b in range(count)
        ]
        for odd, buf in enumerate((acce, acco)):
            for k in range(lead + count):
                accs = [None] * lots
                for t in range(disp // 2):
                    b = k + t - lead
                    if b < 0 or b >= count:
                        continue
                    g = gv[h, 2 * t + odd, 8 * b : 8 * b + 8]
                    for j in range(lots):
                        term = g * here[b][j]
                        accs[j] = term if accs[j] is None else accs[j] + term
                for j in range(lots):
                    x = jnp.zeros((8, 128), F32) if accs[j] is None else accs[j]
                    buf[h, 8 * k : 8 * k + 8, 128 * j : 128 * (j + 1)] = x
        acco[h, 8 * (lead + count) :] = jnp.zeros((8, wide), F32)
        return 0

    lax.fori_loop(0, rows, right_row, 0)
    size = back + cols
    for h in range(rows):
        both[h * size : (h + 1) * size] = (acce[h] + acco[h, STEP : STEP + size]).astype(BF16)
    whole = dot(both[...], channel_table(channels, group_size, True)).astype(BF16)
    half = cols // 2
    for h in range(rows):
        at = h * size + back
        rg2[h] = whole[at - cols - half : at - cols]
        rg1[h] = whole[at - cols : at]
        rg0[h] = whole[at : at + cols]


def left_kernel(gv, fr, fr4, lg, accl):
    rows, cols, channels = lg.shape
    disp, wide = gv.shape[1], fr.shape[2]
    group_size = wide // SLOT
    reach = fr.shape[1] - cols - PAD
    count, times, lots = cols // 8, disp // 2, wide // 128

    def left_row(h, _):
        accs = [[None] * lots for _ in range(count)]
        for odd, band in enumerate((fr, fr4)):
            for r in range(1 - times, count):
                at = reach + 8 * r
                here = [band[h, at : at + 8, 128 * j : 128 * (j + 1)] for j in range(lots)]
                for t in range(max(0, -r), min(times, count - r)):
                    g = gv[h, 2 * t + odd, 8 * (r + t) : 8 * (r + t) + 8]
                    for j in range(lots):
                        term, acc = g * here[j], accs[r + t][j]
                        accs[r + t][j] = term if acc is None else acc + term
        for b in range(count):
            for j in range(lots):
                accl[h, 8 * b : 8 * b + 8, 128 * j : 128 * (j + 1)] = accs[b][j] * (1.0 / group_size)
        return 0

    lax.fori_loop(0, rows, left_row, 0)
    whole = accl[...].reshape(rows * cols, wide).astype(BF16)
    out = dot(whole, channel_table(channels, group_size, True)).astype(BF16)
    lg[...] = out.reshape(rows, cols, channels)


def combine_kernel(got, rg2, out):
    cols = out.shape[1]
    half = cols // 2
    part = jnp.where(parity() == 0, 0.0, got[...].astype(F32))
    out[:, 0:half] = part[:, 0:half].astype(BF16)
    out[:, half:] = (part[:, half:] + rg2[...].astype(F32)).astype(BF16)


def halo_lanes(groups):
    first = SLOT - groups
    assert groups - first <= first
    return (groups, SLOT, groups), (SLOT + groups, SLOT + 2 * groups - first, SLOT + groups - first)


def place_halo(base, row, groups, offset, lane):
    for start, end, shift in halo_lanes(groups):
        moved = pltpu.roll(row, (shift - offset) % 128, 1)
        base = jnp.where((lane >= start) & (lane < end), moved, base)
    return base


def conv_kernel(masks, groups, vbuf, top, bot, wc, out, taps, buf):
    disp, rows, feat, cols = out.shape
    total = buf.shape[2]
    lane = lanes((total, 128))
    zeros = jnp.zeros((cols, taps.shape[3]), BF16)
    taps[0, 0] = zeros
    taps[disp // 2, 1] = zeros
    halos_of = [(ref, mask) for ref, mask in zip((top, bot), masks())]
    for dd in range(disp // 2):
        for p, (ref, mask) in enumerate(halos_of):
            row = ref[dd * total : (dd + 1) * total].astype(F32) * mask
            for o in range(2):
                d = 2 * dd + o
                buf[p, d] = place_halo(vbuf[p, d], row, groups, SLOT * o, lane)
                for e in range(3):
                    at = 256 * e + 128 * p
                    taps[(d + 1) // 2, (d + 1) % 2, :, at : at + 128] = buf[
                        p, d, PAD - 1 + e : PAD - 1 + e + cols
                    ].astype(BF16)
    step = 6

    def conv(q, _):
        slabs = [
            taps[pl.ds(q * step + s // 2, step), s % 2].reshape(step * cols, taps.shape[3])
            for s in range(4)
        ]
        acc = dot(jnp.concatenate(slabs, axis=1), wc[...])
        for j in range(step):
            both = acc[j * cols : (j + 1) * cols].T.astype(BF16)
            for o in range(2):
                block = both[rows * feat * o : rows * feat * (o + 1)]
                out[2 * (q * step + j) + o] = block.reshape(rows, feat, cols)
        return 0

    lax.fori_loop(0, disp // 2 // step, conv, 0)


def finish_kernel(scale, mine, other, own, near, far, weight, right):
    _, _, _, feat, groups = weight.shape
    is_even = parity() == 0
    x, y = mine[...] * scale, other[...] * scale
    total = jnp.concatenate([jnp.where(is_even, x, y), jnp.where(is_even, y, x)], axis=0)
    for a in range(3):
        for e in range(3):
            at = 128 * a + groups * e
            block = total[at : at + groups].T
            for b in range(3):
                weight[2 - a, 2 - b, 2 - e] = block[feat * b : feat * (b + 1)]
    beside = jnp.where(is_even, near[...].astype(F32), 0.0)
    right[...] = (own[...].astype(F32) + beside + far[...].astype(F32)).astype(BF16)


def sum_kernel(*refs):
    *parts, out = refs
    out[...] = tree([ref[...].astype(F32) for ref in parts]).astype(out.dtype)


def tree(terms):
    while len(terms) > 1:
        terms = [terms[i] + terms[i + 1] for i in range(0, len(terms), 2)]
    return terms[0]


def taps_kernel(taps, w2, wc, turned):
    _, _, _, feat, groups = taps.shape
    rows = wc.shape[1] // 2 // feat
    lane_of = lanes((feat, 2 * SLOT))
    low = lanes((feat, 2 * SLOT)) < SLOT
    zero = jnp.zeros((feat, 2 * SLOT), F32)

    def wide(a, b, e):
        if not 0 <= b <= 2:
            return None
        return jnp.concatenate([taps[a, b, e].astype(F32), zero[:, groups:]], axis=1)

    def beside(x, y):
        if x is None and y is None:
            return zero
        x = zero if x is None else x
        y = zero if y is None else pltpu.roll(y, SLOT, 1)
        return jnp.where(low, x, y)

    def build(a, _):
        def at_row(h):
            return pl.multiple_of((a * rows + h) * feat, feat)

        def at_tap(row):
            return pl.multiple_of(a * 3 * 256 + row, feat)

        for e in range(3):
            for h in range(rows):
                for p in range(rows // 2):
                    lane = SLOT * (rows * e + 2 * p)
                    block = beside(wide(a, 2 * p - h + 1, e), wide(a, 2 * p + 1 - h + 1, e))
                    if h == 0 and p == 0:
                        block = place_halo(block, wide(a, 0, e), groups, 0, lane_of)
                    if h == rows - 1 and p == rows // 2 - 1:
                        block = place_halo(block, wide(a, 2, e), groups, 0, lane_of)
                    turned[pl.ds(at_row(h), feat), lane : lane + 2 * SLOT] = block
            for slot, six in enumerate((*range(1, rows + 1), 0, rows + 1)):
                at = 256 * e + feat * slot
                for p in range(rows // 2):
                    back = [2 - (six - 2 * p - o) for o in range(2)]
                    w2[pl.ds(at_tap(at), feat), 2 * SLOT * p : 2 * SLOT * (p + 1)] = beside(
                        wide(2 - a, back[0], 2 - e), wide(2 - a, back[1], 2 - e)
                    ).astype(BF16)
            at = 256 * e + feat * (rows + 2)
            size = 256 - feat * (rows + 2)
            w2[pl.ds(at_tap(at), size)] = jnp.zeros((size, rows * SLOT), BF16)
        return 0

    lax.fori_loop(0, 3, build, 0)
    depth, size = turned.shape[1], rows * feat
    for a in range(3):
        for i in range(depth // 128):
            x = turned[size * a : size * (a + 1), 128 * i : 128 * (i + 1)].T.astype(BF16)
            for o in range(2):
                at = depth * (a + o) + 128 * i
                wc[at : at + 128, size * o : size * (o + 1)] = x
    for o in range(2):
        at = depth * 3 * (1 - o)
        wc[at : at + depth, size * o : size * (o + 1)] = jnp.zeros((depth, size), BF16)


TOKEN = ((8, 128), F32)


def with_token(kernel, inputs, outputs):
    def run(*refs):
        kernel(*refs[: inputs + outputs], *refs[inputs + outputs + 1 :])
        refs[inputs + outputs][...] = jnp.zeros(TOKEN[0], F32)

    return run


def call(kernel, outs, scratch, *args, after=(), token=False, us=0.0):
    skip = len(after)
    if token:
        kernel = with_token(kernel, len(args), len(outs))
        outs = [*outs, TOKEN]
    return pl.pallas_call(
        lambda *refs: kernel(*refs[skip:]),
        out_shape=[jax.ShapeDtypeStruct(s, t) for s, t in outs],
        in_specs=[pl.BlockSpec(memory_space=pl.ANY)] * skip + [VMEM] * len(args),
        out_specs=[VMEM] * len(outs),
        scratch_shapes=scratch,
        compiler_params=pltpu.CompilerParams(vmem_limit_bytes=LIMIT),
        cost_estimate=pl.CostEstimate(
            flops=int(us * 1.15e9), bytes_accessed=int(us * 3.7e6), transcendentals=0
        ),
    )(*after, *args)


def col_shift(block, distance):
    n = lax.axis_size("col")
    route = [(i - distance, i) for i in range(n) if 0 <= i - distance < n]
    return lax.ppermute(block, "col", route)


def row_shift(block, distance):
    n = lax.axis_size("row")
    route = [(i - distance, i) for i in range(n) if 0 <= i - distance < n]
    return lax.ppermute(block, "row", route)


def halos(pays):
    if lax.axis_size("row") == 2:
        got = lax.ppermute(pays[0], "row", [(0, 1), (1, 0)])
        return got, got
    return row_shift(pays[0], 1), row_shift(pays[1], -1)


def stages(n_row, n_col):
    col_bits = [1 << i for i in range(1, n_col.bit_length() - 1)]
    row_bits = [n_col << i for i in range(n_row.bit_length() - 1)]
    assert n_col == 2 << len(col_bits) and n_row == 1 << len(row_bits)
    bits = col_bits[:1] + row_bits + col_bits[1:]
    out = []
    for i in range(0, len(bits), 2):
        pair = bits[i : i + 2]
        out.append(pair + [sum(pair)] if len(pair) == 2 else pair)
    return out


def on_device(left_features, right_features, conv_weight, cotangent):
    rows, cols, channels = left_features.shape
    disp, feat = cotangent.shape[0], cotangent.shape[3]
    groups = conv_weight.shape[3]
    group_size = channels // groups
    wide = group_size * SLOT
    n_row, n_col = lax.axis_size("row"), lax.axis_size("col")
    per = 128 // feat

    if n_row == 2:
        ends = [lambda: (rows - 1) * (1 - lax.axis_index("row"))]
    else:
        ends = [lambda: rows - 1, lambda: 0]
    n = len(ends)

    def masks():
        at = lax.axis_index("row")
        return (
            jnp.where(at > 0, 1.0, 0.0).astype(F32),
            jnp.where(at < n_row - 1, 1.0, 0.0).astype(F32),
        )

    total = cols + 2 * PAD
    count = disp + 2 * rows
    ct = cotangent.transpose(0, 1, 3, 2)

    def swap(block, mask):
        route = [(i, i ^ mask) for i in range(n_row * n_col)]
        return lax.ppermute(block, ("row", "col"), route)

    far = col_shift(right_features, 2)
    by_even, by_odd, ctl, *rims = call(
        functools.partial(pack_kernel, ends),
        [
            ((count, channels), BF16),
            ((count, channels), BF16),
            ((disp, cols, rows * feat), BF16),
        ]
        + [((disp // per, total, 128), F32)] * n,
        [pltpu.VMEM((disp * cols, rows * feat), F32)],
        left_features,
        right_features,
        ct,
        us=0.4,
    )
    by_even = swap(by_even, 1)
    near, by_odd = call(
        pass_kernel,
        [((rows, cols, channels), BF16), ((count, channels), BF16)],
        [],
        right_features,
        far,
        by_odd,
    )
    near = swap(near, 1)
    inner = range(1, n_col - 1, 2)
    by_odd = lax.ppermute(by_odd, "col", [(i, i + 1) for i in inner] + [(i + 1, i) for i in inner])
    row_pays = call(
        functools.partial(row_kernel, ends, rows),
        [((disp // per, total, 128), BF16)] * n,
        [pltpu.VMEM((2, disp, 128), F32), pltpu.VMEM((disp // per, total, 128), F32)],
        by_even,
        by_odd,
        *rims,
    )
    top, bot = halos(row_pays)

    band = 104 + cols + PAD
    spread_rows = 3 * rows * cols + rows * cols // 2 + 2 * count
    vbuf, fl, fr, fr4, *volume_rows = call(
        functools.partial(volume_kernel, ends, group_size),
        [
            ((rows // 2, disp, total, 2 * SLOT), F32),
            ((rows, total, wide), F32),
            ((rows, band, wide), F32),
            ((rows, band, wide), F32),
        ]
        + [((disp // 2 * total, 128), BF16)] * n,
        [
            pltpu.VMEM((spread_rows, channels), BF16),
            pltpu.VMEM((spread_rows, wide), F32),
        ],
        left_features,
        right_features,
        near,
        far,
        by_even,
        by_odd,
        after=row_pays,
        us=2.3,
    )
    vtop, vbot = halos(volume_rows)

    keep, give, ctsh = call(
        functools.partial(weight_kernel, masks, groups),
        [((3 * 64, 128), F32), ((3 * 64, 128), F32), ((disp + 2, cols, 3 * 256), BF16)],
        [
            pltpu.VMEM((rows * SLOT, disp * cols), BF16),
            pltpu.VMEM((disp, total, 256), F32),
            pltpu.VMEM((3 * 128, 128), F32),
        ],
        vbuf, ctl, by_even, by_odd, top, bot,
        us=3.4,
    )
    got = swap(give, 1)
    w2, wc = call(
        taps_kernel,
        [((9 * 256, rows * SLOT), BF16), ((4 * 3 * rows * SLOT, 2 * rows * feat), BF16)],
        [pltpu.VMEM((3 * rows * feat, 3 * rows * SLOT), F32)],
        conv_weight.transpose(0, 1, 2, 4, 3),
        after=[keep],
        us=0.8,
    )
    (part,) = call(sum_kernel, [(keep.shape, BF16)], [], keep, got, after=[w2])
    gv, rg0, rg1, rg2 = call(
        right_kernel,
        [
            ((rows, disp, cols, 128), F32),
            ((rows, cols, channels), BF16),
            ((rows, cols, channels), BF16),
            ((rows, cols // 2, channels), BF16),
        ],
        [
            pltpu.VMEM((rows, cols + cols + cols // 2, wide), F32),
            pltpu.VMEM((rows, cols + cols + cols // 2 + 8, wide), F32),
            pltpu.VMEM((rows * (cols + cols + cols // 2), wide), BF16),
        ],
        ctsh, w2, fl,
        after=[part],
        us=3.8,
    )
    rg1 = swap(rg1, 1)
    *middle, final = stages(n_row, n_col)
    order = [rg0]
    for stage in middle:
        parts = [part] + [swap(part, m) for m in stage]
        (part,) = call(sum_kernel, [(part.shape, BF16)], [], *parts, after=order)
        order = []
    parts = [part] + [swap(part, m) for m in final]
    (rg2,) = call(
        combine_kernel, [((rows, cols, channels), BF16)], [], rg1, rg2, after=[part]
    )
    output, conv_done = call(
        functools.partial(conv_kernel, masks, groups),
        [((disp, rows, feat, cols), BF16)],
        [
            pltpu.VMEM((disp // 2 + 1, 2, cols, 3 * rows * SLOT), BF16),
            pltpu.VMEM((rows // 2, disp, total, 128), F32),
        ],
        vbuf, vtop, vbot, wc,
        after=[part, rg2],
        token=True,
        us=3.8,
    )
    (part,) = call(sum_kernel, [(part.shape, F32)], [], *parts, after=[conv_done])
    lg, left_done = call(
        left_kernel,
        [((rows, cols, channels), BF16)],
        [pltpu.VMEM((rows, cols, wide), F32)],
        gv, fr, fr4,
        after=[part],
        token=True,
        us=1.9,
    )
    rg2 = col_shift(rg2, -2)
    cells = disp * rows * n_row * cols * n_col
    weight_grad, right_grad = call(
        functools.partial(finish_kernel, 1.0 / math.sqrt(cells)),
        [((3, 3, 3, feat, groups), F32), ((rows, cols, channels), BF16)],
        [],
        part, swap(part, 1), rg0, rg1, rg2,
        after=[left_done],
        us=1.0,
    )
    return (
        output.transpose(0, 1, 3, 2),
        weight_grad.transpose(0, 1, 2, 4, 3),
        lg,
        right_grad,
    )


def solution(mesh):
    in_specs = (P("row", "col", None), P("row", "col", None), P(), P(None, "row", "col", None))
    out_specs = (P(None, "row", "col", None), P(), P("row", "col", None), P("row", "col", None))
    return jax.shard_map(
        on_device, mesh=mesh, in_specs=in_specs, out_specs=out_specs, check_vma=False
    )
```

```python
import functools
import math

import jax
import jax.numpy as jnp
from jax import lax
from jax.experimental import pallas as pl
from jax.experimental.pallas import tpu as pltpu
from jax.sharding import PartitionSpec as P

DISP = 24
STEP = 4
SLOT = 64
PAD = 8
F32 = jnp.float32
BF16 = jnp.bfloat16
VMEM = pl.BlockSpec(memory_space=pltpu.VMEM)
LIMIT = 16 * 1024 * 1024


def lanes(shape):
    return lax.broadcasted_iota(jnp.int32, shape, len(shape) - 1)


def channel_table(channels, group_size, flip, value=1.0):
    shape = (group_size * SLOT, channels) if flip else (channels, group_size * SLOT)
    c = lax.broadcasted_iota(jnp.int32, shape, 1 if flip else 0)
    j = lax.broadcasted_iota(jnp.int32, shape, 0 if flip else 1)
    hit = c == (j & (SLOT - 1)) * group_size + (j >> (SLOT.bit_length() - 1))
    return jnp.where(hit, value, 0.0).astype(BF16)


def parity():
    return lax.rem(lax.axis_index("col"), 2)


def dot(a, b):
    return jnp.dot(a, b, preferred_element_type=F32)


def dot_nt(a, b):
    return lax.dot_general(a, b, (((1,), (1,)), ((), ())), preferred_element_type=F32)


def pack_kernel(ends, left, right, ct, even, odd, ctl, *rest):
    rims, ctf = rest[:-1], rest[-1]
    disp, rows, feat, cols = ct.shape
    per = 128 // feat
    for d in range(disp):
        block = ct[d].reshape(rows * feat, cols).astype(F32).T
        ctf[d * cols : (d + 1) * cols] = block
        ctl[d] = block.astype(BF16)
    columns = []
    for col in (cols - 1, 0):
        block = ctf[pl.ds(col, disp, stride=cols), :]
        block = jnp.concatenate([block, jnp.zeros((disp, left.shape[2] - rows * feat), F32)], axis=1)
        edge = [left[h, col : col + 1].astype(F32) for h in range(rows)]
        edge += [right[h, col : col + 1].astype(F32) for h in range(rows)]
        columns.append(jnp.concatenate([block, *edge], axis=0))
    is_even = parity() == 0
    even[...] = jnp.where(is_even, columns[0], columns[1]).astype(BF16)
    odd[...] = jnp.where(is_even, columns[1], columns[0]).astype(BF16)
    for end, rim in zip(ends, rims):
        h = end()
        for q in range(disp // per):
            rim[q, PAD : PAD + cols] = jnp.concatenate(
                [ct[q * per + i, h].astype(F32) for i in range(per)], axis=0
            ).T


def pass_kernel(own, got, out):
    out[...] = jnp.where(parity() == 0, own[...].astype(F32), got[...].astype(F32)).astype(BF16)


def end_columns(by_even, by_odd):
    x, y = by_even[...].astype(F32), by_odd[...].astype(F32)
    is_even = parity() == 0
    return jnp.where(is_even, y, x), jnp.where(is_even, x, y)


def row_kernel(ends, rows, by_even, by_odd, *rest):
    n = len(ends)
    rims, pays, (edges, buf) = rest[:n], rest[n : 2 * n], rest[2 * n :]
    count, total, _ = buf.shape
    disp = edges.shape[1]
    per, cols = disp // count, total - 2 * PAD
    feat = 128 // per
    lane = lanes((count, 128))
    for side, x in enumerate(end_columns(by_even, by_odd)):
        edges[side] = x[0:disp, 0:128]
    for end, rim, pay in zip(ends, rims, pays):
        h = end()
        buf[...] = rim[...]
        for side, at in ((0, PAD - 1), (1, PAD + cols)):
            out = jnp.zeros((count, 128), F32)
            for i in range(per):
                x = edges[side, pl.ds(i, count, stride=per)]
                first = pltpu.roll(x, feat * i, 1) if i else x
                last = pltpu.roll(x, (feat * (i - rows + 1)) % 128, 1) if i != rows - 1 else x
                x = jnp.where(h == 0, first, last)
                out = jnp.where((lane >= feat * i) & (lane < feat * (i + 1)), x, out)
            for q in range(count):
                buf[q, at : at + 1] = out[q : q + 1]
        pay[...] = buf[...].astype(BF16)


def volume_kernel(ends, group_size, left, right, near, far, by_even, by_odd, vbuf, fl, fr, fr4, *rest):
    pays, (mixed, wide_buf) = rest[: len(ends)], rest[len(ends) :]
    rows, cols, channels = left.shape
    disp = vbuf.shape[1]
    reach = fr.shape[1] - cols - PAD
    wide = group_size * SLOT
    base, half = rows * cols, cols // 2
    mixed[0:base] = near[...].reshape(base, channels)
    mixed[base : 2 * base] = right[...].reshape(base, channels)
    mixed[2 * base : 3 * base] = left[...].reshape(base, channels)
    at_far, at_ends = 3 * base, 3 * base + base // 2
    mixed[at_far:at_ends] = far[:, half:].reshape(base // 2, channels)
    count = disp + 2 * rows
    for i, x in enumerate(end_columns(by_even, by_odd)):
        mixed[at_ends + i * count : at_ends + (i + 1) * count] = x.astype(BF16)
    wide_buf[...] = dot(mixed[...], channel_table(channels, group_size, False))
    scale = 1.0 / group_size
    for h in range(rows):
        fl[h, 0:PAD] = jnp.zeros((PAD, wide), F32)
        fl[h, PAD + cols :] = jnp.zeros((PAD, wide), F32)
        at = at_ends + disp + h
        fl[h, PAD - 1 : PAD] = wide_buf[at : at + 1] * scale
        fl[h, PAD : PAD + cols] = wide_buf[2 * base + h * cols : 2 * base + (h + 1) * cols] * scale
        at += count
        fl[h, PAD + cols : PAD + cols + 1] = wide_buf[at : at + 1] * scale
        for ref, off in ((fr, 0), (fr4, STEP)):
            start = reach - cols - half + off
            ref[h, 0:start] = jnp.zeros((start, wide), F32)
            ref[h, start : start + half] = wide_buf[at_far + h * half : at_far + (h + 1) * half]
            for part in range(2):
                at = part * base + h * cols
                to = start + half + part * cols
                ref[h, to : to + cols] = wide_buf[at : at + cols]
            to = start + half + 2 * cols
            ref[h, to:] = jnp.zeros((ref.shape[1] - to, wide), F32)
            at = at_ends + count + disp + rows + h
            ref[h, to : to + 1] = wide_buf[at : at + 1]
    total = cols + 2 * PAD
    low = lanes((8, 128)) < SLOT
    pairs, times, lots = rows // 2, disp // 2, wide // 128
    count = total // 16

    def products(i, _):
        p, at = lax.rem(i, pairs), pl.multiple_of(lax.div(i, pairs) * (8 * count), 8)
        lefts = [
            [
                [fl[2 * p + o, pl.ds(at + 8 * b, 8), 128 * j : 128 * (j + 1)] for j in range(lots)]
                for b in range(count)
            ]
            for o in range(2)
        ]
        for odd, band in enumerate((fr, fr4)):
            for r in range(1 - times, count):
                start = pl.multiple_of(at + reach - PAD + 8 * r, 8)
                here = [
                    [band[2 * p + o, pl.ds(start, 8), 128 * j : 128 * (j + 1)] for j in range(lots)]
                    for o in range(2)
                ]
                for t in range(max(0, -r), min(times, count - r)):
                    sums = []
                    for o in range(2):
                        acc = lefts[o][r + t][0] * here[o][0]
                        for j in range(1, lots):
                            acc = acc + lefts[o][r + t][j] * here[o][j]
                        sums.append(acc + pltpu.roll(acc, SLOT, 1))
                    vbuf[p, 2 * t + odd, pl.ds(at + 8 * (r + t), 8)] = jnp.where(low, *sums)
        return 0

    lax.fori_loop(0, 2 * pairs, products, 0)
    big = lanes((total, 128)) < SLOT

    for dd in range(disp // 2):
        for end, pay in zip(ends, pays):
            h = end()
            if isinstance(h, int):
                halves = [vbuf[h // 2, 2 * dd + o] for o in range(2)]
                if h % 2 == 0:
                    halves[1] = pltpu.roll(halves[1], SLOT, 1)
                else:
                    halves[0] = pltpu.roll(halves[0], SLOT, 1)
                out = jnp.where(big, halves[0], halves[1])
            else:
                last = pairs - 1
                first = jnp.where(big, vbuf[0, 2 * dd], pltpu.roll(vbuf[0, 2 * dd + 1], SLOT, 1))
                final = jnp.where(
                    big, pltpu.roll(vbuf[last, 2 * dd], SLOT, 1), vbuf[last, 2 * dd + 1]
                )
                out = jnp.where(h == 0, first, final)
            pay[dd * total : (dd + 1) * total] = out.astype(BF16)


def weight_kernel(
    masks, groups, feat, vbuf, ctl, by_even, by_odd, top, bot, keep_out, give_out, ctsh, vt, buf, sums
):
    disp, cols, width = ctl.shape
    pairs, per, half = vbuf.shape[0], 128 // feat, disp // 2
    mtop, mbot = masks()
    ctsh[0, 0] = jnp.zeros(ctsh.shape[2:], BF16)
    ctsh[half, 1] = jnp.zeros(ctsh.shape[2:], BF16)
    lane, lane_in, lane_one = lanes(top.shape[1:]), lanes((cols, 128)), lanes((1, 128))
    shifts = (feat, 128 - feat)
    edges = [x[0:disp, 0:128] for x in end_columns(by_even, by_odd)]
    turned = [[pltpu.roll(x, shift, 1) for shift in shifts] for x in edges]
    for q in range(disp // per):
        t = top[q].astype(F32) * mtop
        z = bot[q].astype(F32) * mbot
        for i in range(per):
            d = q * per + i
            rims = (
                t if i == 0 else pltpu.roll(t, 128 - feat * i, 1),
                z if i == per - 1 else pltpu.roll(z, feat * (per - 1 - i), 1),
            )
            inner = ctl[d].astype(F32)
            for p, (rim, shift) in enumerate(zip(rims, shifts)):

                def on_rim(x):
                    return x < feat if p == 0 else x >= 128 - feat

                at = slice(128 * p, 128 * (p + 1))
                buf[d, PAD : PAD + cols, at] = jnp.where(
                    on_rim(lane_in), rim[PAD : PAD + cols], pltpu.roll(inner, shift, 1)
                )
                for side, row in enumerate((PAD - 1, PAD + cols)):
                    buf[d, row : row + 1, at] = jnp.where(
                        on_rim(lane_one), rim[row : row + 1], turned[side][p][d : d + 1]
                    )
            for e in range(3):
                ctsh[(d + 1) // 2, (d + 1) % 2, :, 256 * e : 256 * (e + 1)] = buf[
                    d, PAD - 1 + e : PAD - 1 + e + cols
                ].astype(BF16)
    none = jnp.zeros((cols, 128), F32)
    for p in range(pairs):
        for j in range(-1, half + 1):
            block = [
                vbuf[p, d, PAD : PAD + cols] if 0 <= d < disp and 0 <= j + half * o else none
                for o, d in enumerate((j, j + half))
            ]
            if j == half:
                block[1] = none
            x = jnp.concatenate(block, axis=0).astype(BF16)
            vt[p, :, 128 * (j + 1) : 128 * (j + 2)] = x.T
    size = disp * cols
    left = jnp.concatenate(
        [
            jnp.concatenate([vt[p, :, 128 * (2 - a) : 128 * (2 - a) + size] for p in range(pairs)], axis=1)
            for a in range(3)
        ],
        axis=0,
    )
    right = jnp.concatenate(
        [
            jnp.concatenate(
                [
                    ctsh[(d + 1) // 2, (d + 1) % 2, :, 256 * e + 128 * p : 256 * e + 128 * (p + 1)]
                    for e in range(3)
                ],
                axis=1,
            )
            for p in range(pairs)
            for j in range(half)
            for d in (j, j + half)
        ],
        axis=0,
    )
    full = dot(left, right)
    keep = lanes((groups, 128)) < 3 * feat
    sums[...] = jnp.zeros(sums.shape, F32)
    for a in range(3):
        for e in range(3):
            block = full[128 * a : 128 * (a + 1), 128 * e : 128 * (e + 1)]
            out = block[0:groups] + pltpu.roll(block[SLOT : SLOT + groups], 128 - feat, 1)
            at = 128 * a + groups * e
            sums[at : at + groups] = jnp.where(keep, out, 0.0)
    half = sums.shape[0] // 2
    is_even = parity() == 0
    low, high = sums[0:half], sums[half:]
    keep_out[...] = jnp.where(is_even, low, high)
    give_out[...] = jnp.where(is_even, high, low)


def right_kernel(ctsh, w2, fl, gv, rg0, rg1, rg2, acce, acco, both):
    disp = gv.shape[1]
    rows, cols, channels = rg0.shape
    wide = fl.shape[2]
    group_size = wide // SLOT
    step = disp // 4
    low = lanes((step * cols, 128)) < SLOT

    def conv(q, _):
        for p in range(rows // 2):
            slabs = [
                ctsh[pl.ds(q * step + s // 2, step), s % 2, :, 256 * e + 128 * p : 256 * e + 128 * (p + 1)]
                for s in range(4)
                for e in range(3)
            ]
            slabs = [x.reshape(step * cols, 128) for x in slabs]
            acc = dot(jnp.concatenate(slabs, axis=1), w2[...]).astype(BF16).astype(F32)
            for o in range(2):
                x = acc[:, 128 * o : 128 * (o + 1)]
                r = pltpu.roll(x, SLOT, 1)
                for hh in range(2):
                    y = jnp.where(low, r, x) if hh else jnp.where(low, x, r)
                    for j in range(step):
                        gv[2 * p + hh, 2 * (q * step + j) + o] = y[j * cols : (j + 1) * cols]
        return 0

    lax.fori_loop(0, 2, conv, 0)
    count = cols // 8
    back = acce.shape[1] - cols
    lead = back // 8

    lots = wide // 128

    def right_row(h, _):
        here = [
            [fl[h, PAD + 8 * b : PAD + 8 * b + 8, 128 * j : 128 * (j + 1)] for j in range(lots)]
            for b in range(count)
        ]
        for odd, buf in enumerate((acce, acco)):
            for k in range(lead + count):
                accs = [None] * lots
                for t in range(disp // 2):
                    b = k + t - lead
                    if b < 0 or b >= count:
                        continue
                    g = gv[h, 2 * t + odd, 8 * b : 8 * b + 8]
                    for j in range(lots):
                        term = g * here[b][j]
                        accs[j] = term if accs[j] is None else accs[j] + term
                for j in range(lots):
                    x = jnp.zeros((8, 128), F32) if accs[j] is None else accs[j]
                    buf[h, 8 * k : 8 * k + 8, 128 * j : 128 * (j + 1)] = x
        acco[h, 8 * (lead + count) :] = jnp.zeros((8, wide), F32)
        return 0

    lax.fori_loop(0, rows, right_row, 0)
    size = back + cols
    for h in range(rows):
        both[h * size : (h + 1) * size] = (acce[h] + acco[h, STEP : STEP + size]).astype(BF16)
    whole = dot(both[...], channel_table(channels, group_size, True)).astype(BF16)
    half = cols // 2
    for h in range(rows):
        at = h * size + back
        rg2[h] = whole[at - cols - half : at - cols]
        rg1[h] = whole[at - cols : at]
        rg0[h] = whole[at : at + cols]


def left_kernel(gv, fr, fr4, lg, accl):
    rows, cols, channels = lg.shape
    disp, wide = gv.shape[1], fr.shape[2]
    group_size = wide // SLOT
    reach = fr.shape[1] - cols - PAD
    count, times, lots = cols // 8, disp // 2, wide // 128

    def left_row(h, _):
        accs = [[None] * lots for _ in range(count)]
        for odd, band in enumerate((fr, fr4)):
            for r in range(1 - times, count):
                at = reach + 8 * r
                here = [band[h, at : at + 8, 128 * j : 128 * (j + 1)] for j in range(lots)]
                for t in range(max(0, -r), min(times, count - r)):
                    g = gv[h, 2 * t + odd, 8 * (r + t) : 8 * (r + t) + 8]
                    for j in range(lots):
                        term, acc = g * here[j], accs[r + t][j]
                        accs[r + t][j] = term if acc is None else acc + term
        for b in range(count):
            for j in range(lots):
                accl[h, 8 * b : 8 * b + 8, 128 * j : 128 * (j + 1)] = accs[b][j] * (1.0 / group_size)
        return 0

    lax.fori_loop(0, rows, left_row, 0)
    whole = accl[...].reshape(rows * cols, wide).astype(BF16)
    out = dot(whole, channel_table(channels, group_size, True)).astype(BF16)
    lg[...] = out.reshape(rows, cols, channels)


def combine_kernel(got, rg2, out):
    cols = out.shape[1]
    half = cols // 2
    part = jnp.where(parity() == 0, 0.0, got[...].astype(F32))
    out[:, 0:half] = part[:, 0:half].astype(BF16)
    out[:, half:] = (part[:, half:] + rg2[...].astype(F32)).astype(BF16)


def halo_lanes(groups):
    first = SLOT - groups
    assert groups - first <= first
    return (groups, SLOT, groups), (SLOT + groups, SLOT + 2 * groups - first, SLOT + groups - first)


def place_halo(base, row, groups, offset, lane):
    for start, end, shift in halo_lanes(groups):
        moved = pltpu.roll(row, (shift - offset) % 128, 1)
        base = jnp.where((lane >= start) & (lane < end), moved, base)
    return base


def conv_kernel(masks, groups, vbuf, top, bot, wc, out, taps, buf):
    disp, rows, feat, cols = out.shape
    total = buf.shape[2]
    lane = lanes((total, 128))
    zeros = jnp.zeros((cols, taps.shape[3]), BF16)
    taps[0, 0] = zeros
    taps[disp // 2, 1] = zeros
    halos_of = [(ref, mask) for ref, mask in zip((top, bot), masks())]
    for dd in range(disp // 2):
        for p, (ref, mask) in enumerate(halos_of):
            row = ref[dd * total : (dd + 1) * total].astype(F32) * mask
            for o in range(2):
                d = 2 * dd + o
                buf[p, d] = place_halo(vbuf[p, d], row, groups, SLOT * o, lane)
                for e in range(3):
                    at = 256 * e + 128 * p
                    taps[(d + 1) // 2, (d + 1) % 2, :, at : at + 128] = buf[
                        p, d, PAD - 1 + e : PAD - 1 + e + cols
                    ].astype(BF16)
    step = 6

    def conv(q, _):
        slabs = [
            taps[pl.ds(q * step + s // 2, step), s % 2].reshape(step * cols, taps.shape[3])
            for s in range(4)
        ]
        acc = dot(jnp.concatenate(slabs, axis=1), wc[...])
        for j in range(step):
            both = acc[j * cols : (j + 1) * cols].T.astype(BF16)
            for o in range(2):
                block = both[rows * feat * o : rows * feat * (o + 1)]
                out[2 * (q * step + j) + o] = block.reshape(rows, feat, cols)
        return 0

    lax.fori_loop(0, disp // 2 // step, conv, 0)


def finish_kernel(scale, mine, other, own, near, far, weight, right):
    _, _, _, feat, groups = weight.shape
    is_even = parity() == 0
    x, y = mine[...] * scale, other[...] * scale
    total = jnp.concatenate([jnp.where(is_even, x, y), jnp.where(is_even, y, x)], axis=0)
    for a in range(3):
        for e in range(3):
            at = 128 * a + groups * e
            block = total[at : at + groups].T
            for b in range(3):
                weight[2 - a, 2 - b, 2 - e] = block[feat * b : feat * (b + 1)]
    beside = jnp.where(is_even, near[...].astype(F32), 0.0)
    right[...] = (own[...].astype(F32) + beside + far[...].astype(F32)).astype(BF16)


def sum_kernel(*refs):
    *parts, out = refs
    out[...] = tree([ref[...].astype(F32) for ref in parts]).astype(out.dtype)


def tree(terms):
    while len(terms) > 1:
        terms = [terms[i] + terms[i + 1] for i in range(0, len(terms), 2)]
    return terms[0]


def taps_kernel(taps, w2, wc, turned):
    _, _, _, feat, groups = taps.shape
    rows = wc.shape[1] // 2 // feat
    lane_of = lanes((feat, 2 * SLOT))
    low = lanes((feat, 2 * SLOT)) < SLOT
    zero = jnp.zeros((feat, 2 * SLOT), F32)

    def wide(a, b, e):
        if not 0 <= b <= 2:
            return None
        return jnp.concatenate([taps[a, b, e].astype(F32), zero[:, groups:]], axis=1)

    def beside(x, y):
        if x is None and y is None:
            return zero
        x = zero if x is None else x
        y = zero if y is None else pltpu.roll(y, SLOT, 1)
        return jnp.where(low, x, y)

    def build(a, _):
        def at_row(h):
            return pl.multiple_of((a * rows + h) * feat, feat)

        for e in range(3):
            for h in range(rows):
                for p in range(rows // 2):
                    lane = SLOT * (rows * e + 2 * p)
                    block = beside(wide(a, 2 * p - h + 1, e), wide(a, 2 * p + 1 - h + 1, e))
                    if h == 0 and p == 0:
                        block = place_halo(block, wide(a, 0, e), groups, 0, lane_of)
                    if h == rows - 1 and p == rows // 2 - 1:
                        block = place_halo(block, wide(a, 2, e), groups, 0, lane_of)
                    turned[pl.ds(at_row(h), feat), lane : lane + 2 * SLOT] = block
        return 0

    lax.fori_loop(0, 3, build, 0)
    for s in range(4):
        for e in range(3):
            for r in range(4):
                for o in range(2):
                    taps_of = [None if not 0 <= s - o <= 2 else wide(2 - s + o, 2 - r + i, 2 - e) for i in range(2)]
                    at = 384 * s + 128 * e + feat * r
                    w2[at : at + feat, 128 * o : 128 * (o + 1)] = beside(*taps_of).astype(BF16)
    depth, size = turned.shape[1], rows * feat
    for a in range(3):
        for i in range(depth // 128):
            x = turned[size * a : size * (a + 1), 128 * i : 128 * (i + 1)].T.astype(BF16)
            for o in range(2):
                at = depth * (a + o) + 128 * i
                wc[at : at + 128, size * o : size * (o + 1)] = x
    for o in range(2):
        at = depth * 3 * (1 - o)
        wc[at : at + depth, size * o : size * (o + 1)] = jnp.zeros((depth, size), BF16)


TOKEN = ((8, 128), F32)


def with_token(kernel, inputs, outputs):
    def run(*refs):
        kernel(*refs[: inputs + outputs], *refs[inputs + outputs + 1 :])
        refs[inputs + outputs][...] = jnp.zeros(TOKEN[0], F32)

    return run


def call(kernel, outs, scratch, *args, after=(), token=False, us=0.0):
    skip = len(after)
    if token:
        kernel = with_token(kernel, len(args), len(outs))
        outs = [*outs, TOKEN]
    return pl.pallas_call(
        lambda *refs: kernel(*refs[skip:]),
        out_shape=[jax.ShapeDtypeStruct(s, t) for s, t in outs],
        in_specs=[pl.BlockSpec(memory_space=pl.ANY)] * skip + [VMEM] * len(args),
        out_specs=[VMEM] * len(outs),
        scratch_shapes=scratch,
        compiler_params=pltpu.CompilerParams(vmem_limit_bytes=LIMIT),
        cost_estimate=pl.CostEstimate(
            flops=int(us * 1.15e9), bytes_accessed=int(us * 3.7e6), transcendentals=0
        ),
    )(*after, *args)


def col_shift(block, distance):
    n = lax.axis_size("col")
    route = [(i - distance, i) for i in range(n) if 0 <= i - distance < n]
    return lax.ppermute(block, "col", route)


def row_shift(block, distance):
    n = lax.axis_size("row")
    route = [(i - distance, i) for i in range(n) if 0 <= i - distance < n]
    return lax.ppermute(block, "row", route)


def halos(pays):
    if lax.axis_size("row") == 2:
        got = lax.ppermute(pays[0], "row", [(0, 1), (1, 0)])
        return got, got
    return row_shift(pays[0], 1), row_shift(pays[1], -1)


def stages(n_row, n_col):
    col_bits = [1 << i for i in range(1, n_col.bit_length() - 1)]
    row_bits = [n_col << i for i in range(n_row.bit_length() - 1)]
    assert n_col == 2 << len(col_bits) and n_row == 1 << len(row_bits)
    bits = col_bits[:1] + row_bits + col_bits[1:]
    out = []
    for i in range(0, len(bits), 2):
        pair = bits[i : i + 2]
        out.append(pair + [sum(pair)] if len(pair) == 2 else pair)
    return out


def on_device(left_features, right_features, conv_weight, cotangent):
    rows, cols, channels = left_features.shape
    disp, feat = cotangent.shape[0], cotangent.shape[3]
    groups = conv_weight.shape[3]
    group_size = channels // groups
    wide = group_size * SLOT
    n_row, n_col = lax.axis_size("row"), lax.axis_size("col")
    per = 128 // feat

    if n_row == 2:
        ends = [lambda: (rows - 1) * (1 - lax.axis_index("row"))]
    else:
        ends = [lambda: rows - 1, lambda: 0]
    n = len(ends)

    def masks():
        at = lax.axis_index("row")
        return (
            jnp.where(at > 0, 1.0, 0.0).astype(F32),
            jnp.where(at < n_row - 1, 1.0, 0.0).astype(F32),
        )

    total = cols + 2 * PAD
    count = disp + 2 * rows
    ct = cotangent.transpose(0, 1, 3, 2)

    def swap(block, mask):
        route = [(i, i ^ mask) for i in range(n_row * n_col)]
        return lax.ppermute(block, ("row", "col"), route)

    far = col_shift(right_features, 2)
    by_even, by_odd, ctl, *rims = call(
        functools.partial(pack_kernel, ends),
        [
            ((count, channels), BF16),
            ((count, channels), BF16),
            ((disp, cols, rows * feat), BF16),
        ]
        + [((disp // per, total, 128), F32)] * n,
        [pltpu.VMEM((disp * cols, rows * feat), F32)],
        left_features,
        right_features,
        ct,
        us=0.4,
    )
    inner = range(1, n_col - 1, 2)
    by_even = swap(by_even, 1)
    by_odd = lax.ppermute(by_odd, "col", [(i, i + 1) for i in inner] + [(i + 1, i) for i in inner])
    row_pays = call(
        functools.partial(row_kernel, ends, rows),
        [((disp // per, total, 128), BF16)] * n,
        [pltpu.VMEM((2, disp, 128), F32), pltpu.VMEM((disp // per, total, 128), F32)],
        by_even,
        by_odd,
        *rims,
    )
    top, bot = halos(row_pays)
    (near,) = call(
        pass_kernel, [((rows, cols, channels), BF16)], [], right_features, far, after=row_pays
    )
    near = swap(near, 1)

    band = 104 + cols + PAD
    spread_rows = 3 * rows * cols + rows * cols // 2 + 2 * count
    vbuf, fl, fr, fr4, *volume_rows = call(
        functools.partial(volume_kernel, ends, group_size),
        [
            ((rows // 2, disp, total, 2 * SLOT), F32),
            ((rows, total, wide), F32),
            ((rows, band, wide), F32),
            ((rows, band, wide), F32),
        ]
        + [((disp // 2 * total, 128), BF16)] * n,
        [
            pltpu.VMEM((spread_rows, channels), BF16),
            pltpu.VMEM((spread_rows, wide), F32),
        ],
        left_features,
        right_features,
        near,
        far,
        by_even,
        by_odd,
        us=2.3,
    )
    vtop, vbot = halos(volume_rows)

    keep, give, ctsh = call(
        functools.partial(weight_kernel, masks, groups, feat),
        [((3 * 64, 128), F32), ((3 * 64, 128), F32), ((disp // 2 + 1, 2, cols, 3 * 256), BF16)],
        [
            pltpu.VMEM((rows // 2, 128, (disp // 2 + 2) * 128), BF16),
            pltpu.VMEM((disp, total, 256), F32),
            pltpu.VMEM((3 * 128, 128), F32),
        ],
        vbuf, ctl, by_even, by_odd, top, bot,
        us=2.6,
    )
    got = swap(give, 1)
    w2, wc = call(
        taps_kernel,
        [((12 * 128, 2 * 128), BF16), ((4 * 3 * rows * SLOT, 2 * rows * feat), BF16)],
        [pltpu.VMEM((3 * rows * feat, 3 * rows * SLOT), F32)],
        conv_weight.transpose(0, 1, 2, 4, 3),
        after=[keep],
        us=0.8,
    )
    (part,) = call(sum_kernel, [(keep.shape, BF16)], [], keep, got, after=[w2])
    gv, rg0, rg1, rg2 = call(
        right_kernel,
        [
            ((rows, disp, cols, 128), F32),
            ((rows, cols, channels), BF16),
            ((rows, cols, channels), BF16),
            ((rows, cols // 2, channels), BF16),
        ],
        [
            pltpu.VMEM((rows, cols + cols + cols // 2, wide), F32),
            pltpu.VMEM((rows, cols + cols + cols // 2 + 8, wide), F32),
            pltpu.VMEM((rows * (cols + cols + cols // 2), wide), BF16),
        ],
        ctsh, w2, fl,
        after=[part],
        us=2.9,
    )
    rg1 = swap(rg1, 1)
    *middle, final = stages(n_row, n_col)
    order = [rg0]
    for stage in middle:
        parts = [part] + [swap(part, m) for m in stage]
        (part,) = call(sum_kernel, [(part.shape, BF16)], [], *parts, after=order)
        order = []
    parts = [part] + [swap(part, m) for m in final]
    lg, left_done = call(
        left_kernel,
        [((rows, cols, channels), BF16)],
        [pltpu.VMEM((rows, cols, wide), F32)],
        gv, fr, fr4,
        after=[part],
        token=True,
        us=1.9,
    )
    (rg2,) = call(
        combine_kernel, [((rows, cols, channels), BF16)], [], rg1, rg2, after=[left_done]
    )
    (part,) = call(sum_kernel, [(part.shape, F32)], [], *parts, after=[left_done])
    output, conv_done = call(
        functools.partial(conv_kernel, masks, groups),
        [((disp, rows, feat, cols), BF16)],
        [
            pltpu.VMEM((disp // 2 + 1, 2, cols, 3 * rows * SLOT), BF16),
            pltpu.VMEM((rows // 2, disp, total, 128), F32),
        ],
        vbuf, vtop, vbot, wc,
        after=[part, rg2],
        token=True,
        us=3.9,
    )
    rg2 = col_shift(rg2, -2)
    cells = disp * rows * n_row * cols * n_col
    weight_grad, right_grad = call(
        functools.partial(finish_kernel, 1.0 / math.sqrt(cells)),
        [((3, 3, 3, feat, groups), F32), ((rows, cols, channels), BF16)],
        [],
        part, swap(part, 1), rg0, rg1, rg2,
        after=[conv_done],
        us=1.0,
    )
    return (
        output.transpose(0, 1, 3, 2),
        weight_grad.transpose(0, 1, 2, 4, 3),
        lg,
        right_grad,
    )


def solution(mesh):
    in_specs = (P("row", "col", None), P("row", "col", None), P(), P(None, "row", "col", None))
    out_specs = (P(None, "row", "col", None), P(), P("row", "col", None), P("row", "col", None))
    return jax.shard_map(
        on_device, mesh=mesh, in_specs=in_specs, out_specs=out_specs, check_vma=False
    )
```

```python
import functools
import math

import jax
import jax.numpy as jnp
from jax import lax
from jax.experimental import pallas as pl
from jax.experimental.pallas import tpu as pltpu
from jax.sharding import PartitionSpec as P

DISP = 24
STEP = 4
SLOT = 64
PAD = 8
F32 = jnp.float32
BF16 = jnp.bfloat16
VMEM = pl.BlockSpec(memory_space=pltpu.VMEM)
LIMIT = 16 * 1024 * 1024


def lanes(shape):
    return lax.broadcasted_iota(jnp.int32, shape, len(shape) - 1)


def channel_table(channels, group_size, flip, value=1.0):
    shape = (group_size * SLOT, channels) if flip else (channels, group_size * SLOT)
    c = lax.broadcasted_iota(jnp.int32, shape, 1 if flip else 0)
    j = lax.broadcasted_iota(jnp.int32, shape, 0 if flip else 1)
    hit = c == (j & (SLOT - 1)) * group_size + (j >> (SLOT.bit_length() - 1))
    return jnp.where(hit, value, 0.0).astype(BF16)


def parity():
    return lax.rem(lax.axis_index("col"), 2)


def dot(a, b):
    return jnp.dot(a, b, preferred_element_type=F32)


def dot_nt(a, b):
    return lax.dot_general(a, b, (((1,), (1,)), ((), ())), preferred_element_type=F32)


def pack_kernel(ends, left, right, ct, even, odd, ctl, *rest):
    rims, ctf = rest[:-1], rest[-1]
    disp, rows, feat, cols = ct.shape
    per = 128 // feat
    for d in range(disp):
        block = ct[d].reshape(rows * feat, cols).astype(F32).T
        ctf[d * cols : (d + 1) * cols] = block
        ctl[d] = block.astype(BF16)
    columns = []
    for col in (cols - 1, 0):
        block = ctf[pl.ds(col, disp, stride=cols), :]
        block = jnp.concatenate([block, jnp.zeros((disp, left.shape[2] - rows * feat), F32)], axis=1)
        edge = [left[h, col : col + 1].astype(F32) for h in range(rows)]
        edge += [right[h, col : col + 1].astype(F32) for h in range(rows)]
        columns.append(jnp.concatenate([block, *edge], axis=0))
    is_even = parity() == 0
    even[...] = jnp.where(is_even, columns[0], columns[1]).astype(BF16)
    odd[...] = jnp.where(is_even, columns[1], columns[0]).astype(BF16)
    for end, rim in zip(ends, rims):
        h = end()
        for q in range(disp // per):
            rim[q, PAD : PAD + cols] = jnp.concatenate(
                [ct[q * per + i, h].astype(F32) for i in range(per)], axis=0
            ).T


def pass_kernel(own, got, out):
    out[...] = jnp.where(parity() == 0, own[...].astype(F32), got[...].astype(F32)).astype(BF16)


def end_columns(by_even, by_odd):
    x, y = by_even[...].astype(F32), by_odd[...].astype(F32)
    is_even = parity() == 0
    return jnp.where(is_even, y, x), jnp.where(is_even, x, y)


def row_kernel(ends, rows, by_even, by_odd, *rest):
    n = len(ends)
    rims, pays, (edges, buf) = rest[:n], rest[n : 2 * n], rest[2 * n :]
    count, total, _ = buf.shape
    disp = edges.shape[1]
    per, cols = disp // count, total - 2 * PAD
    feat = 128 // per
    lane = lanes((count, 128))
    for side, x in enumerate(end_columns(by_even, by_odd)):
        edges[side] = x[0:disp, 0:128]
    for end, rim, pay in zip(ends, rims, pays):
        h = end()
        buf[...] = rim[...]
        for side, at in ((0, PAD - 1), (1, PAD + cols)):
            out = jnp.zeros((count, 128), F32)
            for i in range(per):
                x = edges[side, pl.ds(i, count, stride=per)]
                first = pltpu.roll(x, feat * i, 1) if i else x
                last = pltpu.roll(x, (feat * (i - rows + 1)) % 128, 1) if i != rows - 1 else x
                x = jnp.where(h == 0, first, last)
                out = jnp.where((lane >= feat * i) & (lane < feat * (i + 1)), x, out)
            for q in range(count):
                buf[q, at : at + 1] = out[q : q + 1]
        pay[...] = buf[...].astype(BF16)


def volume_kernel(ends, group_size, left, right, near, far, by_even, by_odd, vbuf, fl, fr, fr4, *rest):
    pays, (mixed, wide_buf) = rest[: len(ends)], rest[len(ends) :]
    rows, cols, channels = left.shape
    disp = vbuf.shape[1]
    reach = fr.shape[1] - cols - PAD
    wide = group_size * SLOT
    base, half = rows * cols, cols // 2
    mixed[0:base] = near[...].reshape(base, channels)
    mixed[base : 2 * base] = right[...].reshape(base, channels)
    mixed[2 * base : 3 * base] = left[...].reshape(base, channels)
    at_far, at_ends = 3 * base, 3 * base + base // 2
    mixed[at_far:at_ends] = far[:, half:].reshape(base // 2, channels)
    count = disp + 2 * rows
    for i, x in enumerate(end_columns(by_even, by_odd)):
        mixed[at_ends + i * count : at_ends + (i + 1) * count] = x.astype(BF16)
    wide_buf[...] = dot(mixed[...], channel_table(channels, group_size, False))
    scale = 1.0 / group_size
    for h in range(rows):
        fl[h, 0:PAD] = jnp.zeros((PAD, wide), F32)
        fl[h, PAD + cols :] = jnp.zeros((PAD, wide), F32)
        at = at_ends + disp + h
        fl[h, PAD - 1 : PAD] = wide_buf[at : at + 1] * scale
        fl[h, PAD : PAD + cols] = wide_buf[2 * base + h * cols : 2 * base + (h + 1) * cols] * scale
        at += count
        fl[h, PAD + cols : PAD + cols + 1] = wide_buf[at : at + 1] * scale
        for ref, off in ((fr, 0), (fr4, STEP)):
            start = reach - cols - half + off
            ref[h, 0:start] = jnp.zeros((start, wide), F32)
            ref[h, start : start + half] = wide_buf[at_far + h * half : at_far + (h + 1) * half]
            for part in range(2):
                at = part * base + h * cols
                to = start + half + part * cols
                ref[h, to : to + cols] = wide_buf[at : at + cols]
            to = start + half + 2 * cols
            ref[h, to:] = jnp.zeros((ref.shape[1] - to, wide), F32)
            at = at_ends + count + disp + rows + h
            ref[h, to : to + 1] = wide_buf[at : at + 1]
    total = cols + 2 * PAD
    low = lanes((8, 128)) < SLOT
    pairs, times, lots = rows // 2, disp // 2, wide // 128
    count = total // 16

    def products(i, _):
        p, at = lax.rem(i, pairs), pl.multiple_of(lax.div(i, pairs) * (8 * count), 8)
        lefts = [
            [
                [fl[2 * p + o, pl.ds(at + 8 * b, 8), 128 * j : 128 * (j + 1)] for j in range(lots)]
                for b in range(count)
            ]
            for o in range(2)
        ]
        for odd, band in enumerate((fr, fr4)):
            for r in range(1 - times, count):
                start = pl.multiple_of(at + reach - PAD + 8 * r, 8)
                here = [
                    [band[2 * p + o, pl.ds(start, 8), 128 * j : 128 * (j + 1)] for j in range(lots)]
                    for o in range(2)
                ]
                for t in range(max(0, -r), min(times, count - r)):
                    sums = []
                    for o in range(2):
                        acc = lefts[o][r + t][0] * here[o][0]
                        for j in range(1, lots):
                            acc = acc + lefts[o][r + t][j] * here[o][j]
                        sums.append(acc + pltpu.roll(acc, SLOT, 1))
                    vbuf[p, 2 * t + odd, pl.ds(at + 8 * (r + t), 8)] = jnp.where(low, *sums)
        return 0

    lax.fori_loop(0, 2 * pairs, products, 0)
    big = lanes((total, 128)) < SLOT

    for dd in range(disp // 2):
        for end, pay in zip(ends, pays):
            h = end()
            if isinstance(h, int):
                halves = [vbuf[h // 2, 2 * dd + o] for o in range(2)]
                if h % 2 == 0:
                    halves[1] = pltpu.roll(halves[1], SLOT, 1)
                else:
                    halves[0] = pltpu.roll(halves[0], SLOT, 1)
                out = jnp.where(big, halves[0], halves[1])
            else:
                last = pairs - 1
                first = jnp.where(big, vbuf[0, 2 * dd], pltpu.roll(vbuf[0, 2 * dd + 1], SLOT, 1))
                final = jnp.where(
                    big, pltpu.roll(vbuf[last, 2 * dd], SLOT, 1), vbuf[last, 2 * dd + 1]
                )
                out = jnp.where(h == 0, first, final)
            pay[dd * total : (dd + 1) * total] = out.astype(BF16)


def weight_kernel(
    masks, groups, feat, vbuf, ctl, by_even, by_odd, top, bot, keep_out, give_out, ctsh, vt, buf, sums
):
    disp, cols, width = ctl.shape
    pairs, per, half = vbuf.shape[0], 128 // feat, disp // 2
    mtop, mbot = masks()
    ctsh[0, 0] = jnp.zeros(ctsh.shape[2:], BF16)
    ctsh[half, 1] = jnp.zeros(ctsh.shape[2:], BF16)
    lane, lane_in, lane_one = lanes(top.shape[1:]), lanes((cols, 128)), lanes((1, 128))
    shifts = (feat, 128 - feat)
    edges = [x[0:disp, 0:128] for x in end_columns(by_even, by_odd)]
    turned = [[pltpu.roll(x, shift, 1) for shift in shifts] for x in edges]
    for q in range(disp // per):
        t = top[q].astype(F32) * mtop
        z = bot[q].astype(F32) * mbot
        for i in range(per):
            d = q * per + i
            rims = (
                t if i == 0 else pltpu.roll(t, 128 - feat * i, 1),
                z if i == per - 1 else pltpu.roll(z, feat * (per - 1 - i), 1),
            )
            inner = ctl[d].astype(F32)
            for p, (rim, shift) in enumerate(zip(rims, shifts)):

                def on_rim(x):
                    return x < feat if p == 0 else x >= 128 - feat

                at = slice(128 * p, 128 * (p + 1))
                buf[d, PAD : PAD + cols, at] = jnp.where(
                    on_rim(lane_in), rim[PAD : PAD + cols], pltpu.roll(inner, shift, 1)
                )
                for side, row in enumerate((PAD - 1, PAD + cols)):
                    buf[d, row : row + 1, at] = jnp.where(
                        on_rim(lane_one), rim[row : row + 1], turned[side][p][d : d + 1]
                    )
            for e in range(3):
                ctsh[(d + 1) // 2, (d + 1) % 2, :, 256 * e : 256 * (e + 1)] = buf[
                    d, PAD - 1 + e : PAD - 1 + e + cols
                ].astype(BF16)
    none = jnp.zeros((cols, 128), F32)
    for p in range(pairs):
        for j in range(-1, half + 1):
            block = [
                vbuf[p, d, PAD : PAD + cols] if 0 <= d < disp and 0 <= j + half * o else none
                for o, d in enumerate((j, j + half))
            ]
            if j == half:
                block[1] = none
            x = jnp.concatenate(block, axis=0).astype(BF16)
            vt[p, :, 128 * (j + 1) : 128 * (j + 2)] = x.T
    size = disp * cols
    left = jnp.concatenate(
        [
            jnp.concatenate([vt[p, :, 128 * (2 - a) : 128 * (2 - a) + size] for p in range(pairs)], axis=1)
            for a in range(3)
        ],
        axis=0,
    )
    right = jnp.concatenate(
        [
            jnp.concatenate(
                [
                    ctsh[(d + 1) // 2, (d + 1) % 2, :, 256 * e + 128 * p : 256 * e + 128 * (p + 1)]
                    for e in range(3)
                ],
                axis=1,
            )
            for p in range(pairs)
            for j in range(half)
            for d in (j, j + half)
        ],
        axis=0,
    )
    full = dot(left, right)
    keep = lanes((groups, 128)) < 3 * feat
    sums[...] = jnp.zeros(sums.shape, F32)
    for a in range(3):
        for e in range(3):
            block = full[128 * a : 128 * (a + 1), 128 * e : 128 * (e + 1)]
            out = block[0:groups] + pltpu.roll(block[SLOT : SLOT + groups], 128 - feat, 1)
            at = 128 * a + groups * e
            sums[at : at + groups] = jnp.where(keep, out, 0.0)
    half = sums.shape[0] // 2
    is_even = parity() == 0
    low, high = sums[0:half], sums[half:]
    keep_out[...] = jnp.where(is_even, low, high)
    give_out[...] = jnp.where(is_even, high, low)


def right_kernel(ctsh, w2, fl, gv, rg0, rg1, rg2, acce, acco, both):
    disp = gv.shape[1]
    rows, cols, channels = rg0.shape
    wide = fl.shape[2]
    group_size = wide // SLOT
    step = disp // 4
    low = lanes((step * cols, 128)) < SLOT

    def conv(q, _):
        for p in range(rows // 2):
            slabs = [
                ctsh[pl.ds(q * step + s // 2, step), s % 2, :, 256 * e + 128 * p : 256 * e + 128 * (p + 1)]
                for s in range(4)
                for e in range(3)
            ]
            slabs = [x.reshape(step * cols, 128) for x in slabs]
            acc = dot(jnp.concatenate(slabs, axis=1), w2[...]).astype(BF16).astype(F32)
            for o in range(2):
                x = acc[:, 128 * o : 128 * (o + 1)]
                r = pltpu.roll(x, SLOT, 1)
                for hh in range(2):
                    y = jnp.where(low, r, x) if hh else jnp.where(low, x, r)
                    for j in range(step):
                        gv[2 * p + hh, 2 * (q * step + j) + o] = y[j * cols : (j + 1) * cols]
        return 0

    lax.fori_loop(0, 2, conv, 0)
    count = cols // 8
    back = acce.shape[1] - cols
    lead = back // 8

    lots = wide // 128

    def right_row(h, _):
        here = [
            [fl[h, PAD + 8 * b : PAD + 8 * b + 8, 128 * j : 128 * (j + 1)] for j in range(lots)]
            for b in range(count)
        ]
        for odd, buf in enumerate((acce, acco)):
            for k in range(lead + count):
                accs = [None] * lots
                for t in range(disp // 2):
                    b = k + t - lead
                    if b < 0 or b >= count:
                        continue
                    g = gv[h, 2 * t + odd, 8 * b : 8 * b + 8]
                    for j in range(lots):
                        term = g * here[b][j]
                        accs[j] = term if accs[j] is None else accs[j] + term
                for j in range(lots):
                    x = jnp.zeros((8, 128), F32) if accs[j] is None else accs[j]
                    buf[h, 8 * k : 8 * k + 8, 128 * j : 128 * (j + 1)] = x
        acco[h, 8 * (lead + count) :] = jnp.zeros((8, wide), F32)
        return 0

    lax.fori_loop(0, rows, right_row, 0)
    size = back + cols
    for h in range(rows):
        both[h * size : (h + 1) * size] = (acce[h] + acco[h, STEP : STEP + size]).astype(BF16)
    whole = dot(both[...], channel_table(channels, group_size, True)).astype(BF16)
    half = cols // 2
    for h in range(rows):
        at = h * size + back
        rg2[h] = whole[at - cols - half : at - cols]
        rg1[h] = whole[at - cols : at]
        rg0[h] = whole[at : at + cols]


def left_kernel(gv, fr, fr4, lg, accl):
    rows, cols, channels = lg.shape
    disp, wide = gv.shape[1], fr.shape[2]
    group_size = wide // SLOT
    reach = fr.shape[1] - cols - PAD
    count, times, lots = cols // 8, disp // 2, wide // 128

    def left_row(h, _):
        accs = [[None] * lots for _ in range(count)]
        for odd, band in enumerate((fr, fr4)):
            for r in range(1 - times, count):
                at = reach + 8 * r
                here = [band[h, at : at + 8, 128 * j : 128 * (j + 1)] for j in range(lots)]
                for t in range(max(0, -r), min(times, count - r)):
                    g = gv[h, 2 * t + odd, 8 * (r + t) : 8 * (r + t) + 8]
                    for j in range(lots):
                        term, acc = g * here[j], accs[r + t][j]
                        accs[r + t][j] = term if acc is None else acc + term
        for b in range(count):
            for j in range(lots):
                accl[h, 8 * b : 8 * b + 8, 128 * j : 128 * (j + 1)] = accs[b][j] * (1.0 / group_size)
        return 0

    lax.fori_loop(0, rows, left_row, 0)
    whole = accl[...].reshape(rows * cols, wide).astype(BF16)
    out = dot(whole, channel_table(channels, group_size, True)).astype(BF16)
    lg[...] = out.reshape(rows, cols, channels)


def combine_kernel(got, rg2, out):
    cols = out.shape[1]
    half = cols // 2
    part = jnp.where(parity() == 0, 0.0, got[...].astype(F32))
    out[:, 0:half] = part[:, 0:half].astype(BF16)
    out[:, half:] = (part[:, half:] + rg2[...].astype(F32)).astype(BF16)


def halo_lanes(groups):
    first = SLOT - groups
    assert groups - first <= first
    return (groups, SLOT, groups), (SLOT + groups, SLOT + 2 * groups - first, SLOT + groups - first)


def place_halo(base, row, groups, offset, lane):
    for start, end, shift in halo_lanes(groups):
        moved = pltpu.roll(row, (shift - offset) % 128, 1)
        base = jnp.where((lane >= start) & (lane < end), moved, base)
    return base


def conv_kernel(masks, groups, vbuf, top, bot, wc, out, taps, buf):
    disp, rows, feat, cols = out.shape
    total = buf.shape[2]
    lane = lanes((total, 128))
    zeros = jnp.zeros((cols, taps.shape[3]), BF16)
    taps[0, 0] = zeros
    taps[disp // 2, 1] = zeros
    halos_of = [(ref, mask) for ref, mask in zip((top, bot), masks())]
    for dd in range(disp // 2):
        for p, (ref, mask) in enumerate(halos_of):
            row = ref[dd * total : (dd + 1) * total].astype(F32) * mask
            for o in range(2):
                d = 2 * dd + o
                buf[p, d] = place_halo(vbuf[p, d], row, groups, SLOT * o, lane)
                for e in range(3):
                    at = 256 * e + 128 * p
                    taps[(d + 1) // 2, (d + 1) % 2, :, at : at + 128] = buf[
                        p, d, PAD - 1 + e : PAD - 1 + e + cols
                    ].astype(BF16)
    step = 6

    def conv(q, _):
        slabs = [
            taps[pl.ds(q * step + s // 2, step), s % 2].reshape(step * cols, taps.shape[3])
            for s in range(4)
        ]
        acc = dot(jnp.concatenate(slabs, axis=1), wc[...])
        for j in range(step):
            both = acc[j * cols : (j + 1) * cols].T.astype(BF16)
            for o in range(2):
                block = both[rows * feat * o : rows * feat * (o + 1)]
                out[2 * (q * step + j) + o] = block.reshape(rows, feat, cols)
        return 0

    lax.fori_loop(0, disp // 2 // step, conv, 0)


def finish_kernel(scale, mine, other, own, near, far, weight, right):
    _, _, _, feat, groups = weight.shape
    is_even = parity() == 0
    x, y = mine[...] * scale, other[...] * scale
    total = jnp.concatenate([jnp.where(is_even, x, y), jnp.where(is_even, y, x)], axis=0)
    for a in range(3):
        for e in range(3):
            at = 128 * a + groups * e
            block = total[at : at + groups].T
            for b in range(3):
                weight[2 - a, 2 - b, 2 - e] = block[feat * b : feat * (b + 1)]
    beside = jnp.where(is_even, near[...].astype(F32), 0.0)
    right[...] = (own[...].astype(F32) + beside + far[...].astype(F32)).astype(BF16)


def copy_kernel(*refs):
    half = len(refs) // 2
    for src, dst in zip(refs[:half], refs[half:]):
        dst[...] = src[...]


def sum_kernel(*refs):
    *parts, out = refs
    out[...] = tree([ref[...].astype(F32) for ref in parts]).astype(out.dtype)


def tree(terms):
    while len(terms) > 1:
        terms = [terms[i] + terms[i + 1] for i in range(0, len(terms), 2)]
    return terms[0]


def taps_kernel(taps, w2, wc, turned):
    _, _, _, feat, groups = taps.shape
    rows = wc.shape[1] // 2 // feat
    lane_of = lanes((feat, 2 * SLOT))
    low = lanes((feat, 2 * SLOT)) < SLOT
    zero = jnp.zeros((feat, 2 * SLOT), F32)

    def wide(a, b, e):
        if not 0 <= b <= 2:
            return None
        return jnp.concatenate([taps[a, b, e].astype(F32), zero[:, groups:]], axis=1)

    def beside(x, y):
        if x is None and y is None:
            return zero
        x = zero if x is None else x
        y = zero if y is None else pltpu.roll(y, SLOT, 1)
        return jnp.where(low, x, y)

    def build(a, _):
        def at_row(h):
            return pl.multiple_of((a * rows + h) * feat, feat)

        for e in range(3):
            for h in range(rows):
                for p in range(rows // 2):
                    lane = SLOT * (rows * e + 2 * p)
                    block = beside(wide(a, 2 * p - h + 1, e), wide(a, 2 * p + 1 - h + 1, e))
                    if h == 0 and p == 0:
                        block = place_halo(block, wide(a, 0, e), groups, 0, lane_of)
                    if h == rows - 1 and p == rows // 2 - 1:
                        block = place_halo(block, wide(a, 2, e), groups, 0, lane_of)
                    turned[pl.ds(at_row(h), feat), lane : lane + 2 * SLOT] = block
        return 0

    lax.fori_loop(0, 3, build, 0)
    for s in range(4):
        for e in range(3):
            for r in range(4):
                for o in range(2):
                    taps_of = [None if not 0 <= s - o <= 2 else wide(2 - s + o, 2 - r + i, 2 - e) for i in range(2)]
                    at = 384 * s + 128 * e + feat * r
                    w2[at : at + feat, 128 * o : 128 * (o + 1)] = beside(*taps_of).astype(BF16)
    depth, size = turned.shape[1], rows * feat
    for a in range(3):
        for i in range(depth // 128):
            x = turned[size * a : size * (a + 1), 128 * i : 128 * (i + 1)].T.astype(BF16)
            for o in range(2):
                at = depth * (a + o) + 128 * i
                wc[at : at + 128, size * o : size * (o + 1)] = x
    for o in range(2):
        at = depth * 3 * (1 - o)
        wc[at : at + depth, size * o : size * (o + 1)] = jnp.zeros((depth, size), BF16)


TOKEN = ((8, 128), F32)


def with_token(kernel, inputs, outputs):
    def run(*refs):
        kernel(*refs[: inputs + outputs], *refs[inputs + outputs + 1 :])
        refs[inputs + outputs][...] = jnp.zeros(TOKEN[0], F32)

    return run


def call(kernel, outs, scratch, *args, after=(), token=False, us=0.0):
    skip = len(after)
    if token:
        kernel = with_token(kernel, len(args), len(outs))
        outs = [*outs, TOKEN]
    return pl.pallas_call(
        lambda *refs: kernel(*refs[skip:]),
        out_shape=[jax.ShapeDtypeStruct(s, t) for s, t in outs],
        in_specs=[pl.BlockSpec(memory_space=pl.ANY)] * skip + [VMEM] * len(args),
        out_specs=[VMEM] * len(outs),
        scratch_shapes=scratch,
        compiler_params=pltpu.CompilerParams(vmem_limit_bytes=LIMIT),
        cost_estimate=pl.CostEstimate(
            flops=int(us * 1.15e9), bytes_accessed=int(us * 3.7e6), transcendentals=0
        ),
    )(*after, *args)


def col_shift(block, distance):
    n = lax.axis_size("col")
    route = [(i - distance, i) for i in range(n) if 0 <= i - distance < n]
    return lax.ppermute(block, "col", route)


def row_shift(block, distance):
    n = lax.axis_size("row")
    route = [(i - distance, i) for i in range(n) if 0 <= i - distance < n]
    return lax.ppermute(block, "row", route)


def halos(pays):
    if lax.axis_size("row") == 2:
        got = lax.ppermute(pays[0], "row", [(0, 1), (1, 0)])
        return got, got
    return row_shift(pays[0], 1), row_shift(pays[1], -1)


def stages(n_row, n_col):
    col_bits = [1 << i for i in range(1, n_col.bit_length() - 1)]
    row_bits = [n_col << i for i in range(n_row.bit_length() - 1)]
    assert n_col == 2 << len(col_bits) and n_row == 1 << len(row_bits)
    bits = col_bits[:1] + row_bits + col_bits[1:]
    out = []
    for i in range(0, len(bits), 2):
        pair = bits[i : i + 2]
        out.append(pair + [sum(pair)] if len(pair) == 2 else pair)
    return out


def on_device(left_features, right_features, conv_weight, cotangent):
    rows, cols, channels = left_features.shape
    disp, feat = cotangent.shape[0], cotangent.shape[3]
    groups = conv_weight.shape[3]
    group_size = channels // groups
    wide = group_size * SLOT
    n_row, n_col = lax.axis_size("row"), lax.axis_size("col")
    per = 128 // feat

    if n_row == 2:
        ends = [lambda: (rows - 1) * (1 - lax.axis_index("row"))]
    else:
        ends = [lambda: rows - 1, lambda: 0]
    n = len(ends)

    def masks():
        at = lax.axis_index("row")
        return (
            jnp.where(at > 0, 1.0, 0.0).astype(F32),
            jnp.where(at < n_row - 1, 1.0, 0.0).astype(F32),
        )

    total = cols + 2 * PAD
    count = disp + 2 * rows
    ct = cotangent.transpose(0, 1, 3, 2)

    def swap(block, mask):
        route = [(i, i ^ mask) for i in range(n_row * n_col)]
        return lax.ppermute(block, ("row", "col"), route)

    far = col_shift(right_features, 2)
    by_even, by_odd, ctl, *rims = call(
        functools.partial(pack_kernel, ends),
        [
            ((count, channels), BF16),
            ((count, channels), BF16),
            ((disp, cols, rows * feat), BF16),
        ]
        + [((disp // per, total, 128), F32)] * n,
        [pltpu.VMEM((disp * cols, rows * feat), F32)],
        left_features,
        right_features,
        ct,
        us=0.4,
    )
    inner = range(1, n_col - 1, 2)
    by_even = swap(by_even, 1)
    by_odd = lax.ppermute(by_odd, "col", [(i, i + 1) for i in inner] + [(i + 1, i) for i in inner])
    (passed,) = call(
        pass_kernel, [((rows, cols, channels), BF16)], [], right_features, far, after=[ctl]
    )
    near = swap(passed, 1)
    w2, wc = call(
        taps_kernel,
        [((12 * 128, 2 * 128), BF16), ((4 * 3 * rows * SLOT, 2 * rows * feat), BF16)],
        [pltpu.VMEM((3 * rows * feat, 3 * rows * SLOT), F32)],
        conv_weight.transpose(0, 1, 2, 4, 3),
        after=[passed],
    )
    row_pays = call(
        functools.partial(row_kernel, ends, rows),
        [((disp // per, total, 128), BF16)] * n,
        [pltpu.VMEM((2, disp, 128), F32), pltpu.VMEM((disp // per, total, 128), F32)],
        by_even,
        by_odd,
        *rims,
        after=[w2],
        us=5.0,
    )
    top, bot = halos(row_pays)

    band = 104 + cols + PAD
    spread_rows = 3 * rows * cols + rows * cols // 2 + 2 * count
    vbuf, fl, fr, fr4, *volume_rows = call(
        functools.partial(volume_kernel, ends, group_size),
        [
            ((rows // 2, disp, total, 2 * SLOT), F32),
            ((rows, total, wide), F32),
            ((rows, band, wide), F32),
            ((rows, band, wide), F32),
        ]
        + [((disp // 2 * total, 128), BF16)] * n,
        [
            pltpu.VMEM((spread_rows, channels), BF16),
            pltpu.VMEM((spread_rows, wide), F32),
        ],
        left_features,
        right_features,
        near,
        far,
        by_even,
        by_odd,
        us=2.3,
    )
    keep, give, ctsh = call(
        functools.partial(weight_kernel, masks, groups, feat),
        [((3 * 64, 128), F32), ((3 * 64, 128), F32), ((disp // 2 + 1, 2, cols, 3 * 256), BF16)],
        [
            pltpu.VMEM((rows // 2, 128, (disp // 2 + 2) * 128), BF16),
            pltpu.VMEM((disp, total, 256), F32),
            pltpu.VMEM((3 * 128, 128), F32),
        ],
        vbuf, ctl, by_even, by_odd, top, bot,
        us=2.6,
    )
    got = swap(give, 1)
    (part,) = call(sum_kernel, [(keep.shape, BF16)], [], keep, got)
    gv, rg0, rg1, rg2 = call(
        right_kernel,
        [
            ((rows, disp, cols, 128), F32),
            ((rows, cols, channels), BF16),
            ((rows, cols, channels), BF16),
            ((rows, cols // 2, channels), BF16),
        ],
        [
            pltpu.VMEM((rows, cols + cols + cols // 2, wide), F32),
            pltpu.VMEM((rows, cols + cols + cols // 2 + 8, wide), F32),
            pltpu.VMEM((rows * (cols + cols + cols // 2), wide), BF16),
        ],
        ctsh, w2, fl,
        after=[part],
        us=2.9,
    )
    rg1 = swap(rg1, 1)
    *middle, final = stages(n_row, n_col)
    order = [rg0]
    for stage in middle:
        parts = [part] + [swap(part, m) for m in stage]
        (part,) = call(sum_kernel, [(part.shape, BF16)], [], *parts, after=order, us=4.0)
        order = []
    volume_rows = call(
        copy_kernel, [(x.shape, x.dtype) for x in volume_rows], [], *volume_rows, after=[part]
    )
    vtop, vbot = halos(volume_rows)
    parts = [part] + [swap(part, m) for m in final]
    (rg2,) = call(
        combine_kernel, [((rows, cols, channels), BF16)], [], rg1, rg2, after=volume_rows
    )
    lg, left_done = call(
        left_kernel,
        [((rows, cols, channels), BF16)],
        [pltpu.VMEM((rows, cols, wide), F32)],
        gv, fr, fr4,
        after=[rg2],
        token=True,
        us=1.9,
    )
    (part,) = call(sum_kernel, [(part.shape, F32)], [], *parts, after=[left_done])
    output, conv_done = call(
        functools.partial(conv_kernel, masks, groups),
        [((disp, rows, feat, cols), BF16)],
        [
            pltpu.VMEM((disp // 2 + 1, 2, cols, 3 * rows * SLOT), BF16),
            pltpu.VMEM((rows // 2, disp, total, 128), F32),
        ],
        vbuf, vtop, vbot, wc,
        after=[part],
        token=True,
        us=3.9,
    )
    rg2 = col_shift(rg2, -2)
    cells = disp * rows * n_row * cols * n_col
    weight_grad, right_grad = call(
        functools.partial(finish_kernel, 1.0 / math.sqrt(cells)),
        [((3, 3, 3, feat, groups), F32), ((rows, cols, channels), BF16)],
        [],
        part, swap(part, 1), rg0, rg1, rg2,
        after=[conv_done],
        us=1.0,
    )
    return (
        output.transpose(0, 1, 3, 2),
        weight_grad.transpose(0, 1, 2, 4, 3),
        lg,
        right_grad,
    )


def solution(mesh):
    in_specs = (P("row", "col", None), P("row", "col", None), P(), P(None, "row", "col", None))
    out_specs = (P(None, "row", "col", None), P(), P("row", "col", None), P("row", "col", None))
    return jax.shard_map(
        on_device, mesh=mesh, in_specs=in_specs, out_specs=out_specs, check_vma=False
    )
```

```python
import functools
import math

import jax
import jax.numpy as jnp
from jax import lax
from jax.experimental import pallas as pl
from jax.experimental.pallas import tpu as pltpu
from jax.sharding import PartitionSpec as P

DISP = 24
STEP = 4
SLOT = 64
PAD = 8
F32 = jnp.float32
BF16 = jnp.bfloat16
VMEM = pl.BlockSpec(memory_space=pltpu.VMEM)
LIMIT = 16 * 1024 * 1024


def lanes(shape):
    return lax.broadcasted_iota(jnp.int32, shape, len(shape) - 1)


def channel_table(channels, group_size, flip, value=1.0):
    shape = (group_size * SLOT, channels) if flip else (channels, group_size * SLOT)
    c = lax.broadcasted_iota(jnp.int32, shape, 1 if flip else 0)
    j = lax.broadcasted_iota(jnp.int32, shape, 0 if flip else 1)
    hit = c == (j & (SLOT - 1)) * group_size + (j >> (SLOT.bit_length() - 1))
    return jnp.where(hit, value, 0.0).astype(BF16)


def parity():
    return lax.rem(lax.axis_index("col"), 2)


def dot(a, b):
    return jnp.dot(a, b, preferred_element_type=F32)


def dot_nt(a, b):
    return lax.dot_general(a, b, (((1,), (1,)), ((), ())), preferred_element_type=F32)


def pack_kernel(ends, rims_in, ct, even, odd, ctl, *rest):
    rims, ctf = rest[:-1], rest[-1]
    disp, rows, feat, cols = ct.shape
    per = 128 // feat
    for d in range(disp):
        block = ct[d].reshape(rows * feat, cols).astype(F32).T
        ctf[d * cols : (d + 1) * cols] = block
        ctl[d] = block.astype(BF16)
    columns = []
    for i, col in enumerate((cols - 1, 0)):
        block = ctf[pl.ds(col, disp, stride=cols), :]
        block = jnp.concatenate([block, jnp.zeros((disp, even.shape[1] - rows * feat), F32)], axis=1)
        edge = rims_in[i * 2 * rows : (i + 1) * 2 * rows].astype(F32)
        columns.append(jnp.concatenate([block, edge], axis=0))
    is_even = parity() == 0
    even[...] = jnp.where(is_even, columns[0], columns[1]).astype(BF16)
    odd[...] = jnp.where(is_even, columns[1], columns[0]).astype(BF16)
    for end, rim in zip(ends, rims):
        h = end()
        for q in range(disp // per):
            rim[q, PAD : PAD + cols] = jnp.concatenate(
                [ct[q * per + i, h].astype(F32) for i in range(per)], axis=0
            ).T


def pass_kernel(own, got, out):
    out[...] = jnp.where(parity() == 0, own[...].astype(F32), got[...].astype(F32)).astype(BF16)


def end_columns(by_even, by_odd):
    x, y = by_even[...].astype(F32), by_odd[...].astype(F32)
    is_even = parity() == 0
    return jnp.where(is_even, y, x), jnp.where(is_even, x, y)


def row_kernel(ends, rows, by_even, by_odd, *rest):
    n = len(ends)
    rims, pays, (edges, buf) = rest[:n], rest[n : 2 * n], rest[2 * n :]
    count, total, _ = buf.shape
    disp = edges.shape[1]
    per, cols = disp // count, total - 2 * PAD
    feat = 128 // per
    lane = lanes((count, 128))
    for side, x in enumerate(end_columns(by_even, by_odd)):
        edges[side] = x[0:disp, 0:128]
    for end, rim, pay in zip(ends, rims, pays):
        h = end()
        buf[...] = rim[...]
        for side, at in ((0, PAD - 1), (1, PAD + cols)):
            out = jnp.zeros((count, 128), F32)
            for i in range(per):
                x = edges[side, pl.ds(i, count, stride=per)]
                first = pltpu.roll(x, feat * i, 1) if i else x
                last = pltpu.roll(x, (feat * (i - rows + 1)) % 128, 1) if i != rows - 1 else x
                x = jnp.where(h == 0, first, last)
                out = jnp.where((lane >= feat * i) & (lane < feat * (i + 1)), x, out)
            for q in range(count):
                buf[q, at : at + 1] = out[q : q + 1]
        pay[...] = buf[...].astype(BF16)


def volume_kernel(ends, group_size, left, right, near, far, by_even, by_odd, vbuf, fl, fr, fr4, *rest):
    pays, (mixed, wide_buf) = rest[: len(ends)], rest[len(ends) :]
    rows, cols, channels = left.shape
    disp = vbuf.shape[1]
    reach = fr.shape[1] - cols - PAD
    wide = group_size * SLOT
    base, half = rows * cols, cols // 2
    mixed[0:base] = near[...].reshape(base, channels)
    mixed[base : 2 * base] = right[...].reshape(base, channels)
    mixed[2 * base : 3 * base] = left[...].reshape(base, channels)
    at_far, at_ends = 3 * base, 3 * base + base // 2
    mixed[at_far:at_ends] = far[:, half:].reshape(base // 2, channels)
    count = disp + 2 * rows
    for i, x in enumerate(end_columns(by_even, by_odd)):
        mixed[at_ends + i * count : at_ends + (i + 1) * count] = x.astype(BF16)
    wide_buf[...] = dot(mixed[...], channel_table(channels, group_size, False))
    scale = 1.0 / group_size
    for h in range(rows):
        fl[h, 0:PAD] = jnp.zeros((PAD, wide), F32)
        fl[h, PAD + cols :] = jnp.zeros((PAD, wide), F32)
        at = at_ends + disp + h
        fl[h, PAD - 1 : PAD] = wide_buf[at : at + 1] * scale
        fl[h, PAD : PAD + cols] = wide_buf[2 * base + h * cols : 2 * base + (h + 1) * cols] * scale
        at += count
        fl[h, PAD + cols : PAD + cols + 1] = wide_buf[at : at + 1] * scale
        for ref, off in ((fr, 0), (fr4, STEP)):
            start = reach - cols - half + off
            ref[h, 0:start] = jnp.zeros((start, wide), F32)
            ref[h, start : start + half] = wide_buf[at_far + h * half : at_far + (h + 1) * half]
            for part in range(2):
                at = part * base + h * cols
                to = start + half + part * cols
                ref[h, to : to + cols] = wide_buf[at : at + cols]
            to = start + half + 2 * cols
            ref[h, to:] = jnp.zeros((ref.shape[1] - to, wide), F32)
            at = at_ends + count + disp + rows + h
            ref[h, to : to + 1] = wide_buf[at : at + 1]
    total = cols + 2 * PAD
    low = lanes((8, 128)) < SLOT
    pairs, times, lots = rows // 2, disp // 2, wide // 128
    count = total // 16

    def products(i, _):
        p, at = lax.rem(i, pairs), pl.multiple_of(lax.div(i, pairs) * (8 * count), 8)
        lefts = [
            [
                [fl[2 * p + o, pl.ds(at + 8 * b, 8), 128 * j : 128 * (j + 1)] for j in range(lots)]
                for b in range(count)
            ]
            for o in range(2)
        ]
        for odd, band in enumerate((fr, fr4)):
            for r in range(1 - times, count):
                start = pl.multiple_of(at + reach - PAD + 8 * r, 8)
                here = [
                    [band[2 * p + o, pl.ds(start, 8), 128 * j : 128 * (j + 1)] for j in range(lots)]
                    for o in range(2)
                ]
                for t in range(max(0, -r), min(times, count - r)):
                    sums = []
                    for o in range(2):
                        acc = lefts[o][r + t][0] * here[o][0]
                        for j in range(1, lots):
                            acc = acc + lefts[o][r + t][j] * here[o][j]
                        sums.append(acc + pltpu.roll(acc, SLOT, 1))
                    vbuf[p, 2 * t + odd, pl.ds(at + 8 * (r + t), 8)] = jnp.where(low, *sums)
        return 0

    lax.fori_loop(0, 2 * pairs, products, 0)
    big = lanes((total, 128)) < SLOT

    for dd in range(disp // 2):
        for end, pay in zip(ends, pays):
            h = end()
            if isinstance(h, int):
                halves = [vbuf[h // 2, 2 * dd + o] for o in range(2)]
                if h % 2 == 0:
                    halves[1] = pltpu.roll(halves[1], SLOT, 1)
                else:
                    halves[0] = pltpu.roll(halves[0], SLOT, 1)
                out = jnp.where(big, halves[0], halves[1])
            else:
                last = pairs - 1
                first = jnp.where(big, vbuf[0, 2 * dd], pltpu.roll(vbuf[0, 2 * dd + 1], SLOT, 1))
                final = jnp.where(
                    big, pltpu.roll(vbuf[last, 2 * dd], SLOT, 1), vbuf[last, 2 * dd + 1]
                )
                out = jnp.where(h == 0, first, final)
            pay[dd * total : (dd + 1) * total] = out.astype(BF16)


def weight_kernel(
    masks, groups, feat, vbuf, ctl, by_even, by_odd, top, bot, keep_out, give_out, ctsh, vt, buf, sums
):
    disp, cols, width = ctl.shape
    pairs, per, half = vbuf.shape[0], 128 // feat, disp // 2
    mtop, mbot = masks()
    ctsh[0, 0] = jnp.zeros(ctsh.shape[2:], BF16)
    ctsh[half, 1] = jnp.zeros(ctsh.shape[2:], BF16)
    lane, lane_in, lane_one = lanes(top.shape[1:]), lanes((cols, 128)), lanes((1, 128))
    shifts = (feat, 128 - feat)
    edges = [x[0:disp, 0:128] for x in end_columns(by_even, by_odd)]
    turned = [[pltpu.roll(x, shift, 1) for shift in shifts] for x in edges]
    for q in range(disp // per):
        t = top[q].astype(F32) * mtop
        z = bot[q].astype(F32) * mbot
        for i in range(per):
            d = q * per + i
            rims = (
                t if i == 0 else pltpu.roll(t, 128 - feat * i, 1),
                z if i == per - 1 else pltpu.roll(z, feat * (per - 1 - i), 1),
            )
            inner = ctl[d].astype(F32)
            for p, (rim, shift) in enumerate(zip(rims, shifts)):

                def on_rim(x):
                    return x < feat if p == 0 else x >= 128 - feat

                at = slice(128 * p, 128 * (p + 1))
                buf[d, PAD : PAD + cols, at] = jnp.where(
                    on_rim(lane_in), rim[PAD : PAD + cols], pltpu.roll(inner, shift, 1)
                )
                for side, row in enumerate((PAD - 1, PAD + cols)):
                    buf[d, row : row + 1, at] = jnp.where(
                        on_rim(lane_one), rim[row : row + 1], turned[side][p][d : d + 1]
                    )
            for e in range(3):
                ctsh[(d + 1) // 2, (d + 1) % 2, :, 256 * e : 256 * (e + 1)] = buf[
                    d, PAD - 1 + e : PAD - 1 + e + cols
                ].astype(BF16)
    none = jnp.zeros((cols, 128), F32)
    for p in range(pairs):
        for j in range(-1, half + 1):
            block = [
                vbuf[p, d, PAD : PAD + cols] if 0 <= d < disp and 0 <= j + half * o else none
                for o, d in enumerate((j, j + half))
            ]
            if j == half:
                block[1] = none
            x = jnp.concatenate(block, axis=0).astype(BF16)
            vt[p, :, 128 * (j + 1) : 128 * (j + 2)] = x.T
    size = disp * cols
    left = jnp.concatenate(
        [
            jnp.concatenate([vt[p, :, 128 * (2 - a) : 128 * (2 - a) + size] for p in range(pairs)], axis=1)
            for a in range(3)
        ],
        axis=0,
    )
    right = jnp.concatenate(
        [
            jnp.concatenate(
                [
                    ctsh[(d + 1) // 2, (d + 1) % 2, :, 256 * e + 128 * p : 256 * e + 128 * (p + 1)]
                    for e in range(3)
                ],
                axis=1,
            )
            for p in range(pairs)
            for j in range(half)
            for d in (j, j + half)
        ],
        axis=0,
    )
    full = dot(left, right)
    keep = lanes((groups, 128)) < 3 * feat
    sums[...] = jnp.zeros(sums.shape, F32)
    for a in range(3):
        for e in range(3):
            block = full[128 * a : 128 * (a + 1), 128 * e : 128 * (e + 1)]
            out = block[0:groups] + pltpu.roll(block[SLOT : SLOT + groups], 128 - feat, 1)
            at = 128 * a + groups * e
            sums[at : at + groups] = jnp.where(keep, out, 0.0)
    half = sums.shape[0] // 2
    is_even = parity() == 0
    low, high = sums[0:half], sums[half:]
    keep_out[...] = jnp.where(is_even, low, high)
    give_out[...] = jnp.where(is_even, high, low)


def right_kernel(ctsh, w2, fl, gv, rg0, rg1, rg2, acce, acco, both):
    disp = gv.shape[1]
    rows, cols, channels = rg0.shape
    wide = fl.shape[2]
    group_size = wide // SLOT
    step = disp // 4
    low = lanes((step * cols, 128)) < SLOT

    def conv(q, _):
        for p in range(rows // 2):
            slabs = [
                ctsh[pl.ds(q * step + s // 2, step), s % 2, :, 256 * e + 128 * p : 256 * e + 128 * (p + 1)]
                for s in range(4)
                for e in range(3)
            ]
            slabs = [x.reshape(step * cols, 128) for x in slabs]
            acc = dot(jnp.concatenate(slabs, axis=1), w2[...]).astype(BF16).astype(F32)
            for o in range(2):
                x = acc[:, 128 * o : 128 * (o + 1)]
                r = pltpu.roll(x, SLOT, 1)
                for hh in range(2):
                    y = jnp.where(low, r, x) if hh else jnp.where(low, x, r)
                    for j in range(step):
                        gv[2 * p + hh, 2 * (q * step + j) + o] = y[j * cols : (j + 1) * cols]
        return 0

    lax.fori_loop(0, 2, conv, 0)
    count = cols // 8
    back = acce.shape[1] - cols
    lead = back // 8

    lots = wide // 128

    def right_row(h, _):
        here = [
            [fl[h, PAD + 8 * b : PAD + 8 * b + 8, 128 * j : 128 * (j + 1)] for j in range(lots)]
            for b in range(count)
        ]
        for odd, buf in enumerate((acce, acco)):
            for k in range(lead + count):
                accs = [None] * lots
                for t in range(disp // 2):
                    b = k + t - lead
                    if b < 0 or b >= count:
                        continue
                    g = gv[h, 2 * t + odd, 8 * b : 8 * b + 8]
                    for j in range(lots):
                        term = g * here[b][j]
                        accs[j] = term if accs[j] is None else accs[j] + term
                for j in range(lots):
                    x = jnp.zeros((8, 128), F32) if accs[j] is None else accs[j]
                    buf[h, 8 * k : 8 * k + 8, 128 * j : 128 * (j + 1)] = x
        acco[h, 8 * (lead + count) :] = jnp.zeros((8, wide), F32)
        return 0

    lax.fori_loop(0, rows, right_row, 0)
    size = back + cols
    for h in range(rows):
        both[h * size : (h + 1) * size] = (acce[h] + acco[h, STEP : STEP + size]).astype(BF16)
    whole = dot(both[...], channel_table(channels, group_size, True)).astype(BF16)
    half = cols // 2
    for h in range(rows):
        at = h * size + back
        rg2[h] = whole[at - cols - half : at - cols]
        rg1[h] = whole[at - cols : at]
        rg0[h] = whole[at : at + cols]


def left_kernel(gv, fr, fr4, lg, accl):
    rows, cols, channels = lg.shape
    disp, wide = gv.shape[1], fr.shape[2]
    group_size = wide // SLOT
    reach = fr.shape[1] - cols - PAD
    count, times, lots = cols // 8, disp // 2, wide // 128

    def left_row(h, _):
        accs = [[None] * lots for _ in range(count)]
        for odd, band in enumerate((fr, fr4)):
            for r in range(1 - times, count):
                at = reach + 8 * r
                here = [band[h, at : at + 8, 128 * j : 128 * (j + 1)] for j in range(lots)]
                for t in range(max(0, -r), min(times, count - r)):
                    g = gv[h, 2 * t + odd, 8 * (r + t) : 8 * (r + t) + 8]
                    for j in range(lots):
                        term, acc = g * here[j], accs[r + t][j]
                        accs[r + t][j] = term if acc is None else acc + term
        for b in range(count):
            for j in range(lots):
                accl[h, 8 * b : 8 * b + 8, 128 * j : 128 * (j + 1)] = accs[b][j] * (1.0 / group_size)
        return 0

    lax.fori_loop(0, rows, left_row, 0)
    whole = accl[...].reshape(rows * cols, wide).astype(BF16)
    out = dot(whole, channel_table(channels, group_size, True)).astype(BF16)
    lg[...] = out.reshape(rows, cols, channels)


def combine_kernel(got, rg2, out):
    cols = out.shape[1]
    half = cols // 2
    part = jnp.where(parity() == 0, 0.0, got[...].astype(F32))
    out[:, 0:half] = part[:, 0:half].astype(BF16)
    out[:, half:] = (part[:, half:] + rg2[...].astype(F32)).astype(BF16)


def halo_lanes(groups):
    first = SLOT - groups
    assert groups - first <= first
    return (groups, SLOT, groups), (SLOT + groups, SLOT + 2 * groups - first, SLOT + groups - first)


def place_halo(base, row, groups, offset, lane):
    for start, end, shift in halo_lanes(groups):
        moved = pltpu.roll(row, (shift - offset) % 128, 1)
        base = jnp.where((lane >= start) & (lane < end), moved, base)
    return base


def spread_kernel(masks, groups, vbuf, top, bot, taps, buf):
    cols = taps.shape[2]
    disp, total = buf.shape[1], buf.shape[2]
    lane = lanes((total, 128))
    zeros = jnp.zeros((cols, taps.shape[3]), BF16)
    taps[0, 0] = zeros
    taps[disp // 2, 1] = zeros
    halos_of = [(ref, mask) for ref, mask in zip((top, bot), masks())]
    for dd in range(disp // 2):
        for p, (ref, mask) in enumerate(halos_of):
            row = ref[dd * total : (dd + 1) * total].astype(F32) * mask
            for o in range(2):
                d = 2 * dd + o
                buf[p, d] = place_halo(vbuf[p, d], row, groups, SLOT * o, lane)
                for e in range(3):
                    at = 256 * e + 128 * p
                    taps[(d + 1) // 2, (d + 1) % 2, :, at : at + 128] = buf[
                        p, d, PAD - 1 + e : PAD - 1 + e + cols
                    ].astype(BF16)


def conv_kernel(taps, wc, out):
    disp, rows, feat, cols = out.shape
    step = 6

    def conv(q, _):
        slabs = [
            taps[pl.ds(q * step + s // 2, step), s % 2].reshape(step * cols, taps.shape[3])
            for s in range(4)
        ]
        acc = dot(jnp.concatenate(slabs, axis=1), wc[...])
        for j in range(step):
            both = acc[j * cols : (j + 1) * cols].T.astype(BF16)
            for o in range(2):
                block = both[rows * feat * o : rows * feat * (o + 1)]
                out[2 * (q * step + j) + o] = block.reshape(rows, feat, cols)
        return 0

    lax.fori_loop(0, disp // 2 // step, conv, 0)


def finish_kernel(scale, mine, other, own, near, far, weight, right):
    _, _, _, feat, groups = weight.shape
    is_even = parity() == 0
    x, y = mine[...] * scale, other[...] * scale
    total = jnp.concatenate([jnp.where(is_even, x, y), jnp.where(is_even, y, x)], axis=0)
    for a in range(3):
        for e in range(3):
            at = 128 * a + groups * e
            block = total[at : at + groups].T
            for b in range(3):
                weight[2 - a, 2 - b, 2 - e] = block[feat * b : feat * (b + 1)]
    beside = jnp.where(is_even, near[...].astype(F32), 0.0)
    right[...] = (own[...].astype(F32) + beside + far[...].astype(F32)).astype(BF16)


def copy_kernel(*refs):
    half = len(refs) // 2
    for src, dst in zip(refs[:half], refs[half:]):
        dst[...] = src[...]


def sum_kernel(*refs):
    *parts, out = refs
    out[...] = tree([ref[...].astype(F32) for ref in parts]).astype(out.dtype)


def tree(terms):
    while len(terms) > 1:
        terms = [terms[i] + terms[i + 1] for i in range(0, len(terms), 2)]
    return terms[0]


def taps_kernel(taps, w2, wc, turned):
    _, _, _, feat, groups = taps.shape
    rows = wc.shape[1] // 2 // feat
    lane_of = lanes((feat, 2 * SLOT))
    low = lanes((feat, 2 * SLOT)) < SLOT
    zero = jnp.zeros((feat, 2 * SLOT), F32)

    def wide(a, b, e):
        if not 0 <= b <= 2:
            return None
        return jnp.concatenate([taps[a, b, e].astype(F32), zero[:, groups:]], axis=1)

    def beside(x, y):
        if x is None and y is None:
            return zero
        x = zero if x is None else x
        y = zero if y is None else pltpu.roll(y, SLOT, 1)
        return jnp.where(low, x, y)

    def build(a, _):
        def at_row(h):
            return pl.multiple_of((a * rows + h) * feat, feat)

        for e in range(3):
            for h in range(rows):
                for p in range(rows // 2):
                    lane = SLOT * (rows * e + 2 * p)
                    block = beside(wide(a, 2 * p - h + 1, e), wide(a, 2 * p + 1 - h + 1, e))
                    if h == 0 and p == 0:
                        block = place_halo(block, wide(a, 0, e), groups, 0, lane_of)
                    if h == rows - 1 and p == rows // 2 - 1:
                        block = place_halo(block, wide(a, 2, e), groups, 0, lane_of)
                    turned[pl.ds(at_row(h), feat), lane : lane + 2 * SLOT] = block
        return 0

    lax.fori_loop(0, 3, build, 0)
    for s in range(4):
        for e in range(3):
            for r in range(4):
                for o in range(2):
                    taps_of = [None if not 0 <= s - o <= 2 else wide(2 - s + o, 2 - r + i, 2 - e) for i in range(2)]
                    at = 384 * s + 128 * e + feat * r
                    w2[at : at + feat, 128 * o : 128 * (o + 1)] = beside(*taps_of).astype(BF16)
    depth, size = turned.shape[1], rows * feat
    for a in range(3):
        for i in range(depth // 128):
            x = turned[size * a : size * (a + 1), 128 * i : 128 * (i + 1)].T.astype(BF16)
            for o in range(2):
                at = depth * (a + o) + 128 * i
                wc[at : at + 128, size * o : size * (o + 1)] = x
    for o in range(2):
        at = depth * 3 * (1 - o)
        wc[at : at + depth, size * o : size * (o + 1)] = jnp.zeros((depth, size), BF16)


TOKEN = ((8, 128), F32)


def with_token(kernel, inputs, outputs):
    def run(*refs):
        kernel(*refs[: inputs + outputs], *refs[inputs + outputs + 1 :])
        refs[inputs + outputs][...] = jnp.zeros(TOKEN[0], F32)

    return run


def call(kernel, outs, scratch, *args, after=(), token=False, us=0.0):
    skip = len(after)
    if token:
        kernel = with_token(kernel, len(args), len(outs))
        outs = [*outs, TOKEN]
    return pl.pallas_call(
        lambda *refs: kernel(*refs[skip:]),
        out_shape=[jax.ShapeDtypeStruct(s, t) for s, t in outs],
        in_specs=[pl.BlockSpec(memory_space=pl.ANY)] * skip + [VMEM] * len(args),
        out_specs=[VMEM] * len(outs),
        scratch_shapes=scratch,
        compiler_params=pltpu.CompilerParams(vmem_limit_bytes=LIMIT),
        cost_estimate=pl.CostEstimate(
            flops=int(us * 1.15e9), bytes_accessed=int(us * 3.7e6), transcendentals=0
        ),
    )(*after, *args)


def col_shift(block, distance):
    n = lax.axis_size("col")
    route = [(i - distance, i) for i in range(n) if 0 <= i - distance < n]
    return lax.ppermute(block, "col", route)


def row_shift(block, distance):
    n = lax.axis_size("row")
    route = [(i - distance, i) for i in range(n) if 0 <= i - distance < n]
    return lax.ppermute(block, "row", route)


def halos(pays):
    if lax.axis_size("row") == 2:
        got = lax.ppermute(pays[0], "row", [(0, 1), (1, 0)])
        return got, got
    return row_shift(pays[0], 1), row_shift(pays[1], -1)


def hops(n_row, n_col):
    col_bits = [1 << i for i in range(1, n_col.bit_length() - 1)]
    row_bits = [n_col << i for i in range(n_row.bit_length() - 1)]
    assert n_col == 2 << len(col_bits) and n_row == 1 << len(row_bits)
    return col_bits[:-1] + row_bits + col_bits[-1:]


def on_device(left_features, right_features, conv_weight, cotangent):
    rows, cols, channels = left_features.shape
    disp, feat = cotangent.shape[0], cotangent.shape[3]
    groups = conv_weight.shape[3]
    group_size = channels // groups
    wide = group_size * SLOT
    n_row, n_col = lax.axis_size("row"), lax.axis_size("col")
    per = 128 // feat

    if n_row == 2:
        ends = [lambda: (rows - 1) * (1 - lax.axis_index("row"))]
    else:
        ends = [lambda: rows - 1, lambda: 0]
    n = len(ends)

    def masks():
        at = lax.axis_index("row")
        return (
            jnp.where(at > 0, 1.0, 0.0).astype(F32),
            jnp.where(at < n_row - 1, 1.0, 0.0).astype(F32),
        )

    total = cols + 2 * PAD
    count = disp + 2 * rows
    ct = cotangent.transpose(0, 1, 3, 2)

    def swap(block, mask):
        route = [(i, i ^ mask) for i in range(n_row * n_col)]
        return lax.ppermute(block, ("row", "col"), route)

    far = col_shift(right_features, 2)
    by_even, by_odd, ctl, *rims = call(
        functools.partial(pack_kernel, ends),
        [
            ((count, channels), BF16),
            ((count, channels), BF16),
            ((disp, cols, rows * feat), BF16),
        ]
        + [((disp // per, total, 128), F32)] * n,
        [pltpu.VMEM((disp * cols, rows * feat), F32)],
        jnp.concatenate([x[:, at] for at in (cols - 1, 0) for x in (left_features, right_features)]),
        ct,
        us=0.4,
    )
    inner = range(1, n_col - 1, 2)
    by_even = swap(by_even, 1)
    by_odd = lax.ppermute(by_odd, "col", [(i, i + 1) for i in inner] + [(i + 1, i) for i in inner])
    (passed,) = call(
        pass_kernel, [((rows, cols, channels), BF16)], [], right_features, far, after=[ctl]
    )
    near = swap(passed, 1)
    w2, wc = call(
        taps_kernel,
        [((12 * 128, 2 * 128), BF16), ((4 * 3 * rows * SLOT, 2 * rows * feat), BF16)],
        [pltpu.VMEM((3 * rows * feat, 3 * rows * SLOT), F32)],
        conv_weight.transpose(0, 1, 2, 4, 3),
        after=[passed],
    )
    row_pays = call(
        functools.partial(row_kernel, ends, rows),
        [((disp // per, total, 128), BF16)] * n,
        [pltpu.VMEM((2, disp, 128), F32), pltpu.VMEM((disp // per, total, 128), F32)],
        by_even,
        by_odd,
        *rims,
        after=[w2],
        us=5.0,
    )
    top, bot = halos(row_pays)

    band = 104 + cols + PAD
    spread_rows = 3 * rows * cols + rows * cols // 2 + 2 * count
    vbuf, fl, fr, fr4, *volume_rows = call(
        functools.partial(volume_kernel, ends, group_size),
        [
            ((rows // 2, disp, total, 2 * SLOT), F32),
            ((rows, total, wide), F32),
            ((rows, band, wide), F32),
            ((rows, band, wide), F32),
        ]
        + [((disp // 2 * total, 128), BF16)] * n,
        [
            pltpu.VMEM((spread_rows, channels), BF16),
            pltpu.VMEM((spread_rows, wide), F32),
        ],
        left_features,
        right_features,
        near,
        far,
        by_even,
        by_odd,
        us=2.3,
    )
    keep, give, ctsh = call(
        functools.partial(weight_kernel, masks, groups, feat),
        [((3 * 64, 128), F32), ((3 * 64, 128), F32), ((disp // 2 + 1, 2, cols, 3 * 256), BF16)],
        [
            pltpu.VMEM((rows // 2, 128, (disp // 2 + 2) * 128), BF16),
            pltpu.VMEM((disp, total, 256), F32),
            pltpu.VMEM((3 * 128, 128), F32),
        ],
        vbuf, ctl, by_even, by_odd, top, bot,
        us=2.6,
    )
    got = swap(give, 1)
    def join(part, mask, kind, after=(), us=0.0):
        terms = (part, swap(part, mask))
        return call(sum_kernel, [(part.shape, kind)], [], *terms, after=after, us=us)[0]

    *early, second, last = hops(n_row, n_col)
    (part,) = call(sum_kernel, [(keep.shape, BF16)], [], keep, got)
    gv, rg0, rg1, rg2 = call(
        right_kernel,
        [
            ((rows, disp, cols, 128), F32),
            ((rows, cols, channels), BF16),
            ((rows, cols, channels), BF16),
            ((rows, cols // 2, channels), BF16),
        ],
        [
            pltpu.VMEM((rows, cols + cols + cols // 2, wide), F32),
            pltpu.VMEM((rows, cols + cols + cols // 2 + 8, wide), F32),
            pltpu.VMEM((rows * (cols + cols + cols // 2), wide), BF16),
        ],
        ctsh, w2, fl,
        after=[part],
        us=2.9,
    )
    rg1 = swap(rg1, 1)
    part = join(part, early[0], F32, after=[rg0], us=4.0)
    volume_rows = call(
        copy_kernel, [(x.shape, x.dtype) for x in volume_rows], [], *volume_rows, after=[part]
    )
    vtop, vbot = halos(volume_rows)
    (rg2,) = call(
        combine_kernel, [((rows, cols, channels), BF16)], [], rg1, rg2, after=volume_rows
    )
    for mask in early[1:-1]:
        part = join(part, mask, F32)
    part = join(part, early[-1], BF16, after=[rg2], us=4.0)
    lg, left_done = call(
        left_kernel,
        [((rows, cols, channels), BF16)],
        [pltpu.VMEM((rows, cols, wide), F32)],
        gv, fr, fr4,
        after=[part],
        token=True,
        us=1.9,
    )
    part = join(part, second, BF16, after=[left_done], us=4.0)
    (spread,) = call(
        functools.partial(spread_kernel, masks, groups),
        [((disp // 2 + 1, 2, cols, 3 * rows * SLOT), BF16)],
        [pltpu.VMEM((rows // 2, disp, total, 128), F32)],
        vbuf, vtop, vbot,
        after=[part],
        us=1.9,
    )
    part = join(part, last, F32, after=[spread], us=4.0)
    output, conv_done = call(
        conv_kernel,
        [((disp, rows, feat, cols), BF16)],
        [],
        spread, wc,
        after=[part],
        token=True,
        us=2.0,
    )
    rg2 = col_shift(rg2, -2)
    cells = disp * rows * n_row * cols * n_col
    weight_grad, right_grad = call(
        functools.partial(finish_kernel, 1.0 / math.sqrt(cells)),
        [((3, 3, 3, feat, groups), F32), ((rows, cols, channels), BF16)],
        [],
        part, swap(part, 1), rg0, rg1, rg2,
        after=[conv_done],
        us=1.0,
    )
    return (
        output.transpose(0, 1, 3, 2),
        weight_grad.transpose(0, 1, 2, 4, 3),
        lg,
        right_grad,
    )


def solution(mesh):
    in_specs = (P("row", "col", None), P("row", "col", None), P(), P(None, "row", "col", None))
    out_specs = (P(None, "row", "col", None), P(), P("row", "col", None), P("row", "col", None))
    return jax.shard_map(
        on_device, mesh=mesh, in_specs=in_specs, out_specs=out_specs, check_vma=False
    )
```

```python
import functools
import math

import jax
import jax.numpy as jnp
from jax import lax
from jax.experimental import pallas as pl
from jax.experimental.pallas import tpu as pltpu
from jax.sharding import PartitionSpec as P

DISP = 24
STEP = 4
SLOT = 64
PAD = 8
F32 = jnp.float32
BF16 = jnp.bfloat16
VMEM = pl.BlockSpec(memory_space=pltpu.VMEM)
LIMIT = 16 * 1024 * 1024


def lanes(shape):
    return lax.broadcasted_iota(jnp.int32, shape, len(shape) - 1)


def channel_table(channels, group_size, flip, value=1.0):
    shape = (group_size * SLOT, channels) if flip else (channels, group_size * SLOT)
    c = lax.broadcasted_iota(jnp.int32, shape, 1 if flip else 0)
    j = lax.broadcasted_iota(jnp.int32, shape, 0 if flip else 1)
    hit = c == (j & (SLOT - 1)) * group_size + (j >> (SLOT.bit_length() - 1))
    return jnp.where(hit, value, 0.0).astype(BF16)


def parity():
    return lax.rem(lax.axis_index("col"), 2)


def dot(a, b):
    return jnp.dot(a, b, preferred_element_type=F32)


def dot_nt(a, b):
    return lax.dot_general(a, b, (((1,), (1,)), ((), ())), preferred_element_type=F32)


def pack_kernel(ends, rims_in, ct, even, odd, ctl, *rest):
    rims, ctf = rest[:-1], rest[-1]
    disp, rows, feat, cols = ct.shape
    per = 128 // feat
    for d in range(disp):
        block = ct[d].reshape(rows * feat, cols).astype(F32).T
        ctf[d * cols : (d + 1) * cols] = block
        ctl[d] = block.astype(BF16)
    columns = []
    for i, col in enumerate((cols - 1, 0)):
        block = ctf[pl.ds(col, disp, stride=cols), :]
        block = jnp.concatenate([block, jnp.zeros((disp, even.shape[1] - rows * feat), F32)], axis=1)
        edge = rims_in[i * 2 * rows : (i + 1) * 2 * rows].astype(F32)
        columns.append(jnp.concatenate([block, edge], axis=0))
    is_even = parity() == 0
    even[...] = jnp.where(is_even, columns[0], columns[1]).astype(BF16)
    odd[...] = jnp.where(is_even, columns[1], columns[0]).astype(BF16)
    for end, rim in zip(ends, rims):
        h = end()
        for q in range(disp // per):
            rim[q, PAD : PAD + cols] = jnp.concatenate(
                [ct[q * per + i, h].astype(F32) for i in range(per)], axis=0
            ).T


def pass_kernel(own, got, out):
    out[...] = jnp.where(parity() == 0, own[...].astype(F32), got[...].astype(F32)).astype(BF16)


def end_columns(by_even, by_odd):
    x, y = by_even[...].astype(F32), by_odd[...].astype(F32)
    is_even = parity() == 0
    return jnp.where(is_even, y, x), jnp.where(is_even, x, y)


def row_kernel(ends, rows, by_even, by_odd, *rest):
    n = len(ends)
    rims, pays, (edges, buf) = rest[:n], rest[n : 2 * n], rest[2 * n :]
    count, total, _ = buf.shape
    disp = edges.shape[1]
    per, cols = disp // count, total - 2 * PAD
    feat = 128 // per
    lane = lanes((count, 128))
    for side, x in enumerate(end_columns(by_even, by_odd)):
        edges[side] = x[0:disp, 0:128]
    for end, rim, pay in zip(ends, rims, pays):
        h = end()
        buf[...] = rim[...]
        for side, at in ((0, PAD - 1), (1, PAD + cols)):
            out = jnp.zeros((count, 128), F32)
            for i in range(per):
                x = edges[side, pl.ds(i, count, stride=per)]
                first = pltpu.roll(x, feat * i, 1) if i else x
                last = pltpu.roll(x, (feat * (i - rows + 1)) % 128, 1) if i != rows - 1 else x
                x = jnp.where(h == 0, first, last)
                out = jnp.where((lane >= feat * i) & (lane < feat * (i + 1)), x, out)
            for q in range(count):
                buf[q, at : at + 1] = out[q : q + 1]
        pay[...] = buf[...].astype(BF16)


def volume_kernel(ends, group_size, left, right, near, far, by_even, by_odd, vbuf, fl, fr, fr4, *rest):
    pays, (mixed, wide_buf) = rest[: len(ends)], rest[len(ends) :]
    rows, cols, channels = left.shape
    disp = vbuf.shape[1]
    reach = fr.shape[1] - cols - PAD
    wide = group_size * SLOT
    base, half = rows * cols, cols // 2
    mixed[0:base] = near[...].reshape(base, channels)
    mixed[base : 2 * base] = right[...].reshape(base, channels)
    mixed[2 * base : 3 * base] = left[...].reshape(base, channels)
    at_far, at_ends = 3 * base, 3 * base + base // 2
    mixed[at_far:at_ends] = far[:, half:].reshape(base // 2, channels)
    count = disp + 2 * rows
    for i, x in enumerate(end_columns(by_even, by_odd)):
        mixed[at_ends + i * count : at_ends + (i + 1) * count] = x.astype(BF16)
    wide_buf[...] = dot(mixed[...], channel_table(channels, group_size, False))
    scale = 1.0 / group_size
    for h in range(rows):
        fl[h, 0:PAD] = jnp.zeros((PAD, wide), F32)
        fl[h, PAD + cols :] = jnp.zeros((PAD, wide), F32)
        at = at_ends + disp + h
        fl[h, PAD - 1 : PAD] = wide_buf[at : at + 1] * scale
        fl[h, PAD : PAD + cols] = wide_buf[2 * base + h * cols : 2 * base + (h + 1) * cols] * scale
        at += count
        fl[h, PAD + cols : PAD + cols + 1] = wide_buf[at : at + 1] * scale
        for ref, off in ((fr, 0), (fr4, STEP)):
            start = reach - cols - half + off
            ref[h, 0:start] = jnp.zeros((start, wide), F32)
            ref[h, start : start + half] = wide_buf[at_far + h * half : at_far + (h + 1) * half]
            for part in range(2):
                at = part * base + h * cols
                to = start + half + part * cols
                ref[h, to : to + cols] = wide_buf[at : at + cols]
            to = start + half + 2 * cols
            ref[h, to:] = jnp.zeros((ref.shape[1] - to, wide), F32)
            at = at_ends + count + disp + rows + h
            ref[h, to : to + 1] = wide_buf[at : at + 1]
    total = cols + 2 * PAD
    low = lanes((8, 128)) < SLOT
    pairs, times, lots = rows // 2, disp // 2, wide // 128
    count = total // 16

    def products(i, _):
        p, at = lax.rem(i, pairs), pl.multiple_of(lax.div(i, pairs) * (8 * count), 8)
        lefts = [
            [
                [fl[2 * p + o, pl.ds(at + 8 * b, 8), 128 * j : 128 * (j + 1)] for j in range(lots)]
                for b in range(count)
            ]
            for o in range(2)
        ]
        for odd, band in enumerate((fr, fr4)):
            for r in range(1 - times, count):
                start = pl.multiple_of(at + reach - PAD + 8 * r, 8)
                here = [
                    [band[2 * p + o, pl.ds(start, 8), 128 * j : 128 * (j + 1)] for j in range(lots)]
                    for o in range(2)
                ]
                for t in range(max(0, -r), min(times, count - r)):
                    sums = []
                    for o in range(2):
                        acc = lefts[o][r + t][0] * here[o][0]
                        for j in range(1, lots):
                            acc = acc + lefts[o][r + t][j] * here[o][j]
                        sums.append(acc + pltpu.roll(acc, SLOT, 1))
                    vbuf[p, 2 * t + odd, pl.ds(at + 8 * (r + t), 8)] = jnp.where(low, *sums)
        return 0

    lax.fori_loop(0, 2 * pairs, products, 0)
    big = lanes((total, 128)) < SLOT

    for dd in range(disp // 2):
        for end, pay in zip(ends, pays):
            h = end()
            if isinstance(h, int):
                halves = [vbuf[h // 2, 2 * dd + o] for o in range(2)]
                if h % 2 == 0:
                    halves[1] = pltpu.roll(halves[1], SLOT, 1)
                else:
                    halves[0] = pltpu.roll(halves[0], SLOT, 1)
                out = jnp.where(big, halves[0], halves[1])
            else:
                last = pairs - 1
                first = jnp.where(big, vbuf[0, 2 * dd], pltpu.roll(vbuf[0, 2 * dd + 1], SLOT, 1))
                final = jnp.where(
                    big, pltpu.roll(vbuf[last, 2 * dd], SLOT, 1), vbuf[last, 2 * dd + 1]
                )
                out = jnp.where(h == 0, first, final)
            pay[dd * total : (dd + 1) * total] = out.astype(BF16)


def weight_kernel(
    masks, groups, feat, vbuf, ctl, by_even, by_odd, top, bot, keep_out, give_out, ctsh, vt, buf, sums
):
    disp, cols, width = ctl.shape
    pairs, per, half = vbuf.shape[0], 128 // feat, disp // 2
    mtop, mbot = masks()
    ctsh[0, 0] = jnp.zeros(ctsh.shape[2:], BF16)
    ctsh[half, 1] = jnp.zeros(ctsh.shape[2:], BF16)
    lane, lane_in, lane_one = lanes(top.shape[1:]), lanes((cols, 128)), lanes((1, 128))
    shifts = (feat, 128 - feat)
    edges = [x[0:disp, 0:128] for x in end_columns(by_even, by_odd)]
    turned = [[pltpu.roll(x, shift, 1) for shift in shifts] for x in edges]
    for q in range(disp // per):
        t = top[q].astype(F32) * mtop
        z = bot[q].astype(F32) * mbot
        for i in range(per):
            d = q * per + i
            rims = (
                t if i == 0 else pltpu.roll(t, 128 - feat * i, 1),
                z if i == per - 1 else pltpu.roll(z, feat * (per - 1 - i), 1),
            )
            inner = ctl[d].astype(F32)
            for p, (rim, shift) in enumerate(zip(rims, shifts)):

                def on_rim(x):
                    return x < feat if p == 0 else x >= 128 - feat

                at = slice(128 * p, 128 * (p + 1))
                buf[d, PAD : PAD + cols, at] = jnp.where(
                    on_rim(lane_in), rim[PAD : PAD + cols], pltpu.roll(inner, shift, 1)
                )
                for side, row in enumerate((PAD - 1, PAD + cols)):
                    buf[d, row : row + 1, at] = jnp.where(
                        on_rim(lane_one), rim[row : row + 1], turned[side][p][d : d + 1]
                    )
            for e in range(3):
                ctsh[(d + 1) // 2, (d + 1) % 2, :, 256 * e : 256 * (e + 1)] = buf[
                    d, PAD - 1 + e : PAD - 1 + e + cols
                ].astype(BF16)
    none = jnp.zeros((cols, 128), F32)
    for p in range(pairs):
        for j in range(-1, half + 1):
            block = [
                vbuf[p, d, PAD : PAD + cols] if 0 <= d < disp and 0 <= j + half * o else none
                for o, d in enumerate((j, j + half))
            ]
            if j == half:
                block[1] = none
            x = jnp.concatenate(block, axis=0).astype(BF16)
            vt[p, :, 128 * (j + 1) : 128 * (j + 2)] = x.T
    size = disp * cols
    left = jnp.concatenate(
        [
            jnp.concatenate([vt[p, :, 128 * (2 - a) : 128 * (2 - a) + size] for p in range(pairs)], axis=1)
            for a in range(3)
        ],
        axis=0,
    )
    right = jnp.concatenate(
        [
            jnp.concatenate(
                [
                    ctsh[(d + 1) // 2, (d + 1) % 2, :, 256 * e + 128 * p : 256 * e + 128 * (p + 1)]
                    for e in range(3)
                ],
                axis=1,
            )
            for p in range(pairs)
            for j in range(half)
            for d in (j, j + half)
        ],
        axis=0,
    )
    full = dot(left, right)
    keep = lanes((groups, 128)) < 3 * feat
    sums[...] = jnp.zeros(sums.shape, F32)
    for a in range(3):
        for e in range(3):
            block = full[128 * a : 128 * (a + 1), 128 * e : 128 * (e + 1)]
            out = block[0:groups] + pltpu.roll(block[SLOT : SLOT + groups], 128 - feat, 1)
            at = 128 * a + groups * e
            sums[at : at + groups] = jnp.where(keep, out, 0.0)
    half = sums.shape[0] // 2
    is_even = parity() == 0
    low, high = sums[0:half], sums[half:]
    keep_out[...] = jnp.where(is_even, low, high)
    give_out[...] = jnp.where(is_even, high, low)


def dgrad_kernel(ctsh, w2, gv):
    rows, disp, cols, _ = gv.shape
    step = disp // 4
    low = lanes((step * cols, 128)) < SLOT

    def conv(q, _):
        for p in range(rows // 2):
            slabs = [
                ctsh[pl.ds(q * step + s // 2, step), s % 2, :, 256 * e + 128 * p : 256 * e + 128 * (p + 1)]
                for s in range(4)
                for e in range(3)
            ]
            slabs = [x.reshape(step * cols, 128) for x in slabs]
            acc = dot(jnp.concatenate(slabs, axis=1), w2[...]).astype(BF16).astype(F32)
            for o in range(2):
                x = acc[:, 128 * o : 128 * (o + 1)]
                r = pltpu.roll(x, SLOT, 1)
                for hh in range(2):
                    y = jnp.where(low, r, x) if hh else jnp.where(low, x, r)
                    for j in range(step):
                        gv[2 * p + hh, 2 * (q * step + j) + o] = y[j * cols : (j + 1) * cols]
        return 0

    lax.fori_loop(0, 2, conv, 0)


def right_kernel(gv, fl, rg0, rg1, rg2, acce, acco, both):
    disp = gv.shape[1]
    rows, cols, channels = rg0.shape
    wide = fl.shape[2]
    group_size = wide // SLOT
    count = cols // 8
    back = acce.shape[1] - cols
    lead = back // 8

    lots = wide // 128

    def right_row(h, _):
        here = [
            [fl[h, PAD + 8 * b : PAD + 8 * b + 8, 128 * j : 128 * (j + 1)] for j in range(lots)]
            for b in range(count)
        ]
        for odd, buf in enumerate((acce, acco)):
            for k in range(lead + count):
                accs = [None] * lots
                for t in range(disp // 2):
                    b = k + t - lead
                    if b < 0 or b >= count:
                        continue
                    g = gv[h, 2 * t + odd, 8 * b : 8 * b + 8]
                    for j in range(lots):
                        term = g * here[b][j]
                        accs[j] = term if accs[j] is None else accs[j] + term
                for j in range(lots):
                    x = jnp.zeros((8, 128), F32) if accs[j] is None else accs[j]
                    buf[h, 8 * k : 8 * k + 8, 128 * j : 128 * (j + 1)] = x
        acco[h, 8 * (lead + count) :] = jnp.zeros((8, wide), F32)
        return 0

    lax.fori_loop(0, rows, right_row, 0)
    size = back + cols
    for h in range(rows):
        both[h * size : (h + 1) * size] = (acce[h] + acco[h, STEP : STEP + size]).astype(BF16)
    whole = dot(both[...], channel_table(channels, group_size, True)).astype(BF16)
    half = cols // 2
    for h in range(rows):
        at = h * size + back
        rg2[h] = whole[at - cols - half : at - cols]
        rg1[h] = whole[at - cols : at]
        rg0[h] = whole[at : at + cols]


def left_kernel(gv, fr, fr4, lg, accl):
    rows, cols, channels = lg.shape
    disp, wide = gv.shape[1], fr.shape[2]
    group_size = wide // SLOT
    reach = fr.shape[1] - cols - PAD
    count, times, lots = cols // 8, disp // 2, wide // 128

    def left_row(h, _):
        accs = [[None] * lots for _ in range(count)]
        for odd, band in enumerate((fr, fr4)):
            for r in range(1 - times, count):
                at = reach + 8 * r
                here = [band[h, at : at + 8, 128 * j : 128 * (j + 1)] for j in range(lots)]
                for t in range(max(0, -r), min(times, count - r)):
                    g = gv[h, 2 * t + odd, 8 * (r + t) : 8 * (r + t) + 8]
                    for j in range(lots):
                        term, acc = g * here[j], accs[r + t][j]
                        accs[r + t][j] = term if acc is None else acc + term
        for b in range(count):
            for j in range(lots):
                accl[h, 8 * b : 8 * b + 8, 128 * j : 128 * (j + 1)] = accs[b][j] * (1.0 / group_size)
        return 0

    lax.fori_loop(0, rows, left_row, 0)
    whole = accl[...].reshape(rows * cols, wide).astype(BF16)
    out = dot(whole, channel_table(channels, group_size, True)).astype(BF16)
    lg[...] = out.reshape(rows, cols, channels)


def combine_kernel(got, rg2, out):
    cols = out.shape[1]
    half = cols // 2
    part = jnp.where(parity() == 0, 0.0, got[...].astype(F32))
    out[:, 0:half] = part[:, 0:half].astype(BF16)
    out[:, half:] = (part[:, half:] + rg2[...].astype(F32)).astype(BF16)


def halo_lanes(groups):
    first = SLOT - groups
    assert groups - first <= first
    return (groups, SLOT, groups), (SLOT + groups, SLOT + 2 * groups - first, SLOT + groups - first)


def place_halo(base, row, groups, offset, lane):
    for start, end, shift in halo_lanes(groups):
        moved = pltpu.roll(row, (shift - offset) % 128, 1)
        base = jnp.where((lane >= start) & (lane < end), moved, base)
    return base


def spread_kernel(masks, groups, vbuf, top, bot, taps, buf):
    cols = taps.shape[2]
    disp, total = buf.shape[1], buf.shape[2]
    lane = lanes((total, 128))
    zeros = jnp.zeros((cols, taps.shape[3]), BF16)
    taps[0, 0] = zeros
    taps[disp // 2, 1] = zeros
    halos_of = [(ref, mask) for ref, mask in zip((top, bot), masks())]
    for dd in range(disp // 2):
        for p, (ref, mask) in enumerate(halos_of):
            row = ref[dd * total : (dd + 1) * total].astype(F32) * mask
            for o in range(2):
                d = 2 * dd + o
                buf[p, d] = place_halo(vbuf[p, d], row, groups, SLOT * o, lane)
                for e in range(3):
                    at = 256 * e + 128 * p
                    taps[(d + 1) // 2, (d + 1) % 2, :, at : at + 128] = buf[
                        p, d, PAD - 1 + e : PAD - 1 + e + cols
                    ].astype(BF16)


def conv_kernel(taps, wc, out):
    disp, rows, feat, cols = out.shape
    step = 6

    def conv(q, _):
        slabs = [
            taps[pl.ds(q * step + s // 2, step), s % 2].reshape(step * cols, taps.shape[3])
            for s in range(4)
        ]
        acc = dot(jnp.concatenate(slabs, axis=1), wc[...])
        for j in range(step):
            both = acc[j * cols : (j + 1) * cols].T.astype(BF16)
            for o in range(2):
                block = both[rows * feat * o : rows * feat * (o + 1)]
                out[2 * (q * step + j) + o] = block.reshape(rows, feat, cols)
        return 0

    lax.fori_loop(0, disp // 2 // step, conv, 0)


def finish_kernel(scale, mine, other, own, near, far, weight, right):
    _, _, _, feat, groups = weight.shape
    is_even = parity() == 0
    x, y = mine[...] * scale, other[...] * scale
    total = jnp.concatenate([jnp.where(is_even, x, y), jnp.where(is_even, y, x)], axis=0)
    for a in range(3):
        for e in range(3):
            at = 128 * a + groups * e
            block = total[at : at + groups].T
            for b in range(3):
                weight[2 - a, 2 - b, 2 - e] = block[feat * b : feat * (b + 1)]
    beside = jnp.where(is_even, near[...].astype(F32), 0.0)
    right[...] = (own[...].astype(F32) + beside + far[...].astype(F32)).astype(BF16)


def copy_kernel(*refs):
    half = len(refs) // 2
    for src, dst in zip(refs[:half], refs[half:]):
        dst[...] = src[...]


def sum_kernel(*refs):
    *parts, out = refs
    out[...] = tree([ref[...].astype(F32) for ref in parts]).astype(out.dtype)


def tree(terms):
    while len(terms) > 1:
        terms = [terms[i] + terms[i + 1] for i in range(0, len(terms), 2)]
    return terms[0]


def taps_kernel(taps, w2, wc, turned):
    _, _, _, feat, groups = taps.shape
    rows = wc.shape[1] // 2 // feat
    lane_of = lanes((feat, 2 * SLOT))
    low = lanes((feat, 2 * SLOT)) < SLOT
    zero = jnp.zeros((feat, 2 * SLOT), F32)

    def wide(a, b, e):
        if not 0 <= b <= 2:
            return None
        return jnp.concatenate([taps[a, b, e].astype(F32), zero[:, groups:]], axis=1)

    def beside(x, y):
        if x is None and y is None:
            return zero
        x = zero if x is None else x
        y = zero if y is None else pltpu.roll(y, SLOT, 1)
        return jnp.where(low, x, y)

    def build(a, _):
        def at_row(h):
            return pl.multiple_of((a * rows + h) * feat, feat)

        for e in range(3):
            for h in range(rows):
                for p in range(rows // 2):
                    lane = SLOT * (rows * e + 2 * p)
                    block = beside(wide(a, 2 * p - h + 1, e), wide(a, 2 * p + 1 - h + 1, e))
                    if h == 0 and p == 0:
                        block = place_halo(block, wide(a, 0, e), groups, 0, lane_of)
                    if h == rows - 1 and p == rows // 2 - 1:
                        block = place_halo(block, wide(a, 2, e), groups, 0, lane_of)
                    turned[pl.ds(at_row(h), feat), lane : lane + 2 * SLOT] = block
        return 0

    lax.fori_loop(0, 3, build, 0)
    for s in range(4):
        for e in range(3):
            for r in range(4):
                for o in range(2):
                    taps_of = [None if not 0 <= s - o <= 2 else wide(2 - s + o, 2 - r + i, 2 - e) for i in range(2)]
                    at = 384 * s + 128 * e + feat * r
                    w2[at : at + feat, 128 * o : 128 * (o + 1)] = beside(*taps_of).astype(BF16)
    depth, size = turned.shape[1], rows * feat
    for a in range(3):
        for i in range(depth // 128):
            x = turned[size * a : size * (a + 1), 128 * i : 128 * (i + 1)].T.astype(BF16)
            for o in range(2):
                at = depth * (a + o) + 128 * i
                wc[at : at + 128, size * o : size * (o + 1)] = x
    for o in range(2):
        at = depth * 3 * (1 - o)
        wc[at : at + depth, size * o : size * (o + 1)] = jnp.zeros((depth, size), BF16)


TOKEN = ((8, 128), F32)


def with_token(kernel, inputs, outputs):
    def run(*refs):
        kernel(*refs[: inputs + outputs], *refs[inputs + outputs + 1 :])
        refs[inputs + outputs][...] = jnp.zeros(TOKEN[0], F32)

    return run


def call(kernel, outs, scratch, *args, after=(), token=False, us=0.0):
    skip = len(after)
    if token:
        kernel = with_token(kernel, len(args), len(outs))
        outs = [*outs, TOKEN]
    return pl.pallas_call(
        lambda *refs: kernel(*refs[skip:]),
        out_shape=[jax.ShapeDtypeStruct(s, t) for s, t in outs],
        in_specs=[pl.BlockSpec(memory_space=pl.ANY)] * skip + [VMEM] * len(args),
        out_specs=[VMEM] * len(outs),
        scratch_shapes=scratch,
        compiler_params=pltpu.CompilerParams(vmem_limit_bytes=LIMIT),
        cost_estimate=pl.CostEstimate(
            flops=int(us * 1.15e9), bytes_accessed=int(us * 3.7e6), transcendentals=0
        ),
    )(*after, *args)


def col_shift(block, distance):
    n = lax.axis_size("col")
    route = [(i - distance, i) for i in range(n) if 0 <= i - distance < n]
    return lax.ppermute(block, "col", route)


def row_shift(block, distance):
    n = lax.axis_size("row")
    route = [(i - distance, i) for i in range(n) if 0 <= i - distance < n]
    return lax.ppermute(block, "row", route)


def halos(pays):
    if lax.axis_size("row") == 2:
        got = lax.ppermute(pays[0], "row", [(0, 1), (1, 0)])
        return got, got
    return row_shift(pays[0], 1), row_shift(pays[1], -1)


def hops(n_row, n_col):
    col_bits = [1 << i for i in range(1, n_col.bit_length() - 1)]
    row_bits = [n_col << i for i in range(n_row.bit_length() - 1)]
    assert n_col == 2 << len(col_bits) and n_row == 1 << len(row_bits)
    return col_bits[::-1] + row_bits


def on_device(left_features, right_features, conv_weight, cotangent):
    rows, cols, channels = left_features.shape
    disp, feat = cotangent.shape[0], cotangent.shape[3]
    groups = conv_weight.shape[3]
    group_size = channels // groups
    wide = group_size * SLOT
    n_row, n_col = lax.axis_size("row"), lax.axis_size("col")
    per = 128 // feat

    if n_row == 2:
        ends = [lambda: (rows - 1) * (1 - lax.axis_index("row"))]
    else:
        ends = [lambda: rows - 1, lambda: 0]
    n = len(ends)

    def masks():
        at = lax.axis_index("row")
        return (
            jnp.where(at > 0, 1.0, 0.0).astype(F32),
            jnp.where(at < n_row - 1, 1.0, 0.0).astype(F32),
        )

    total = cols + 2 * PAD
    count = disp + 2 * rows
    ct = cotangent.transpose(0, 1, 3, 2)

    def swap(block, mask):
        route = [(i, i ^ mask) for i in range(n_row * n_col)]
        return lax.ppermute(block, ("row", "col"), route)

    far = col_shift(right_features, 2)
    by_even, by_odd, ctl, *rims = call(
        functools.partial(pack_kernel, ends),
        [
            ((count, channels), BF16),
            ((count, channels), BF16),
            ((disp, cols, rows * feat), BF16),
        ]
        + [((disp // per, total, 128), F32)] * n,
        [pltpu.VMEM((disp * cols, rows * feat), F32)],
        jnp.concatenate([x[:, at] for at in (cols - 1, 0) for x in (left_features, right_features)]),
        ct,
        us=0.4,
    )
    inner = range(1, n_col - 1, 2)
    by_even = swap(by_even, 1)
    by_odd = lax.ppermute(by_odd, "col", [(i, i + 1) for i in inner] + [(i + 1, i) for i in inner])
    (passed,) = call(
        pass_kernel, [((rows, cols, channels), BF16)], [], right_features, far, after=[ctl]
    )
    near = swap(passed, 1)
    w2, wc = call(
        taps_kernel,
        [((12 * 128, 2 * 128), BF16), ((4 * 3 * rows * SLOT, 2 * rows * feat), BF16)],
        [pltpu.VMEM((3 * rows * feat, 3 * rows * SLOT), F32)],
        conv_weight.transpose(0, 1, 2, 4, 3),
        after=[passed],
    )
    row_pays = call(
        functools.partial(row_kernel, ends, rows),
        [((disp // per, total, 128), BF16)] * n,
        [pltpu.VMEM((2, disp, 128), F32), pltpu.VMEM((disp // per, total, 128), F32)],
        by_even,
        by_odd,
        *rims,
        after=[w2],
        us=5.0,
    )
    top, bot = halos(row_pays)

    band = 104 + cols + PAD
    spread_rows = 3 * rows * cols + rows * cols // 2 + 2 * count
    vbuf, fl, fr, fr4, *volume_rows = call(
        functools.partial(volume_kernel, ends, group_size),
        [
            ((rows // 2, disp, total, 2 * SLOT), F32),
            ((rows, total, wide), F32),
            ((rows, band, wide), F32),
            ((rows, band, wide), F32),
        ]
        + [((disp // 2 * total, 128), BF16)] * n,
        [
            pltpu.VMEM((spread_rows, channels), BF16),
            pltpu.VMEM((spread_rows, wide), F32),
        ],
        left_features,
        right_features,
        near,
        far,
        by_even,
        by_odd,
        us=2.3,
    )
    vtop, vbot = halos(volume_rows)
    keep, give, ctsh = call(
        functools.partial(weight_kernel, masks, groups, feat),
        [((3 * 64, 128), F32), ((3 * 64, 128), F32), ((disp // 2 + 1, 2, cols, 3 * 256), BF16)],
        [
            pltpu.VMEM((rows // 2, 128, (disp // 2 + 2) * 128), BF16),
            pltpu.VMEM((disp, total, 256), F32),
            pltpu.VMEM((3 * 128, 128), F32),
        ],
        vbuf, ctl, by_even, by_odd, top, bot,
        us=2.6,
    )
    got = swap(give, 1)
    def join(part, mask, kind, after=(), us=0.0):
        terms = (part, swap(part, mask))
        return call(sum_kernel, [(part.shape, kind)], [], *terms, after=after, us=us)[0]

    (gv,) = call(dgrad_kernel, [((rows, disp, cols, 128), F32)], [], ctsh, w2, us=2.0)
    (part,) = call(sum_kernel, [(keep.shape, BF16)], [], keep, got, after=[gv], us=4.0)
    first, *others, last = hops(n_row, n_col)
    rg0, rg1, rg2 = call(
        right_kernel,
        [
            ((rows, cols, channels), BF16),
            ((rows, cols, channels), BF16),
            ((rows, cols // 2, channels), BF16),
        ],
        [
            pltpu.VMEM((rows, cols + cols + cols // 2, wide), F32),
            pltpu.VMEM((rows, cols + cols + cols // 2 + 8, wide), F32),
            pltpu.VMEM((rows * (cols + cols + cols // 2), wide), BF16),
        ],
        gv, fl,
        after=[part],
        us=1.0,
    )
    rg1 = swap(rg1, 1)
    part = join(part, first, F32, after=[rg0], us=4.0)
    lg, left_done = call(
        left_kernel,
        [((rows, cols, channels), BF16)],
        [pltpu.VMEM((rows, cols, wide), F32)],
        gv, fr, fr4,
        after=[part],
        token=True,
        us=1.9,
    )
    part = join(part, others[0], BF16, after=[left_done], us=4.0)
    (spread,) = call(
        functools.partial(spread_kernel, masks, groups),
        [((disp // 2 + 1, 2, cols, 3 * rows * SLOT), BF16)],
        [pltpu.VMEM((rows // 2, disp, total, 128), F32)],
        vbuf, vtop, vbot,
        after=[part],
        us=1.3,
    )
    order = [spread]
    for mask in others[1:]:
        part = join(part, mask, BF16, after=order, us=4.0)
        order = []
    (rg2,) = call(
        combine_kernel, [((rows, cols, channels), BF16)], [], rg1, rg2, after=[part]
    )
    part = join(part, last, F32, after=[rg2], us=4.0)
    output, conv_done = call(
        conv_kernel,
        [((disp, rows, feat, cols), BF16)],
        [],
        spread, wc,
        after=[part],
        token=True,
        us=2.6,
    )
    rg2 = col_shift(rg2, -2)
    cells = disp * rows * n_row * cols * n_col
    weight_grad, right_grad = call(
        functools.partial(finish_kernel, 1.0 / math.sqrt(cells)),
        [((3, 3, 3, feat, groups), F32), ((rows, cols, channels), BF16)],
        [],
        part, swap(part, 1), rg0, rg1, rg2,
        after=[conv_done],
        us=1.0,
    )
    return (
        output.transpose(0, 1, 3, 2),
        weight_grad.transpose(0, 1, 2, 4, 3),
        lg,
        right_grad,
    )


def solution(mesh):
    in_specs = (P("row", "col", None), P("row", "col", None), P(), P(None, "row", "col", None))
    out_specs = (P(None, "row", "col", None), P(), P("row", "col", None), P("row", "col", None))
    return jax.shard_map(
        on_device, mesh=mesh, in_specs=in_specs, out_specs=out_specs, check_vma=False
    )
```

```python
import functools
import math

import jax
import jax.numpy as jnp
from jax import lax
from jax.experimental import pallas as pl
from jax.experimental.pallas import tpu as pltpu
from jax.sharding import PartitionSpec as P

DISP = 24
STEP = 4
SLOT = 64
PAD = 8
F32 = jnp.float32
BF16 = jnp.bfloat16
VMEM = pl.BlockSpec(memory_space=pltpu.VMEM)
LIMIT = 16 * 1024 * 1024


def lanes(shape):
    return lax.broadcasted_iota(jnp.int32, shape, len(shape) - 1)


def channel_table(channels, group_size, flip, value=1.0):
    shape = (group_size * SLOT, channels) if flip else (channels, group_size * SLOT)
    c = lax.broadcasted_iota(jnp.int32, shape, 1 if flip else 0)
    j = lax.broadcasted_iota(jnp.int32, shape, 0 if flip else 1)
    hit = c == (j & (SLOT - 1)) * group_size + (j >> (SLOT.bit_length() - 1))
    return jnp.where(hit, value, 0.0).astype(BF16)


def parity():
    return lax.rem(lax.axis_index("col"), 2)


def dot(a, b):
    return jnp.dot(a, b, preferred_element_type=F32)


def dot_nt(a, b):
    return lax.dot_general(a, b, (((1,), (1,)), ((), ())), preferred_element_type=F32)


def pack_kernel(ends, rims_in, ct, even, odd, ctl, *rest):
    rims, ctf = rest[:-1], rest[-1]
    disp, rows, feat, cols = ct.shape
    per = 128 // feat
    for d in range(disp):
        block = ct[d].reshape(rows * feat, cols).astype(F32).T
        ctf[d * cols : (d + 1) * cols] = block
        ctl[d] = block.astype(BF16)
    columns = []
    for i, col in enumerate((cols - 1, 0)):
        block = ctf[pl.ds(col, disp, stride=cols), :]
        block = jnp.concatenate([block, jnp.zeros((disp, even.shape[1] - rows * feat), F32)], axis=1)
        edge = rims_in[i * 2 * rows : (i + 1) * 2 * rows].astype(F32)
        columns.append(jnp.concatenate([block, edge], axis=0))
    is_even = parity() == 0
    even[...] = jnp.where(is_even, columns[0], columns[1]).astype(BF16)
    odd[...] = jnp.where(is_even, columns[1], columns[0]).astype(BF16)
    for end, rim in zip(ends, rims):
        h = end()
        for q in range(disp // per):
            rim[q, PAD : PAD + cols] = jnp.concatenate(
                [ct[q * per + i, h].astype(F32) for i in range(per)], axis=0
            ).T


def pass_kernel(own, got, out):
    out[...] = jnp.where(parity() == 0, own[...].astype(F32), got[...].astype(F32)).astype(BF16)


def end_columns(by_even, by_odd):
    x, y = by_even[...].astype(F32), by_odd[...].astype(F32)
    is_even = parity() == 0
    return jnp.where(is_even, y, x), jnp.where(is_even, x, y)


def row_kernel(ends, rows, by_even, by_odd, *rest):
    n = len(ends)
    rims, pays, (edges, buf) = rest[:n], rest[n : 2 * n], rest[2 * n :]
    count, total, _ = buf.shape
    disp = edges.shape[1]
    per, cols = disp // count, total - 2 * PAD
    feat = 128 // per
    lane = lanes((count, 128))
    for side, x in enumerate(end_columns(by_even, by_odd)):
        edges[side] = x[0:disp, 0:128]
    for end, rim, pay in zip(ends, rims, pays):
        h = end()
        buf[...] = rim[...]
        for side, at in ((0, PAD - 1), (1, PAD + cols)):
            out = jnp.zeros((count, 128), F32)
            for i in range(per):
                x = edges[side, pl.ds(i, count, stride=per)]
                first = pltpu.roll(x, feat * i, 1) if i else x
                last = pltpu.roll(x, (feat * (i - rows + 1)) % 128, 1) if i != rows - 1 else x
                x = jnp.where(h == 0, first, last)
                out = jnp.where((lane >= feat * i) & (lane < feat * (i + 1)), x, out)
            for q in range(count):
                buf[q, at : at + 1] = out[q : q + 1]
        pay[...] = buf[...].astype(BF16)


def put_band(refs, h, column, block):
    fr, fr4, cols = refs
    at = fr.shape[1] - cols - PAD + column
    fr[h, at : at + block.shape[0]] = block
    fr4[h, at + STEP : at + STEP + block.shape[0]] = block


def own_kernel(group_size, left, right, far, fl, fr, fr4, mixed, wide_buf):
    rows, cols, channels = left.shape
    base, half, wide = rows * cols, cols // 2, group_size * SLOT
    mixed[0:base] = right[...].reshape(base, channels)
    mixed[base : 2 * base] = left[...].reshape(base, channels)
    mixed[2 * base :] = far[:, half:].reshape(base // 2, channels)
    wide_buf[...] = dot(mixed[...], channel_table(channels, group_size, False))
    tail = fr.shape[1]
    for h in range(rows):
        for ref in (fr, fr4):
            ref[h, 0:16] = jnp.zeros((16, wide), F32)
            ref[h, tail - 16 :] = jnp.zeros((16, wide), F32)
        put_band((fr, fr4, cols), h, -cols - half, wide_buf[2 * base + h * half : 2 * base + (h + 1) * half])
        put_band((fr, fr4, cols), h, 0, wide_buf[h * cols : (h + 1) * cols])
        fl[h, 0:PAD] = jnp.zeros((PAD, wide), F32)
        fl[h, PAD + cols :] = jnp.zeros((PAD, wide), F32)
        fl[h, PAD : PAD + cols] = wide_buf[base + h * cols : base + (h + 1) * cols] * (1.0 / group_size)


def volume_kernel(ends, group_size, near, by_even, by_odd, _fl, _fr, _fr4, fl, fr, fr4, vbuf, *rest):
    pays, (mixed, wide_buf) = rest[: len(ends)], rest[len(ends) :]
    rows, cols, channels = near.shape
    disp = vbuf.shape[1]
    reach = fr.shape[1] - cols - PAD
    wide = group_size * SLOT
    base = rows * cols
    mixed[0:base] = near[...].reshape(base, channels)
    count = disp + 2 * rows
    for i, x in enumerate(end_columns(by_even, by_odd)):
        mixed[base + i * count : base + (i + 1) * count] = x.astype(BF16)
    wide_buf[...] = dot(mixed[...], channel_table(channels, group_size, False))
    for h in range(rows):
        put_band((fr, fr4, cols), h, -cols, wide_buf[h * cols : (h + 1) * cols])
        at = base + disp + h
        fl[h, PAD - 1 : PAD] = wide_buf[at : at + 1] * (1.0 / group_size)
        at += count
        fl[h, PAD + cols : PAD + cols + 1] = wide_buf[at : at + 1] * (1.0 / group_size)
        put_band((fr, fr4, cols), h, cols, wide_buf[at + rows : at + rows + 1])
    total = cols + 2 * PAD
    low = lanes((8, 128)) < SLOT
    pairs, times, lots = rows // 2, disp // 2, wide // 128
    count = total // 16

    def products(i, _):
        p, at = lax.rem(i, pairs), pl.multiple_of(lax.div(i, pairs) * (8 * count), 8)
        lefts = [
            [
                [fl[2 * p + o, pl.ds(at + 8 * b, 8), 128 * j : 128 * (j + 1)] for j in range(lots)]
                for b in range(count)
            ]
            for o in range(2)
        ]
        for odd, band in enumerate((fr, fr4)):
            for r in range(1 - times, count):
                start = pl.multiple_of(at + reach - PAD + 8 * r, 8)
                here = [
                    [band[2 * p + o, pl.ds(start, 8), 128 * j : 128 * (j + 1)] for j in range(lots)]
                    for o in range(2)
                ]
                for t in range(max(0, -r), min(times, count - r)):
                    sums = []
                    for o in range(2):
                        acc = lefts[o][r + t][0] * here[o][0]
                        for j in range(1, lots):
                            acc = acc + lefts[o][r + t][j] * here[o][j]
                        sums.append(acc + pltpu.roll(acc, SLOT, 1))
                    vbuf[p, 2 * t + odd, pl.ds(at + 8 * (r + t), 8)] = jnp.where(low, *sums)
        return 0

    lax.fori_loop(0, 2 * pairs, products, 0)
    big = lanes((total, 128)) < SLOT

    for dd in range(disp // 2):
        for end, pay in zip(ends, pays):
            h = end()
            if isinstance(h, int):
                halves = [vbuf[h // 2, 2 * dd + o] for o in range(2)]
                if h % 2 == 0:
                    halves[1] = pltpu.roll(halves[1], SLOT, 1)
                else:
                    halves[0] = pltpu.roll(halves[0], SLOT, 1)
                out = jnp.where(big, halves[0], halves[1])
            else:
                last = pairs - 1
                first = jnp.where(big, vbuf[0, 2 * dd], pltpu.roll(vbuf[0, 2 * dd + 1], SLOT, 1))
                final = jnp.where(
                    big, pltpu.roll(vbuf[last, 2 * dd], SLOT, 1), vbuf[last, 2 * dd + 1]
                )
                out = jnp.where(h == 0, first, final)
            pay[dd * total : (dd + 1) * total] = out.astype(BF16)


def weight_kernel(
    masks, groups, feat, vbuf, ctl, by_even, by_odd, top, bot, keep_out, give_out, ctsh, vt, buf, sums
):
    disp, cols, width = ctl.shape
    pairs, per, half = vbuf.shape[0], 128 // feat, disp // 2
    mtop, mbot = masks()
    ctsh[0, 0] = jnp.zeros(ctsh.shape[2:], BF16)
    ctsh[half, 1] = jnp.zeros(ctsh.shape[2:], BF16)
    lane, lane_in, lane_one = lanes(top.shape[1:]), lanes((cols, 128)), lanes((1, 128))
    shifts = (feat, 128 - feat)
    edges = [x[0:disp, 0:128] for x in end_columns(by_even, by_odd)]
    turned = [[pltpu.roll(x, shift, 1) for shift in shifts] for x in edges]
    for q in range(disp // per):
        t = top[q].astype(F32) * mtop
        z = bot[q].astype(F32) * mbot
        for i in range(per):
            d = q * per + i
            rims = (
                t if i == 0 else pltpu.roll(t, 128 - feat * i, 1),
                z if i == per - 1 else pltpu.roll(z, feat * (per - 1 - i), 1),
            )
            inner = ctl[d].astype(F32)
            for p, (rim, shift) in enumerate(zip(rims, shifts)):

                def on_rim(x):
                    return x < feat if p == 0 else x >= 128 - feat

                at = slice(128 * p, 128 * (p + 1))
                buf[d, PAD : PAD + cols, at] = jnp.where(
                    on_rim(lane_in), rim[PAD : PAD + cols], pltpu.roll(inner, shift, 1)
                )
                for side, row in enumerate((PAD - 1, PAD + cols)):
                    buf[d, row : row + 1, at] = jnp.where(
                        on_rim(lane_one), rim[row : row + 1], turned[side][p][d : d + 1]
                    )
            for e in range(3):
                ctsh[(d + 1) // 2, (d + 1) % 2, :, 256 * e : 256 * (e + 1)] = buf[
                    d, PAD - 1 + e : PAD - 1 + e + cols
                ].astype(BF16)
    none = jnp.zeros((cols, 128), F32)
    for p in range(pairs):
        for j in range(-1, half + 1):
            block = [
                vbuf[p, d, PAD : PAD + cols] if 0 <= d < disp and 0 <= j + half * o else none
                for o, d in enumerate((j, j + half))
            ]
            if j == half:
                block[1] = none
            x = jnp.concatenate(block, axis=0).astype(BF16)
            vt[p, :, 128 * (j + 1) : 128 * (j + 2)] = x.T
    size = disp * cols
    left = jnp.concatenate(
        [
            jnp.concatenate([vt[p, :, 128 * (2 - a) : 128 * (2 - a) + size] for p in range(pairs)], axis=1)
            for a in range(3)
        ],
        axis=0,
    )
    right = jnp.concatenate(
        [
            jnp.concatenate(
                [
                    ctsh[(d + 1) // 2, (d + 1) % 2, :, 256 * e + 128 * p : 256 * e + 128 * (p + 1)]
                    for e in range(3)
                ],
                axis=1,
            )
            for p in range(pairs)
            for j in range(half)
            for d in (j, j + half)
        ],
        axis=0,
    )
    full = dot(left, right)
    keep = lanes((groups, 128)) < 3 * feat
    sums[...] = jnp.zeros(sums.shape, F32)
    for a in range(3):
        for e in range(3):
            block = full[128 * a : 128 * (a + 1), 128 * e : 128 * (e + 1)]
            out = block[0:groups] + pltpu.roll(block[SLOT : SLOT + groups], 128 - feat, 1)
            at = 128 * a + groups * e
            sums[at : at + groups] = jnp.where(keep, out, 0.0)
    half = sums.shape[0] // 2
    is_even = parity() == 0
    low, high = sums[0:half], sums[half:]
    keep_out[...] = jnp.where(is_even, low, high)
    give_out[...] = jnp.where(is_even, high, low)


def dgrad_kernel(p, ctsh, w2, gv):
    _, disp, cols, _ = gv.shape
    step = disp // 4
    low = lanes((step * cols, 128)) < SLOT

    def conv(q, _):
        slabs = [
            ctsh[pl.ds(q * step + s // 2, step), s % 2, :, 256 * e + 128 * p : 256 * e + 128 * (p + 1)]
            for s in range(4)
            for e in range(3)
        ]
        slabs = [x.reshape(step * cols, 128) for x in slabs]
        acc = dot(jnp.concatenate(slabs, axis=1), w2[...]).astype(BF16).astype(F32)
        for o in range(2):
            x = acc[:, 128 * o : 128 * (o + 1)]
            r = pltpu.roll(x, SLOT, 1)
            for hh in range(2):
                y = jnp.where(low, r, x) if hh else jnp.where(low, x, r)
                for j in range(step):
                    gv[hh, 2 * (q * step + j) + o] = y[j * cols : (j + 1) * cols]
        return 0

    lax.fori_loop(0, 2, conv, 0)


def right_kernel(fl, *rest):
    *grads, rg0, rg1, rg2, acce, acco, both = rest
    disp = grads[0].shape[1]
    rows, cols, channels = rg0.shape
    wide = fl.shape[2]
    group_size = wide // SLOT
    count = cols // 8
    back = acce.shape[1] - cols
    lead = back // 8

    lots = wide // 128

    def right_row(gv, p, hh):
        h = 2 * p + hh
        here = [
            [fl[h, PAD + 8 * b : PAD + 8 * b + 8, 128 * j : 128 * (j + 1)] for j in range(lots)]
            for b in range(count)
        ]
        for odd, buf in enumerate((acce, acco)):
            for k in range(lead + count):
                accs = [None] * lots
                for t in range(disp // 2):
                    b = k + t - lead
                    if b < 0 or b >= count:
                        continue
                    g = gv[hh, 2 * t + odd, 8 * b : 8 * b + 8]
                    for j in range(lots):
                        term = g * here[b][j]
                        accs[j] = term if accs[j] is None else accs[j] + term
                for j in range(lots):
                    x = jnp.zeros((8, 128), F32) if accs[j] is None else accs[j]
                    buf[h, 8 * k : 8 * k + 8, 128 * j : 128 * (j + 1)] = x
        acco[h, 8 * (lead + count) :] = jnp.zeros((8, wide), F32)

    for p, gv in enumerate(grads):
        pl.loop(0, 2)(functools.partial(right_row, gv, p))
    size = back + cols
    for h in range(rows):
        both[h * size : (h + 1) * size] = (acce[h] + acco[h, STEP : STEP + size]).astype(BF16)
    whole = dot(both[...], channel_table(channels, group_size, True)).astype(BF16)
    half = cols // 2
    for h in range(rows):
        at = h * size + back
        rg2[h] = whole[at - cols - half : at - cols]
        rg1[h] = whole[at - cols : at]
        rg0[h] = whole[at : at + cols]


def left_kernel(fr, fr4, *rest):
    *grads, lg, accl = rest
    rows, cols, channels = lg.shape
    disp, wide = grads[0].shape[1], fr.shape[2]
    group_size = wide // SLOT
    reach = fr.shape[1] - cols - PAD
    count, times, lots = cols // 8, disp // 2, wide // 128

    def left_row(gv, p, hh):
        h = 2 * p + hh
        accs = [[None] * lots for _ in range(count)]
        for odd, band in enumerate((fr, fr4)):
            for r in range(1 - times, count):
                at = reach + 8 * r
                here = [band[h, at : at + 8, 128 * j : 128 * (j + 1)] for j in range(lots)]
                for t in range(max(0, -r), min(times, count - r)):
                    g = gv[hh, 2 * t + odd, 8 * (r + t) : 8 * (r + t) + 8]
                    for j in range(lots):
                        term, acc = g * here[j], accs[r + t][j]
                        accs[r + t][j] = term if acc is None else acc + term
        for b in range(count):
            for j in range(lots):
                accl[h, 8 * b : 8 * b + 8, 128 * j : 128 * (j + 1)] = accs[b][j] * (1.0 / group_size)

    for p, gv in enumerate(grads):
        pl.loop(0, 2)(functools.partial(left_row, gv, p))
    whole = accl[...].reshape(rows * cols, wide).astype(BF16)
    out = dot(whole, channel_table(channels, group_size, True)).astype(BF16)
    lg[...] = out.reshape(rows, cols, channels)


def combine_kernel(got, rg2, out):
    cols = out.shape[1]
    half = cols // 2
    part = jnp.where(parity() == 0, 0.0, got[...].astype(F32))
    out[:, 0:half] = part[:, 0:half].astype(BF16)
    out[:, half:] = (part[:, half:] + rg2[...].astype(F32)).astype(BF16)


def halo_lanes(groups):
    first = SLOT - groups
    assert groups - first <= first
    return (groups, SLOT, groups), (SLOT + groups, SLOT + 2 * groups - first, SLOT + groups - first)


def place_halo(base, row, groups, offset, lane):
    for start, end, shift in halo_lanes(groups):
        moved = pltpu.roll(row, (shift - offset) % 128, 1)
        base = jnp.where((lane >= start) & (lane < end), moved, base)
    return base


def spread_kernel(masks, groups, vbuf, top, bot, taps, buf):
    cols = taps.shape[2]
    disp, total = buf.shape[1], buf.shape[2]
    lane = lanes((total, 128))
    zeros = jnp.zeros((cols, taps.shape[3]), BF16)
    taps[0, 0] = zeros
    taps[disp // 2, 1] = zeros
    halos_of = [(ref, mask) for ref, mask in zip((top, bot), masks())]
    for dd in range(disp // 2):
        for p, (ref, mask) in enumerate(halos_of):
            row = ref[dd * total : (dd + 1) * total].astype(F32) * mask
            for o in range(2):
                d = 2 * dd + o
                buf[p, d] = place_halo(vbuf[p, d], row, groups, SLOT * o, lane)
                for e in range(3):
                    at = 256 * e + 128 * p
                    taps[(d + 1) // 2, (d + 1) % 2, :, at : at + 128] = buf[
                        p, d, PAD - 1 + e : PAD - 1 + e + cols
                    ].astype(BF16)


def conv_kernel(taps, wc, out):
    disp, rows, feat, cols = out.shape
    step = 6

    def conv(q, _):
        slabs = [
            taps[pl.ds(q * step + s // 2, step), s % 2].reshape(step * cols, taps.shape[3])
            for s in range(4)
        ]
        acc = dot(jnp.concatenate(slabs, axis=1), wc[...])
        for j in range(step):
            both = acc[j * cols : (j + 1) * cols].T.astype(BF16)
            for o in range(2):
                block = both[rows * feat * o : rows * feat * (o + 1)]
                out[2 * (q * step + j) + o] = block.reshape(rows, feat, cols)
        return 0

    lax.fori_loop(0, disp // 2 // step, conv, 0)


def finish_kernel(scale, mine, other, own, near, far, weight, right):
    _, _, _, feat, groups = weight.shape
    is_even = parity() == 0
    x, y = mine[...] * scale, other[...] * scale
    total = jnp.concatenate([jnp.where(is_even, x, y), jnp.where(is_even, y, x)], axis=0)
    for a in range(3):
        for e in range(3):
            at = 128 * a + groups * e
            block = total[at : at + groups].T
            for b in range(3):
                weight[2 - a, 2 - b, 2 - e] = block[feat * b : feat * (b + 1)]
    beside = jnp.where(is_even, near[...].astype(F32), 0.0)
    right[...] = (own[...].astype(F32) + beside + far[...].astype(F32)).astype(BF16)


def copy_kernel(*refs):
    half = len(refs) // 2
    for src, dst in zip(refs[:half], refs[half:]):
        dst[...] = src[...]


def sum_kernel(*refs):
    *parts, out = refs
    out[...] = tree([ref[...].astype(F32) for ref in parts]).astype(out.dtype)


def tree(terms):
    while len(terms) > 1:
        terms = [terms[i] + terms[i + 1] for i in range(0, len(terms), 2)]
    return terms[0]


def taps_kernel(taps, w2, wc, turned):
    _, _, _, feat, groups = taps.shape
    rows = wc.shape[1] // 2 // feat
    lane_of = lanes((feat, 2 * SLOT))
    low = lanes((feat, 2 * SLOT)) < SLOT
    zero = jnp.zeros((feat, 2 * SLOT), F32)

    def wide(a, b, e):
        if not 0 <= b <= 2:
            return None
        return jnp.concatenate([taps[a, b, e].astype(F32), zero[:, groups:]], axis=1)

    def beside(x, y):
        if x is None and y is None:
            return zero
        x = zero if x is None else x
        y = zero if y is None else pltpu.roll(y, SLOT, 1)
        return jnp.where(low, x, y)

    def build(a, _):
        def at_row(h):
            return pl.multiple_of((a * rows + h) * feat, feat)

        for e in range(3):
            for h in range(rows):
                for p in range(rows // 2):
                    lane = SLOT * (rows * e + 2 * p)
                    block = beside(wide(a, 2 * p - h + 1, e), wide(a, 2 * p + 1 - h + 1, e))
                    if h == 0 and p == 0:
                        block = place_halo(block, wide(a, 0, e), groups, 0, lane_of)
                    if h == rows - 1 and p == rows // 2 - 1:
                        block = place_halo(block, wide(a, 2, e), groups, 0, lane_of)
                    turned[pl.ds(at_row(h), feat), lane : lane + 2 * SLOT] = block
        return 0

    lax.fori_loop(0, 3, build, 0)
    for s in range(4):
        for e in range(3):
            for r in range(4):
                for o in range(2):
                    taps_of = [None if not 0 <= s - o <= 2 else wide(2 - s + o, 2 - r + i, 2 - e) for i in range(2)]
                    at = 384 * s + 128 * e + feat * r
                    w2[at : at + feat, 128 * o : 128 * (o + 1)] = beside(*taps_of).astype(BF16)
    depth, size = turned.shape[1], rows * feat
    for a in range(3):
        for i in range(depth // 128):
            x = turned[size * a : size * (a + 1), 128 * i : 128 * (i + 1)].T.astype(BF16)
            for o in range(2):
                at = depth * (a + o) + 128 * i
                wc[at : at + 128, size * o : size * (o + 1)] = x
    for o in range(2):
        at = depth * 3 * (1 - o)
        wc[at : at + depth, size * o : size * (o + 1)] = jnp.zeros((depth, size), BF16)


TOKEN = ((8, 128), F32)


def with_token(kernel, inputs, outputs):
    def run(*refs):
        kernel(*refs[: inputs + outputs], *refs[inputs + outputs + 1 :])
        refs[inputs + outputs][...] = jnp.zeros(TOKEN[0], F32)

    return run


def call(kernel, outs, scratch, *args, after=(), token=False, us=0.0, alias=()):
    skip = len(after)
    if token:
        kernel = with_token(kernel, len(args), len(outs))
        outs = [*outs, TOKEN]
    return pl.pallas_call(
        lambda *refs: kernel(*refs[skip:]),
        out_shape=[jax.ShapeDtypeStruct(s, t) for s, t in outs],
        in_specs=[pl.BlockSpec(memory_space=pl.ANY)] * skip + [VMEM] * len(args),
        out_specs=[VMEM] * len(outs),
        scratch_shapes=scratch,
        input_output_aliases={skip + i: o for i, o in alias},
        compiler_params=pltpu.CompilerParams(vmem_limit_bytes=LIMIT),
        cost_estimate=pl.CostEstimate(
            flops=int(us * 1.15e9), bytes_accessed=int(us * 3.7e6), transcendentals=0
        ),
    )(*after, *args)


def col_shift(block, distance):
    n = lax.axis_size("col")
    route = [(i - distance, i) for i in range(n) if 0 <= i - distance < n]
    return lax.ppermute(block, "col", route)


def row_shift(block, distance):
    n = lax.axis_size("row")
    route = [(i - distance, i) for i in range(n) if 0 <= i - distance < n]
    return lax.ppermute(block, "row", route)


def halos(pays):
    if lax.axis_size("row") == 2:
        got = lax.ppermute(pays[0], "row", [(0, 1), (1, 0)])
        return got, got
    return row_shift(pays[0], 1), row_shift(pays[1], -1)


def stages(n_row, n_col):
    col_bits = [1 << i for i in range(1, n_col.bit_length() - 1)]
    row_bits = [n_col << i for i in range(n_row.bit_length() - 1)]
    assert n_col == 2 << len(col_bits) and n_row == 1 << len(row_bits)
    bits = col_bits + row_bits
    pairs = [bits[i : i + 2] for i in range(0, len(bits), 2)]
    return [pair + [sum(pair)] if len(pair) == 2 else pair for pair in pairs]


def on_device(left_features, right_features, conv_weight, cotangent):
    rows, cols, channels = left_features.shape
    disp, feat = cotangent.shape[0], cotangent.shape[3]
    groups = conv_weight.shape[3]
    group_size = channels // groups
    wide = group_size * SLOT
    n_row, n_col = lax.axis_size("row"), lax.axis_size("col")
    per = 128 // feat

    if n_row == 2:
        ends = [lambda: (rows - 1) * (1 - lax.axis_index("row"))]
    else:
        ends = [lambda: rows - 1, lambda: 0]
    n = len(ends)

    def masks():
        at = lax.axis_index("row")
        return (
            jnp.where(at > 0, 1.0, 0.0).astype(F32),
            jnp.where(at < n_row - 1, 1.0, 0.0).astype(F32),
        )

    total = cols + 2 * PAD
    count = disp + 2 * rows
    ct = cotangent.transpose(0, 1, 3, 2)

    def swap(block, mask):
        route = [(i, i ^ mask) for i in range(n_row * n_col)]
        return lax.ppermute(block, ("row", "col"), route)

    far = col_shift(right_features, 2)
    by_even, by_odd, ctl, *rims = call(
        functools.partial(pack_kernel, ends),
        [
            ((count, channels), BF16),
            ((count, channels), BF16),
            ((disp, cols, rows * feat), BF16),
        ]
        + [((disp // per, total, 128), F32)] * n,
        [pltpu.VMEM((disp * cols, rows * feat), F32)],
        jnp.concatenate([x[:, at] for at in (cols - 1, 0) for x in (left_features, right_features)]),
        ct,
        us=0.4,
    )
    inner = range(1, n_col - 1, 2)
    by_even = swap(by_even, 1)
    by_odd = lax.ppermute(by_odd, "col", [(i, i + 1) for i in inner] + [(i + 1, i) for i in inner])
    (passed,) = call(
        pass_kernel, [((rows, cols, channels), BF16)], [], right_features, far, after=[ctl]
    )
    near = swap(passed, 1)
    w2, wc = call(
        taps_kernel,
        [((12 * 128, 2 * 128), BF16), ((4 * 3 * rows * SLOT, 2 * rows * feat), BF16)],
        [pltpu.VMEM((3 * rows * feat, 3 * rows * SLOT), F32)],
        conv_weight.transpose(0, 1, 2, 4, 3),
        after=[passed],
    )
    band = 104 + cols + PAD
    banks = [((rows, total, wide), F32), ((rows, band, wide), F32), ((rows, band, wide), F32)]
    spread_rows = 2 * rows * cols + rows * cols // 2
    fl, fr, fr4 = call(
        functools.partial(own_kernel, group_size),
        banks,
        [pltpu.VMEM((spread_rows, channels), BF16), pltpu.VMEM((spread_rows, wide), F32)],
        left_features,
        right_features,
        far,
        after=[w2],
    )
    row_pays = call(
        functools.partial(row_kernel, ends, rows),
        [((disp // per, total, 128), BF16)] * n,
        [pltpu.VMEM((2, disp, 128), F32), pltpu.VMEM((disp // per, total, 128), F32)],
        by_even,
        by_odd,
        *rims,
        after=[fl],
        us=5.0,
    )
    top, bot = halos(row_pays)
    spread_rows = rows * cols + 2 * count
    fl, fr, fr4, vbuf, *volume_rows = call(
        functools.partial(volume_kernel, ends, group_size),
        banks
        + [((rows // 2, disp, total, 2 * SLOT), F32)]
        + [((disp // 2 * total, 128), BF16)] * n,
        [pltpu.VMEM((spread_rows, channels), BF16), pltpu.VMEM((spread_rows, wide), F32)],
        near,
        by_even,
        by_odd,
        fl,
        fr,
        fr4,
        us=1.8,
        alias=[(3, 0), (4, 1), (5, 2)],
    )
    vtop, vbot = halos(volume_rows)
    keep, give, ctsh = call(
        functools.partial(weight_kernel, masks, groups, feat),
        [((3 * 64, 128), F32), ((3 * 64, 128), F32), ((disp // 2 + 1, 2, cols, 3 * 256), BF16)],
        [
            pltpu.VMEM((rows // 2, 128, (disp // 2 + 2) * 128), BF16),
            pltpu.VMEM((disp, total, 256), F32),
            pltpu.VMEM((3 * 128, 128), F32),
        ],
        vbuf, ctl, by_even, by_odd, top, bot,
        us=2.0,
    )

    def gradient(p, after):
        kernel = functools.partial(dgrad_kernel, p)
        us = 0.2 if after else 0.9
        return call(kernel, [((2, disp, cols, 128), F32)], [], ctsh, w2, after=after, us=us)[0]

    got = swap(give, 1)
    grads = [gradient(0, [])]
    (part,) = call(sum_kernel, [(keep.shape, BF16)], [], keep, got, after=grads, us=4.0)
    grads += [gradient(p, [part]) for p in range(1, rows // 2)]
    rg0, rg1, rg2 = call(
        right_kernel,
        [
            ((rows, cols, channels), BF16),
            ((rows, cols, channels), BF16),
            ((rows, cols // 2, channels), BF16),
        ],
        [
            pltpu.VMEM((rows, cols + cols + cols // 2, wide), F32),
            pltpu.VMEM((rows, cols + cols + cols // 2 + 8, wide), F32),
            pltpu.VMEM((rows * (cols + cols + cols // 2), wide), BF16),
        ],
        fl, *grads,
        after=[part, vtop],
        us=0.2,
    )
    rg1 = swap(rg1, 1)
    *middle, final = stages(n_row, n_col)
    order = [rg0]
    for stage in middle:
        parts = [part] + [swap(part, m) for m in stage]
        (part,) = call(sum_kernel, [(part.shape, BF16)], [], *parts, after=order, us=4.0)
        order = []
    parts = [part] + [swap(part, m) for m in final]
    (rg2,) = call(
        combine_kernel, [((rows, cols, channels), BF16)], [], rg1, rg2, after=[part]
    )
    lg, left_done = call(
        left_kernel,
        [((rows, cols, channels), BF16)],
        [pltpu.VMEM((rows, cols, wide), F32)],
        fr, fr4, *grads,
        after=[rg2],
        token=True,
        us=1.9,
    )
    (part,) = call(sum_kernel, [(part.shape, F32)], [], *parts, after=[left_done])
    (spread,) = call(
        functools.partial(spread_kernel, masks, groups),
        [((disp // 2 + 1, 2, cols, 3 * rows * SLOT), BF16)],
        [pltpu.VMEM((rows // 2, disp, total, 128), F32)],
        vbuf, vtop, vbot,
        after=[part],
        us=1.3,
    )
    output, conv_done = call(
        conv_kernel,
        [((disp, rows, feat, cols), BF16)],
        [],
        spread, wc,
        after=[part],
        token=True,
        us=2.6,
    )
    rg2 = col_shift(rg2, -2)
    cells = disp * rows * n_row * cols * n_col
    weight_grad, right_grad = call(
        functools.partial(finish_kernel, 1.0 / math.sqrt(cells)),
        [((3, 3, 3, feat, groups), F32), ((rows, cols, channels), BF16)],
        [],
        part, swap(part, 1), rg0, rg1, rg2,
        after=[conv_done],
        us=1.0,
    )
    return (
        output.transpose(0, 1, 3, 2),
        weight_grad.transpose(0, 1, 2, 4, 3),
        lg,
        right_grad,
    )


def solution(mesh):
    in_specs = (P("row", "col", None), P("row", "col", None), P(), P(None, "row", "col", None))
    out_specs = (P(None, "row", "col", None), P(), P("row", "col", None), P("row", "col", None))
    return jax.shard_map(
        on_device, mesh=mesh, in_specs=in_specs, out_specs=out_specs, check_vma=False
    )
```

```python
import functools
import math

import jax
import jax.numpy as jnp
from jax import lax
from jax.experimental import pallas as pl
from jax.experimental.pallas import tpu as pltpu
from jax.sharding import PartitionSpec as P

DISP = 24
STEP = 4
SLOT = 64
PAD = 8
F32 = jnp.float32
BF16 = jnp.bfloat16
VMEM = pl.BlockSpec(memory_space=pltpu.VMEM)
LIMIT = 16 * 1024 * 1024


def lanes(shape):
    return lax.broadcasted_iota(jnp.int32, shape, len(shape) - 1)


def channel_table(channels, group_size, flip, value=1.0):
    shape = (group_size * SLOT, channels) if flip else (channels, group_size * SLOT)
    c = lax.broadcasted_iota(jnp.int32, shape, 1 if flip else 0)
    j = lax.broadcasted_iota(jnp.int32, shape, 0 if flip else 1)
    hit = c == (j & (SLOT - 1)) * group_size + (j >> (SLOT.bit_length() - 1))
    return jnp.where(hit, value, 0.0).astype(BF16)


def parity():
    return lax.rem(lax.axis_index("col"), 2)


def dot(a, b):
    return jnp.dot(a, b, preferred_element_type=F32)


def dot_nt(a, b):
    return lax.dot_general(a, b, (((1,), (1,)), ((), ())), preferred_element_type=F32)


def pack_kernel(ends, rims_in, ct, even, odd, ctl, *rest):
    rims, ctf = rest[:-1], rest[-1]
    disp, rows, feat, cols = ct.shape
    per = 128 // feat
    for d in range(disp):
        block = ct[d].reshape(rows * feat, cols).astype(F32).T
        ctf[d * cols : (d + 1) * cols] = block
        ctl[d] = block.astype(BF16)
    columns = []
    for i, col in enumerate((cols - 1, 0)):
        block = ctf[pl.ds(col, disp, stride=cols), :]
        block = jnp.concatenate([block, jnp.zeros((disp, even.shape[1] - rows * feat), F32)], axis=1)
        edge = [rims_in[h, 2 * i + x : 2 * i + x + 1].astype(F32) for x in range(2) for h in range(rows)]
        columns.append(jnp.concatenate([block, *edge], axis=0))
    is_even = parity() == 0
    even[...] = jnp.where(is_even, columns[0], columns[1]).astype(BF16)
    odd[...] = jnp.where(is_even, columns[1], columns[0]).astype(BF16)
    for end, rim in zip(ends, rims):
        h = end()
        for q in range(disp // per):
            block = [ct[q * per + i, h].astype(F32) for i in range(per)]
            rim[q] = jnp.concatenate(block, axis=0).T.astype(BF16)


def pass_kernel(own, got, out):
    out[...] = jnp.where(parity() == 0, own[...].astype(F32), got[...].astype(F32)).astype(BF16)


def end_columns(by_even, by_odd):
    x, y = by_even[...].astype(F32), by_odd[...].astype(F32)
    is_even = parity() == 0
    return jnp.where(is_even, y, x), jnp.where(is_even, x, y)


def corner_kernel(ends, rows, disp, by_even, by_odd, *rest):
    pays, (edges, buf) = rest[: len(ends)], rest[len(ends) :]
    feat = 128 // rows
    per = 128 // feat
    count = disp // per
    lane = lanes((count, 128))
    for side, x in enumerate(end_columns(by_even, by_odd)):
        edges[side] = x[0:disp, 0:128]
    for end, pay in zip(ends, pays):
        h = end()
        buf[...] = jnp.zeros(buf.shape, F32)
        for side in range(2):
            out = jnp.zeros((count, 128), F32)
            for i in range(per):
                x = edges[side, pl.ds(i, count, stride=per)]
                first = pltpu.roll(x, feat * i, 1) if i else x
                last = pltpu.roll(x, (feat * (i - rows + 1)) % 128, 1) if i != rows - 1 else x
                x = jnp.where(h == 0, first, last)
                out = jnp.where((lane >= feat * i) & (lane < feat * (i + 1)), x, out)
            buf[8 * side : 8 * side + count] = out
        pay[...] = buf[...].astype(BF16)


def put_band(refs, h, column, block):
    fr, fr4, cols = refs
    at = fr.shape[1] - cols - PAD + column
    fr[h, at : at + block.shape[0]] = block
    fr4[h, at + STEP : at + STEP + block.shape[0]] = block


def own_kernel(group_size, left, right, far, fl, fr, fr4, mixed, wide_buf):
    rows, cols, channels = left.shape
    base, half, wide = rows * cols, cols // 2, group_size * SLOT
    mixed[0:base] = right[...].reshape(base, channels)
    mixed[base : 2 * base] = left[...].reshape(base, channels)
    mixed[2 * base :] = far[:, half:].reshape(base // 2, channels)
    wide_buf[...] = dot(mixed[...], channel_table(channels, group_size, False))
    tail = fr.shape[1]
    for h in range(rows):
        for ref in (fr, fr4):
            ref[h, 0:16] = jnp.zeros((16, wide), F32)
            ref[h, tail - 16 :] = jnp.zeros((16, wide), F32)
        put_band((fr, fr4, cols), h, -cols - half, wide_buf[2 * base + h * half : 2 * base + (h + 1) * half])
        put_band((fr, fr4, cols), h, 0, wide_buf[h * cols : (h + 1) * cols])
        fl[h, 0:PAD] = jnp.zeros((PAD, wide), F32)
        fl[h, PAD + cols :] = jnp.zeros((PAD, wide), F32)
        fl[h, PAD : PAD + cols] = wide_buf[base + h * cols : base + (h + 1) * cols] * (1.0 / group_size)


def volume_kernel(ends, group_size, near, by_even, by_odd, _fl, _fr, _fr4, fl, fr, fr4, vbuf, *rest):
    pays, (mixed, wide_buf) = rest[: len(ends)], rest[len(ends) :]
    rows, cols, channels = near.shape
    disp = vbuf.shape[1]
    reach = fr.shape[1] - cols - PAD
    wide = group_size * SLOT
    base = rows * cols
    mixed[0:base] = near[...].reshape(base, channels)
    count = disp + 2 * rows
    for i, x in enumerate(end_columns(by_even, by_odd)):
        mixed[base + i * count : base + (i + 1) * count] = x.astype(BF16)
    wide_buf[...] = dot(mixed[...], channel_table(channels, group_size, False))
    for h in range(rows):
        put_band((fr, fr4, cols), h, -cols, wide_buf[h * cols : (h + 1) * cols])
        at = base + disp + h
        fl[h, PAD - 1 : PAD] = wide_buf[at : at + 1] * (1.0 / group_size)
        at += count
        fl[h, PAD + cols : PAD + cols + 1] = wide_buf[at : at + 1] * (1.0 / group_size)
        put_band((fr, fr4, cols), h, cols, wide_buf[at + rows : at + rows + 1])
    total = cols + 2 * PAD
    low = lanes((8, 128)) < SLOT
    pairs, times, lots = rows // 2, disp // 2, wide // 128
    count = total // 16

    def products(i, _):
        p, at = lax.rem(i, pairs), pl.multiple_of(lax.div(i, pairs) * (8 * count), 8)
        lefts = [
            [
                [fl[2 * p + o, pl.ds(at + 8 * b, 8), 128 * j : 128 * (j + 1)] for j in range(lots)]
                for b in range(count)
            ]
            for o in range(2)
        ]
        for odd, band in enumerate((fr, fr4)):
            for r in range(1 - times, count):
                start = pl.multiple_of(at + reach - PAD + 8 * r, 8)
                here = [
                    [band[2 * p + o, pl.ds(start, 8), 128 * j : 128 * (j + 1)] for j in range(lots)]
                    for o in range(2)
                ]
                for t in range(max(0, -r), min(times, count - r)):
                    sums = []
                    for o in range(2):
                        acc = lefts[o][r + t][0] * here[o][0]
                        for j in range(1, lots):
                            acc = acc + lefts[o][r + t][j] * here[o][j]
                        sums.append(acc + pltpu.roll(acc, SLOT, 1))
                    vbuf[p, 2 * t + odd, pl.ds(at + 8 * (r + t), 8)] = jnp.where(low, *sums)
        return 0

    lax.fori_loop(0, 2 * pairs, products, 0)
    big = lanes((total, 128)) < SLOT

    for dd in range(disp // 2):
        for end, pay in zip(ends, pays):
            h = end()
            if isinstance(h, int):
                halves = [vbuf[h // 2, 2 * dd + o] for o in range(2)]
                if h % 2 == 0:
                    halves[1] = pltpu.roll(halves[1], SLOT, 1)
                else:
                    halves[0] = pltpu.roll(halves[0], SLOT, 1)
                out = jnp.where(big, halves[0], halves[1])
            else:
                last = pairs - 1
                first = jnp.where(big, vbuf[0, 2 * dd], pltpu.roll(vbuf[0, 2 * dd + 1], SLOT, 1))
                final = jnp.where(
                    big, pltpu.roll(vbuf[last, 2 * dd], SLOT, 1), vbuf[last, 2 * dd + 1]
                )
                out = jnp.where(h == 0, first, final)
            pay[dd * total : (dd + 1) * total] = out.astype(BF16)


def weight_kernel(
    masks, groups, feat, vbuf, ctl, by_even, by_odd, top, bot, tops, bots, *rest
):
    keep_out, give_out, ctsh, vt, buf, sums = rest
    disp, cols, width = ctl.shape
    pairs, per, half = vbuf.shape[0], 128 // feat, disp // 2
    mtop, mbot = masks()
    ctsh[0, 0] = jnp.zeros(ctsh.shape[2:], BF16)
    ctsh[half, 1] = jnp.zeros(ctsh.shape[2:], BF16)
    lane_in, lane_one = lanes((cols, 128)), lanes((1, 128))
    shifts = (feat, 128 - feat)
    edges = [x[0:disp, 0:128] for x in end_columns(by_even, by_odd)]
    turned = [[pltpu.roll(x, shift, 1) for shift in shifts] for x in edges]

    def aligned(t, z, i):
        return (
            t if i == 0 else pltpu.roll(t, 128 - feat * i, 1),
            z if i == per - 1 else pltpu.roll(z, feat * (per - 1 - i), 1),
        )

    corners = [aligned(tops[...].astype(F32) * mtop, bots[...].astype(F32) * mbot, i) for i in range(per)]
    for q in range(disp // per):
        t = top[q].astype(F32) * mtop
        z = bot[q].astype(F32) * mbot
        for i in range(per):
            d = q * per + i
            rims = aligned(t, z, i)
            inner = ctl[d].astype(F32)
            for p, (rim, shift) in enumerate(zip(rims, shifts)):

                def on_rim(x):
                    return x < feat if p == 0 else x >= 128 - feat

                at = slice(128 * p, 128 * (p + 1))
                buf[d, PAD : PAD + cols, at] = jnp.where(
                    on_rim(lane_in), rim, pltpu.roll(inner, shift, 1)
                )
                for side, row in enumerate((PAD - 1, PAD + cols)):
                    corner = corners[i][p][8 * side + q : 8 * side + q + 1]
                    buf[d, row : row + 1, at] = jnp.where(
                        on_rim(lane_one), corner, turned[side][p][d : d + 1]
                    )
            for e in range(3):
                ctsh[(d + 1) // 2, (d + 1) % 2, :, 256 * e : 256 * (e + 1)] = buf[
                    d, PAD - 1 + e : PAD - 1 + e + cols
                ].astype(BF16)
    none = jnp.zeros((cols, 128), F32)
    for p in range(pairs):
        for j in range(-1, half + 1):
            block = [
                vbuf[p, d, PAD : PAD + cols] if 0 <= d < disp and 0 <= j + half * o else none
                for o, d in enumerate((j, j + half))
            ]
            if j == half:
                block[1] = none
            x = jnp.concatenate(block, axis=0).astype(BF16)
            vt[p, :, 128 * (j + 1) : 128 * (j + 2)] = x.T
    size = disp * cols
    left = jnp.concatenate(
        [
            jnp.concatenate([vt[p, :, 128 * (2 - a) : 128 * (2 - a) + size] for p in range(pairs)], axis=1)
            for a in range(3)
        ],
        axis=0,
    )
    right = jnp.concatenate(
        [
            jnp.concatenate(
                [
                    ctsh[(d + 1) // 2, (d + 1) % 2, :, 256 * e + 128 * p : 256 * e + 128 * (p + 1)]
                    for e in range(3)
                ],
                axis=1,
            )
            for p in range(pairs)
            for j in range(half)
            for d in (j, j + half)
        ],
        axis=0,
    )
    full = dot(left, right)
    keep = lanes((groups, 128)) < 3 * feat
    sums[...] = jnp.zeros(sums.shape, F32)
    for a in range(3):
        for e in range(3):
            block = full[128 * a : 128 * (a + 1), 128 * e : 128 * (e + 1)]
            out = block[0:groups] + pltpu.roll(block[SLOT : SLOT + groups], 128 - feat, 1)
            at = 128 * a + groups * e
            sums[at : at + groups] = jnp.where(keep, out, 0.0)
    half = sums.shape[0] // 2
    is_even = parity() == 0
    low, high = sums[0:half], sums[half:]
    keep_out[...] = jnp.where(is_even, low, high)
    give_out[...] = jnp.where(is_even, high, low)


def dgrad_kernel(ctsh, w2, *grads):
    _, disp, cols, _ = grads[0].shape
    step = disp // 4
    low = lanes((step * cols, 128)) < SLOT

    def conv(q, p, gv):
        slabs = [
            ctsh[pl.ds(q * step + s // 2, step), s % 2, :, 256 * e + 128 * p : 256 * e + 128 * (p + 1)]
            for s in range(4)
            for e in range(3)
        ]
        slabs = [x.reshape(step * cols, 128) for x in slabs]
        acc = dot(jnp.concatenate(slabs, axis=1), w2[...]).astype(BF16).astype(F32)
        for o in range(2):
            x = acc[:, 128 * o : 128 * (o + 1)]
            r = pltpu.roll(x, SLOT, 1)
            for hh in range(2):
                y = jnp.where(low, r, x) if hh else jnp.where(low, x, r)
                for j in range(step):
                    gv[hh, 2 * (q * step + j) + o] = y[j * cols : (j + 1) * cols]

    @pl.loop(0, 2)
    def _(q):
        for p, gv in enumerate(grads):
            conv(q, p, gv)


def right_kernel(fl, *rest):
    *grads, rg0, rg1, rg2, acce, acco, both = rest
    disp = grads[0].shape[1]
    rows, cols, channels = rg0.shape
    wide = fl.shape[2]
    group_size = wide // SLOT
    count = cols // 8
    back = acce.shape[1] - cols
    lead = back // 8

    lots = wide // 128

    def right_row(gv, p, hh):
        h = 2 * p + hh
        here = [
            [fl[h, PAD + 8 * b : PAD + 8 * b + 8, 128 * j : 128 * (j + 1)] for j in range(lots)]
            for b in range(count)
        ]
        for odd, buf in enumerate((acce, acco)):
            for k in range(lead + count):
                accs = [None] * lots
                for t in range(disp // 2):
                    b = k + t - lead
                    if b < 0 or b >= count:
                        continue
                    g = gv[hh, 2 * t + odd, 8 * b : 8 * b + 8]
                    for j in range(lots):
                        term = g * here[b][j]
                        accs[j] = term if accs[j] is None else accs[j] + term
                for j in range(lots):
                    x = jnp.zeros((8, 128), F32) if accs[j] is None else accs[j]
                    buf[h, 8 * k : 8 * k + 8, 128 * j : 128 * (j + 1)] = x
        acco[h, 8 * (lead + count) :] = jnp.zeros((8, wide), F32)

    for p, gv in enumerate(grads):
        pl.loop(0, 2)(functools.partial(right_row, gv, p))
    size = back + cols
    for h in range(rows):
        both[h * size : (h + 1) * size] = (acce[h] + acco[h, STEP : STEP + size]).astype(BF16)
    whole = dot(both[...], channel_table(channels, group_size, True)).astype(BF16)
    half = cols // 2
    for h in range(rows):
        at = h * size + back
        rg2[h] = whole[at - cols - half : at - cols]
        rg1[h] = whole[at - cols : at]
        rg0[h] = whole[at : at + cols]


def left_kernel(fr, fr4, *rest):
    *grads, lg, accl = rest
    rows, cols, channels = lg.shape
    disp, wide = grads[0].shape[1], fr.shape[2]
    group_size = wide // SLOT
    reach = fr.shape[1] - cols - PAD
    count, times, lots = cols // 8, disp // 2, wide // 128

    def left_row(gv, p, hh):
        h = 2 * p + hh
        accs = [[None] * lots for _ in range(count)]
        for odd, band in enumerate((fr, fr4)):
            for r in range(1 - times, count):
                at = reach + 8 * r
                here = [band[h, at : at + 8, 128 * j : 128 * (j + 1)] for j in range(lots)]
                for t in range(max(0, -r), min(times, count - r)):
                    g = gv[hh, 2 * t + odd, 8 * (r + t) : 8 * (r + t) + 8]
                    for j in range(lots):
                        term, acc = g * here[j], accs[r + t][j]
                        accs[r + t][j] = term if acc is None else acc + term
        for b in range(count):
            for j in range(lots):
                accl[h, 8 * b : 8 * b + 8, 128 * j : 128 * (j + 1)] = accs[b][j] * (1.0 / group_size)

    for p, gv in enumerate(grads):
        pl.loop(0, 2)(functools.partial(left_row, gv, p))
    whole = accl[...].reshape(rows * cols, wide).astype(BF16)
    out = dot(whole, channel_table(channels, group_size, True)).astype(BF16)
    lg[...] = out.reshape(rows, cols, channels)


def combine_kernel(got, rg2, out):
    cols = out.shape[1]
    half = cols // 2
    part = jnp.where(parity() == 0, 0.0, got[...].astype(F32))
    out[:, 0:half] = part[:, 0:half].astype(BF16)
    out[:, half:] = (part[:, half:] + rg2[...].astype(F32)).astype(BF16)


def halo_lanes(groups):
    first = SLOT - groups
    assert groups - first <= first
    return (groups, SLOT, groups), (SLOT + groups, SLOT + 2 * groups - first, SLOT + groups - first)


def place_halo(base, row, groups, offset, lane):
    for start, end, shift in halo_lanes(groups):
        moved = pltpu.roll(row, (shift - offset) % 128, 1)
        base = jnp.where((lane >= start) & (lane < end), moved, base)
    return base


def spread_kernel(masks, groups, vbuf, top, bot, taps, buf):
    cols = taps.shape[2]
    disp, total = buf.shape[1], buf.shape[2]
    lane = lanes((total, 128))
    zeros = jnp.zeros((cols, taps.shape[3]), BF16)
    taps[0, 0] = zeros
    taps[disp // 2, 1] = zeros
    halos_of = [(ref, mask) for ref, mask in zip((top, bot), masks())]
    for dd in range(disp // 2):
        for p, (ref, mask) in enumerate(halos_of):
            row = ref[dd * total : (dd + 1) * total].astype(F32) * mask
            for o in range(2):
                d = 2 * dd + o
                buf[p, d] = place_halo(vbuf[p, d], row, groups, SLOT * o, lane)
                for e in range(3):
                    at = 256 * e + 128 * p
                    taps[(d + 1) // 2, (d + 1) % 2, :, at : at + 128] = buf[
                        p, d, PAD - 1 + e : PAD - 1 + e + cols
                    ].astype(BF16)


def conv_kernel(taps, wc, out, held, sems):
    disp, rows, feat, cols = out.shape
    parts = sems.shape[0]
    step = disp // 2 // parts
    copies = []
    for q in range(parts):
        slabs = [
            taps[q * step + s // 2 : q * step + s // 2 + step, s % 2].reshape(step * cols, taps.shape[3])
            for s in range(4)
        ]
        acc = dot(jnp.concatenate(slabs, axis=1), wc[...])
        for j in range(step):
            both = acc[j * cols : (j + 1) * cols].T.astype(BF16)
            for o in range(2):
                block = both[rows * feat * o : rows * feat * (o + 1)]
                held[2 * (q * step + j) + o] = block.reshape(rows, feat, cols)
        at = pl.ds(2 * q * step, 2 * step)
        copies.append(pltpu.make_async_copy(held.at[at], out.at[at], sems.at[q]))
        copies[-1].start()
    for copy in copies:
        copy.wait()


def finish_kernel(scale, mine, other, own, near, far, weight, right):
    _, _, _, feat, groups = weight.shape
    is_even = parity() == 0
    x, y = mine[...] * scale, other[...] * scale
    total = jnp.concatenate([jnp.where(is_even, x, y), jnp.where(is_even, y, x)], axis=0)
    for a in range(3):
        for e in range(3):
            at = 128 * a + groups * e
            block = total[at : at + groups].T
            for b in range(3):
                weight[2 - a, 2 - b, 2 - e] = block[feat * b : feat * (b + 1)]
    beside = jnp.where(is_even, near[...].astype(F32), 0.0)
    right[...] = (own[...].astype(F32) + beside + far[...].astype(F32)).astype(BF16)


def copy_kernel(*refs):
    half = len(refs) // 2
    for src, dst in zip(refs[:half], refs[half:]):
        dst[...] = src[...]


def sum_kernel(*refs):
    *parts, out = refs
    out[...] = tree([ref[...].astype(F32) for ref in parts]).astype(out.dtype)


def tree(terms):
    while len(terms) > 1:
        terms = [terms[i] + terms[i + 1] for i in range(0, len(terms), 2)]
    return terms[0]


def taps_kernel(taps, w2, wc, turned):
    _, _, _, feat, groups = taps.shape
    rows = wc.shape[1] // 2 // feat
    lane_of = lanes((feat, 2 * SLOT))
    low = lanes((feat, 2 * SLOT)) < SLOT
    zero = jnp.zeros((feat, 2 * SLOT), F32)

    def wide(a, b, e):
        if not 0 <= b <= 2:
            return None
        return jnp.concatenate([taps[a, b, e].astype(F32), zero[:, groups:]], axis=1)

    def beside(x, y):
        if x is None and y is None:
            return zero
        x = zero if x is None else x
        y = zero if y is None else pltpu.roll(y, SLOT, 1)
        return jnp.where(low, x, y)

    def build(a, _):
        def at_row(h):
            return pl.multiple_of((a * rows + h) * feat, feat)

        for e in range(3):
            for h in range(rows):
                for p in range(rows // 2):
                    lane = SLOT * (rows * e + 2 * p)
                    block = beside(wide(a, 2 * p - h + 1, e), wide(a, 2 * p + 1 - h + 1, e))
                    if h == 0 and p == 0:
                        block = place_halo(block, wide(a, 0, e), groups, 0, lane_of)
                    if h == rows - 1 and p == rows // 2 - 1:
                        block = place_halo(block, wide(a, 2, e), groups, 0, lane_of)
                    turned[pl.ds(at_row(h), feat), lane : lane + 2 * SLOT] = block
        return 0

    lax.fori_loop(0, 3, build, 0)
    for s in range(4):
        for e in range(3):
            for r in range(4):
                for o in range(2):
                    taps_of = [None if not 0 <= s - o <= 2 else wide(2 - s + o, 2 - r + i, 2 - e) for i in range(2)]
                    at = 384 * s + 128 * e + feat * r
                    w2[at : at + feat, 128 * o : 128 * (o + 1)] = beside(*taps_of).astype(BF16)
    depth, size = turned.shape[1], rows * feat
    for a in range(3):
        for i in range(depth // 128):
            x = turned[size * a : size * (a + 1), 128 * i : 128 * (i + 1)].T.astype(BF16)
            for o in range(2):
                at = depth * (a + o) + 128 * i
                wc[at : at + 128, size * o : size * (o + 1)] = x
    for o in range(2):
        at = depth * 3 * (1 - o)
        wc[at : at + depth, size * o : size * (o + 1)] = jnp.zeros((depth, size), BF16)


TOKEN = ((8, 128), F32)


def with_token(kernel, inputs, outputs):
    def run(*refs):
        kernel(*refs[: inputs + outputs], *refs[inputs + outputs + 1 :])
        refs[inputs + outputs][...] = jnp.zeros(TOKEN[0], F32)

    return run


def call(kernel, outs, scratch, *args, after=(), token=False, us=0.0, alias=(), hbm=()):
    skip = len(after)
    if token:
        kernel = with_token(kernel, len(args), len(outs))
        outs = [*outs, TOKEN]
    return pl.pallas_call(
        lambda *refs: kernel(*refs[skip:]),
        out_shape=[jax.ShapeDtypeStruct(s, t) for s, t in outs],
        in_specs=[pl.BlockSpec(memory_space=pl.ANY)] * skip + [VMEM] * len(args),
        out_specs=[pl.BlockSpec(memory_space=pl.ANY) if i in hbm else VMEM for i in range(len(outs))],
        scratch_shapes=scratch,
        input_output_aliases={skip + i: o for i, o in alias},
        compiler_params=pltpu.CompilerParams(vmem_limit_bytes=LIMIT),
        cost_estimate=pl.CostEstimate(
            flops=int(us * 1.15e9), bytes_accessed=int(us * 3.7e6), transcendentals=0
        ),
    )(*after, *args)


def col_shift(block, distance):
    n = lax.axis_size("col")
    route = [(i - distance, i) for i in range(n) if 0 <= i - distance < n]
    return lax.ppermute(block, "col", route)


def row_shift(block, distance):
    n = lax.axis_size("row")
    route = [(i - distance, i) for i in range(n) if 0 <= i - distance < n]
    return lax.ppermute(block, "row", route)


def halos(pays):
    if lax.axis_size("row") == 2:
        got = lax.ppermute(pays[0], "row", [(0, 1), (1, 0)])
        return got, got
    return row_shift(pays[0], 1), row_shift(pays[1], -1)


def stages(n_row, n_col):
    col_bits = [1 << i for i in range(1, n_col.bit_length() - 1)]
    row_bits = [n_col << i for i in range(n_row.bit_length() - 1)]
    assert n_col == 2 << len(col_bits) and n_row == 1 << len(row_bits)
    bits = col_bits + row_bits
    pairs = [bits[i : i + 2] for i in range(0, len(bits), 2)]
    return [pair + [sum(pair)] if len(pair) == 2 else pair for pair in pairs]


def on_device(left_features, right_features, conv_weight, cotangent):
    rows, cols, channels = left_features.shape
    disp, feat = cotangent.shape[0], cotangent.shape[3]
    groups = conv_weight.shape[3]
    group_size = channels // groups
    wide = group_size * SLOT
    n_row, n_col = lax.axis_size("row"), lax.axis_size("col")
    per = 128 // feat

    if n_row == 2:
        ends = [lambda: (rows - 1) * (1 - lax.axis_index("row"))]
    else:
        ends = [lambda: rows - 1, lambda: 0]
    n = len(ends)

    def masks():
        at = lax.axis_index("row")
        return (
            jnp.where(at > 0, 1.0, 0.0).astype(F32),
            jnp.where(at < n_row - 1, 1.0, 0.0).astype(F32),
        )

    total = cols + 2 * PAD
    count = disp + 2 * rows
    ct = cotangent.transpose(0, 1, 3, 2)

    def swap(block, mask):
        route = [(i, i ^ mask) for i in range(n_row * n_col)]
        return lax.ppermute(block, ("row", "col"), route)

    far = col_shift(right_features, 2)
    by_even, by_odd, ctl, *rims = call(
        functools.partial(pack_kernel, ends),
        [
            ((count, channels), BF16),
            ((count, channels), BF16),
            ((disp, cols, rows * feat), BF16),
        ]
        + [((disp // per, cols, 128), BF16)] * n,
        [pltpu.VMEM((disp * cols, rows * feat), F32)],
        jnp.concatenate(
            [x[:, at : at + 1] for at in (cols - 1, 0) for x in (left_features, right_features)], axis=1
        ),
        ct,
        us=0.4,
    )
    inner = range(1, n_col - 1, 2)
    by_even = swap(by_even, 1)
    by_odd = lax.ppermute(by_odd, "col", [(i, i + 1) for i in inner] + [(i + 1, i) for i in inner])
    (passed,) = call(
        pass_kernel, [((rows, cols, channels), BF16)], [], right_features, far, after=[ctl]
    )
    near = swap(passed, 1)
    top, bot = halos(rims)
    w2, wc = call(
        taps_kernel,
        [((12 * 128, 2 * 128), BF16), ((4 * 3 * rows * SLOT, 2 * rows * feat), BF16)],
        [pltpu.VMEM((3 * rows * feat, 3 * rows * SLOT), F32)],
        conv_weight.transpose(0, 1, 2, 4, 3),
        after=[passed],
    )
    band = 104 + cols + PAD
    banks = [((rows, total, wide), F32), ((rows, band, wide), F32), ((rows, band, wide), F32)]
    spread_rows = 2 * rows * cols + rows * cols // 2
    fl, fr, fr4 = call(
        functools.partial(own_kernel, group_size),
        banks,
        [pltpu.VMEM((spread_rows, channels), BF16), pltpu.VMEM((spread_rows, wide), F32)],
        left_features,
        right_features,
        far,
        after=[w2],
    )
    corner_pays = call(
        functools.partial(corner_kernel, ends, rows, disp),
        [((16, 128), BF16)] * n,
        [pltpu.VMEM((2, disp, 128), F32), pltpu.VMEM((16, 128), F32)],
        by_even,
        by_odd,
        after=[fl],
        us=5.0,
    )
    tops, bots = halos(corner_pays)
    spread_rows = rows * cols + 2 * count
    fl, fr, fr4, vbuf, *volume_rows = call(
        functools.partial(volume_kernel, ends, group_size),
        banks
        + [((rows // 2, disp, total, 2 * SLOT), F32)]
        + [((disp // 2 * total, 128), BF16)] * n,
        [pltpu.VMEM((spread_rows, channels), BF16), pltpu.VMEM((spread_rows, wide), F32)],
        near,
        by_even,
        by_odd,
        fl,
        fr,
        fr4,
        us=1.8,
        alias=[(3, 0), (4, 1), (5, 2)],
    )
    vtop, vbot = halos(volume_rows)
    keep, give, ctsh = call(
        functools.partial(weight_kernel, masks, groups, feat),
        [((3 * 64, 128), F32), ((3 * 64, 128), F32), ((disp // 2 + 1, 2, cols, 3 * 256), BF16)],
        [
            pltpu.VMEM((rows // 2, 128, (disp // 2 + 2) * 128), BF16),
            pltpu.VMEM((disp, total, 256), F32),
            pltpu.VMEM((3 * 128, 128), F32),
        ],
        vbuf, ctl, by_even, by_odd, top, bot, tops, bots,
        us=2.0,
    )

    got = swap(give, 1)
    (part,) = call(sum_kernel, [(keep.shape, BF16)], [], keep, got)
    grads = call(
        dgrad_kernel, [((2, disp, cols, 128), F32)] * (rows // 2), [], ctsh, w2, after=[part], us=0.2
    )
    rg0, rg1, rg2 = call(
        right_kernel,
        [
            ((rows, cols, channels), BF16),
            ((rows, cols, channels), BF16),
            ((rows, cols // 2, channels), BF16),
        ],
        [
            pltpu.VMEM((rows, cols + cols + cols // 2, wide), F32),
            pltpu.VMEM((rows, cols + cols + cols // 2 + 8, wide), F32),
            pltpu.VMEM((rows * (cols + cols + cols // 2), wide), BF16),
        ],
        fl, *grads,
        us=0.2,
    )
    rg1 = swap(rg1, 1)
    *middle, final = stages(n_row, n_col)
    order = [rg0, vtop]
    for stage in middle:
        parts = [part] + [swap(part, m) for m in stage]
        (part,) = call(sum_kernel, [(part.shape, BF16)], [], *parts, after=order, us=4.0)
        order = []
    parts = [part] + [swap(part, m) for m in final]
    (rg2,) = call(
        combine_kernel, [((rows, cols, channels), BF16)], [], rg1, rg2, after=[part]
    )
    lg, left_done = call(
        left_kernel,
        [((rows, cols, channels), BF16)],
        [pltpu.VMEM((rows, cols, wide), F32)],
        fr, fr4, *grads,
        after=[rg2],
        token=True,
        us=1.9,
    )
    (part,) = call(sum_kernel, [(part.shape, F32)], [], *parts, after=[left_done])
    (spread,) = call(
        functools.partial(spread_kernel, masks, groups),
        [((disp // 2 + 1, 2, cols, 3 * rows * SLOT), BF16)],
        [pltpu.VMEM((rows // 2, disp, total, 128), F32)],
        vbuf, vtop, vbot,
        after=[part],
        us=1.3,
    )
    output, conv_done = call(
        conv_kernel,
        [((disp, rows, feat, cols), BF16)],
        [pltpu.VMEM((disp, rows, feat, cols), BF16), pltpu.SemaphoreType.DMA((2,))],
        spread, wc,
        after=[part],
        token=True,
        us=2.6,
        hbm=[0],
    )
    rg2 = col_shift(rg2, -2)
    cells = disp * rows * n_row * cols * n_col
    weight_grad, right_grad = call(
        functools.partial(finish_kernel, 1.0 / math.sqrt(cells)),
        [((3, 3, 3, feat, groups), F32), ((rows, cols, channels), BF16)],
        [],
        part, swap(part, 1), rg0, rg1, rg2,
        after=[conv_done],
        us=1.0,
    )
    return (
        output.transpose(0, 1, 3, 2),
        weight_grad.transpose(0, 1, 2, 4, 3),
        lg,
        right_grad,
    )


def solution(mesh):
    in_specs = (P("row", "col", None), P("row", "col", None), P(), P(None, "row", "col", None))
    out_specs = (P(None, "row", "col", None), P(), P("row", "col", None), P("row", "col", None))
    return jax.shard_map(
        on_device, mesh=mesh, in_specs=in_specs, out_specs=out_specs, check_vma=False
    )
```

```python
import functools
import math

import jax
import jax.numpy as jnp
from jax import lax
from jax.experimental import pallas as pl
from jax.experimental.pallas import tpu as pltpu
from jax.sharding import PartitionSpec as P

DISP = 24
STEP = 4
SLOT = 64
PAD = 8
F32 = jnp.float32
BF16 = jnp.bfloat16
VMEM = pl.BlockSpec(memory_space=pltpu.VMEM)
LIMIT = 16 * 1024 * 1024


def lanes(shape):
    return lax.broadcasted_iota(jnp.int32, shape, len(shape) - 1)


def channel_table(channels, group_size, flip, value=1.0):
    shape = (group_size * SLOT, channels) if flip else (channels, group_size * SLOT)
    c = lax.broadcasted_iota(jnp.int32, shape, 1 if flip else 0)
    j = lax.broadcasted_iota(jnp.int32, shape, 0 if flip else 1)
    hit = c == (j & (SLOT - 1)) * group_size + (j >> (SLOT.bit_length() - 1))
    return jnp.where(hit, value, 0.0).astype(BF16)


def parity():
    return lax.rem(lax.axis_index("col"), 2)


def dot(a, b):
    return jnp.dot(a, b, preferred_element_type=F32)


def dot_nt(a, b):
    return lax.dot_general(a, b, (((1,), (1,)), ((), ())), preferred_element_type=F32)


def pack_kernel(ends, rims_in, ct, even, odd, ctl, *rest):
    rims, ctf = rest[:-1], rest[-1]
    disp, rows, feat, cols = ct.shape
    per = 128 // feat
    for d in range(disp):
        block = ct[d].reshape(rows * feat, cols).astype(F32).T
        ctf[d * cols : (d + 1) * cols] = block
        ctl[d] = block.astype(BF16)
    columns = []
    for i, col in enumerate((cols - 1, 0)):
        block = ctf[pl.ds(col, disp, stride=cols), :]
        block = jnp.concatenate([block, jnp.zeros((disp, even.shape[1] - rows * feat), F32)], axis=1)
        edge = [rims_in[h, 2 * i + x : 2 * i + x + 1].astype(F32) for x in range(2) for h in range(rows)]
        columns.append(jnp.concatenate([block, *edge], axis=0))
    is_even = parity() == 0
    even[...] = jnp.where(is_even, columns[0], columns[1]).astype(BF16)
    odd[...] = jnp.where(is_even, columns[1], columns[0]).astype(BF16)
    for end, rim in zip(ends, rims):
        h = end()
        for q in range(disp // per):
            block = [ct[q * per + i, h].astype(F32) for i in range(per)]
            rim[q] = jnp.concatenate(block, axis=0).T.astype(BF16)


def pass_kernel(own, got, out):
    out[...] = jnp.where(parity() == 0, own[...].astype(F32), got[...].astype(F32)).astype(BF16)


def end_columns(by_even, by_odd):
    x, y = by_even[...].astype(F32), by_odd[...].astype(F32)
    is_even = parity() == 0
    return jnp.where(is_even, y, x), jnp.where(is_even, x, y)


def corner_kernel(ends, rows, disp, by_even, by_odd, *rest):
    pays, (edges, buf) = rest[: len(ends)], rest[len(ends) :]
    feat = 128 // rows
    per = 128 // feat
    count = disp // per
    lane = lanes((count, 128))
    for side, x in enumerate(end_columns(by_even, by_odd)):
        edges[side] = x[0:disp, 0:128]
    for end, pay in zip(ends, pays):
        h = end()
        buf[...] = jnp.zeros(buf.shape, F32)
        for side in range(2):
            out = jnp.zeros((count, 128), F32)
            for i in range(per):
                x = edges[side, pl.ds(i, count, stride=per)]
                first = pltpu.roll(x, feat * i, 1) if i else x
                last = pltpu.roll(x, (feat * (i - rows + 1)) % 128, 1) if i != rows - 1 else x
                x = jnp.where(h == 0, first, last)
                out = jnp.where((lane >= feat * i) & (lane < feat * (i + 1)), x, out)
            buf[8 * side : 8 * side + count] = out
        pay[...] = buf[...].astype(BF16)


def put_band(refs, h, column, block):
    fr, fr4, cols = refs
    at = fr.shape[1] - cols - PAD + column
    fr[h, at : at + block.shape[0]] = block
    fr4[h, at + STEP : at + STEP + block.shape[0]] = block


def own_kernel(group_size, left, right, far, fl, fr, fr4, mixed, wide_buf):
    rows, cols, channels = left.shape
    base, half, wide = rows * cols, cols // 2, group_size * SLOT
    mixed[0:base] = right[...].reshape(base, channels)
    mixed[base : 2 * base] = left[...].reshape(base, channels)
    mixed[2 * base :] = far[:, half:].reshape(base // 2, channels)
    wide_buf[...] = dot(mixed[...], channel_table(channels, group_size, False))
    tail = fr.shape[1]
    for h in range(rows):
        for ref in (fr, fr4):
            ref[h, 0:16] = jnp.zeros((16, wide), F32)
            ref[h, tail - 16 :] = jnp.zeros((16, wide), F32)
        put_band((fr, fr4, cols), h, -cols - half, wide_buf[2 * base + h * half : 2 * base + (h + 1) * half])
        put_band((fr, fr4, cols), h, 0, wide_buf[h * cols : (h + 1) * cols])
        fl[h, 0:PAD] = jnp.zeros((PAD, wide), F32)
        fl[h, PAD + cols :] = jnp.zeros((PAD, wide), F32)
        fl[h, PAD : PAD + cols] = wide_buf[base + h * cols : base + (h + 1) * cols] * (1.0 / group_size)


def volume_kernel(ends, group_size, near, by_even, by_odd, _fl, _fr, _fr4, fl, fr, fr4, vbuf, *rest):
    pays, (mixed, wide_buf) = rest[: len(ends)], rest[len(ends) :]
    rows, cols, channels = near.shape
    disp = vbuf.shape[1]
    reach = fr.shape[1] - cols - PAD
    wide = group_size * SLOT
    base = rows * cols
    mixed[0:base] = near[...].reshape(base, channels)
    count = disp + 2 * rows
    for i, x in enumerate(end_columns(by_even, by_odd)):
        mixed[base + i * count : base + (i + 1) * count] = x.astype(BF16)
    wide_buf[...] = dot(mixed[...], channel_table(channels, group_size, False))
    for h in range(rows):
        put_band((fr, fr4, cols), h, -cols, wide_buf[h * cols : (h + 1) * cols])
        at = base + disp + h
        fl[h, PAD - 1 : PAD] = wide_buf[at : at + 1] * (1.0 / group_size)
        at += count
        fl[h, PAD + cols : PAD + cols + 1] = wide_buf[at : at + 1] * (1.0 / group_size)
        put_band((fr, fr4, cols), h, cols, wide_buf[at + rows : at + rows + 1])
    total = cols + 2 * PAD
    low = lanes((8, 128)) < SLOT
    pairs, times, lots = rows // 2, disp // 2, wide // 128
    count = total // 16

    def products(i, _):
        p, at = lax.rem(i, pairs), pl.multiple_of(lax.div(i, pairs) * (8 * count), 8)
        lefts = [
            [
                [fl[2 * p + o, pl.ds(at + 8 * b, 8), 128 * j : 128 * (j + 1)] for j in range(lots)]
                for b in range(count)
            ]
            for o in range(2)
        ]
        for odd, band in enumerate((fr, fr4)):
            for r in range(1 - times, count):
                start = pl.multiple_of(at + reach - PAD + 8 * r, 8)
                here = [
                    [band[2 * p + o, pl.ds(start, 8), 128 * j : 128 * (j + 1)] for j in range(lots)]
                    for o in range(2)
                ]
                for t in range(max(0, -r), min(times, count - r)):
                    sums = []
                    for o in range(2):
                        acc = lefts[o][r + t][0] * here[o][0]
                        for j in range(1, lots):
                            acc = acc + lefts[o][r + t][j] * here[o][j]
                        sums.append(acc + pltpu.roll(acc, SLOT, 1))
                    vbuf[p, 2 * t + odd, pl.ds(at + 8 * (r + t), 8)] = jnp.where(low, *sums)
        return 0

    lax.fori_loop(0, 2 * pairs, products, 0)
    big = lanes((total, 128)) < SLOT

    for dd in range(disp // 2):
        for end, pay in zip(ends, pays):
            h = end()
            if isinstance(h, int):
                halves = [vbuf[h // 2, 2 * dd + o] for o in range(2)]
                if h % 2 == 0:
                    halves[1] = pltpu.roll(halves[1], SLOT, 1)
                else:
                    halves[0] = pltpu.roll(halves[0], SLOT, 1)
                out = jnp.where(big, halves[0], halves[1])
            else:
                last = pairs - 1
                first = jnp.where(big, vbuf[0, 2 * dd], pltpu.roll(vbuf[0, 2 * dd + 1], SLOT, 1))
                final = jnp.where(
                    big, pltpu.roll(vbuf[last, 2 * dd], SLOT, 1), vbuf[last, 2 * dd + 1]
                )
                out = jnp.where(h == 0, first, final)
            pay[dd * total : (dd + 1) * total] = out.astype(BF16)


def weight_kernel(
    masks, groups, feat, vbuf, ctl, by_even, by_odd, top, bot, tops, bots, *rest
):
    keep_out, give_out, ctsh, vt, buf, sums = rest
    disp, cols, width = ctl.shape
    pairs, per, half = vbuf.shape[0], 128 // feat, disp // 2
    mtop, mbot = masks()
    ctsh[0, 0] = jnp.zeros(ctsh.shape[2:], BF16)
    ctsh[half, 1] = jnp.zeros(ctsh.shape[2:], BF16)
    lane_in, lane_one = lanes((cols, 128)), lanes((1, 128))
    shifts = (feat, 128 - feat)
    edges = [x[0:disp, 0:128] for x in end_columns(by_even, by_odd)]
    turned = [[pltpu.roll(x, shift, 1) for shift in shifts] for x in edges]

    def aligned(t, z, i):
        return (
            t if i == 0 else pltpu.roll(t, 128 - feat * i, 1),
            z if i == per - 1 else pltpu.roll(z, feat * (per - 1 - i), 1),
        )

    corners = [aligned(tops[...].astype(F32) * mtop, bots[...].astype(F32) * mbot, i) for i in range(per)]

    def fill(q):
        t = top[q].astype(F32) * mtop
        z = bot[q].astype(F32) * mbot
        for i in range(per):
            d = q * per + i
            rims = aligned(t, z, i)
            inner = ctl[d].astype(F32)
            for p, (rim, shift) in enumerate(zip(rims, shifts)):

                def on_rim(x):
                    return x < feat if p == 0 else x >= 128 - feat

                at = slice(128 * p, 128 * (p + 1))
                buf[d, PAD : PAD + cols, at] = jnp.where(
                    on_rim(lane_in), rim, pltpu.roll(inner, shift, 1)
                )
                for side, row in enumerate((PAD - 1, PAD + cols)):
                    corner = corners[i][p][8 * side + q : 8 * side + q + 1]
                    buf[d, row : row + 1, at] = jnp.where(
                        on_rim(lane_one), corner, turned[side][p][d : d + 1]
                    )
            for e in range(3):
                ctsh[(d + 1) // 2, (d + 1) % 2, :, 256 * e : 256 * (e + 1)] = buf[
                    d, PAD - 1 + e : PAD - 1 + e + cols
                ].astype(BF16)

    none = jnp.zeros((cols, 128), F32)
    for p in range(pairs):
        for j in range(-1, half + 1):
            block = [
                vbuf[p, d, PAD : PAD + cols] if 0 <= d < disp and 0 <= j + half * o else none
                for o, d in enumerate((j, j + half))
            ]
            if j == half:
                block[1] = none
            x = jnp.concatenate(block, axis=0).astype(BF16)
            vt[p, :, 128 * (j + 1) : 128 * (j + 2)] = x.T
    full = None
    for q in range(half // per):
        fill(q)
        fill(q + half // per)
        first, size = q * per, per * 128
        left = jnp.concatenate(
            [
                jnp.concatenate(
                    [vt[p, :, 128 * (2 - a + first) : 128 * (2 - a + first) + size] for p in range(pairs)],
                    axis=1,
                )
                for a in range(3)
            ],
            axis=0,
        )
        right = jnp.concatenate(
            [
                jnp.concatenate(
                    [
                        ctsh[(d + 1) // 2, (d + 1) % 2, :, 256 * e + 128 * p : 256 * e + 128 * (p + 1)]
                        for e in range(3)
                    ],
                    axis=1,
                )
                for p in range(pairs)
                for j in range(first, first + per)
                for d in (j, j + half)
            ],
            axis=0,
        )
        part = dot(left, right)
        full = part if full is None else full + part
    keep = lanes((groups, 128)) < 3 * feat
    sums[...] = jnp.zeros(sums.shape, F32)
    for a in range(3):
        for e in range(3):
            block = full[128 * a : 128 * (a + 1), 128 * e : 128 * (e + 1)]
            out = block[0:groups] + pltpu.roll(block[SLOT : SLOT + groups], 128 - feat, 1)
            at = 128 * a + groups * e
            sums[at : at + groups] = jnp.where(keep, out, 0.0)
    half = sums.shape[0] // 2
    is_even = parity() == 0
    low, high = sums[0:half], sums[half:]
    keep_out[...] = jnp.where(is_even, low, high)
    give_out[...] = jnp.where(is_even, high, low)


def dgrad_kernel(ctsh, w2, *grads):
    _, disp, cols, _ = grads[0].shape
    step = disp // 4
    low = lanes((step * cols, 128)) < SLOT

    def conv(q, p, gv):
        slabs = [
            ctsh[pl.ds(q * step + s // 2, step), s % 2, :, 256 * e + 128 * p : 256 * e + 128 * (p + 1)]
            for s in range(4)
            for e in range(3)
        ]
        slabs = [x.reshape(step * cols, 128) for x in slabs]
        acc = dot(jnp.concatenate(slabs, axis=1), w2[...]).astype(BF16).astype(F32)
        for o in range(2):
            x = acc[:, 128 * o : 128 * (o + 1)]
            r = pltpu.roll(x, SLOT, 1)
            for hh in range(2):
                y = jnp.where(low, r, x) if hh else jnp.where(low, x, r)
                for j in range(step):
                    gv[hh, 2 * (q * step + j) + o] = y[j * cols : (j + 1) * cols]

    for q in range(2):
        for p, gv in enumerate(grads):
            conv(q, p, gv)


def right_kernel(fl, *rest):
    *grads, rg0, rg1, rg2, acce, acco, both = rest
    disp = grads[0].shape[1]
    rows, cols, channels = rg0.shape
    wide = fl.shape[2]
    group_size = wide // SLOT
    count = cols // 8
    back = acce.shape[1] - cols
    lead = back // 8

    lots = wide // 128

    def right_row(gv, p, hh):
        h = 2 * p + hh
        here = [
            [fl[h, PAD + 8 * b : PAD + 8 * b + 8, 128 * j : 128 * (j + 1)] for j in range(lots)]
            for b in range(count)
        ]
        for odd, buf in enumerate((acce, acco)):
            for k in range(lead + count):
                accs = [None] * lots
                for t in range(disp // 2):
                    b = k + t - lead
                    if b < 0 or b >= count:
                        continue
                    g = gv[hh, 2 * t + odd, 8 * b : 8 * b + 8]
                    for j in range(lots):
                        term = g * here[b][j]
                        accs[j] = term if accs[j] is None else accs[j] + term
                for j in range(lots):
                    x = jnp.zeros((8, 128), F32) if accs[j] is None else accs[j]
                    buf[h, 8 * k : 8 * k + 8, 128 * j : 128 * (j + 1)] = x
        acco[h, 8 * (lead + count) :] = jnp.zeros((8, wide), F32)

    for p, gv in enumerate(grads):
        pl.loop(0, 2)(functools.partial(right_row, gv, p))
    size = back + cols
    for h in range(rows):
        both[h * size : (h + 1) * size] = (acce[h] + acco[h, STEP : STEP + size]).astype(BF16)
    whole = dot(both[...], channel_table(channels, group_size, True)).astype(BF16)
    half = cols // 2
    for h in range(rows):
        at = h * size + back
        rg2[h] = whole[at - cols - half : at - cols]
        rg1[h] = whole[at - cols : at]
        rg0[h] = whole[at : at + cols]


def left_kernel(fr, fr4, *rest):
    *grads, lg, accl = rest
    rows, cols, channels = lg.shape
    disp, wide = grads[0].shape[1], fr.shape[2]
    group_size = wide // SLOT
    reach = fr.shape[1] - cols - PAD
    count, times, lots = cols // 8, disp // 2, wide // 128

    def left_row(gv, p, hh):
        h = 2 * p + hh
        accs = [[None] * lots for _ in range(count)]
        for odd, band in enumerate((fr, fr4)):
            for r in range(1 - times, count):
                at = reach + 8 * r
                here = [band[h, at : at + 8, 128 * j : 128 * (j + 1)] for j in range(lots)]
                for t in range(max(0, -r), min(times, count - r)):
                    g = gv[hh, 2 * t + odd, 8 * (r + t) : 8 * (r + t) + 8]
                    for j in range(lots):
                        term, acc = g * here[j], accs[r + t][j]
                        accs[r + t][j] = term if acc is None else acc + term
        for b in range(count):
            for j in range(lots):
                accl[h, 8 * b : 8 * b + 8, 128 * j : 128 * (j + 1)] = accs[b][j] * (1.0 / group_size)

    for p, gv in enumerate(grads):
        pl.loop(0, 2)(functools.partial(left_row, gv, p))
    whole = accl[...].reshape(rows * cols, wide).astype(BF16)
    out = dot(whole, channel_table(channels, group_size, True)).astype(BF16)
    lg[...] = out.reshape(rows, cols, channels)


def combine_kernel(got, rg2, out):
    cols = out.shape[1]
    half = cols // 2
    part = jnp.where(parity() == 0, 0.0, got[...].astype(F32))
    out[:, 0:half] = part[:, 0:half].astype(BF16)
    out[:, half:] = (part[:, half:] + rg2[...].astype(F32)).astype(BF16)


def halo_lanes(groups):
    first = SLOT - groups
    assert groups - first <= first
    return (groups, SLOT, groups), (SLOT + groups, SLOT + 2 * groups - first, SLOT + groups - first)


def place_halo(base, row, groups, offset, lane):
    for start, end, shift in halo_lanes(groups):
        moved = pltpu.roll(row, (shift - offset) % 128, 1)
        base = jnp.where((lane >= start) & (lane < end), moved, base)
    return base


def conv_kernel(masks, groups, vbuf, top, bot, wc, out, taps, buf, held, sems):
    disp, rows, feat, cols = out.shape
    total = buf.shape[2]
    lane = lanes((total, 128))
    zeros = jnp.zeros((cols, taps.shape[3]), BF16)
    taps[0, 0] = zeros
    taps[disp // 2, 1] = zeros
    halos_of = [(ref, mask) for ref, mask in zip((top, bot), masks())]

    def build(dd):
        for p, (ref, mask) in enumerate(halos_of):
            row = ref[dd * total : (dd + 1) * total].astype(F32) * mask
            for o in range(2):
                d = 2 * dd + o
                buf[p, d] = place_halo(vbuf[p, d], row, groups, SLOT * o, lane)
                for e in range(3):
                    at = 256 * e + 128 * p
                    taps[(d + 1) // 2, (d + 1) % 2, :, at : at + 128] = buf[
                        p, d, PAD - 1 + e : PAD - 1 + e + cols
                    ].astype(BF16)

    parts = sems.shape[0]
    step = disp // 2 // parts
    copies = []
    build(0)
    for q in range(parts):
        for dd in range(q * step + 1, min((q + 1) * step + 1, disp // 2)):
            build(dd)
        slabs = [
            taps[q * step + s // 2 : q * step + s // 2 + step, s % 2].reshape(step * cols, taps.shape[3])
            for s in range(4)
        ]
        acc = dot(jnp.concatenate(slabs, axis=1), wc[...])
        for j in range(step):
            both = acc[j * cols : (j + 1) * cols].T.astype(BF16)
            for o in range(2):
                block = both[rows * feat * o : rows * feat * (o + 1)]
                held[2 * (q * step + j) + o] = block.reshape(rows, feat, cols)
        at = pl.ds(2 * q * step, 2 * step)
        copies.append(pltpu.make_async_copy(held.at[at], out.at[at], sems.at[q]))
        copies[-1].start()
    for copy in copies:
        copy.wait()


def finish_kernel(scale, mine, other, own, near, far, left, weight, right, left_out, held_w, held_r, sems):
    _, _, _, feat, groups = weight.shape
    copies = [pltpu.make_async_copy(left, left_out, sems.at[0])]
    copies[0].start()
    is_even = parity() == 0
    beside = jnp.where(is_even, near[...].astype(F32), 0.0)
    held_r[...] = (own[...].astype(F32) + beside + far[...].astype(F32)).astype(BF16)
    copies.append(pltpu.make_async_copy(held_r, right, sems.at[1]))
    copies[1].start()
    x, y = mine[...] * scale, other[...] * scale
    total = jnp.concatenate([jnp.where(is_even, x, y), jnp.where(is_even, y, x)], axis=0)
    for a in range(3):
        for e in range(3):
            at = 128 * a + groups * e
            block = total[at : at + groups].T
            for b in range(3):
                held_w[2 - a, 2 - b, 2 - e] = block[feat * b : feat * (b + 1)]
        copies.append(pltpu.make_async_copy(held_w.at[2 - a], weight.at[2 - a], sems.at[2 + a]))
        copies[-1].start()
    for copy in copies:
        copy.wait()


def copy_kernel(*refs):
    half = len(refs) // 2
    for src, dst in zip(refs[:half], refs[half:]):
        dst[...] = src[...]


def sum_kernel(*refs):
    *parts, out = refs
    out[...] = tree([ref[...].astype(F32) for ref in parts]).astype(out.dtype)


def tree(terms):
    while len(terms) > 1:
        terms = [terms[i] + terms[i + 1] for i in range(0, len(terms), 2)]
    return terms[0]


def taps_kernel(taps, w2, wc, turned):
    _, _, _, feat, groups = taps.shape
    rows = wc.shape[1] // 2 // feat
    lane_of = lanes((feat, 2 * SLOT))
    low = lanes((feat, 2 * SLOT)) < SLOT
    zero = jnp.zeros((feat, 2 * SLOT), F32)

    def wide(a, b, e):
        if not 0 <= b <= 2:
            return None
        return jnp.concatenate([taps[a, b, e].astype(F32), zero[:, groups:]], axis=1)

    def beside(x, y):
        if x is None and y is None:
            return zero
        x = zero if x is None else x
        y = zero if y is None else pltpu.roll(y, SLOT, 1)
        return jnp.where(low, x, y)

    def build(a, _):
        def at_row(h):
            return pl.multiple_of((a * rows + h) * feat, feat)

        for e in range(3):
            for h in range(rows):
                for p in range(rows // 2):
                    lane = SLOT * (rows * e + 2 * p)
                    block = beside(wide(a, 2 * p - h + 1, e), wide(a, 2 * p + 1 - h + 1, e))
                    if h == 0 and p == 0:
                        block = place_halo(block, wide(a, 0, e), groups, 0, lane_of)
                    if h == rows - 1 and p == rows // 2 - 1:
                        block = place_halo(block, wide(a, 2, e), groups, 0, lane_of)
                    turned[pl.ds(at_row(h), feat), lane : lane + 2 * SLOT] = block
        return 0

    lax.fori_loop(0, 3, build, 0)
    for s in range(4):
        for e in range(3):
            for r in range(4):
                for o in range(2):
                    taps_of = [None if not 0 <= s - o <= 2 else wide(2 - s + o, 2 - r + i, 2 - e) for i in range(2)]
                    at = 384 * s + 128 * e + feat * r
                    w2[at : at + feat, 128 * o : 128 * (o + 1)] = beside(*taps_of).astype(BF16)
    depth, size = turned.shape[1], rows * feat
    for a in range(3):
        for i in range(depth // 128):
            x = turned[size * a : size * (a + 1), 128 * i : 128 * (i + 1)].T.astype(BF16)
            for o in range(2):
                at = depth * (a + o) + 128 * i
                wc[at : at + 128, size * o : size * (o + 1)] = x
    for o in range(2):
        at = depth * 3 * (1 - o)
        wc[at : at + depth, size * o : size * (o + 1)] = jnp.zeros((depth, size), BF16)


TOKEN = ((8, 128), F32)


def with_token(kernel, inputs, outputs):
    def run(*refs):
        kernel(*refs[: inputs + outputs], *refs[inputs + outputs + 1 :])
        refs[inputs + outputs][...] = jnp.zeros(TOKEN[0], F32)

    return run


def call(kernel, outs, scratch, *args, after=(), token=False, us=0.0, alias=(), hbm=()):
    skip = len(after)
    if token:
        kernel = with_token(kernel, len(args), len(outs))
        outs = [*outs, TOKEN]
    return pl.pallas_call(
        lambda *refs: kernel(*refs[skip:]),
        out_shape=[jax.ShapeDtypeStruct(s, t) for s, t in outs],
        in_specs=[pl.BlockSpec(memory_space=pl.ANY)] * skip + [VMEM] * len(args),
        out_specs=[pl.BlockSpec(memory_space=pl.ANY) if i in hbm else VMEM for i in range(len(outs))],
        scratch_shapes=scratch,
        input_output_aliases={skip + i: o for i, o in alias},
        compiler_params=pltpu.CompilerParams(vmem_limit_bytes=LIMIT),
        cost_estimate=pl.CostEstimate(
            flops=int(us * 1.15e9), bytes_accessed=int(us * 3.7e6), transcendentals=0
        ),
    )(*after, *args)


def col_shift(block, distance):
    n = lax.axis_size("col")
    route = [(i - distance, i) for i in range(n) if 0 <= i - distance < n]
    return lax.ppermute(block, "col", route)


def row_shift(block, distance):
    n = lax.axis_size("row")
    route = [(i - distance, i) for i in range(n) if 0 <= i - distance < n]
    return lax.ppermute(block, "row", route)


def halos(pays):
    if lax.axis_size("row") == 2:
        got = lax.ppermute(pays[0], "row", [(0, 1), (1, 0)])
        return got, got
    return row_shift(pays[0], 1), row_shift(pays[1], -1)


def stages(n_row, n_col):
    col_bits = [1 << i for i in range(1, n_col.bit_length() - 1)]
    row_bits = [n_col << i for i in range(n_row.bit_length() - 1)]
    assert n_col == 2 << len(col_bits) and n_row == 1 << len(row_bits)
    bits = col_bits + row_bits
    pairs = [bits[i : i + 2] for i in range(0, len(bits), 2)]
    return [pair + [sum(pair)] if len(pair) == 2 else pair for pair in pairs]


def on_device(left_features, right_features, conv_weight, cotangent):
    rows, cols, channels = left_features.shape
    disp, feat = cotangent.shape[0], cotangent.shape[3]
    groups = conv_weight.shape[3]
    group_size = channels // groups
    wide = group_size * SLOT
    n_row, n_col = lax.axis_size("row"), lax.axis_size("col")
    per = 128 // feat

    if n_row == 2:
        ends = [lambda: (rows - 1) * (1 - lax.axis_index("row"))]
    else:
        ends = [lambda: rows - 1, lambda: 0]
    n = len(ends)

    def masks():
        at = lax.axis_index("row")
        return (
            jnp.where(at > 0, 1.0, 0.0).astype(F32),
            jnp.where(at < n_row - 1, 1.0, 0.0).astype(F32),
        )

    total = cols + 2 * PAD
    count = disp + 2 * rows
    ct = cotangent.transpose(0, 1, 3, 2)

    def swap(block, mask):
        route = [(i, i ^ mask) for i in range(n_row * n_col)]
        return lax.ppermute(block, ("row", "col"), route)

    far = col_shift(right_features, 2)
    by_even, by_odd, ctl, *rims = call(
        functools.partial(pack_kernel, ends),
        [
            ((count, channels), BF16),
            ((count, channels), BF16),
            ((disp, cols, rows * feat), BF16),
        ]
        + [((disp // per, cols, 128), BF16)] * n,
        [pltpu.VMEM((disp * cols, rows * feat), F32)],
        jnp.concatenate(
            [x[:, at : at + 1] for at in (cols - 1, 0) for x in (left_features, right_features)], axis=1
        ),
        ct,
        us=0.4,
    )
    inner = range(1, n_col - 1, 2)
    by_even = swap(by_even, 1)
    by_odd = lax.ppermute(by_odd, "col", [(i, i + 1) for i in inner] + [(i + 1, i) for i in inner])
    (passed,) = call(
        pass_kernel, [((rows, cols, channels), BF16)], [], right_features, far, after=[ctl]
    )
    near = swap(passed, 1)
    top, bot = halos(rims)
    band = 104 + cols + PAD
    banks = [((rows, total, wide), F32), ((rows, band, wide), F32), ((rows, band, wide), F32)]
    spread_rows = 2 * rows * cols + rows * cols // 2
    fl, fr, fr4 = call(
        functools.partial(own_kernel, group_size),
        banks,
        [pltpu.VMEM((spread_rows, channels), BF16), pltpu.VMEM((spread_rows, wide), F32)],
        left_features,
        right_features,
        far,
        after=[passed],
    )
    corner_pays = call(
        functools.partial(corner_kernel, ends, rows, disp),
        [((16, 128), BF16)] * n,
        [pltpu.VMEM((2, disp, 128), F32), pltpu.VMEM((16, 128), F32)],
        by_even,
        by_odd,
        after=[fl],
        us=5.0,
    )
    tops, bots = halos(corner_pays)
    spread_rows = rows * cols + 2 * count
    fl, fr, fr4, vbuf, *volume_rows = call(
        functools.partial(volume_kernel, ends, group_size),
        banks
        + [((rows // 2, disp, total, 2 * SLOT), F32)]
        + [((disp // 2 * total, 128), BF16)] * n,
        [pltpu.VMEM((spread_rows, channels), BF16), pltpu.VMEM((spread_rows, wide), F32)],
        near,
        by_even,
        by_odd,
        fl,
        fr,
        fr4,
        us=1.8,
        alias=[(3, 0), (4, 1), (5, 2)],
    )
    vtop, vbot = halos(volume_rows)
    keep, give, ctsh = call(
        functools.partial(weight_kernel, masks, groups, feat),
        [((3 * 64, 128), F32), ((3 * 64, 128), F32), ((disp // 2 + 1, 2, cols, 3 * 256), BF16)],
        [
            pltpu.VMEM((rows // 2, 128, (disp // 2 + 2) * 128), BF16),
            pltpu.VMEM((disp, total, 256), F32),
            pltpu.VMEM((3 * 128, 128), F32),
        ],
        vbuf, ctl, by_even, by_odd, top, bot, tops, bots,
        us=2.0,
    )

    got = swap(give, 1)
    w2, wc = call(
        taps_kernel,
        [((12 * 128, 2 * 128), BF16), ((4 * 3 * rows * SLOT, 2 * rows * feat), BF16)],
        [pltpu.VMEM((3 * rows * feat, 3 * rows * SLOT), F32)],
        conv_weight.transpose(0, 1, 2, 4, 3),
        after=[keep],
    )
    (part,) = call(sum_kernel, [(keep.shape, BF16)], [], keep, got, after=[w2])
    grads = call(
        dgrad_kernel, [((2, disp, cols, 128), F32)] * (rows // 2), [], ctsh, w2, after=[part], us=0.2
    )
    rg0, rg1, rg2 = call(
        right_kernel,
        [
            ((rows, cols, channels), BF16),
            ((rows, cols, channels), BF16),
            ((rows, cols // 2, channels), BF16),
        ],
        [
            pltpu.VMEM((rows, cols + cols + cols // 2, wide), F32),
            pltpu.VMEM((rows, cols + cols + cols // 2 + 8, wide), F32),
            pltpu.VMEM((rows * (cols + cols + cols // 2), wide), BF16),
        ],
        fl, *grads,
        us=0.2,
    )
    rg1 = swap(rg1, 1)
    *middle, final = stages(n_row, n_col)
    order = [rg0, vtop]
    for stage in middle:
        parts = [part] + [swap(part, m) for m in stage]
        (part,) = call(sum_kernel, [(part.shape, BF16)], [], *parts, after=order, us=4.0)
        order = []
    parts = [part] + [swap(part, m) for m in final]
    (rg2,) = call(
        combine_kernel, [((rows, cols, channels), BF16)], [], rg1, rg2, after=[part]
    )
    (lg,) = call(
        left_kernel,
        [((rows, cols, channels), BF16)],
        [pltpu.VMEM((rows, cols, wide), F32)],
        fr, fr4, *grads,
        after=[rg2],
        us=1.9,
    )
    (part,) = call(sum_kernel, [(part.shape, F32)], [], *parts, after=[lg])
    output, conv_done = call(
        functools.partial(conv_kernel, masks, groups),
        [((disp, rows, feat, cols), BF16)],
        [
            pltpu.VMEM((disp // 2 + 1, 2, cols, 3 * rows * SLOT), BF16),
            pltpu.VMEM((rows // 2, disp, total, 128), F32),
            pltpu.VMEM((disp, rows, feat, cols), BF16),
            pltpu.SemaphoreType.DMA((3,)),
        ],
        vbuf, vtop, vbot, wc,
        after=[part],
        token=True,
        us=3.5,
        hbm=[0],
    )
    rg2 = col_shift(rg2, -2)
    cells = disp * rows * n_row * cols * n_col
    weight_grad, right_grad, left_grad = call(
        functools.partial(finish_kernel, 1.0 / math.sqrt(cells)),
        [
            ((3, 3, 3, feat, groups), F32),
            ((rows, cols, channels), BF16),
            ((rows, cols, channels), BF16),
        ],
        [
            pltpu.VMEM((3, 3, 3, feat, groups), F32),
            pltpu.VMEM((rows, cols, channels), BF16),
            pltpu.SemaphoreType.DMA((5,)),
        ],
        part, swap(part, 1), rg0, rg1, rg2, lg,
        after=[conv_done],
        us=1.0,
        hbm=[0, 1, 2],
    )
    return (
        output.transpose(0, 1, 3, 2),
        weight_grad.transpose(0, 1, 2, 4, 3),
        left_grad,
        right_grad,
    )


def solution(mesh):
    in_specs = (P("row", "col", None), P("row", "col", None), P(), P(None, "row", "col", None))
    out_specs = (P(None, "row", "col", None), P(), P("row", "col", None), P("row", "col", None))
    return jax.shard_map(
        on_device, mesh=mesh, in_specs=in_specs, out_specs=out_specs, check_vma=False
    )
```

```python
import functools
import math

import jax
import jax.numpy as jnp
from jax import lax
from jax.experimental import pallas as pl
from jax.experimental.pallas import tpu as pltpu
from jax.sharding import PartitionSpec as P

DISP = 24
STEP = 4
SLOT = 64
PAD = 8
F32 = jnp.float32
BF16 = jnp.bfloat16
VMEM = pl.BlockSpec(memory_space=pltpu.VMEM)
LIMIT = 16 * 1024 * 1024


def lanes(shape):
    return lax.broadcasted_iota(jnp.int32, shape, len(shape) - 1)


def channel_table(channels, group_size, flip, value=1.0):
    shape = (group_size * SLOT, channels) if flip else (channels, group_size * SLOT)
    c = lax.broadcasted_iota(jnp.int32, shape, 1 if flip else 0)
    j = lax.broadcasted_iota(jnp.int32, shape, 0 if flip else 1)
    hit = c == (j & (SLOT - 1)) * group_size + (j >> (SLOT.bit_length() - 1))
    return jnp.where(hit, value, 0.0).astype(BF16)


def parity():
    return lax.rem(lax.axis_index("col"), 2)


def dot(a, b):
    return jnp.dot(a, b, preferred_element_type=F32)


def dot_nt(a, b):
    return lax.dot_general(a, b, (((1,), (1,)), ((), ())), preferred_element_type=F32)


def begin_kernel(out):
    out[...] = jnp.zeros(out.shape, F32)


def pack_kernel(ends, left, right, ct, even, odd, ctl, *rest):
    rims, ctf = rest[:-1], rest[-1]
    disp, rows, feat, cols = ct.shape
    per = 128 // feat
    for d in range(disp):
        block = ct[d].reshape(rows * feat, cols).astype(F32).T
        ctf[d * cols : (d + 1) * cols] = block
        ctl[d] = block.astype(BF16)
    columns = []
    for i, col in enumerate((cols - 1, 0)):
        block = ctf[pl.ds(col, disp, stride=cols), :]
        block = jnp.concatenate([block, jnp.zeros((disp, even.shape[1] - rows * feat), F32)], axis=1)
        edge = [x[h, col : col + 1].astype(F32) for x in (left, right) for h in range(rows)]
        columns.append(jnp.concatenate([block, *edge], axis=0))
    is_even = parity() == 0
    even[...] = jnp.where(is_even, columns[0], columns[1]).astype(BF16)
    odd[...] = jnp.where(is_even, columns[1], columns[0]).astype(BF16)
    for end, rim in zip(ends, rims):
        h = end()
        for q in range(disp // per):
            block = [ct[q * per + i, h].astype(F32) for i in range(per)]
            rim[q] = jnp.concatenate(block, axis=0).T.astype(BF16)


def pass_kernel(own, got, out):
    out[...] = jnp.where(parity() == 0, own[...].astype(F32), got[...].astype(F32)).astype(BF16)


def end_columns(by_even, by_odd):
    x, y = by_even[...].astype(F32), by_odd[...].astype(F32)
    is_even = parity() == 0
    return jnp.where(is_even, y, x), jnp.where(is_even, x, y)


def corner_kernel(ends, rows, disp, by_even, by_odd, *rest):
    pays, (edges, buf) = rest[: len(ends)], rest[len(ends) :]
    feat = 128 // rows
    per = 128 // feat
    count = disp // per
    lane = lanes((count, 128))
    for side, x in enumerate(end_columns(by_even, by_odd)):
        edges[side] = x[0:disp, 0:128]
    for end, pay in zip(ends, pays):
        h = end()
        buf[...] = jnp.zeros(buf.shape, F32)
        for side in range(2):
            out = jnp.zeros((count, 128), F32)
            for i in range(per):
                x = edges[side, pl.ds(i, count, stride=per)]
                first = pltpu.roll(x, feat * i, 1) if i else x
                last = pltpu.roll(x, (feat * (i - rows + 1)) % 128, 1) if i != rows - 1 else x
                x = jnp.where(h == 0, first, last)
                out = jnp.where((lane >= feat * i) & (lane < feat * (i + 1)), x, out)
            buf[8 * side : 8 * side + count] = out
        pay[...] = buf[...].astype(BF16)


def put_band(refs, h, column, block):
    fr, fr4, cols = refs
    at = fr.shape[1] - cols - PAD + column
    fr[h, at : at + block.shape[0]] = block
    fr4[h, at + STEP : at + STEP + block.shape[0]] = block


def own_kernel(group_size, left, right, far, fl, fr, fr4, mixed, wide_buf):
    rows, cols, channels = left.shape
    base, half, wide = rows * cols, cols // 2, group_size * SLOT
    mixed[0:base] = right[...].reshape(base, channels)
    mixed[base : 2 * base] = left[...].reshape(base, channels)
    mixed[2 * base :] = far[:, half:].reshape(base // 2, channels)
    wide_buf[...] = dot(mixed[...], channel_table(channels, group_size, False))
    tail = fr.shape[1]
    for h in range(rows):
        for ref in (fr, fr4):
            ref[h, 0:16] = jnp.zeros((16, wide), F32)
            ref[h, tail - 16 :] = jnp.zeros((16, wide), F32)
        put_band((fr, fr4, cols), h, -cols - half, wide_buf[2 * base + h * half : 2 * base + (h + 1) * half])
        put_band((fr, fr4, cols), h, 0, wide_buf[h * cols : (h + 1) * cols])
        fl[h, 0:PAD] = jnp.zeros((PAD, wide), F32)
        fl[h, PAD + cols :] = jnp.zeros((PAD, wide), F32)
        fl[h, PAD : PAD + cols] = wide_buf[base + h * cols : base + (h + 1) * cols] * (1.0 / group_size)


def volume_kernel(ends, group_size, near, by_even, by_odd, _fl, _fr, _fr4, fl, fr, fr4, vbuf, *rest):
    pays, (mixed, wide_buf) = rest[: len(ends)], rest[len(ends) :]
    rows, cols, channels = near.shape
    disp = vbuf.shape[1]
    reach = fr.shape[1] - cols - PAD
    wide = group_size * SLOT
    base = rows * cols
    mixed[0:base] = near[...].reshape(base, channels)
    count = disp + 2 * rows
    for i, x in enumerate(end_columns(by_even, by_odd)):
        mixed[base + i * count : base + (i + 1) * count] = x.astype(BF16)
    wide_buf[...] = dot(mixed[...], channel_table(channels, group_size, False))
    for h in range(rows):
        put_band((fr, fr4, cols), h, -cols, wide_buf[h * cols : (h + 1) * cols])
        at = base + disp + h
        fl[h, PAD - 1 : PAD] = wide_buf[at : at + 1] * (1.0 / group_size)
        at += count
        fl[h, PAD + cols : PAD + cols + 1] = wide_buf[at : at + 1] * (1.0 / group_size)
        put_band((fr, fr4, cols), h, cols, wide_buf[at + rows : at + rows + 1])
    total = cols + 2 * PAD
    low = lanes((8, 128)) < SLOT
    pairs, times, lots = rows // 2, disp // 2, wide // 128
    count = total // 16

    def products(i, _):
        p, at = lax.rem(i, pairs), pl.multiple_of(lax.div(i, pairs) * (8 * count), 8)
        lefts = [
            [
                [fl[2 * p + o, pl.ds(at + 8 * b, 8), 128 * j : 128 * (j + 1)] for j in range(lots)]
                for b in range(count)
            ]
            for o in range(2)
        ]
        for odd, band in enumerate((fr, fr4)):
            for r in range(1 - times, count):
                start = pl.multiple_of(at + reach - PAD + 8 * r, 8)
                here = [
                    [band[2 * p + o, pl.ds(start, 8), 128 * j : 128 * (j + 1)] for j in range(lots)]
                    for o in range(2)
                ]
                for t in range(max(0, -r), min(times, count - r)):
                    sums = []
                    for o in range(2):
                        acc = lefts[o][r + t][0] * here[o][0]
                        for j in range(1, lots):
                            acc = acc + lefts[o][r + t][j] * here[o][j]
                        sums.append(acc + pltpu.roll(acc, SLOT, 1))
                    vbuf[p, 2 * t + odd, pl.ds(at + 8 * (r + t), 8)] = jnp.where(low, *sums)
        return 0

    lax.fori_loop(0, 2 * pairs, products, 0)
    big = lanes((total, 128)) < SLOT

    for dd in range(disp // 2):
        for end, pay in zip(ends, pays):
            h = end()
            if isinstance(h, int):
                halves = [vbuf[h // 2, 2 * dd + o] for o in range(2)]
                if h % 2 == 0:
                    halves[1] = pltpu.roll(halves[1], SLOT, 1)
                else:
                    halves[0] = pltpu.roll(halves[0], SLOT, 1)
                out = jnp.where(big, halves[0], halves[1])
            else:
                last = pairs - 1
                first = jnp.where(big, vbuf[0, 2 * dd], pltpu.roll(vbuf[0, 2 * dd + 1], SLOT, 1))
                final = jnp.where(
                    big, pltpu.roll(vbuf[last, 2 * dd], SLOT, 1), vbuf[last, 2 * dd + 1]
                )
                out = jnp.where(h == 0, first, final)
            pay[dd * total : (dd + 1) * total] = out.astype(BF16)


def weight_kernel(
    masks, groups, feat, vbuf, ctl, by_even, by_odd, top, bot, tops, bots, *rest
):
    keep_out, give_out, ctsh, vt, buf, sums = rest
    disp, cols, width = ctl.shape
    pairs, per, half = vbuf.shape[0], 128 // feat, disp // 2
    mtop, mbot = masks()
    ctsh[0, 0] = jnp.zeros(ctsh.shape[2:], BF16)
    ctsh[half, 1] = jnp.zeros(ctsh.shape[2:], BF16)
    lane_in, lane_one = lanes((cols, 128)), lanes((1, 128))
    shifts = (feat, 128 - feat)
    edges = [x[0:disp, 0:128] for x in end_columns(by_even, by_odd)]
    turned = [[pltpu.roll(x, shift, 1) for shift in shifts] for x in edges]

    def aligned(t, z, i):
        return (
            t if i == 0 else pltpu.roll(t, 128 - feat * i, 1),
            z if i == per - 1 else pltpu.roll(z, feat * (per - 1 - i), 1),
        )

    corners = [aligned(tops[...].astype(F32) * mtop, bots[...].astype(F32) * mbot, i) for i in range(per)]

    def fill(q):
        t = top[q].astype(F32) * mtop
        z = bot[q].astype(F32) * mbot
        for i in range(per):
            d = q * per + i
            rims = aligned(t, z, i)
            inner = ctl[d].astype(F32)
            for p, (rim, shift) in enumerate(zip(rims, shifts)):

                def on_rim(x):
                    return x < feat if p == 0 else x >= 128 - feat

                at = slice(128 * p, 128 * (p + 1))
                buf[d, PAD : PAD + cols, at] = jnp.where(
                    on_rim(lane_in), rim, pltpu.roll(inner, shift, 1)
                )
                for side, row in enumerate((PAD - 1, PAD + cols)):
                    corner = corners[i][p][8 * side + q : 8 * side + q + 1]
                    buf[d, row : row + 1, at] = jnp.where(
                        on_rim(lane_one), corner, turned[side][p][d : d + 1]
                    )
            for e in range(3):
                ctsh[(d + 1) // 2, (d + 1) % 2, :, 256 * e : 256 * (e + 1)] = buf[
                    d, PAD - 1 + e : PAD - 1 + e + cols
                ].astype(BF16)

    none = jnp.zeros((cols, 128), F32)
    for p in range(pairs):
        for j in range(-1, half + 1):
            block = [
                vbuf[p, d, PAD : PAD + cols] if 0 <= d < disp and 0 <= j + half * o else none
                for o, d in enumerate((j, j + half))
            ]
            if j == half:
                block[1] = none
            x = jnp.concatenate(block, axis=0).astype(BF16)
            vt[p, :, 128 * (j + 1) : 128 * (j + 2)] = x.T
    full = None
    for q in range(half // per):
        fill(q)
        fill(q + half // per)
        first, size = q * per, per * 128
        left = jnp.concatenate(
            [
                jnp.concatenate(
                    [vt[p, :, 128 * (2 - a + first) : 128 * (2 - a + first) + size] for p in range(pairs)],
                    axis=1,
                )
                for a in range(3)
            ],
            axis=0,
        )
        right = jnp.concatenate(
            [
                jnp.concatenate(
                    [
                        ctsh[(d + 1) // 2, (d + 1) % 2, :, 256 * e + 128 * p : 256 * e + 128 * (p + 1)]
                        for e in range(3)
                    ],
                    axis=1,
                )
                for p in range(pairs)
                for j in range(first, first + per)
                for d in (j, j + half)
            ],
            axis=0,
        )
        part = dot(left, right)
        full = part if full is None else full + part
    keep = lanes((groups, 128)) < 3 * feat
    sums[...] = jnp.zeros(sums.shape, F32)
    for a in range(3):
        for e in range(3):
            block = full[128 * a : 128 * (a + 1), 128 * e : 128 * (e + 1)]
            out = block[0:groups] + pltpu.roll(block[SLOT : SLOT + groups], 128 - feat, 1)
            at = 128 * a + groups * e
            sums[at : at + groups] = jnp.where(keep, out, 0.0)
    half = sums.shape[0] // 2
    is_even = parity() == 0
    low, high = sums[0:half], sums[half:]
    keep_out[...] = jnp.where(is_even, low, high)
    give_out[...] = jnp.where(is_even, high, low)


def dgrad_kernel(ctsh, w2, *grads):
    _, disp, cols, _ = grads[0].shape
    step = disp // 4
    low = lanes((step * cols, 128)) < SLOT

    def conv(q, p, gv):
        slabs = [
            ctsh[pl.ds(q * step + s // 2, step), s % 2, :, 256 * e + 128 * p : 256 * e + 128 * (p + 1)]
            for s in range(4)
            for e in range(3)
        ]
        slabs = [x.reshape(step * cols, 128) for x in slabs]
        acc = dot(jnp.concatenate(slabs, axis=1), w2[...]).astype(BF16).astype(F32)
        for o in range(2):
            x = acc[:, 128 * o : 128 * (o + 1)]
            r = pltpu.roll(x, SLOT, 1)
            for hh in range(2):
                y = jnp.where(low, r, x) if hh else jnp.where(low, x, r)
                for j in range(step):
                    gv[hh, 2 * (q * step + j) + o] = y[j * cols : (j + 1) * cols]

    for q in range(2):
        for p, gv in enumerate(grads):
            conv(q, p, gv)


def right_kernel(fl, *rest):
    *grads, rg0, rg1, rg2, acce, acco, both = rest
    disp = grads[0].shape[1]
    rows, cols, channels = rg0.shape
    wide = fl.shape[2]
    group_size = wide // SLOT
    count = cols // 8
    back = acce.shape[1] - cols
    lead = back // 8

    lots = wide // 128

    def right_row(gv, p, hh):
        h = 2 * p + hh
        here = [
            [fl[h, PAD + 8 * b : PAD + 8 * b + 8, 128 * j : 128 * (j + 1)] for j in range(lots)]
            for b in range(count)
        ]
        for odd, buf in enumerate((acce, acco)):
            for k in range(lead + count):
                accs = [None] * lots
                for t in range(disp // 2):
                    b = k + t - lead
                    if b < 0 or b >= count:
                        continue
                    g = gv[hh, 2 * t + odd, 8 * b : 8 * b + 8]
                    for j in range(lots):
                        term = g * here[b][j]
                        accs[j] = term if accs[j] is None else accs[j] + term
                for j in range(lots):
                    x = jnp.zeros((8, 128), F32) if accs[j] is None else accs[j]
                    buf[h, 8 * k : 8 * k + 8, 128 * j : 128 * (j + 1)] = x
        acco[h, 8 * (lead + count) :] = jnp.zeros((8, wide), F32)

    for p, gv in enumerate(grads):
        pl.loop(0, 2)(functools.partial(right_row, gv, p))
    size = back + cols
    for h in range(rows):
        both[h * size : (h + 1) * size] = (acce[h] + acco[h, STEP : STEP + size]).astype(BF16)
    whole = dot(both[...], channel_table(channels, group_size, True)).astype(BF16)
    half = cols // 2
    for h in range(rows):
        at = h * size + back
        rg2[h] = whole[at - cols - half : at - cols]
        rg1[h] = whole[at - cols : at]
        rg0[h] = whole[at : at + cols]


def left_kernel(fr, fr4, *rest):
    *grads, lg, accl = rest
    rows, cols, channels = lg.shape
    disp, wide = grads[0].shape[1], fr.shape[2]
    group_size = wide // SLOT
    reach = fr.shape[1] - cols - PAD
    count, times, lots = cols // 8, disp // 2, wide // 128

    def left_row(gv, p, hh):
        h = 2 * p + hh
        accs = [[None] * lots for _ in range(count)]
        for odd, band in enumerate((fr, fr4)):
            for r in range(1 - times, count):
                at = reach + 8 * r
                here = [band[h, at : at + 8, 128 * j : 128 * (j + 1)] for j in range(lots)]
                for t in range(max(0, -r), min(times, count - r)):
                    g = gv[hh, 2 * t + odd, 8 * (r + t) : 8 * (r + t) + 8]
                    for j in range(lots):
                        term, acc = g * here[j], accs[r + t][j]
                        accs[r + t][j] = term if acc is None else acc + term
        for b in range(count):
            for j in range(lots):
                accl[h, 8 * b : 8 * b + 8, 128 * j : 128 * (j + 1)] = accs[b][j] * (1.0 / group_size)

    for p, gv in enumerate(grads):
        pl.loop(0, 2)(functools.partial(left_row, gv, p))
    whole = accl[...].reshape(rows * cols, wide).astype(BF16)
    out = dot(whole, channel_table(channels, group_size, True)).astype(BF16)
    lg[...] = out.reshape(rows, cols, channels)


def combine_kernel(got, rg2, out):
    cols = out.shape[1]
    half = cols // 2
    part = jnp.where(parity() == 0, 0.0, got[...].astype(F32))
    out[:, 0:half] = part[:, 0:half].astype(BF16)
    out[:, half:] = (part[:, half:] + rg2[...].astype(F32)).astype(BF16)


def halo_lanes(groups):
    first = SLOT - groups
    assert groups - first <= first
    return (groups, SLOT, groups), (SLOT + groups, SLOT + 2 * groups - first, SLOT + groups - first)


def place_halo(base, row, groups, offset, lane):
    for start, end, shift in halo_lanes(groups):
        moved = pltpu.roll(row, (shift - offset) % 128, 1)
        base = jnp.where((lane >= start) & (lane < end), moved, base)
    return base


def conv_kernel(masks, groups, vbuf, top, bot, wc, out, taps, buf, held, sems):
    disp, rows, feat, cols = out.shape
    total = buf.shape[2]
    lane = lanes((total, 128))
    zeros = jnp.zeros((cols, taps.shape[3]), BF16)
    taps[0, 0] = zeros
    taps[disp // 2, 1] = zeros
    halos_of = [(ref, mask) for ref, mask in zip((top, bot), masks())]

    def build(dd):
        for p, (ref, mask) in enumerate(halos_of):
            row = ref[dd * total : (dd + 1) * total].astype(F32) * mask
            for o in range(2):
                d = 2 * dd + o
                buf[p, d] = place_halo(vbuf[p, d], row, groups, SLOT * o, lane)
                for e in range(3):
                    at = 256 * e + 128 * p
                    taps[(d + 1) // 2, (d + 1) % 2, :, at : at + 128] = buf[
                        p, d, PAD - 1 + e : PAD - 1 + e + cols
                    ].astype(BF16)

    parts = sems.shape[0]
    step = disp // 2 // parts
    copies = []
    build(0)
    for q in range(parts):
        for dd in range(q * step + 1, min((q + 1) * step + 1, disp // 2)):
            build(dd)
        slabs = [
            taps[q * step + s // 2 : q * step + s // 2 + step, s % 2].reshape(step * cols, taps.shape[3])
            for s in range(4)
        ]
        acc = dot(jnp.concatenate(slabs, axis=1), wc[...])
        for j in range(step):
            both = acc[j * cols : (j + 1) * cols].T.astype(BF16)
            for o in range(2):
                block = both[rows * feat * o : rows * feat * (o + 1)]
                held[2 * (q * step + j) + o] = block.reshape(rows, feat, cols)
        at = pl.ds(2 * q * step, 2 * step)
        copies.append(pltpu.make_async_copy(held.at[at], out.at[at], sems.at[q]))
        copies[-1].start()
    for copy in copies:
        copy.wait()


def finish_kernel(scale, mine, other, own, near, far, left, weight, right, left_out, held_w, held_r, sems):
    _, _, _, feat, groups = weight.shape
    copies = [pltpu.make_async_copy(left, left_out, sems.at[0])]
    copies[0].start()
    is_even = parity() == 0
    beside = jnp.where(is_even, near[...].astype(F32), 0.0)
    held_r[...] = (own[...].astype(F32) + beside + far[...].astype(F32)).astype(BF16)
    copies.append(pltpu.make_async_copy(held_r, right, sems.at[1]))
    copies[1].start()
    x, y = mine[...] * scale, other[...] * scale
    total = jnp.concatenate([jnp.where(is_even, x, y), jnp.where(is_even, y, x)], axis=0)
    for a in range(3):
        for e in range(3):
            at = 128 * a + groups * e
            block = total[at : at + groups].T
            for b in range(3):
                held_w[2 - a, 2 - b, 2 - e] = block[feat * b : feat * (b + 1)]
        copies.append(pltpu.make_async_copy(held_w.at[2 - a], weight.at[2 - a], sems.at[2 + a]))
        copies[-1].start()
    for copy in copies:
        copy.wait()


def copy_kernel(*refs):
    half = len(refs) // 2
    for src, dst in zip(refs[:half], refs[half:]):
        dst[...] = src[...]


def sum_kernel(*refs):
    *parts, out = refs
    out[...] = tree([ref[...].astype(F32) for ref in parts]).astype(out.dtype)


def tree(terms):
    while len(terms) > 1:
        terms = [terms[i] + terms[i + 1] for i in range(0, len(terms), 2)]
    return terms[0]


def taps_kernel(taps, w2, wc, turned):
    _, _, _, feat, groups = taps.shape
    rows = wc.shape[1] // 2 // feat
    lane_of = lanes((feat, 2 * SLOT))
    low = lanes((feat, 2 * SLOT)) < SLOT
    zero = jnp.zeros((feat, 2 * SLOT), F32)

    def wide(a, b, e):
        if not 0 <= b <= 2:
            return None
        return jnp.concatenate([taps[a, b, e].astype(F32), zero[:, groups:]], axis=1)

    def beside(x, y):
        if x is None and y is None:
            return zero
        x = zero if x is None else x
        y = zero if y is None else pltpu.roll(y, SLOT, 1)
        return jnp.where(low, x, y)

    def build(a, _):
        def at_row(h):
            return pl.multiple_of((a * rows + h) * feat, feat)

        for e in range(3):
            for h in range(rows):
                for p in range(rows // 2):
                    lane = SLOT * (rows * e + 2 * p)
                    block = beside(wide(a, 2 * p - h + 1, e), wide(a, 2 * p + 1 - h + 1, e))
                    if h == 0 and p == 0:
                        block = place_halo(block, wide(a, 0, e), groups, 0, lane_of)
                    if h == rows - 1 and p == rows // 2 - 1:
                        block = place_halo(block, wide(a, 2, e), groups, 0, lane_of)
                    turned[pl.ds(at_row(h), feat), lane : lane + 2 * SLOT] = block
        return 0

    lax.fori_loop(0, 3, build, 0)
    for s in range(4):
        for e in range(3):
            for r in range(4):
                for o in range(2):
                    taps_of = [None if not 0 <= s - o <= 2 else wide(2 - s + o, 2 - r + i, 2 - e) for i in range(2)]
                    at = 384 * s + 128 * e + feat * r
                    w2[at : at + feat, 128 * o : 128 * (o + 1)] = beside(*taps_of).astype(BF16)
    depth, size = turned.shape[1], rows * feat
    for a in range(3):
        for i in range(depth // 128):
            x = turned[size * a : size * (a + 1), 128 * i : 128 * (i + 1)].T.astype(BF16)
            for o in range(2):
                at = depth * (a + o) + 128 * i
                wc[at : at + 128, size * o : size * (o + 1)] = x
    for o in range(2):
        at = depth * 3 * (1 - o)
        wc[at : at + depth, size * o : size * (o + 1)] = jnp.zeros((depth, size), BF16)


TOKEN = ((8, 128), F32)


def with_token(kernel, inputs, outputs):
    def run(*refs):
        kernel(*refs[: inputs + outputs], *refs[inputs + outputs + 1 :])
        refs[inputs + outputs][...] = jnp.zeros(TOKEN[0], F32)

    return run


def call(kernel, outs, scratch, *args, after=(), token=False, us=0.0, alias=(), hbm=()):
    skip = len(after)
    if token:
        kernel = with_token(kernel, len(args), len(outs))
        outs = [*outs, TOKEN]
    return pl.pallas_call(
        lambda *refs: kernel(*refs[skip:]),
        out_shape=[jax.ShapeDtypeStruct(s, t) for s, t in outs],
        in_specs=[pl.BlockSpec(memory_space=pl.ANY)] * skip + [VMEM] * len(args),
        out_specs=[pl.BlockSpec(memory_space=pl.ANY) if i in hbm else VMEM for i in range(len(outs))],
        scratch_shapes=scratch,
        input_output_aliases={skip + i: o for i, o in alias},
        compiler_params=pltpu.CompilerParams(vmem_limit_bytes=LIMIT),
        cost_estimate=pl.CostEstimate(
            flops=int(us * 1.15e9), bytes_accessed=int(us * 3.7e6), transcendentals=0
        ),
    )(*after, *args)


def col_shift(block, distance):
    n = lax.axis_size("col")
    route = [(i - distance, i) for i in range(n) if 0 <= i - distance < n]
    return lax.ppermute(block, "col", route)


def row_shift(block, distance):
    n = lax.axis_size("row")
    route = [(i - distance, i) for i in range(n) if 0 <= i - distance < n]
    return lax.ppermute(block, "row", route)


def halos(pays):
    if lax.axis_size("row") == 2:
        got = lax.ppermute(pays[0], "row", [(0, 1), (1, 0)])
        return got, got
    return row_shift(pays[0], 1), row_shift(pays[1], -1)


def stages(n_row, n_col):
    col_bits = [1 << i for i in range(1, n_col.bit_length() - 1)]
    row_bits = [n_col << i for i in range(n_row.bit_length() - 1)]
    assert n_col == 2 << len(col_bits) and n_row == 1 << len(row_bits)
    bits = col_bits + row_bits
    pairs = [bits[i : i + 2] for i in range(0, len(bits), 2)]
    return [pair + [sum(pair)] if len(pair) == 2 else pair for pair in pairs]


def on_device(left_features, right_features, conv_weight, cotangent):
    rows, cols, channels = left_features.shape
    disp, feat = cotangent.shape[0], cotangent.shape[3]
    groups = conv_weight.shape[3]
    group_size = channels // groups
    wide = group_size * SLOT
    n_row, n_col = lax.axis_size("row"), lax.axis_size("col")
    per = 128 // feat

    if n_row == 2:
        ends = [lambda: (rows - 1) * (1 - lax.axis_index("row"))]
    else:
        ends = [lambda: rows - 1, lambda: 0]
    n = len(ends)

    def masks():
        at = lax.axis_index("row")
        return (
            jnp.where(at > 0, 1.0, 0.0).astype(F32),
            jnp.where(at < n_row - 1, 1.0, 0.0).astype(F32),
        )

    total = cols + 2 * PAD
    count = disp + 2 * rows
    ct = cotangent.transpose(0, 1, 3, 2)

    def swap(block, mask):
        route = [(i, i ^ mask) for i in range(n_row * n_col)]
        return lax.ppermute(block, ("row", "col"), route)

    far = col_shift(right_features, 2)
    (begun,) = call(begin_kernel, [TOKEN], [], us=3.0)
    by_even, by_odd, ctl, *rims = call(
        functools.partial(pack_kernel, ends),
        [
            ((count, channels), BF16),
            ((count, channels), BF16),
            ((disp, cols, rows * feat), BF16),
        ]
        + [((disp // per, cols, 128), BF16)] * n,
        [pltpu.VMEM((disp * cols, rows * feat), F32)],
        left_features,
        right_features,
        ct,
        after=[begun],
        us=0.4,
    )
    inner = range(1, n_col - 1, 2)
    by_even = swap(by_even, 1)
    by_odd = lax.ppermute(by_odd, "col", [(i, i + 1) for i in inner] + [(i + 1, i) for i in inner])
    (passed,) = call(
        pass_kernel, [((rows, cols, channels), BF16)], [], right_features, far, after=[ctl]
    )
    near = swap(passed, 1)
    top, bot = halos(rims)
    band = 104 + cols + PAD
    banks = [((rows, total, wide), F32), ((rows, band, wide), F32), ((rows, band, wide), F32)]
    spread_rows = 2 * rows * cols + rows * cols // 2
    fl, fr, fr4 = call(
        functools.partial(own_kernel, group_size),
        banks,
        [pltpu.VMEM((spread_rows, channels), BF16), pltpu.VMEM((spread_rows, wide), F32)],
        left_features,
        right_features,
        far,
        after=[passed],
    )
    corner_pays = call(
        functools.partial(corner_kernel, ends, rows, disp),
        [((16, 128), BF16)] * n,
        [pltpu.VMEM((2, disp, 128), F32), pltpu.VMEM((16, 128), F32)],
        by_even,
        by_odd,
        after=[fl],
        us=5.0,
    )
    tops, bots = halos(corner_pays)
    spread_rows = rows * cols + 2 * count
    fl, fr, fr4, vbuf, *volume_rows = call(
        functools.partial(volume_kernel, ends, group_size),
        banks
        + [((rows // 2, disp, total, 2 * SLOT), F32)]
        + [((disp // 2 * total, 128), BF16)] * n,
        [pltpu.VMEM((spread_rows, channels), BF16), pltpu.VMEM((spread_rows, wide), F32)],
        near,
        by_even,
        by_odd,
        fl,
        fr,
        fr4,
        us=1.8,
        alias=[(3, 0), (4, 1), (5, 2)],
    )
    vtop, vbot = halos(volume_rows)
    keep, give, ctsh = call(
        functools.partial(weight_kernel, masks, groups, feat),
        [((3 * 64, 128), F32), ((3 * 64, 128), F32), ((disp // 2 + 1, 2, cols, 3 * 256), BF16)],
        [
            pltpu.VMEM((rows // 2, 128, (disp // 2 + 2) * 128), BF16),
            pltpu.VMEM((disp, total, 256), F32),
            pltpu.VMEM((3 * 128, 128), F32),
        ],
        vbuf, ctl, by_even, by_odd, top, bot, tops, bots,
        us=2.0,
    )

    got = swap(give, 1)
    w2, wc = call(
        taps_kernel,
        [((12 * 128, 2 * 128), BF16), ((4 * 3 * rows * SLOT, 2 * rows * feat), BF16)],
        [pltpu.VMEM((3 * rows * feat, 3 * rows * SLOT), F32)],
        conv_weight.transpose(0, 1, 2, 4, 3),
        after=[keep],
    )
    (part,) = call(sum_kernel, [(keep.shape, BF16)], [], keep, got, after=[w2])
    grads = call(
        dgrad_kernel, [((2, disp, cols, 128), F32)] * (rows // 2), [], ctsh, w2, after=[part], us=0.2
    )
    rg0, rg1, rg2 = call(
        right_kernel,
        [
            ((rows, cols, channels), BF16),
            ((rows, cols, channels), BF16),
            ((rows, cols // 2, channels), BF16),
        ],
        [
            pltpu.VMEM((rows, cols + cols + cols // 2, wide), F32),
            pltpu.VMEM((rows, cols + cols + cols // 2 + 8, wide), F32),
            pltpu.VMEM((rows * (cols + cols + cols // 2), wide), BF16),
        ],
        fl, *grads,
        us=0.2,
    )
    rg1 = swap(rg1, 1)
    *middle, final = stages(n_row, n_col)
    order = [rg0, vtop]
    for stage in middle:
        parts = [part] + [swap(part, m) for m in stage]
        (part,) = call(sum_kernel, [(part.shape, BF16)], [], *parts, after=order, us=4.0)
        order = []
    parts = [part] + [swap(part, m) for m in final]
    (rg2,) = call(
        combine_kernel, [((rows, cols, channels), BF16)], [], rg1, rg2, after=[part]
    )
    output, conv_done = call(
        functools.partial(conv_kernel, masks, groups),
        [((disp, rows, feat, cols), BF16)],
        [
            pltpu.VMEM((disp // 2 + 1, 2, cols, 3 * rows * SLOT), BF16),
            pltpu.VMEM((rows // 2, disp, total, 128), F32),
            pltpu.VMEM((disp, rows, feat, cols), BF16),
            pltpu.SemaphoreType.DMA((3,)),
        ],
        vbuf, vtop, vbot, wc,
        after=[rg2],
        token=True,
        us=3.0,
        hbm=[0],
    )
    (part,) = call(sum_kernel, [(part.shape, F32)], [], *parts, after=[conv_done], us=4.0)
    (lg,) = call(
        left_kernel,
        [((rows, cols, channels), BF16)],
        [pltpu.VMEM((rows, cols, wide), F32)],
        fr, fr4, *grads,
        after=[part],
        us=1.9,
    )
    rg2 = col_shift(rg2, -2)
    cells = disp * rows * n_row * cols * n_col
    weight_grad, right_grad, left_grad = call(
        functools.partial(finish_kernel, 1.0 / math.sqrt(cells)),
        [
            ((3, 3, 3, feat, groups), F32),
            ((rows, cols, channels), BF16),
            ((rows, cols, channels), BF16),
        ],
        [
            pltpu.VMEM((3, 3, 3, feat, groups), F32),
            pltpu.VMEM((rows, cols, channels), BF16),
            pltpu.SemaphoreType.DMA((5,)),
        ],
        part, swap(part, 1), rg0, rg1, rg2, lg,
        us=1.0,
        hbm=[0, 1, 2],
    )
    return (
        output.transpose(0, 1, 3, 2),
        weight_grad.transpose(0, 1, 2, 4, 3),
        left_grad,
        right_grad,
    )


def solution(mesh):
    in_specs = (P("row", "col", None), P("row", "col", None), P(), P(None, "row", "col", None))
    out_specs = (P(None, "row", "col", None), P(), P("row", "col", None), P("row", "col", None))
    return jax.shard_map(
        on_device, mesh=mesh, in_specs=in_specs, out_specs=out_specs, check_vma=False
    )
```

```python
import functools
import math

import jax
import jax.numpy as jnp
from jax import lax
from jax.experimental import pallas as pl
from jax.experimental.pallas import tpu as pltpu
from jax.sharding import PartitionSpec as P

DISP = 24
STEP = 4
SLOT = 64
PAD = 8
F32 = jnp.float32
BF16 = jnp.bfloat16
VMEM = pl.BlockSpec(memory_space=pltpu.VMEM)
LIMIT = 16 * 1024 * 1024


def lanes(shape):
    return lax.broadcasted_iota(jnp.int32, shape, len(shape) - 1)


def channel_table(channels, group_size, flip, value=1.0):
    shape = (group_size * SLOT, channels) if flip else (channels, group_size * SLOT)
    c = lax.broadcasted_iota(jnp.int32, shape, 1 if flip else 0)
    j = lax.broadcasted_iota(jnp.int32, shape, 0 if flip else 1)
    hit = c == (j & (SLOT - 1)) * group_size + (j >> (SLOT.bit_length() - 1))
    return jnp.where(hit, value, 0.0).astype(BF16)


def parity():
    return lax.rem(lax.axis_index("col"), 2)


def dot(a, b):
    return jnp.dot(a, b, preferred_element_type=F32)


def dot_nt(a, b):
    return lax.dot_general(a, b, (((1,), (1,)), ((), ())), preferred_element_type=F32)


def begin_kernel(out):
    out[...] = jnp.zeros(out.shape, F32)


def pack_kernel(ends, left, right, ct, even, odd, ctl, *rest):
    rims, ctf = rest[:-1], rest[-1]
    disp, rows, feat, cols = ct.shape
    per = 128 // feat
    for d in range(disp):
        block = ct[d].reshape(rows * feat, cols).astype(F32).T
        ctf[d * cols : (d + 1) * cols] = block
        ctl[d] = block.astype(BF16)
    columns = []
    for i, col in enumerate((cols - 1, 0)):
        block = ctf[pl.ds(col, disp, stride=cols), :]
        block = jnp.concatenate([block, jnp.zeros((disp, even.shape[1] - rows * feat), F32)], axis=1)
        edge = [x[h, col : col + 1].astype(F32) for x in (left, right) for h in range(rows)]
        columns.append(jnp.concatenate([block, *edge], axis=0))
    is_even = parity() == 0
    even[...] = jnp.where(is_even, columns[0], columns[1]).astype(BF16)
    odd[...] = jnp.where(is_even, columns[1], columns[0]).astype(BF16)
    for end, rim in zip(ends, rims):
        h = end()
        for q in range(disp // per):
            block = [ct[q * per + i, h].astype(F32) for i in range(per)]
            rim[q] = jnp.concatenate(block, axis=0).T.astype(BF16)


def pass_kernel(own, got, out):
    out[...] = jnp.where(parity() == 0, own[...].astype(F32), got[...].astype(F32)).astype(BF16)


def end_columns(by_even, by_odd):
    x, y = by_even[...].astype(F32), by_odd[...].astype(F32)
    is_even = parity() == 0
    return jnp.where(is_even, y, x), jnp.where(is_even, x, y)


def corner_kernel(ends, rows, disp, by_even, by_odd, *rest):
    pays, (edges, buf) = rest[: len(ends)], rest[len(ends) :]
    feat = 128 // rows
    per = 128 // feat
    count = disp // per
    lane = lanes((count, 128))
    for side, x in enumerate(end_columns(by_even, by_odd)):
        edges[side] = x[0:disp, 0:128]
    for end, pay in zip(ends, pays):
        h = end()
        buf[...] = jnp.zeros(buf.shape, F32)
        for side in range(2):
            out = jnp.zeros((count, 128), F32)
            for i in range(per):
                x = edges[side, pl.ds(i, count, stride=per)]
                first = pltpu.roll(x, feat * i, 1) if i else x
                last = pltpu.roll(x, (feat * (i - rows + 1)) % 128, 1) if i != rows - 1 else x
                x = jnp.where(h == 0, first, last)
                out = jnp.where((lane >= feat * i) & (lane < feat * (i + 1)), x, out)
            buf[8 * side : 8 * side + count] = out
        pay[...] = buf[...].astype(BF16)


def put_band(refs, h, column, block):
    fr, fr4, cols = refs
    at = fr.shape[1] - cols - PAD + column
    fr[h, at : at + block.shape[0]] = block
    fr4[h, at + STEP : at + STEP + block.shape[0]] = block


def own_kernel(group_size, left, right, far, fl, fr, fr4, mixed, wide_buf):
    rows, cols, channels = left.shape
    base, half, wide = rows * cols, cols // 2, group_size * SLOT
    mixed[0:base] = right[...].reshape(base, channels)
    mixed[base : 2 * base] = left[...].reshape(base, channels)
    mixed[2 * base :] = far[:, half:].reshape(base // 2, channels)
    wide_buf[...] = dot(mixed[...], channel_table(channels, group_size, False))
    tail = fr.shape[1]
    for h in range(rows):
        for ref in (fr, fr4):
            ref[h, 0:16] = jnp.zeros((16, wide), F32)
            ref[h, tail - 16 :] = jnp.zeros((16, wide), F32)
        put_band((fr, fr4, cols), h, -cols - half, wide_buf[2 * base + h * half : 2 * base + (h + 1) * half])
        put_band((fr, fr4, cols), h, 0, wide_buf[h * cols : (h + 1) * cols])
        fl[h, 0:PAD] = jnp.zeros((PAD, wide), F32)
        fl[h, PAD + cols :] = jnp.zeros((PAD, wide), F32)
        fl[h, PAD : PAD + cols] = wide_buf[base + h * cols : base + (h + 1) * cols] * (1.0 / group_size)


def volume_kernel(ends, group_size, near, by_even, by_odd, _fl, _fr, _fr4, fl, fr, fr4, vbuf, *rest):
    pays, (mixed, wide_buf) = rest[: len(ends)], rest[len(ends) :]
    rows, cols, channels = near.shape
    disp = vbuf.shape[1]
    reach = fr.shape[1] - cols - PAD
    wide = group_size * SLOT
    base = rows * cols
    mixed[0:base] = near[...].reshape(base, channels)
    count = disp + 2 * rows
    for i, x in enumerate(end_columns(by_even, by_odd)):
        mixed[base + i * count : base + (i + 1) * count] = x.astype(BF16)
    wide_buf[...] = dot(mixed[...], channel_table(channels, group_size, False))
    for h in range(rows):
        put_band((fr, fr4, cols), h, -cols, wide_buf[h * cols : (h + 1) * cols])
        at = base + disp + h
        fl[h, PAD - 1 : PAD] = wide_buf[at : at + 1] * (1.0 / group_size)
        at += count
        fl[h, PAD + cols : PAD + cols + 1] = wide_buf[at : at + 1] * (1.0 / group_size)
        put_band((fr, fr4, cols), h, cols, wide_buf[at + rows : at + rows + 1])
    total = cols + 2 * PAD
    low = lanes((8, 128)) < SLOT
    pairs, times, lots = rows // 2, disp // 2, wide // 128
    count = total // 16

    def products(i, _):
        p, at = lax.rem(i, pairs), pl.multiple_of(lax.div(i, pairs) * (8 * count), 8)
        lefts = [
            [
                [fl[2 * p + o, pl.ds(at + 8 * b, 8), 128 * j : 128 * (j + 1)] for j in range(lots)]
                for b in range(count)
            ]
            for o in range(2)
        ]
        for odd, band in enumerate((fr, fr4)):
            for r in range(1 - times, count):
                start = pl.multiple_of(at + reach - PAD + 8 * r, 8)
                here = [
                    [band[2 * p + o, pl.ds(start, 8), 128 * j : 128 * (j + 1)] for j in range(lots)]
                    for o in range(2)
                ]
                for t in range(max(0, -r), min(times, count - r)):
                    sums = []
                    for o in range(2):
                        acc = lefts[o][r + t][0] * here[o][0]
                        for j in range(1, lots):
                            acc = acc + lefts[o][r + t][j] * here[o][j]
                        sums.append(acc + pltpu.roll(acc, SLOT, 1))
                    vbuf[p, 2 * t + odd, pl.ds(at + 8 * (r + t), 8)] = jnp.where(low, *sums)
        return 0

    lax.fori_loop(0, 2 * pairs, products, 0)
    big = lanes((total, 128)) < SLOT

    for dd in range(disp // 2):
        for end, pay in zip(ends, pays):
            h = end()
            if isinstance(h, int):
                halves = [vbuf[h // 2, 2 * dd + o] for o in range(2)]
                if h % 2 == 0:
                    halves[1] = pltpu.roll(halves[1], SLOT, 1)
                else:
                    halves[0] = pltpu.roll(halves[0], SLOT, 1)
                out = jnp.where(big, halves[0], halves[1])
            else:
                last = pairs - 1
                first = jnp.where(big, vbuf[0, 2 * dd], pltpu.roll(vbuf[0, 2 * dd + 1], SLOT, 1))
                final = jnp.where(
                    big, pltpu.roll(vbuf[last, 2 * dd], SLOT, 1), vbuf[last, 2 * dd + 1]
                )
                out = jnp.where(h == 0, first, final)
            pay[dd * total : (dd + 1) * total] = out.astype(BF16)


def weight_kernel(
    masks, groups, feat, vbuf, ctl, by_even, by_odd, top, bot, tops, bots, *rest
):
    keep_out, give_out, ctsh, vt, buf, sums = rest
    disp, cols, width = ctl.shape
    pairs, per, half = vbuf.shape[0], 128 // feat, disp // 2
    mtop, mbot = masks()
    ctsh[0, 0] = jnp.zeros(ctsh.shape[2:], BF16)
    ctsh[half, 1] = jnp.zeros(ctsh.shape[2:], BF16)
    lane_in, lane_one = lanes((cols, 128)), lanes((1, 128))
    shifts = (feat, 128 - feat)
    edges = [x[0:disp, 0:128] for x in end_columns(by_even, by_odd)]
    turned = [[pltpu.roll(x, shift, 1) for shift in shifts] for x in edges]

    def aligned(t, z, i):
        return (
            t if i == 0 else pltpu.roll(t, 128 - feat * i, 1),
            z if i == per - 1 else pltpu.roll(z, feat * (per - 1 - i), 1),
        )

    corners = [aligned(tops[...].astype(F32) * mtop, bots[...].astype(F32) * mbot, i) for i in range(per)]

    def fill(q):
        t = top[q].astype(F32) * mtop
        z = bot[q].astype(F32) * mbot
        for i in range(per):
            d = q * per + i
            rims = aligned(t, z, i)
            inner = ctl[d].astype(F32)
            for p, (rim, shift) in enumerate(zip(rims, shifts)):

                def on_rim(x):
                    return x < feat if p == 0 else x >= 128 - feat

                at = slice(128 * p, 128 * (p + 1))
                buf[d, PAD : PAD + cols, at] = jnp.where(
                    on_rim(lane_in), rim, pltpu.roll(inner, shift, 1)
                )
                for side, row in enumerate((PAD - 1, PAD + cols)):
                    corner = corners[i][p][8 * side + q : 8 * side + q + 1]
                    buf[d, row : row + 1, at] = jnp.where(
                        on_rim(lane_one), corner, turned[side][p][d : d + 1]
                    )
            for e in range(3):
                ctsh[(d + 1) // 2, (d + 1) % 2, :, 256 * e : 256 * (e + 1)] = buf[
                    d, PAD - 1 + e : PAD - 1 + e + cols
                ].astype(BF16)

    none = jnp.zeros((cols, 128), F32)
    for p in range(pairs):
        for j in range(-1, half + 1):
            block = [
                vbuf[p, d, PAD : PAD + cols] if 0 <= d < disp and 0 <= j + half * o else none
                for o, d in enumerate((j, j + half))
            ]
            if j == half:
                block[1] = none
            x = jnp.concatenate(block, axis=0).astype(BF16)
            vt[p, :, 128 * (j + 1) : 128 * (j + 2)] = x.T
    full = None
    for q in range(half // per):
        fill(q)
        fill(q + half // per)
        first, size = q * per, per * 128
        left = jnp.concatenate(
            [
                jnp.concatenate(
                    [vt[p, :, 128 * (2 - a + first) : 128 * (2 - a + first) + size] for p in range(pairs)],
                    axis=1,
                )
                for a in range(3)
            ],
            axis=0,
        )
        right = jnp.concatenate(
            [
                jnp.concatenate(
                    [
                        ctsh[(d + 1) // 2, (d + 1) % 2, :, 256 * e + 128 * p : 256 * e + 128 * (p + 1)]
                        for e in range(3)
                    ],
                    axis=1,
                )
                for p in range(pairs)
                for j in range(first, first + per)
                for d in (j, j + half)
            ],
            axis=0,
        )
        part = dot(left, right)
        full = part if full is None else full + part
    keep = lanes((groups, 128)) < 3 * feat
    sums[...] = jnp.zeros(sums.shape, F32)
    for a in range(3):
        for e in range(3):
            block = full[128 * a : 128 * (a + 1), 128 * e : 128 * (e + 1)]
            out = block[0:groups] + pltpu.roll(block[SLOT : SLOT + groups], 128 - feat, 1)
            at = 128 * a + groups * e
            sums[at : at + groups] = jnp.where(keep, out, 0.0)
    half = sums.shape[0] // 2
    is_even = parity() == 0
    low, high = sums[0:half], sums[half:]
    keep_out[...] = jnp.where(is_even, low, high)
    give_out[...] = jnp.where(is_even, high, low)


def right_kernel(ctsh, w2, fl, *rest):
    *grads, rg0, rg1, rg2, acce, acco, both = rest
    rows, cols, channels = rg0.shape
    disp, wide = grads[0].shape[1], fl.shape[2]
    group_size = wide // SLOT
    step = disp // 4
    low = lanes((step * cols, 128)) < SLOT

    def conv(q, p, gv):
        slabs = [
            ctsh[pl.ds(q * step + s // 2, step), s % 2, :, 256 * e + 128 * p : 256 * e + 128 * (p + 1)]
            for s in range(4)
            for e in range(3)
        ]
        slabs = [x.reshape(step * cols, 128) for x in slabs]
        acc = dot(jnp.concatenate(slabs, axis=1), w2[...]).astype(BF16).astype(F32)
        for o in range(2):
            x = acc[:, 128 * o : 128 * (o + 1)]
            r = pltpu.roll(x, SLOT, 1)
            for hh in range(2):
                y = jnp.where(low, r, x) if hh else jnp.where(low, x, r)
                for j in range(step):
                    gv[hh, 2 * (q * step + j) + o] = y[j * cols : (j + 1) * cols]

    count = cols // 8
    back = acce.shape[1] - cols
    lead = back // 8

    lots = wide // 128

    def right_row(gv, p, hh):
        h = 2 * p + hh
        here = [
            [fl[h, PAD + 8 * b : PAD + 8 * b + 8, 128 * j : 128 * (j + 1)] for j in range(lots)]
            for b in range(count)
        ]
        for odd, buf in enumerate((acce, acco)):
            for k in range(lead + count):
                accs = [None] * lots
                for t in range(disp // 2):
                    b = k + t - lead
                    if b < 0 or b >= count:
                        continue
                    g = gv[hh, 2 * t + odd, 8 * b : 8 * b + 8]
                    for j in range(lots):
                        term = g * here[b][j]
                        accs[j] = term if accs[j] is None else accs[j] + term
                for j in range(lots):
                    x = jnp.zeros((8, 128), F32) if accs[j] is None else accs[j]
                    buf[h, 8 * k : 8 * k + 8, 128 * j : 128 * (j + 1)] = x
        acco[h, 8 * (lead + count) :] = jnp.zeros((8, wide), F32)

    for p, gv in enumerate(grads):
        for q in range(2):
            conv(q, p, gv)
    for p, gv in enumerate(grads):
        for hh in range(2):
            right_row(gv, p, hh)
    size = back + cols
    for h in range(rows):
        both[h * size : (h + 1) * size] = (acce[h] + acco[h, STEP : STEP + size]).astype(BF16)
    whole = dot(both[...], channel_table(channels, group_size, True)).astype(BF16)
    half = cols // 2
    for h in range(rows):
        at = h * size + back
        rg2[h] = whole[at - cols - half : at - cols]
        rg1[h] = whole[at - cols : at]
        rg0[h] = whole[at : at + cols]


def left_kernel(fr, fr4, *rest):
    *grads, lg, accl = rest
    rows, cols, channels = lg.shape
    disp, wide = grads[0].shape[1], fr.shape[2]
    group_size = wide // SLOT
    reach = fr.shape[1] - cols - PAD
    count, times, lots = cols // 8, disp // 2, wide // 128

    def left_row(gv, p, hh):
        h = 2 * p + hh
        accs = [[None] * lots for _ in range(count)]
        for odd, band in enumerate((fr, fr4)):
            for r in range(1 - times, count):
                at = reach + 8 * r
                here = [band[h, at : at + 8, 128 * j : 128 * (j + 1)] for j in range(lots)]
                for t in range(max(0, -r), min(times, count - r)):
                    g = gv[hh, 2 * t + odd, 8 * (r + t) : 8 * (r + t) + 8]
                    for j in range(lots):
                        term, acc = g * here[j], accs[r + t][j]
                        accs[r + t][j] = term if acc is None else acc + term
        for b in range(count):
            for j in range(lots):
                accl[h, 8 * b : 8 * b + 8, 128 * j : 128 * (j + 1)] = accs[b][j] * (1.0 / group_size)

    for p, gv in enumerate(grads):
        pl.loop(0, 2)(functools.partial(left_row, gv, p))
    whole = accl[...].reshape(rows * cols, wide).astype(BF16)
    out = dot(whole, channel_table(channels, group_size, True)).astype(BF16)
    lg[...] = out.reshape(rows, cols, channels)


def combine_kernel(got, rg2, out):
    cols = out.shape[1]
    half = cols // 2
    part = jnp.where(parity() == 0, 0.0, got[...].astype(F32))
    out[:, 0:half] = part[:, 0:half].astype(BF16)
    out[:, half:] = (part[:, half:] + rg2[...].astype(F32)).astype(BF16)


def halo_lanes(groups):
    first = SLOT - groups
    assert groups - first <= first
    return (groups, SLOT, groups), (SLOT + groups, SLOT + 2 * groups - first, SLOT + groups - first)


def place_halo(base, row, groups, offset, lane):
    for start, end, shift in halo_lanes(groups):
        moved = pltpu.roll(row, (shift - offset) % 128, 1)
        base = jnp.where((lane >= start) & (lane < end), moved, base)
    return base


def conv_kernel(masks, groups, vbuf, top, bot, wc, out, taps, buf, held, sems):
    disp, rows, feat, cols = out.shape
    total = buf.shape[2]
    lane = lanes((total, 128))
    zeros = jnp.zeros((cols, taps.shape[3]), BF16)
    taps[0, 0] = zeros
    taps[disp // 2, 1] = zeros
    halos_of = [(ref, mask) for ref, mask in zip((top, bot), masks())]

    def build(dd):
        for p, (ref, mask) in enumerate(halos_of):
            row = ref[dd * total : (dd + 1) * total].astype(F32) * mask
            for o in range(2):
                d = 2 * dd + o
                buf[p, d] = place_halo(vbuf[p, d], row, groups, SLOT * o, lane)
                for e in range(3):
                    at = 256 * e + 128 * p
                    taps[(d + 1) // 2, (d + 1) % 2, :, at : at + 128] = buf[
                        p, d, PAD - 1 + e : PAD - 1 + e + cols
                    ].astype(BF16)

    parts = sems.shape[0]
    step = disp // 2 // parts
    copies = []
    build(0)
    for q in range(parts):
        for dd in range(q * step + 1, min((q + 1) * step + 1, disp // 2)):
            build(dd)
        slabs = [
            taps[q * step + s // 2 : q * step + s // 2 + step, s % 2].reshape(step * cols, taps.shape[3])
            for s in range(4)
        ]
        acc = dot(jnp.concatenate(slabs, axis=1), wc[...])
        for j in range(step):
            both = acc[j * cols : (j + 1) * cols].T.astype(BF16)
            for o in range(2):
                block = both[rows * feat * o : rows * feat * (o + 1)]
                held[2 * (q * step + j) + o] = block.reshape(rows, feat, cols)
        at = pl.ds(2 * q * step, 2 * step)
        copies.append(pltpu.make_async_copy(held.at[at], out.at[at], sems.at[q]))
        copies[-1].start()
    for copy in copies:
        copy.wait()


def finish_kernel(scale, mine, other, own, near, far, left, weight, right, left_out, held_w, held_r, sems):
    _, _, _, feat, groups = weight.shape
    copies = [pltpu.make_async_copy(left, left_out, sems.at[0])]
    copies[0].start()
    is_even = parity() == 0
    beside = jnp.where(is_even, near[...].astype(F32), 0.0)
    held_r[...] = (own[...].astype(F32) + beside + far[...].astype(F32)).astype(BF16)
    copies.append(pltpu.make_async_copy(held_r, right, sems.at[1]))
    copies[1].start()
    x, y = mine[...] * scale, other[...] * scale
    total = jnp.concatenate([jnp.where(is_even, x, y), jnp.where(is_even, y, x)], axis=0)
    for a in range(3):
        for e in range(3):
            at = 128 * a + groups * e
            block = total[at : at + groups].T
            for b in range(3):
                held_w[2 - a, 2 - b, 2 - e] = block[feat * b : feat * (b + 1)]
        copies.append(pltpu.make_async_copy(held_w.at[2 - a], weight.at[2 - a], sems.at[2 + a]))
        copies[-1].start()
    for copy in copies:
        copy.wait()


def copy_kernel(*refs):
    half = len(refs) // 2
    for src, dst in zip(refs[:half], refs[half:]):
        dst[...] = src[...]


def sum_kernel(*refs):
    *parts, out = refs
    out[...] = tree([ref[...].astype(F32) for ref in parts]).astype(out.dtype)


def tree(terms):
    while len(terms) > 1:
        terms = [terms[i] + terms[i + 1] for i in range(0, len(terms), 2)]
    return terms[0]


def taps_kernel(taps, w2, wc, turned):
    _, _, _, feat, groups = taps.shape
    rows = wc.shape[1] // 2 // feat
    lane_of = lanes((feat, 2 * SLOT))
    low = lanes((feat, 2 * SLOT)) < SLOT
    zero = jnp.zeros((feat, 2 * SLOT), F32)

    def wide(a, b, e):
        if not 0 <= b <= 2:
            return None
        return jnp.concatenate([taps[a, b, e].astype(F32), zero[:, groups:]], axis=1)

    def beside(x, y):
        if x is None and y is None:
            return zero
        x = zero if x is None else x
        y = zero if y is None else pltpu.roll(y, SLOT, 1)
        return jnp.where(low, x, y)

    def build(a, _):
        def at_row(h):
            return pl.multiple_of((a * rows + h) * feat, feat)

        for e in range(3):
            for h in range(rows):
                for p in range(rows // 2):
                    lane = SLOT * (rows * e + 2 * p)
                    block = beside(wide(a, 2 * p - h + 1, e), wide(a, 2 * p + 1 - h + 1, e))
                    if h == 0 and p == 0:
                        block = place_halo(block, wide(a, 0, e), groups, 0, lane_of)
                    if h == rows - 1 and p == rows // 2 - 1:
                        block = place_halo(block, wide(a, 2, e), groups, 0, lane_of)
                    turned[pl.ds(at_row(h), feat), lane : lane + 2 * SLOT] = block
        return 0

    lax.fori_loop(0, 3, build, 0)
    for s in range(4):
        for e in range(3):
            for r in range(4):
                for o in range(2):
                    taps_of = [None if not 0 <= s - o <= 2 else wide(2 - s + o, 2 - r + i, 2 - e) for i in range(2)]
                    at = 384 * s + 128 * e + feat * r
                    w2[at : at + feat, 128 * o : 128 * (o + 1)] = beside(*taps_of).astype(BF16)
    depth, size = turned.shape[1], rows * feat
    for a in range(3):
        for i in range(depth // 128):
            x = turned[size * a : size * (a + 1), 128 * i : 128 * (i + 1)].T.astype(BF16)
            for o in range(2):
                at = depth * (a + o) + 128 * i
                wc[at : at + 128, size * o : size * (o + 1)] = x
    for o in range(2):
        at = depth * 3 * (1 - o)
        wc[at : at + depth, size * o : size * (o + 1)] = jnp.zeros((depth, size), BF16)


TOKEN = ((8, 128), F32)


def with_token(kernel, inputs, outputs):
    def run(*refs):
        kernel(*refs[: inputs + outputs], *refs[inputs + outputs + 1 :])
        refs[inputs + outputs][...] = jnp.zeros(TOKEN[0], F32)

    return run


def call(kernel, outs, scratch, *args, after=(), token=False, us=0.0, alias=(), hbm=()):
    skip = len(after)
    if token:
        kernel = with_token(kernel, len(args), len(outs))
        outs = [*outs, TOKEN]
    return pl.pallas_call(
        lambda *refs: kernel(*refs[skip:]),
        out_shape=[jax.ShapeDtypeStruct(s, t) for s, t in outs],
        in_specs=[pl.BlockSpec(memory_space=pl.ANY)] * skip + [VMEM] * len(args),
        out_specs=[pl.BlockSpec(memory_space=pl.ANY) if i in hbm else VMEM for i in range(len(outs))],
        scratch_shapes=scratch,
        input_output_aliases={skip + i: o for i, o in alias},
        compiler_params=pltpu.CompilerParams(vmem_limit_bytes=LIMIT),
        cost_estimate=pl.CostEstimate(
            flops=int(us * 1.15e9), bytes_accessed=int(us * 3.7e6), transcendentals=0
        ),
    )(*after, *args)


def col_shift(block, distance):
    n = lax.axis_size("col")
    route = [(i - distance, i) for i in range(n) if 0 <= i - distance < n]
    return lax.ppermute(block, "col", route)


def row_shift(block, distance):
    n = lax.axis_size("row")
    route = [(i - distance, i) for i in range(n) if 0 <= i - distance < n]
    return lax.ppermute(block, "row", route)


def halos(pays):
    if lax.axis_size("row") == 2:
        got = lax.ppermute(pays[0], "row", [(0, 1), (1, 0)])
        return got, got
    return row_shift(pays[0], 1), row_shift(pays[1], -1)


def partners(n_row, n_col):
    col_bits = [1 << i for i in range(1, n_col.bit_length() - 1)]
    row_bits = [n_col << i for i in range(n_row.bit_length() - 1)]
    assert n_col == 2 << len(col_bits) and n_row == 1 << len(row_bits)
    return [*col_bits[:2], sum(col_bits[:2])], col_bits[2:], row_bits


def on_device(left_features, right_features, conv_weight, cotangent):
    rows, cols, channels = left_features.shape
    disp, feat = cotangent.shape[0], cotangent.shape[3]
    groups = conv_weight.shape[3]
    group_size = channels // groups
    wide = group_size * SLOT
    n_row, n_col = lax.axis_size("row"), lax.axis_size("col")
    per = 128 // feat

    if n_row == 2:
        ends = [lambda: (rows - 1) * (1 - lax.axis_index("row"))]
    else:
        ends = [lambda: rows - 1, lambda: 0]
    n = len(ends)

    def masks():
        at = lax.axis_index("row")
        return (
            jnp.where(at > 0, 1.0, 0.0).astype(F32),
            jnp.where(at < n_row - 1, 1.0, 0.0).astype(F32),
        )

    total = cols + 2 * PAD
    count = disp + 2 * rows
    ct = cotangent.transpose(0, 1, 3, 2)

    def swap(block, mask):
        route = [(i, i ^ mask) for i in range(n_row * n_col)]
        return lax.ppermute(block, ("row", "col"), route)

    far = col_shift(right_features, 2)
    (begun,) = call(begin_kernel, [TOKEN], [], us=3.0)
    by_even, by_odd, ctl, *rims = call(
        functools.partial(pack_kernel, ends),
        [
            ((count, channels), BF16),
            ((count, channels), BF16),
            ((disp, cols, rows * feat), BF16),
        ]
        + [((disp // per, cols, 128), BF16)] * n,
        [pltpu.VMEM((disp * cols, rows * feat), F32)],
        left_features,
        right_features,
        ct,
        after=[begun],
        us=0.4,
    )
    inner = range(1, n_col - 1, 2)
    by_even = swap(by_even, 1)
    by_odd = lax.ppermute(by_odd, "col", [(i, i + 1) for i in inner] + [(i + 1, i) for i in inner])
    (passed,) = call(
        pass_kernel, [((rows, cols, channels), BF16)], [], right_features, far, after=[ctl]
    )
    near = swap(passed, 1)
    top, bot = halos(rims)
    band = 104 + cols + PAD
    banks = [((rows, total, wide), F32), ((rows, band, wide), F32), ((rows, band, wide), F32)]
    spread_rows = 2 * rows * cols + rows * cols // 2
    fl, fr, fr4 = call(
        functools.partial(own_kernel, group_size),
        banks,
        [pltpu.VMEM((spread_rows, channels), BF16), pltpu.VMEM((spread_rows, wide), F32)],
        left_features,
        right_features,
        far,
        after=[passed],
    )
    corner_pays = call(
        functools.partial(corner_kernel, ends, rows, disp),
        [((16, 128), BF16)] * n,
        [pltpu.VMEM((2, disp, 128), F32), pltpu.VMEM((16, 128), F32)],
        by_even,
        by_odd,
        after=[fl],
        us=5.0,
    )
    tops, bots = halos(corner_pays)
    spread_rows = rows * cols + 2 * count
    fl, fr, fr4, vbuf, *volume_rows = call(
        functools.partial(volume_kernel, ends, group_size),
        banks
        + [((rows // 2, disp, total, 2 * SLOT), F32)]
        + [((disp // 2 * total, 128), BF16)] * n,
        [pltpu.VMEM((spread_rows, channels), BF16), pltpu.VMEM((spread_rows, wide), F32)],
        near,
        by_even,
        by_odd,
        fl,
        fr,
        fr4,
        us=1.8,
        alias=[(3, 0), (4, 1), (5, 2)],
    )
    vtop, vbot = halos(volume_rows)
    keep, give, ctsh = call(
        functools.partial(weight_kernel, masks, groups, feat),
        [((3 * 64, 128), F32), ((3 * 64, 128), F32), ((disp // 2 + 1, 2, cols, 3 * 256), BF16)],
        [
            pltpu.VMEM((rows // 2, 128, (disp // 2 + 2) * 128), BF16),
            pltpu.VMEM((disp, total, 256), F32),
            pltpu.VMEM((3 * 128, 128), F32),
        ],
        vbuf, ctl, by_even, by_odd, top, bot, tops, bots,
        us=2.0,
    )

    got = swap(give, 1)
    w2, wc = call(
        taps_kernel,
        [((12 * 128, 2 * 128), BF16), ((4 * 3 * rows * SLOT, 2 * rows * feat), BF16)],
        [pltpu.VMEM((3 * rows * feat, 3 * rows * SLOT), F32)],
        conv_weight.transpose(0, 1, 2, 4, 3),
        after=[keep],
    )
    (part,) = call(sum_kernel, [(keep.shape, BF16)], [], keep, got, after=[w2])
    *grads, rg0, rg1, rg2 = call(
        right_kernel,
        [((2, disp, cols, 128), F32)] * (rows // 2)
        + [
            ((rows, cols, channels), BF16),
            ((rows, cols, channels), BF16),
            ((rows, cols // 2, channels), BF16),
        ],
        [
            pltpu.VMEM((rows, cols + cols + cols // 2, wide), F32),
            pltpu.VMEM((rows, cols + cols + cols // 2 + 8, wide), F32),
            pltpu.VMEM((rows * (cols + cols + cols // 2), wide), BF16),
        ],
        ctsh, w2, fl,
        after=[part],
        us=0.4,
    )
    rg1 = swap(rg1, 1)
    def join(part, mask, kind, after, us):
        terms = (part, swap(part, mask))
        return call(sum_kernel, [(part.shape, kind)], [], *terms, after=after, us=us)[0]

    three, along_cols, along_rows = partners(n_row, n_col)
    parts = [part] + [swap(part, m) for m in three]
    (part,) = call(sum_kernel, [(part.shape, BF16)], [], *parts, after=[rg0, vtop], us=4.0)
    (rg2,) = call(
        combine_kernel, [((rows, cols, channels), BF16)], [], rg1, rg2, after=[part]
    )
    order = [rg2]
    for mask in along_cols:
        part = join(part, mask, F32, after=order, us=4.0)
        order = []
    output, conv_done = call(
        functools.partial(conv_kernel, masks, groups),
        [((disp, rows, feat, cols), BF16)],
        [
            pltpu.VMEM((disp // 2 + 1, 2, cols, 3 * rows * SLOT), BF16),
            pltpu.VMEM((rows // 2, disp, total, 128), F32),
            pltpu.VMEM((disp, rows, feat, cols), BF16),
            pltpu.SemaphoreType.DMA((3,)),
        ],
        vbuf, vtop, vbot, wc,
        after=[part],
        token=True,
        us=3.0,
        hbm=[0],
    )
    order = [conv_done]
    for mask in along_rows:
        part = join(part, mask, F32, after=order, us=4.0)
        order = []
    (lg,) = call(
        left_kernel,
        [((rows, cols, channels), BF16)],
        [pltpu.VMEM((rows, cols, wide), F32)],
        fr, fr4, *grads,
        after=[part],
        us=1.9,
    )
    rg2 = col_shift(rg2, -2)
    cells = disp * rows * n_row * cols * n_col
    weight_grad, right_grad, left_grad = call(
        functools.partial(finish_kernel, 1.0 / math.sqrt(cells)),
        [
            ((3, 3, 3, feat, groups), F32),
            ((rows, cols, channels), BF16),
            ((rows, cols, channels), BF16),
        ],
        [
            pltpu.VMEM((3, 3, 3, feat, groups), F32),
            pltpu.VMEM((rows, cols, channels), BF16),
            pltpu.SemaphoreType.DMA((5,)),
        ],
        part, swap(part, 1), rg0, rg1, rg2, lg,
        us=1.0,
        hbm=[0, 1, 2],
    )
    return (
        output.transpose(0, 1, 3, 2),
        weight_grad.transpose(0, 1, 2, 4, 3),
        left_grad,
        right_grad,
    )


def solution(mesh):
    in_specs = (P("row", "col", None), P("row", "col", None), P(), P(None, "row", "col", None))
    out_specs = (P(None, "row", "col", None), P(), P("row", "col", None), P("row", "col", None))
    return jax.shard_map(
        on_device, mesh=mesh, in_specs=in_specs, out_specs=out_specs, check_vma=False
    )
```

```python
import functools
import math

import jax
import jax.numpy as jnp
from jax import lax
from jax.experimental import pallas as pl
from jax.experimental.pallas import tpu as pltpu
from jax.sharding import PartitionSpec as P

DISP = 24
STEP = 4
SLOT = 64
PAD = 8
F32 = jnp.float32
BF16 = jnp.bfloat16
VMEM = pl.BlockSpec(memory_space=pltpu.VMEM)
LIMIT = 16 * 1024 * 1024


def lanes(shape):
    return lax.broadcasted_iota(jnp.int32, shape, len(shape) - 1)


def channel_table(channels, group_size, flip, value=1.0):
    shape = (group_size * SLOT, channels) if flip else (channels, group_size * SLOT)
    c = lax.broadcasted_iota(jnp.int32, shape, 1 if flip else 0)
    j = lax.broadcasted_iota(jnp.int32, shape, 0 if flip else 1)
    hit = c == (j & (SLOT - 1)) * group_size + (j >> (SLOT.bit_length() - 1))
    return jnp.where(hit, value, 0.0).astype(BF16)


def parity():
    return lax.rem(lax.axis_index("col"), 2)


def dot(a, b):
    return jnp.dot(a, b, preferred_element_type=F32)


def dot_nt(a, b):
    return lax.dot_general(a, b, (((1,), (1,)), ((), ())), preferred_element_type=F32)


def begin_kernel(out):
    out[...] = jnp.zeros(out.shape, F32)


def pack_kernel(ends, left, right, ct, even, odd, ctl, *rest):
    rims, ctf = rest[:-1], rest[-1]
    disp, rows, feat, cols = ct.shape
    per = 128 // feat
    for d in range(disp):
        block = ct[d].reshape(rows * feat, cols).astype(F32).T
        ctf[d * cols : (d + 1) * cols] = block
        ctl[d] = block.astype(BF16)
    columns = []
    for i, col in enumerate((cols - 1, 0)):
        block = ctf[pl.ds(col, disp, stride=cols), :]
        block = jnp.concatenate([block, jnp.zeros((disp, even.shape[1] - rows * feat), F32)], axis=1)
        edge = [x[h, col : col + 1].astype(F32) for x in (left, right) for h in range(rows)]
        columns.append(jnp.concatenate([block, *edge], axis=0))
    is_even = parity() == 0
    even[...] = jnp.where(is_even, columns[0], columns[1]).astype(BF16)
    odd[...] = jnp.where(is_even, columns[1], columns[0]).astype(BF16)
    for end, rim in zip(ends, rims):
        h = end()
        for q in range(disp // per):
            block = [ct[q * per + i, h].astype(F32) for i in range(per)]
            rim[q] = jnp.concatenate(block, axis=0).T.astype(BF16)


def pass_kernel(own, got, out):
    out[...] = jnp.where(parity() == 0, own[...].astype(F32), got[...].astype(F32)).astype(BF16)


def end_columns(by_even, by_odd):
    x, y = by_even[...].astype(F32), by_odd[...].astype(F32)
    is_even = parity() == 0
    return jnp.where(is_even, y, x), jnp.where(is_even, x, y)


def corner_kernel(ends, rows, disp, by_even, by_odd, *rest):
    pays, (edges, buf) = rest[: len(ends)], rest[len(ends) :]
    feat = 128 // rows
    per = 128 // feat
    count = disp // per
    lane = lanes((count, 128))
    for side, x in enumerate(end_columns(by_even, by_odd)):
        edges[side] = x[0:disp, 0:128]
    for end, pay in zip(ends, pays):
        h = end()
        buf[...] = jnp.zeros(buf.shape, F32)
        for side in range(2):
            out = jnp.zeros((count, 128), F32)
            for i in range(per):
                x = edges[side, pl.ds(i, count, stride=per)]
                first = pltpu.roll(x, feat * i, 1) if i else x
                last = pltpu.roll(x, (feat * (i - rows + 1)) % 128, 1) if i != rows - 1 else x
                x = jnp.where(h == 0, first, last)
                out = jnp.where((lane >= feat * i) & (lane < feat * (i + 1)), x, out)
            buf[8 * side : 8 * side + count] = out
        pay[...] = buf[...].astype(BF16)


def put_band(refs, h, column, block):
    fr, fr4, cols = refs
    at = fr.shape[1] - cols - PAD + column
    fr[h, at : at + block.shape[0]] = block
    fr4[h, at + STEP : at + STEP + block.shape[0]] = block


def own_kernel(group_size, left, right, fl, fr, fr4, mixed, wide_buf):
    rows, cols, channels = left.shape
    base, wide = rows * cols, group_size * SLOT
    mixed[0:base] = right[...].reshape(base, channels)
    mixed[base : 2 * base] = left[...].reshape(base, channels)
    wide_buf[...] = dot(mixed[...], channel_table(channels, group_size, False))
    tail = fr.shape[1]
    for h in range(rows):
        for ref in (fr, fr4):
            ref[h, 0:16] = jnp.zeros((16, wide), F32)
            ref[h, tail - 16 :] = jnp.zeros((16, wide), F32)
        put_band((fr, fr4, cols), h, 0, wide_buf[h * cols : (h + 1) * cols])
        fl[h, 0:PAD] = jnp.zeros((PAD, wide), F32)
        fl[h, PAD + cols :] = jnp.zeros((PAD, wide), F32)
        fl[h, PAD : PAD + cols] = wide_buf[base + h * cols : base + (h + 1) * cols] * (1.0 / group_size)


def volume_kernel(ends, group_size, near, far, by_even, by_odd, _fl, _fr, _fr4, fl, fr, fr4, vbuf, *rest):
    pays, (mixed, wide_buf) = rest[: len(ends)], rest[len(ends) :]
    rows, cols, channels = near.shape
    disp = vbuf.shape[1]
    reach = fr.shape[1] - cols - PAD
    wide = group_size * SLOT
    half, at_far = cols // 2, rows * cols
    base = at_far + rows * half
    mixed[0:at_far] = near[...].reshape(at_far, channels)
    mixed[at_far:base] = far[:, half:].reshape(rows * half, channels)
    count = disp + 2 * rows
    for i, x in enumerate(end_columns(by_even, by_odd)):
        mixed[base + i * count : base + (i + 1) * count] = x.astype(BF16)
    wide_buf[...] = dot(mixed[...], channel_table(channels, group_size, False))
    for h in range(rows):
        put_band((fr, fr4, cols), h, -cols, wide_buf[h * cols : (h + 1) * cols])
        at = at_far + h * half
        put_band((fr, fr4, cols), h, -cols - half, wide_buf[at : at + half])
        at = base + disp + h
        fl[h, PAD - 1 : PAD] = wide_buf[at : at + 1] * (1.0 / group_size)
        at += count
        fl[h, PAD + cols : PAD + cols + 1] = wide_buf[at : at + 1] * (1.0 / group_size)
        put_band((fr, fr4, cols), h, cols, wide_buf[at + rows : at + rows + 1])
    total = cols + 2 * PAD
    low = lanes((8, 128)) < SLOT
    pairs, times, lots = rows // 2, disp // 2, wide // 128
    count = total // 16

    def products(i, _):
        p, at = lax.rem(i, pairs), pl.multiple_of(lax.div(i, pairs) * (8 * count), 8)
        lefts = [
            [
                [fl[2 * p + o, pl.ds(at + 8 * b, 8), 128 * j : 128 * (j + 1)] for j in range(lots)]
                for b in range(count)
            ]
            for o in range(2)
        ]
        for odd, band in enumerate((fr, fr4)):
            for r in range(1 - times, count):
                start = pl.multiple_of(at + reach - PAD + 8 * r, 8)
                here = [
                    [band[2 * p + o, pl.ds(start, 8), 128 * j : 128 * (j + 1)] for j in range(lots)]
                    for o in range(2)
                ]
                for t in range(max(0, -r), min(times, count - r)):
                    sums = []
                    for o in range(2):
                        acc = lefts[o][r + t][0] * here[o][0]
                        for j in range(1, lots):
                            acc = acc + lefts[o][r + t][j] * here[o][j]
                        sums.append(acc + pltpu.roll(acc, SLOT, 1))
                    vbuf[p, 2 * t + odd, pl.ds(at + 8 * (r + t), 8)] = jnp.where(low, *sums)
        return 0

    lax.fori_loop(0, 2 * pairs, products, 0)
    big = lanes((total, 128)) < SLOT

    for dd in range(disp // 2):
        for end, pay in zip(ends, pays):
            h = end()
            if isinstance(h, int):
                halves = [vbuf[h // 2, 2 * dd + o] for o in range(2)]
                if h % 2 == 0:
                    halves[1] = pltpu.roll(halves[1], SLOT, 1)
                else:
                    halves[0] = pltpu.roll(halves[0], SLOT, 1)
                out = jnp.where(big, halves[0], halves[1])
            else:
                last = pairs - 1
                first = jnp.where(big, vbuf[0, 2 * dd], pltpu.roll(vbuf[0, 2 * dd + 1], SLOT, 1))
                final = jnp.where(
                    big, pltpu.roll(vbuf[last, 2 * dd], SLOT, 1), vbuf[last, 2 * dd + 1]
                )
                out = jnp.where(h == 0, first, final)
            pay[dd * total : (dd + 1) * total] = out.astype(BF16)


def weight_kernel(
    masks, groups, feat, vbuf, ctl, by_even, by_odd, top, bot, tops, bots, *rest
):
    keep_out, give_out, ctsh, vt, buf, sums = rest
    disp, cols, width = ctl.shape
    pairs, per, half = vbuf.shape[0], 128 // feat, disp // 2
    mtop, mbot = masks()
    ctsh[0, 0] = jnp.zeros(ctsh.shape[2:], BF16)
    ctsh[half, 1] = jnp.zeros(ctsh.shape[2:], BF16)
    lane_in, lane_one = lanes((cols, 128)), lanes((1, 128))
    shifts = (feat, 128 - feat)
    edges = [x[0:disp, 0:128] for x in end_columns(by_even, by_odd)]
    turned = [[pltpu.roll(x, shift, 1) for shift in shifts] for x in edges]

    def aligned(t, z, i):
        return (
            t if i == 0 else pltpu.roll(t, 128 - feat * i, 1),
            z if i == per - 1 else pltpu.roll(z, feat * (per - 1 - i), 1),
        )

    corners = [aligned(tops[...].astype(F32) * mtop, bots[...].astype(F32) * mbot, i) for i in range(per)]

    def fill(q):
        t = top[q].astype(F32) * mtop
        z = bot[q].astype(F32) * mbot
        for i in range(per):
            d = q * per + i
            rims = aligned(t, z, i)
            inner = ctl[d].astype(F32)
            for p, (rim, shift) in enumerate(zip(rims, shifts)):

                def on_rim(x):
                    return x < feat if p == 0 else x >= 128 - feat

                at = slice(128 * p, 128 * (p + 1))
                buf[d, PAD : PAD + cols, at] = jnp.where(
                    on_rim(lane_in), rim, pltpu.roll(inner, shift, 1)
                )
                for side, row in enumerate((PAD - 1, PAD + cols)):
                    corner = corners[i][p][8 * side + q : 8 * side + q + 1]
                    buf[d, row : row + 1, at] = jnp.where(
                        on_rim(lane_one), corner, turned[side][p][d : d + 1]
                    )
            for e in range(3):
                ctsh[(d + 1) // 2, (d + 1) % 2, :, 256 * e : 256 * (e + 1)] = buf[
                    d, PAD - 1 + e : PAD - 1 + e + cols
                ].astype(BF16)

    none = jnp.zeros((cols, 128), F32)
    for p in range(pairs):
        for j in range(-1, half + 1):
            block = [
                vbuf[p, d, PAD : PAD + cols] if 0 <= d < disp and 0 <= j + half * o else none
                for o, d in enumerate((j, j + half))
            ]
            if j == half:
                block[1] = none
            x = jnp.concatenate(block, axis=0).astype(BF16)
            vt[p, :, 128 * (j + 1) : 128 * (j + 2)] = x.T
    full = None
    for q in range(half // per):
        fill(q)
        fill(q + half // per)
        first, size = q * per, per * 128
        left = jnp.concatenate(
            [
                jnp.concatenate(
                    [vt[p, :, 128 * (2 - a + first) : 128 * (2 - a + first) + size] for p in range(pairs)],
                    axis=1,
                )
                for a in range(3)
            ],
            axis=0,
        )
        right = jnp.concatenate(
            [
                jnp.concatenate(
                    [
                        ctsh[(d + 1) // 2, (d + 1) % 2, :, 256 * e + 128 * p : 256 * e + 128 * (p + 1)]
                        for e in range(3)
                    ],
                    axis=1,
                )
                for p in range(pairs)
                for j in range(first, first + per)
                for d in (j, j + half)
            ],
            axis=0,
        )
        part = dot(left, right)
        full = part if full is None else full + part
    keep = lanes((groups, 128)) < 3 * feat
    sums[...] = jnp.zeros(sums.shape, F32)
    for a in range(3):
        for e in range(3):
            block = full[128 * a : 128 * (a + 1), 128 * e : 128 * (e + 1)]
            out = block[0:groups] + pltpu.roll(block[SLOT : SLOT + groups], 128 - feat, 1)
            at = 128 * a + groups * e
            sums[at : at + groups] = jnp.where(keep, out, 0.0)
    half = sums.shape[0] // 2
    is_even = parity() == 0
    low, high = sums[0:half], sums[half:]
    keep_out[...] = jnp.where(is_even, low, high)
    give_out[...] = jnp.where(is_even, high, low)


def right_kernel(ctsh, w2, fl, *rest):
    *grads, rg0, rg1, rg2, acce, acco, both = rest
    rows, cols, channels = rg0.shape
    disp, wide = grads[0].shape[1], fl.shape[2]
    group_size = wide // SLOT
    step = disp // 4
    low = lanes((step * cols, 128)) < SLOT

    def conv(q, p, gv):
        slabs = [
            ctsh[pl.ds(q * step + s // 2, step), s % 2, :, 256 * e + 128 * p : 256 * e + 128 * (p + 1)]
            for s in range(4)
            for e in range(3)
        ]
        slabs = [x.reshape(step * cols, 128) for x in slabs]
        acc = dot(jnp.concatenate(slabs, axis=1), w2[...]).astype(BF16).astype(F32)
        for o in range(2):
            x = acc[:, 128 * o : 128 * (o + 1)]
            r = pltpu.roll(x, SLOT, 1)
            for hh in range(2):
                y = jnp.where(low, r, x) if hh else jnp.where(low, x, r)
                for j in range(step):
                    gv[hh, 2 * (q * step + j) + o] = y[j * cols : (j + 1) * cols]

    count = cols // 8
    back = acce.shape[1] - cols
    lead = back // 8

    lots = wide // 128

    def right_row(gv, p, hh):
        h = 2 * p + hh
        here = [
            [fl[h, PAD + 8 * b : PAD + 8 * b + 8, 128 * j : 128 * (j + 1)] for j in range(lots)]
            for b in range(count)
        ]
        for odd, buf in enumerate((acce, acco)):
            for k in range(lead + count):
                accs = [None] * lots
                for t in range(disp // 2):
                    b = k + t - lead
                    if b < 0 or b >= count:
                        continue
                    g = gv[hh, 2 * t + odd, 8 * b : 8 * b + 8]
                    for j in range(lots):
                        term = g * here[b][j]
                        accs[j] = term if accs[j] is None else accs[j] + term
                for j in range(lots):
                    x = jnp.zeros((8, 128), F32) if accs[j] is None else accs[j]
                    buf[h, 8 * k : 8 * k + 8, 128 * j : 128 * (j + 1)] = x
        acco[h, 8 * (lead + count) :] = jnp.zeros((8, wide), F32)

    for p, gv in enumerate(grads):
        for q in range(2):
            conv(q, p, gv)
    for p, gv in enumerate(grads):
        for hh in range(2):
            right_row(gv, p, hh)
    size = back + cols
    for h in range(rows):
        both[h * size : (h + 1) * size] = (acce[h] + acco[h, STEP : STEP + size]).astype(BF16)
    whole = dot(both[...], channel_table(channels, group_size, True)).astype(BF16)
    half = cols // 2
    for h in range(rows):
        at = h * size + back
        rg2[h] = whole[at - cols - half : at - cols]
        rg1[h] = whole[at - cols : at]
        rg0[h] = whole[at : at + cols]


def left_kernel(fr, fr4, *rest):
    *grads, lg, accl = rest
    rows, cols, channels = lg.shape
    disp, wide = grads[0].shape[1], fr.shape[2]
    group_size = wide // SLOT
    reach = fr.shape[1] - cols - PAD
    count, times, lots = cols // 8, disp // 2, wide // 128

    def left_row(gv, p, hh):
        h = 2 * p + hh
        accs = [[None] * lots for _ in range(count)]
        for odd, band in enumerate((fr, fr4)):
            for r in range(1 - times, count):
                at = reach + 8 * r
                here = [band[h, at : at + 8, 128 * j : 128 * (j + 1)] for j in range(lots)]
                for t in range(max(0, -r), min(times, count - r)):
                    g = gv[hh, 2 * t + odd, 8 * (r + t) : 8 * (r + t) + 8]
                    for j in range(lots):
                        term, acc = g * here[j], accs[r + t][j]
                        accs[r + t][j] = term if acc is None else acc + term
        for b in range(count):
            for j in range(lots):
                accl[h, 8 * b : 8 * b + 8, 128 * j : 128 * (j + 1)] = accs[b][j] * (1.0 / group_size)

    for p, gv in enumerate(grads):
        for hh in range(2):
            left_row(gv, p, hh)
    whole = accl[...].reshape(rows * cols, wide).astype(BF16)
    out = dot(whole, channel_table(channels, group_size, True)).astype(BF16)
    lg[...] = out.reshape(rows, cols, channels)


def combine_kernel(got, rg2, out):
    cols = out.shape[1]
    half = cols // 2
    part = jnp.where(parity() == 0, 0.0, got[...].astype(F32))
    out[:, 0:half] = part[:, 0:half].astype(BF16)
    out[:, half:] = (part[:, half:] + rg2[...].astype(F32)).astype(BF16)


def halo_lanes(groups):
    first = SLOT - groups
    assert groups - first <= first
    return (groups, SLOT, groups), (SLOT + groups, SLOT + 2 * groups - first, SLOT + groups - first)


def place_halo(base, row, groups, offset, lane):
    for start, end, shift in halo_lanes(groups):
        moved = pltpu.roll(row, (shift - offset) % 128, 1)
        base = jnp.where((lane >= start) & (lane < end), moved, base)
    return base


def conv_kernel(masks, groups, vbuf, top, bot, wc, out, taps, buf, held, sems):
    disp, rows, feat, cols = out.shape
    total = buf.shape[2]
    lane = lanes((total, 128))
    zeros = jnp.zeros((cols, taps.shape[3]), BF16)
    taps[0, 0] = zeros
    taps[disp // 2, 1] = zeros
    halos_of = [(ref, mask) for ref, mask in zip((top, bot), masks())]

    def build(dd):
        for p, (ref, mask) in enumerate(halos_of):
            row = ref[dd * total : (dd + 1) * total].astype(F32) * mask
            for o in range(2):
                d = 2 * dd + o
                buf[p, d] = place_halo(vbuf[p, d], row, groups, SLOT * o, lane)
                for e in range(3):
                    at = 256 * e + 128 * p
                    taps[(d + 1) // 2, (d + 1) % 2, :, at : at + 128] = buf[
                        p, d, PAD - 1 + e : PAD - 1 + e + cols
                    ].astype(BF16)

    parts = sems.shape[0]
    step = disp // 2 // parts
    copies = []
    build(0)
    for q in range(parts):
        for dd in range(q * step + 1, min((q + 1) * step + 1, disp // 2)):
            build(dd)
        slabs = [
            taps[q * step + s // 2 : q * step + s // 2 + step, s % 2].reshape(step * cols, taps.shape[3])
            for s in range(4)
        ]
        acc = dot(jnp.concatenate(slabs, axis=1), wc[...])
        for j in range(step):
            both = acc[j * cols : (j + 1) * cols].astype(BF16).T
            for o in range(2):
                block = both[rows * feat * o : rows * feat * (o + 1)]
                held[2 * (q * step + j) + o] = block.reshape(rows, feat, cols)
        at = pl.ds(2 * q * step, 2 * step)
        copies.append(pltpu.make_async_copy(held.at[at], out.at[at], sems.at[q]))
        copies[-1].start()
    for copy in copies:
        copy.wait()


def finish_kernel(scale, mine, other, own, near, far, left, weight, right, left_out, held_w, held_r, sems):
    _, _, _, feat, groups = weight.shape
    copies = [pltpu.make_async_copy(left, left_out, sems.at[0])]
    copies[0].start()
    is_even = parity() == 0
    beside = jnp.where(is_even, near[...].astype(F32), 0.0)
    held_r[...] = (own[...].astype(F32) + beside + far[...].astype(F32)).astype(BF16)
    copies.append(pltpu.make_async_copy(held_r, right, sems.at[1]))
    copies[1].start()
    x, y = mine[...] * scale, other[...] * scale
    total = jnp.concatenate([jnp.where(is_even, x, y), jnp.where(is_even, y, x)], axis=0)
    for a in range(3):
        for e in range(3):
            at = 128 * a + groups * e
            block = total[at : at + groups].T
            for b in range(3):
                held_w[2 - a, 2 - b, 2 - e] = block[feat * b : feat * (b + 1)]
        copies.append(pltpu.make_async_copy(held_w.at[2 - a], weight.at[2 - a], sems.at[2 + a]))
        copies[-1].start()
    for copy in copies:
        copy.wait()


def copy_kernel(*refs):
    half = len(refs) // 2
    for src, dst in zip(refs[:half], refs[half:]):
        dst[...] = src[...]


def sum_kernel(*refs):
    *parts, out = refs
    out[...] = tree([ref[...].astype(F32) for ref in parts]).astype(out.dtype)


def tree(terms):
    while len(terms) > 1:
        terms = [terms[i] + terms[i + 1] for i in range(0, len(terms), 2)]
    return terms[0]


def taps_kernel(taps, w2, wc, turned):
    _, _, _, feat, groups = taps.shape
    rows = wc.shape[1] // 2 // feat
    lane_of = lanes((feat, 2 * SLOT))
    low = lanes((feat, 2 * SLOT)) < SLOT
    zero = jnp.zeros((feat, 2 * SLOT), F32)

    def wide(a, b, e):
        if not 0 <= b <= 2:
            return None
        return jnp.concatenate([taps[a, b, e].astype(F32), zero[:, groups:]], axis=1)

    def beside(x, y):
        if x is None and y is None:
            return zero
        x = zero if x is None else x
        y = zero if y is None else pltpu.roll(y, SLOT, 1)
        return jnp.where(low, x, y)

    def build(a, _):
        def at_row(h):
            return pl.multiple_of((a * rows + h) * feat, feat)

        for e in range(3):
            for h in range(rows):
                for p in range(rows // 2):
                    lane = SLOT * (rows * e + 2 * p)
                    block = beside(wide(a, 2 * p - h + 1, e), wide(a, 2 * p + 1 - h + 1, e))
                    if h == 0 and p == 0:
                        block = place_halo(block, wide(a, 0, e), groups, 0, lane_of)
                    if h == rows - 1 and p == rows // 2 - 1:
                        block = place_halo(block, wide(a, 2, e), groups, 0, lane_of)
                    turned[pl.ds(at_row(h), feat), lane : lane + 2 * SLOT] = block
        return 0

    lax.fori_loop(0, 3, build, 0)
    for s in range(4):
        for e in range(3):
            for r in range(4):
                for o in range(2):
                    taps_of = [None if not 0 <= s - o <= 2 else wide(2 - s + o, 2 - r + i, 2 - e) for i in range(2)]
                    at = 384 * s + 128 * e + feat * r
                    w2[at : at + feat, 128 * o : 128 * (o + 1)] = beside(*taps_of).astype(BF16)
    depth, size = turned.shape[1], rows * feat
    for a in range(3):
        for i in range(depth // 128):
            x = turned[size * a : size * (a + 1), 128 * i : 128 * (i + 1)].T.astype(BF16)
            for o in range(2):
                at = depth * (a + o) + 128 * i
                wc[at : at + 128, size * o : size * (o + 1)] = x
    for o in range(2):
        at = depth * 3 * (1 - o)
        wc[at : at + depth, size * o : size * (o + 1)] = jnp.zeros((depth, size), BF16)


TOKEN = ((8, 128), F32)


def with_token(kernel, inputs, outputs):
    def run(*refs):
        kernel(*refs[: inputs + outputs], *refs[inputs + outputs + 1 :])
        refs[inputs + outputs][...] = jnp.zeros(TOKEN[0], F32)

    return run


def call(kernel, outs, scratch, *args, after=(), token=False, us=0.0, alias=(), hbm=()):
    skip = len(after)
    if token:
        kernel = with_token(kernel, len(args), len(outs))
        outs = [*outs, TOKEN]
    return pl.pallas_call(
        lambda *refs: kernel(*refs[skip:]),
        out_shape=[jax.ShapeDtypeStruct(s, t) for s, t in outs],
        in_specs=[pl.BlockSpec(memory_space=pl.ANY)] * skip + [VMEM] * len(args),
        out_specs=[pl.BlockSpec(memory_space=pl.ANY) if i in hbm else VMEM for i in range(len(outs))],
        scratch_shapes=scratch,
        input_output_aliases={skip + i: o for i, o in alias},
        compiler_params=pltpu.CompilerParams(vmem_limit_bytes=LIMIT),
        cost_estimate=pl.CostEstimate(
            flops=int(us * 1.15e9), bytes_accessed=int(us * 3.7e6), transcendentals=0
        ),
    )(*after, *args)


def col_shift(block, distance):
    n = lax.axis_size("col")
    route = [(i - distance, i) for i in range(n) if 0 <= i - distance < n]
    return lax.ppermute(block, "col", route)


def row_shift(block, distance):
    n = lax.axis_size("row")
    route = [(i - distance, i) for i in range(n) if 0 <= i - distance < n]
    return lax.ppermute(block, "row", route)


def halos(pays):
    if lax.axis_size("row") == 2:
        got = lax.ppermute(pays[0], "row", [(0, 1), (1, 0)])
        return got, got
    return row_shift(pays[0], 1), row_shift(pays[1], -1)


def partners(n_row, n_col):
    col_bits = [1 << i for i in range(1, n_col.bit_length() - 1)]
    row_bits = [n_col << i for i in range(n_row.bit_length() - 1)]
    assert n_col == 2 << len(col_bits) and n_row == 1 << len(row_bits)
    return [*col_bits[:2], sum(col_bits[:2])], col_bits[2:], row_bits


def on_device(left_features, right_features, conv_weight, cotangent):
    rows, cols, channels = left_features.shape
    disp, feat = cotangent.shape[0], cotangent.shape[3]
    groups = conv_weight.shape[3]
    group_size = channels // groups
    wide = group_size * SLOT
    n_row, n_col = lax.axis_size("row"), lax.axis_size("col")
    per = 128 // feat

    if n_row == 2:
        ends = [lambda: (rows - 1) * (1 - lax.axis_index("row"))]
    else:
        ends = [lambda: rows - 1, lambda: 0]
    n = len(ends)

    def masks():
        at = lax.axis_index("row")
        return (
            jnp.where(at > 0, 1.0, 0.0).astype(F32),
            jnp.where(at < n_row - 1, 1.0, 0.0).astype(F32),
        )

    total = cols + 2 * PAD
    count = disp + 2 * rows
    ct = cotangent.transpose(0, 1, 3, 2)

    def swap(block, mask):
        route = [(i, i ^ mask) for i in range(n_row * n_col)]
        return lax.ppermute(block, ("row", "col"), route)

    far = col_shift(right_features, 2)
    (begun,) = call(begin_kernel, [TOKEN], [], us=3.0)
    by_even, by_odd, ctl, *rims = call(
        functools.partial(pack_kernel, ends),
        [
            ((count, channels), BF16),
            ((count, channels), BF16),
            ((disp, cols, rows * feat), BF16),
        ]
        + [((disp // per, cols, 128), BF16)] * n,
        [pltpu.VMEM((disp * cols, rows * feat), F32)],
        left_features,
        right_features,
        ct,
        after=[begun],
        us=0.4,
    )
    inner = range(1, n_col - 1, 2)
    by_even = swap(by_even, 1)
    by_odd = lax.ppermute(by_odd, "col", [(i, i + 1) for i in inner] + [(i + 1, i) for i in inner])
    band = 104 + cols + PAD
    banks = [((rows, total, wide), F32), ((rows, band, wide), F32), ((rows, band, wide), F32)]
    spread_rows = 2 * rows * cols
    fl, fr, fr4 = call(
        functools.partial(own_kernel, group_size),
        banks,
        [pltpu.VMEM((spread_rows, channels), BF16), pltpu.VMEM((spread_rows, wide), F32)],
        left_features,
        right_features,
        after=[ctl],
    )
    (passed,) = call(
        pass_kernel, [((rows, cols, channels), BF16)], [], right_features, far, after=[fl]
    )
    near = swap(passed, 1)
    top, bot = halos(rims)
    corner_pays = call(
        functools.partial(corner_kernel, ends, rows, disp),
        [((16, 128), BF16)] * n,
        [pltpu.VMEM((2, disp, 128), F32), pltpu.VMEM((16, 128), F32)],
        by_even,
        by_odd,
        after=[passed],
        us=5.0,
    )
    tops, bots = halos(corner_pays)
    spread_rows = rows * cols + rows * cols // 2 + 2 * count
    fl, fr, fr4, vbuf, *volume_rows = call(
        functools.partial(volume_kernel, ends, group_size),
        banks
        + [((rows // 2, disp, total, 2 * SLOT), F32)]
        + [((disp // 2 * total, 128), BF16)] * n,
        [pltpu.VMEM((spread_rows, channels), BF16), pltpu.VMEM((spread_rows, wide), F32)],
        near,
        far,
        by_even,
        by_odd,
        fl,
        fr,
        fr4,
        us=1.8,
        alias=[(4, 0), (5, 1), (6, 2)],
    )
    vtop, vbot = halos(volume_rows)
    keep, give, ctsh = call(
        functools.partial(weight_kernel, masks, groups, feat),
        [((3 * 64, 128), F32), ((3 * 64, 128), F32), ((disp // 2 + 1, 2, cols, 3 * 256), BF16)],
        [
            pltpu.VMEM((rows // 2, 128, (disp // 2 + 2) * 128), BF16),
            pltpu.VMEM((disp, total, 256), F32),
            pltpu.VMEM((3 * 128, 128), F32),
        ],
        vbuf, ctl, by_even, by_odd, top, bot, tops, bots,
        us=2.0,
    )

    got = swap(give, 1)
    w2, wc = call(
        taps_kernel,
        [((12 * 128, 2 * 128), BF16), ((4 * 3 * rows * SLOT, 2 * rows * feat), BF16)],
        [pltpu.VMEM((3 * rows * feat, 3 * rows * SLOT), F32)],
        conv_weight.transpose(0, 1, 2, 4, 3),
        after=[keep],
    )
    (part,) = call(sum_kernel, [(keep.shape, BF16)], [], keep, got, after=[w2])
    *grads, rg0, rg1, rg2 = call(
        right_kernel,
        [((2, disp, cols, 128), F32)] * (rows // 2)
        + [
            ((rows, cols, channels), BF16),
            ((rows, cols, channels), BF16),
            ((rows, cols // 2, channels), BF16),
        ],
        [
            pltpu.VMEM((rows, cols + cols + cols // 2, wide), F32),
            pltpu.VMEM((rows, cols + cols + cols // 2 + 8, wide), F32),
            pltpu.VMEM((rows * (cols + cols + cols // 2), wide), BF16),
        ],
        ctsh, w2, fl,
        after=[part],
        us=0.4,
    )
    rg1 = swap(rg1, 1)
    def join(part, mask, kind, after, us):
        terms = (part, swap(part, mask))
        return call(sum_kernel, [(part.shape, kind)], [], *terms, after=after, us=us)[0]

    three, along_cols, along_rows = partners(n_row, n_col)
    parts = [part] + [swap(part, m) for m in three]
    (part,) = call(sum_kernel, [(part.shape, BF16)], [], *parts, after=[rg0, vtop], us=4.0)
    (rg2,) = call(
        combine_kernel, [((rows, cols, channels), BF16)], [], rg1, rg2, after=[part]
    )
    order = [rg2]
    for mask in along_cols:
        part = join(part, mask, F32, after=order, us=4.0)
        order = []
    output, conv_done = call(
        functools.partial(conv_kernel, masks, groups),
        [((disp, rows, feat, cols), BF16)],
        [
            pltpu.VMEM((disp // 2 + 1, 2, cols, 3 * rows * SLOT), BF16),
            pltpu.VMEM((rows // 2, disp, total, 128), F32),
            pltpu.VMEM((disp, rows, feat, cols), BF16),
            pltpu.SemaphoreType.DMA((3,)),
        ],
        vbuf, vtop, vbot, wc,
        after=[part],
        token=True,
        us=3.0,
        hbm=[0],
    )
    order = [conv_done]
    for mask in along_rows:
        part = join(part, mask, F32, after=order, us=4.0)
        order = []
    (lg,) = call(
        left_kernel,
        [((rows, cols, channels), BF16)],
        [pltpu.VMEM((rows, cols, wide), F32)],
        fr, fr4, *grads,
        after=[part],
        us=1.9,
    )
    rg2 = col_shift(rg2, -2)
    cells = disp * rows * n_row * cols * n_col
    weight_grad, right_grad, left_grad = call(
        functools.partial(finish_kernel, 1.0 / math.sqrt(cells)),
        [
            ((3, 3, 3, feat, groups), F32),
            ((rows, cols, channels), BF16),
            ((rows, cols, channels), BF16),
        ],
        [
            pltpu.VMEM((3, 3, 3, feat, groups), F32),
            pltpu.VMEM((rows, cols, channels), BF16),
            pltpu.SemaphoreType.DMA((5,)),
        ],
        part, swap(part, 1), rg0, rg1, rg2, lg,
        us=1.0,
        hbm=[0, 1, 2],
    )
    return (
        output.transpose(0, 1, 3, 2),
        weight_grad.transpose(0, 1, 2, 4, 3),
        left_grad,
        right_grad,
    )


def solution(mesh):
    in_specs = (P("row", "col", None), P("row", "col", None), P(), P(None, "row", "col", None))
    out_specs = (P(None, "row", "col", None), P(), P("row", "col", None), P("row", "col", None))
    return jax.shard_map(
        on_device, mesh=mesh, in_specs=in_specs, out_specs=out_specs, check_vma=False
    )
```

```python
import functools
import math

import jax
import jax.numpy as jnp
from jax import lax
from jax.experimental import pallas as pl
from jax.experimental.pallas import tpu as pltpu
from jax.sharding import PartitionSpec as P

DISP = 24
STEP = 4
SLOT = 64
PAD = 8
F32 = jnp.float32
BF16 = jnp.bfloat16
VMEM = pl.BlockSpec(memory_space=pltpu.VMEM)
LIMIT = 16 * 1024 * 1024


def lanes(shape):
    return lax.broadcasted_iota(jnp.int32, shape, len(shape) - 1)


def channel_table(channels, group_size, flip, value=1.0):
    shape = (group_size * SLOT, channels) if flip else (channels, group_size * SLOT)
    c = lax.broadcasted_iota(jnp.int32, shape, 1 if flip else 0)
    j = lax.broadcasted_iota(jnp.int32, shape, 0 if flip else 1)
    hit = c == (j & (SLOT - 1)) * group_size + (j >> (SLOT.bit_length() - 1))
    return jnp.where(hit, value, 0.0).astype(BF16)


def parity():
    return lax.rem(lax.axis_index("col"), 2)


def dot(a, b):
    return jnp.dot(a, b, preferred_element_type=F32)


def dot_nt(a, b):
    return lax.dot_general(a, b, (((1,), (1,)), ((), ())), preferred_element_type=F32)


def begin_kernel(out):
    out[...] = jnp.zeros(out.shape, F32)


def pack_kernel(ends, left, right, ct, even, odd, ctl, *rest):
    rims, ctf = rest[:-1], rest[-1]
    disp, rows, feat, cols = ct.shape
    per = 128 // feat
    for d in range(disp):
        block = ct[d].reshape(rows * feat, cols).astype(F32).T
        ctf[d * cols : (d + 1) * cols] = block
        ctl[d] = block.astype(BF16)
    columns = []
    for i, col in enumerate((cols - 1, 0)):
        block = ctf[pl.ds(col, disp, stride=cols), :]
        block = jnp.concatenate([block, jnp.zeros((disp, even.shape[1] - rows * feat), F32)], axis=1)
        edge = [x[h, col : col + 1].astype(F32) for x in (left, right) for h in range(rows)]
        columns.append(jnp.concatenate([block, *edge], axis=0))
    is_even = parity() == 0
    even[...] = jnp.where(is_even, columns[0], columns[1]).astype(BF16)
    odd[...] = jnp.where(is_even, columns[1], columns[0]).astype(BF16)
    for end, rim in zip(ends, rims):
        h = end()
        for q in range(disp // per):
            block = [ct[q * per + i, h].astype(F32) for i in range(per)]
            rim[q] = jnp.concatenate(block, axis=0).T.astype(BF16)


def pass_kernel(own, got, out):
    out[...] = jnp.where(parity() == 0, own[...].astype(F32), got[...].astype(F32)).astype(BF16)


def end_columns(by_even, by_odd):
    x, y = by_even[...].astype(F32), by_odd[...].astype(F32)
    is_even = parity() == 0
    return jnp.where(is_even, y, x), jnp.where(is_even, x, y)


def corner_kernel(ends, rows, disp, by_even, by_odd, *rest):
    pays, (edges, buf) = rest[: len(ends)], rest[len(ends) :]
    feat = 128 // rows
    per = 128 // feat
    count = disp // per
    lane = lanes((count, 128))
    for side, x in enumerate(end_columns(by_even, by_odd)):
        edges[side] = x[0:disp, 0:128]
    for end, pay in zip(ends, pays):
        h = end()
        buf[...] = jnp.zeros(buf.shape, F32)
        for side in range(2):
            out = jnp.zeros((count, 128), F32)
            for i in range(per):
                x = edges[side, pl.ds(i, count, stride=per)]
                first = pltpu.roll(x, feat * i, 1) if i else x
                last = pltpu.roll(x, (feat * (i - rows + 1)) % 128, 1) if i != rows - 1 else x
                x = jnp.where(h == 0, first, last)
                out = jnp.where((lane >= feat * i) & (lane < feat * (i + 1)), x, out)
            buf[8 * side : 8 * side + count] = out
        pay[...] = buf[...].astype(BF16)


def put_band(refs, h, column, block):
    fr, fr4, cols = refs
    at = fr.shape[1] - cols - PAD + column
    fr[h, at : at + block.shape[0]] = block
    fr4[h, at + STEP : at + STEP + block.shape[0]] = block


def own_kernel(group_size, left, right, fl, fr, fr4, mixed, wide_buf):
    rows, cols, channels = left.shape
    base, wide = rows * cols, group_size * SLOT
    mixed[0:base] = right[...].reshape(base, channels)
    mixed[base : 2 * base] = left[...].reshape(base, channels)
    wide_buf[...] = dot(mixed[...], channel_table(channels, group_size, False))
    tail = fr.shape[1]
    for h in range(rows):
        for ref in (fr, fr4):
            ref[h, 0:16] = jnp.zeros((16, wide), F32)
            ref[h, tail - 16 :] = jnp.zeros((16, wide), F32)
        put_band((fr, fr4, cols), h, 0, wide_buf[h * cols : (h + 1) * cols])
        fl[h, 0:PAD] = jnp.zeros((PAD, wide), F32)
        fl[h, PAD + cols :] = jnp.zeros((PAD, wide), F32)
        fl[h, PAD : PAD + cols] = wide_buf[base + h * cols : base + (h + 1) * cols] * (1.0 / group_size)


def volume_kernel(ends, group_size, near, far, by_even, by_odd, _fl, _fr, _fr4, fl, fr, fr4, vbuf, *rest):
    pays, (mixed, wide_buf) = rest[: len(ends)], rest[len(ends) :]
    rows, cols, channels = near.shape
    disp = vbuf.shape[1]
    reach = fr.shape[1] - cols - PAD
    wide = group_size * SLOT
    half, at_far = cols // 2, rows * cols
    base = at_far + rows * half
    mixed[0:at_far] = near[...].reshape(at_far, channels)
    mixed[at_far:base] = far[:, half:].reshape(rows * half, channels)
    count = disp + 2 * rows
    for i, x in enumerate(end_columns(by_even, by_odd)):
        mixed[base + i * count : base + (i + 1) * count] = x.astype(BF16)
    wide_buf[...] = dot(mixed[...], channel_table(channels, group_size, False))
    for h in range(rows):
        put_band((fr, fr4, cols), h, -cols, wide_buf[h * cols : (h + 1) * cols])
        at = at_far + h * half
        put_band((fr, fr4, cols), h, -cols - half, wide_buf[at : at + half])
        at = base + disp + h
        fl[h, PAD - 1 : PAD] = wide_buf[at : at + 1] * (1.0 / group_size)
        at += count
        fl[h, PAD + cols : PAD + cols + 1] = wide_buf[at : at + 1] * (1.0 / group_size)
        put_band((fr, fr4, cols), h, cols, wide_buf[at + rows : at + rows + 1])
    total = cols + 2 * PAD
    low = lanes((8, 128)) < SLOT
    pairs, times, lots = rows // 2, disp // 2, wide // 128
    count = total // 16

    def products(i, _):
        p, at = lax.rem(i, pairs), pl.multiple_of(lax.div(i, pairs) * (8 * count), 8)
        lefts = [
            [
                [fl[2 * p + o, pl.ds(at + 8 * b, 8), 128 * j : 128 * (j + 1)] for j in range(lots)]
                for b in range(count)
            ]
            for o in range(2)
        ]
        for odd, band in enumerate((fr, fr4)):
            for r in range(1 - times, count):
                start = pl.multiple_of(at + reach - PAD + 8 * r, 8)
                here = [
                    [band[2 * p + o, pl.ds(start, 8), 128 * j : 128 * (j + 1)] for j in range(lots)]
                    for o in range(2)
                ]
                for t in range(max(0, -r), min(times, count - r)):
                    sums = []
                    for o in range(2):
                        acc = lefts[o][r + t][0] * here[o][0]
                        for j in range(1, lots):
                            acc = acc + lefts[o][r + t][j] * here[o][j]
                        sums.append(acc + pltpu.roll(acc, SLOT, 1))
                    vbuf[p, 2 * t + odd, pl.ds(at + 8 * (r + t), 8)] = jnp.where(low, *sums)
        return 0

    lax.fori_loop(0, 2 * pairs, products, 0)
    big = lanes((total, 128)) < SLOT

    for dd in range(disp // 2):
        for end, pay in zip(ends, pays):
            h = end()
            if isinstance(h, int):
                halves = [vbuf[h // 2, 2 * dd + o] for o in range(2)]
                if h % 2 == 0:
                    halves[1] = pltpu.roll(halves[1], SLOT, 1)
                else:
                    halves[0] = pltpu.roll(halves[0], SLOT, 1)
                out = jnp.where(big, halves[0], halves[1])
            else:
                last = pairs - 1
                first = jnp.where(big, vbuf[0, 2 * dd], pltpu.roll(vbuf[0, 2 * dd + 1], SLOT, 1))
                final = jnp.where(
                    big, pltpu.roll(vbuf[last, 2 * dd], SLOT, 1), vbuf[last, 2 * dd + 1]
                )
                out = jnp.where(h == 0, first, final)
            pay[dd * total : (dd + 1) * total] = out.astype(BF16)


def weight_kernel(
    masks, groups, feat, vbuf, ctl, by_even, by_odd, top, bot, tops, bots, *rest
):
    keep_out, give_out, ctsh, vt, buf, sums = rest
    disp, cols, width = ctl.shape
    pairs, per, half = vbuf.shape[0], 128 // feat, disp // 2
    mtop, mbot = masks()
    ctsh[0, 0] = jnp.zeros(ctsh.shape[2:], BF16)
    ctsh[half, 1] = jnp.zeros(ctsh.shape[2:], BF16)
    lane_in, lane_one = lanes((cols, 128)), lanes((1, 128))
    shifts = (feat, 128 - feat)
    edges = [x[0:disp, 0:128] for x in end_columns(by_even, by_odd)]
    turned = [[pltpu.roll(x, shift, 1) for shift in shifts] for x in edges]

    def aligned(t, z, i):
        return (
            t if i == 0 else pltpu.roll(t, 128 - feat * i, 1),
            z if i == per - 1 else pltpu.roll(z, feat * (per - 1 - i), 1),
        )

    corners = [aligned(tops[...].astype(F32) * mtop, bots[...].astype(F32) * mbot, i) for i in range(per)]

    def fill(q):
        t = top[q].astype(F32) * mtop
        z = bot[q].astype(F32) * mbot
        for i in range(per):
            d = q * per + i
            rims = aligned(t, z, i)
            inner = ctl[d].astype(F32)
            for p, (rim, shift) in enumerate(zip(rims, shifts)):

                def on_rim(x):
                    return x < feat if p == 0 else x >= 128 - feat

                at = slice(128 * p, 128 * (p + 1))
                buf[d, PAD : PAD + cols, at] = jnp.where(
                    on_rim(lane_in), rim, pltpu.roll(inner, shift, 1)
                )
                for side, row in enumerate((PAD - 1, PAD + cols)):
                    corner = corners[i][p][8 * side + q : 8 * side + q + 1]
                    buf[d, row : row + 1, at] = jnp.where(
                        on_rim(lane_one), corner, turned[side][p][d : d + 1]
                    )
            for e in range(3):
                ctsh[(d + 1) // 2, (d + 1) % 2, :, 256 * e : 256 * (e + 1)] = buf[
                    d, PAD - 1 + e : PAD - 1 + e + cols
                ].astype(BF16)

    none = jnp.zeros((cols, 128), F32)
    for p in range(pairs):
        for j in range(-1, half + 1):
            block = [
                vbuf[p, d, PAD : PAD + cols] if 0 <= d < disp and 0 <= j + half * o else none
                for o, d in enumerate((j, j + half))
            ]
            if j == half:
                block[1] = none
            x = jnp.concatenate(block, axis=0).astype(BF16)
            vt[p, :, 128 * (j + 1) : 128 * (j + 2)] = x.T
    full = None
    for q in range(half // per):
        fill(q)
        fill(q + half // per)
        first, size = q * per, per * 128
        left = jnp.concatenate(
            [
                jnp.concatenate(
                    [vt[p, :, 128 * (2 - a + first) : 128 * (2 - a + first) + size] for p in range(pairs)],
                    axis=1,
                )
                for a in range(3)
            ],
            axis=0,
        )
        right = jnp.concatenate(
            [
                jnp.concatenate(
                    [
                        ctsh[(d + 1) // 2, (d + 1) % 2, :, 256 * e + 128 * p : 256 * e + 128 * (p + 1)]
                        for e in range(3)
                    ],
                    axis=1,
                )
                for p in range(pairs)
                for j in range(first, first + per)
                for d in (j, j + half)
            ],
            axis=0,
        )
        part = dot(left, right)
        full = part if full is None else full + part
    keep = lanes((groups, 128)) < 3 * feat
    sums[...] = jnp.zeros(sums.shape, F32)
    for a in range(3):
        for e in range(3):
            block = full[128 * a : 128 * (a + 1), 128 * e : 128 * (e + 1)]
            out = block[0:groups] + pltpu.roll(block[SLOT : SLOT + groups], 128 - feat, 1)
            at = 128 * a + groups * e
            sums[at : at + groups] = jnp.where(keep, out, 0.0)
    half = sums.shape[0] // 2
    is_even = parity() == 0
    low, high = sums[0:half], sums[half:]
    keep_out[...] = jnp.where(is_even, low, high)
    give_out[...] = jnp.where(is_even, high, low)


def right_kernel(ctsh, w2, fl, *rest):
    *grads, rg0, rg1, rg2, acce, acco, both = rest
    rows, cols, channels = rg0.shape
    disp, wide = grads[0].shape[1], fl.shape[2]
    group_size = wide // SLOT
    step = disp // 4
    low = lanes((step * cols, 128)) < SLOT

    def conv(q):
        rows_of = []
        for p in range(len(grads)):
            slabs = [
                ctsh[pl.ds(q * step + s // 2, step), s % 2, :, 256 * e + 128 * p : 256 * e + 128 * (p + 1)]
                for s in range(4)
                for e in range(3)
            ]
            slabs = [x.reshape(step * cols, 128) for x in slabs]
            rows_of.append(jnp.concatenate(slabs, axis=1))
        acc = dot(jnp.concatenate(rows_of, axis=0), w2[...]).astype(BF16).astype(F32)
        for p, gv in enumerate(grads):
            for o in range(2):
                x = acc[p * step * cols : (p + 1) * step * cols, 128 * o : 128 * (o + 1)]
                r = pltpu.roll(x, SLOT, 1)
                for hh in range(2):
                    y = jnp.where(low, r, x) if hh else jnp.where(low, x, r)
                    for j in range(step):
                        gv[hh, 2 * (q * step + j) + o] = y[j * cols : (j + 1) * cols]

    count = cols // 8
    back = acce.shape[1] - cols
    lead = back // 8

    lots = wide // 128

    def right_row(gv, p, hh):
        h = 2 * p + hh
        here = [
            [fl[h, PAD + 8 * b : PAD + 8 * b + 8, 128 * j : 128 * (j + 1)] for j in range(lots)]
            for b in range(count)
        ]
        for odd, buf in enumerate((acce, acco)):
            for k in range(lead + count):
                accs = [None] * lots
                for t in range(disp // 2):
                    b = k + t - lead
                    if b < 0 or b >= count:
                        continue
                    g = gv[hh, 2 * t + odd, 8 * b : 8 * b + 8]
                    for j in range(lots):
                        term = g * here[b][j]
                        accs[j] = term if accs[j] is None else accs[j] + term
                for j in range(lots):
                    x = jnp.zeros((8, 128), F32) if accs[j] is None else accs[j]
                    buf[h, 8 * k : 8 * k + 8, 128 * j : 128 * (j + 1)] = x
        acco[h, 8 * (lead + count) :] = jnp.zeros((8, wide), F32)

    for q in range(2):
        conv(q)
    for p, gv in enumerate(grads):
        for hh in range(2):
            right_row(gv, p, hh)
    size = back + cols
    for h in range(rows):
        both[h * size : (h + 1) * size] = (acce[h] + acco[h, STEP : STEP + size]).astype(BF16)
    whole = dot(both[...], channel_table(channels, group_size, True)).astype(BF16)
    half = cols // 2
    for h in range(rows):
        at = h * size + back
        rg2[h] = whole[at - cols - half : at - cols]
        rg1[h] = whole[at - cols : at]
        rg0[h] = whole[at : at + cols]


def left_kernel(fr, fr4, *rest):
    *grads, lg, accl = rest
    rows, cols, channels = lg.shape
    disp, wide = grads[0].shape[1], fr.shape[2]
    group_size = wide // SLOT
    reach = fr.shape[1] - cols - PAD
    count, times, lots = cols // 8, disp // 2, wide // 128

    def left_row(gv, p, hh):
        h = 2 * p + hh
        accs = [[None] * lots for _ in range(count)]
        for odd, band in enumerate((fr, fr4)):
            for r in range(1 - times, count):
                at = reach + 8 * r
                here = [band[h, at : at + 8, 128 * j : 128 * (j + 1)] for j in range(lots)]
                for t in range(max(0, -r), min(times, count - r)):
                    g = gv[hh, 2 * t + odd, 8 * (r + t) : 8 * (r + t) + 8]
                    for j in range(lots):
                        term, acc = g * here[j], accs[r + t][j]
                        accs[r + t][j] = term if acc is None else acc + term
        for b in range(count):
            for j in range(lots):
                accl[h, 8 * b : 8 * b + 8, 128 * j : 128 * (j + 1)] = accs[b][j] * (1.0 / group_size)

    for p, gv in enumerate(grads):
        for hh in range(2):
            left_row(gv, p, hh)
    whole = accl[...].reshape(rows * cols, wide).astype(BF16)
    out = dot(whole, channel_table(channels, group_size, True)).astype(BF16)
    lg[...] = out.reshape(rows, cols, channels)


def combine_kernel(got, rg2, out):
    cols = out.shape[1]
    half = cols // 2
    part = jnp.where(parity() == 0, 0.0, got[...].astype(F32))
    out[:, 0:half] = part[:, 0:half].astype(BF16)
    out[:, half:] = (part[:, half:] + rg2[...].astype(F32)).astype(BF16)


def halo_lanes(groups):
    first = SLOT - groups
    assert groups - first <= first
    return (groups, SLOT, groups), (SLOT + groups, SLOT + 2 * groups - first, SLOT + groups - first)


def place_halo(base, row, groups, offset, lane):
    for start, end, shift in halo_lanes(groups):
        moved = pltpu.roll(row, (shift - offset) % 128, 1)
        base = jnp.where((lane >= start) & (lane < end), moved, base)
    return base


def conv_kernel(masks, groups, vbuf, top, bot, wc, out, taps, buf, held, sems):
    disp, rows, feat, cols = out.shape
    total = buf.shape[2]
    lane = lanes((total, 128))
    zeros = jnp.zeros((cols, taps.shape[3]), BF16)
    taps[0, 0] = zeros
    taps[disp // 2, 1] = zeros
    halos_of = [(ref, mask) for ref, mask in zip((top, bot), masks())]

    def build(dd):
        for p, (ref, mask) in enumerate(halos_of):
            row = ref[dd * total : (dd + 1) * total].astype(F32) * mask
            for o in range(2):
                d = 2 * dd + o
                buf[p, d] = place_halo(vbuf[p, d], row, groups, SLOT * o, lane)
                for e in range(3):
                    at = 256 * e + 128 * p
                    taps[(d + 1) // 2, (d + 1) % 2, :, at : at + 128] = buf[
                        p, d, PAD - 1 + e : PAD - 1 + e + cols
                    ].astype(BF16)

    parts = sems.shape[0]
    step = disp // 2 // parts
    copies = []
    build(0)
    for q in range(parts):
        for dd in range(q * step + 1, min((q + 1) * step + 1, disp // 2)):
            build(dd)
        slabs = [
            taps[q * step + s // 2 : q * step + s // 2 + step, s % 2].reshape(step * cols, taps.shape[3])
            for s in range(4)
        ]
        acc = dot(jnp.concatenate(slabs, axis=1), wc[...])
        for j in range(step):
            both = acc[j * cols : (j + 1) * cols].astype(BF16).T
            for o in range(2):
                block = both[rows * feat * o : rows * feat * (o + 1)]
                held[2 * (q * step + j) + o] = block.reshape(rows, feat, cols)
        at = pl.ds(2 * q * step, 2 * step)
        copies.append(pltpu.make_async_copy(held.at[at], out.at[at], sems.at[q]))
        copies[-1].start()
    for copy in copies:
        copy.wait()


def finish_kernel(scale, mine, other, own, near, far, left, weight, right, left_out, held_w, held_r, sems):
    _, _, _, feat, groups = weight.shape
    copies = [pltpu.make_async_copy(left, left_out, sems.at[0])]
    copies[0].start()
    is_even = parity() == 0
    beside = jnp.where(is_even, near[...].astype(F32), 0.0)
    held_r[...] = (own[...].astype(F32) + beside + far[...].astype(F32)).astype(BF16)
    copies.append(pltpu.make_async_copy(held_r, right, sems.at[1]))
    copies[1].start()
    x, y = mine[...] * scale, other[...] * scale
    total = jnp.concatenate([jnp.where(is_even, x, y), jnp.where(is_even, y, x)], axis=0)
    for a in range(3):
        for e in range(3):
            at = 128 * a + groups * e
            block = total[at : at + groups].T
            for b in range(3):
                held_w[2 - a, 2 - b, 2 - e] = block[feat * b : feat * (b + 1)]
        copies.append(pltpu.make_async_copy(held_w.at[2 - a], weight.at[2 - a], sems.at[2 + a]))
        copies[-1].start()
    for copy in copies:
        copy.wait()


def copy_kernel(*refs):
    half = len(refs) // 2
    for src, dst in zip(refs[:half], refs[half:]):
        dst[...] = src[...]


def sum_kernel(*refs):
    *parts, out = refs
    out[...] = tree([ref[...].astype(F32) for ref in parts]).astype(out.dtype)


def tree(terms):
    while len(terms) > 1:
        terms = [terms[i] + terms[i + 1] for i in range(0, len(terms), 2)]
    return terms[0]


def taps_kernel(taps, w2, wc, turned):
    _, _, _, feat, groups = taps.shape
    rows = wc.shape[1] // 2 // feat
    lane_of = lanes((feat, 2 * SLOT))
    low = lanes((feat, 2 * SLOT)) < SLOT
    zero = jnp.zeros((feat, 2 * SLOT), F32)

    def wide(a, b, e):
        if not 0 <= b <= 2:
            return None
        return jnp.concatenate([taps[a, b, e].astype(F32), zero[:, groups:]], axis=1)

    def beside(x, y):
        if x is None and y is None:
            return zero
        x = zero if x is None else x
        y = zero if y is None else pltpu.roll(y, SLOT, 1)
        return jnp.where(low, x, y)

    def build(a, _):
        def at_row(h):
            return pl.multiple_of((a * rows + h) * feat, feat)

        for e in range(3):
            for h in range(rows):
                for p in range(rows // 2):
                    lane = SLOT * (rows * e + 2 * p)
                    block = beside(wide(a, 2 * p - h + 1, e), wide(a, 2 * p + 1 - h + 1, e))
                    if h == 0 and p == 0:
                        block = place_halo(block, wide(a, 0, e), groups, 0, lane_of)
                    if h == rows - 1 and p == rows // 2 - 1:
                        block = place_halo(block, wide(a, 2, e), groups, 0, lane_of)
                    turned[pl.ds(at_row(h), feat), lane : lane + 2 * SLOT] = block
        return 0

    lax.fori_loop(0, 3, build, 0)
    for s in range(4):
        for e in range(3):
            for r in range(4):
                for o in range(2):
                    taps_of = [None if not 0 <= s - o <= 2 else wide(2 - s + o, 2 - r + i, 2 - e) for i in range(2)]
                    at = 384 * s + 128 * e + feat * r
                    w2[at : at + feat, 128 * o : 128 * (o + 1)] = beside(*taps_of).astype(BF16)
    depth, size = turned.shape[1], rows * feat
    for a in range(3):
        for i in range(depth // 128):
            x = turned[size * a : size * (a + 1), 128 * i : 128 * (i + 1)].T.astype(BF16)
            for o in range(2):
                at = depth * (a + o) + 128 * i
                wc[at : at + 128, size * o : size * (o + 1)] = x
    for o in range(2):
        at = depth * 3 * (1 - o)
        wc[at : at + depth, size * o : size * (o + 1)] = jnp.zeros((depth, size), BF16)


TOKEN = ((8, 128), F32)


def with_token(kernel, inputs, outputs):
    def run(*refs):
        kernel(*refs[: inputs + outputs], *refs[inputs + outputs + 1 :])
        refs[inputs + outputs][...] = jnp.zeros(TOKEN[0], F32)

    return run


def call(kernel, outs, scratch, *args, after=(), token=False, us=0.0, alias=(), hbm=()):
    skip = len(after)
    if token:
        kernel = with_token(kernel, len(args), len(outs))
        outs = [*outs, TOKEN]
    return pl.pallas_call(
        lambda *refs: kernel(*refs[skip:]),
        out_shape=[jax.ShapeDtypeStruct(s, t) for s, t in outs],
        in_specs=[pl.BlockSpec(memory_space=pl.ANY)] * skip + [VMEM] * len(args),
        out_specs=[pl.BlockSpec(memory_space=pl.ANY) if i in hbm else VMEM for i in range(len(outs))],
        scratch_shapes=scratch,
        input_output_aliases={skip + i: o for i, o in alias},
        compiler_params=pltpu.CompilerParams(vmem_limit_bytes=LIMIT),
        cost_estimate=pl.CostEstimate(
            flops=int(us * 1.15e9), bytes_accessed=int(us * 3.7e6), transcendentals=0
        ),
    )(*after, *args)


def col_shift(block, distance):
    n = lax.axis_size("col")
    route = [(i - distance, i) for i in range(n) if 0 <= i - distance < n]
    return lax.ppermute(block, "col", route)


def row_shift(block, distance):
    n = lax.axis_size("row")
    route = [(i - distance, i) for i in range(n) if 0 <= i - distance < n]
    return lax.ppermute(block, "row", route)


def halos(pays):
    if lax.axis_size("row") == 2:
        got = lax.ppermute(pays[0], "row", [(0, 1), (1, 0)])
        return got, got
    return row_shift(pays[0], 1), row_shift(pays[1], -1)


def partners(n_row, n_col):
    col_bits = [1 << i for i in range(1, n_col.bit_length() - 1)]
    row_bits = [n_col << i for i in range(n_row.bit_length() - 1)]
    assert n_col == 2 << len(col_bits) and n_row == 1 << len(row_bits)
    return [*col_bits[:2], sum(col_bits[:2])], col_bits[2:], row_bits


def on_device(left_features, right_features, conv_weight, cotangent):
    rows, cols, channels = left_features.shape
    disp, feat = cotangent.shape[0], cotangent.shape[3]
    groups = conv_weight.shape[3]
    group_size = channels // groups
    wide = group_size * SLOT
    n_row, n_col = lax.axis_size("row"), lax.axis_size("col")
    per = 128 // feat

    if n_row == 2:
        ends = [lambda: (rows - 1) * (1 - lax.axis_index("row"))]
    else:
        ends = [lambda: rows - 1, lambda: 0]
    n = len(ends)

    def masks():
        at = lax.axis_index("row")
        return (
            jnp.where(at > 0, 1.0, 0.0).astype(F32),
            jnp.where(at < n_row - 1, 1.0, 0.0).astype(F32),
        )

    total = cols + 2 * PAD
    count = disp + 2 * rows
    ct = cotangent.transpose(0, 1, 3, 2)

    def swap(block, mask):
        route = [(i, i ^ mask) for i in range(n_row * n_col)]
        return lax.ppermute(block, ("row", "col"), route)

    far = col_shift(right_features, 2)
    (begun,) = call(begin_kernel, [TOKEN], [], us=3.0)
    by_even, by_odd, ctl, *rims = call(
        functools.partial(pack_kernel, ends),
        [
            ((count, channels), BF16),
            ((count, channels), BF16),
            ((disp, cols, rows * feat), BF16),
        ]
        + [((disp // per, cols, 128), BF16)] * n,
        [pltpu.VMEM((disp * cols, rows * feat), F32)],
        left_features,
        right_features,
        ct,
        after=[begun],
        us=0.4,
    )
    inner = range(1, n_col - 1, 2)
    by_even = swap(by_even, 1)
    by_odd = lax.ppermute(by_odd, "col", [(i, i + 1) for i in inner] + [(i + 1, i) for i in inner])
    band = 104 + cols + PAD
    banks = [((rows, total, wide), F32), ((rows, band, wide), F32), ((rows, band, wide), F32)]
    spread_rows = 2 * rows * cols
    fl, fr, fr4 = call(
        functools.partial(own_kernel, group_size),
        banks,
        [pltpu.VMEM((spread_rows, channels), BF16), pltpu.VMEM((spread_rows, wide), F32)],
        left_features,
        right_features,
        after=[ctl],
    )
    (passed,) = call(
        pass_kernel, [((rows, cols, channels), BF16)], [], right_features, far, after=[fl]
    )
    near = swap(passed, 1)
    top, bot = halos(rims)
    corner_pays = call(
        functools.partial(corner_kernel, ends, rows, disp),
        [((16, 128), BF16)] * n,
        [pltpu.VMEM((2, disp, 128), F32), pltpu.VMEM((16, 128), F32)],
        by_even,
        by_odd,
        after=[passed],
        us=5.0,
    )
    tops, bots = halos(corner_pays)
    spread_rows = rows * cols + rows * cols // 2 + 2 * count
    fl, fr, fr4, vbuf, *volume_rows = call(
        functools.partial(volume_kernel, ends, group_size),
        banks
        + [((rows // 2, disp, total, 2 * SLOT), F32)]
        + [((disp // 2 * total, 128), BF16)] * n,
        [pltpu.VMEM((spread_rows, channels), BF16), pltpu.VMEM((spread_rows, wide), F32)],
        near,
        far,
        by_even,
        by_odd,
        fl,
        fr,
        fr4,
        us=1.8,
        alias=[(4, 0), (5, 1), (6, 2)],
    )
    vtop, vbot = halos(volume_rows)
    keep, give, ctsh = call(
        functools.partial(weight_kernel, masks, groups, feat),
        [((3 * 64, 128), F32), ((3 * 64, 128), F32), ((disp // 2 + 1, 2, cols, 3 * 256), BF16)],
        [
            pltpu.VMEM((rows // 2, 128, (disp // 2 + 2) * 128), BF16),
            pltpu.VMEM((disp, total, 256), F32),
            pltpu.VMEM((3 * 128, 128), F32),
        ],
        vbuf, ctl, by_even, by_odd, top, bot, tops, bots,
        us=2.0,
    )

    got = swap(give, 1)
    w2, wc = call(
        taps_kernel,
        [((12 * 128, 2 * 128), BF16), ((4 * 3 * rows * SLOT, 2 * rows * feat), BF16)],
        [pltpu.VMEM((3 * rows * feat, 3 * rows * SLOT), F32)],
        conv_weight.transpose(0, 1, 2, 4, 3),
        after=[keep],
    )
    (part,) = call(sum_kernel, [(keep.shape, BF16)], [], keep, got, after=[w2])
    *grads, rg0, rg1, rg2 = call(
        right_kernel,
        [((2, disp, cols, 128), F32)] * (rows // 2)
        + [
            ((rows, cols, channels), BF16),
            ((rows, cols, channels), BF16),
            ((rows, cols // 2, channels), BF16),
        ],
        [
            pltpu.VMEM((rows, cols + cols + cols // 2, wide), F32),
            pltpu.VMEM((rows, cols + cols + cols // 2 + 8, wide), F32),
            pltpu.VMEM((rows * (cols + cols + cols // 2), wide), BF16),
        ],
        ctsh, w2, fl,
        after=[part],
        us=0.4,
    )
    rg1 = swap(rg1, 1)
    def join(part, mask, kind, after, us):
        terms = (part, swap(part, mask))
        return call(sum_kernel, [(part.shape, kind)], [], *terms, after=after, us=us)[0]

    three, along_cols, along_rows = partners(n_row, n_col)
    parts = [part] + [swap(part, m) for m in three]
    (part,) = call(sum_kernel, [(part.shape, BF16)], [], *parts, after=[rg0, vtop], us=4.0)
    (rg2,) = call(
        combine_kernel, [((rows, cols, channels), BF16)], [], rg1, rg2, after=[part]
    )
    order = [rg2]
    for mask in along_cols:
        part = join(part, mask, BF16, after=order, us=4.0)
        order = []
    output, conv_done = call(
        functools.partial(conv_kernel, masks, groups),
        [((disp, rows, feat, cols), BF16)],
        [
            pltpu.VMEM((disp // 2 + 1, 2, cols, 3 * rows * SLOT), BF16),
            pltpu.VMEM((rows // 2, disp, total, 128), F32),
            pltpu.VMEM((disp, rows, feat, cols), BF16),
            pltpu.SemaphoreType.DMA((2,)),
        ],
        vbuf, vtop, vbot, wc,
        after=[part],
        token=True,
        us=3.0,
        hbm=[0],
    )
    order = [conv_done]
    for mask in along_rows:
        part = join(part, mask, F32, after=order, us=4.0)
        order = []
    (lg,) = call(
        left_kernel,
        [((rows, cols, channels), BF16)],
        [pltpu.VMEM((rows, cols, wide), F32)],
        fr, fr4, *grads,
        after=[part],
        us=1.9,
    )
    rg2 = col_shift(rg2, -2)
    cells = disp * rows * n_row * cols * n_col
    weight_grad, right_grad, left_grad = call(
        functools.partial(finish_kernel, 1.0 / math.sqrt(cells)),
        [
            ((3, 3, 3, feat, groups), F32),
            ((rows, cols, channels), BF16),
            ((rows, cols, channels), BF16),
        ],
        [
            pltpu.VMEM((3, 3, 3, feat, groups), F32),
            pltpu.VMEM((rows, cols, channels), BF16),
            pltpu.SemaphoreType.DMA((5,)),
        ],
        part, swap(part, 1), rg0, rg1, rg2, lg,
        us=1.0,
        hbm=[0, 1, 2],
    )
    return (
        output.transpose(0, 1, 3, 2),
        weight_grad.transpose(0, 1, 2, 4, 3),
        left_grad,
        right_grad,
    )


def solution(mesh):
    in_specs = (P("row", "col", None), P("row", "col", None), P(), P(None, "row", "col", None))
    out_specs = (P(None, "row", "col", None), P(), P("row", "col", None), P("row", "col", None))
    return jax.shard_map(
        on_device, mesh=mesh, in_specs=in_specs, out_specs=out_specs, check_vma=False
    )
```

```python
import functools
import math

import jax
import jax.numpy as jnp
from jax import lax
from jax.experimental import pallas as pl
from jax.experimental.pallas import tpu as pltpu
from jax.sharding import PartitionSpec as P

DISP = 24
STEP = 4
SLOT = 64
PAD = 8
F32 = jnp.float32
BF16 = jnp.bfloat16
VMEM = pl.BlockSpec(memory_space=pltpu.VMEM)
LIMIT = 16 * 1024 * 1024


def lanes(shape):
    return lax.broadcasted_iota(jnp.int32, shape, len(shape) - 1)


def channel_table(channels, group_size, flip, value=1.0):
    shape = (group_size * SLOT, channels) if flip else (channels, group_size * SLOT)
    c = lax.broadcasted_iota(jnp.int32, shape, 1 if flip else 0)
    j = lax.broadcasted_iota(jnp.int32, shape, 0 if flip else 1)
    hit = c == (j & (SLOT - 1)) * group_size + (j >> (SLOT.bit_length() - 1))
    return jnp.where(hit, value, 0.0).astype(BF16)


def parity():
    return lax.rem(lax.axis_index("col"), 2)


def dot(a, b):
    return jnp.dot(a, b, preferred_element_type=F32)


def dot_nt(a, b):
    return lax.dot_general(a, b, (((1,), (1,)), ((), ())), preferred_element_type=F32)


def begin_kernel(out):
    out[...] = jnp.zeros(out.shape, F32)


def pack_kernel(ends, left, right, ct, even, odd, ctl, *rest):
    rims, ctf = rest[:-1], rest[-1]
    disp, rows, feat, cols = ct.shape
    per = 128 // feat
    for d in range(disp):
        block = ct[d].reshape(rows * feat, cols).astype(F32).T
        ctf[d * cols : (d + 1) * cols] = block
        ctl[d] = block.astype(BF16)
    columns = []
    for i, col in enumerate((cols - 1, 0)):
        block = ctf[pl.ds(col, disp, stride=cols), :]
        block = jnp.concatenate([block, jnp.zeros((disp, even.shape[1] - rows * feat), F32)], axis=1)
        edge = [x[h, col : col + 1].astype(F32) for x in (left, right) for h in range(rows)]
        columns.append(jnp.concatenate([block, *edge], axis=0))
    is_even = parity() == 0
    even[...] = jnp.where(is_even, columns[0], columns[1]).astype(BF16)
    odd[...] = jnp.where(is_even, columns[1], columns[0]).astype(BF16)
    for end, rim in zip(ends, rims):
        h = end()
        for q in range(disp // per):
            block = [ct[q * per + i, h].astype(F32) for i in range(per)]
            rim[q] = jnp.concatenate(block, axis=0).T.astype(BF16)


def pass_kernel(own, got, out):
    out[...] = jnp.where(parity() == 0, own[...].astype(F32), got[...].astype(F32)).astype(BF16)


def end_columns(by_even, by_odd):
    x, y = by_even[...].astype(F32), by_odd[...].astype(F32)
    is_even = parity() == 0
    return jnp.where(is_even, y, x), jnp.where(is_even, x, y)


def corner_kernel(ends, rows, disp, by_even, by_odd, *rest):
    pays, (edges, buf) = rest[: len(ends)], rest[len(ends) :]
    feat = 128 // rows
    per = 128 // feat
    count = disp // per
    lane = lanes((count, 128))
    for side, x in enumerate(end_columns(by_even, by_odd)):
        edges[side] = x[0:disp, 0:128]
    for end, pay in zip(ends, pays):
        h = end()
        buf[...] = jnp.zeros(buf.shape, F32)
        for side in range(2):
            out = jnp.zeros((count, 128), F32)
            for i in range(per):
                x = edges[side, pl.ds(i, count, stride=per)]
                first = pltpu.roll(x, feat * i, 1) if i else x
                last = pltpu.roll(x, (feat * (i - rows + 1)) % 128, 1) if i != rows - 1 else x
                x = jnp.where(h == 0, first, last)
                out = jnp.where((lane >= feat * i) & (lane < feat * (i + 1)), x, out)
            buf[8 * side : 8 * side + count] = out
        pay[...] = buf[...].astype(BF16)


def put_band(refs, h, column, block):
    fr, fr4, cols = refs
    at = fr.shape[1] - cols - PAD + column
    fr[h, at : at + block.shape[0]] = block
    fr4[h, at + STEP : at + STEP + block.shape[0]] = block


def own_kernel(group_size, left, right, fl, fr, fr4, mixed, wide_buf):
    rows, cols, channels = left.shape
    base, wide = rows * cols, group_size * SLOT
    mixed[0:base] = right[...].reshape(base, channels)
    mixed[base : 2 * base] = left[...].reshape(base, channels)
    wide_buf[...] = dot(mixed[...], channel_table(channels, group_size, False))
    tail = fr.shape[1]
    for h in range(rows):
        for ref in (fr, fr4):
            ref[h, 0:16] = jnp.zeros((16, wide), F32)
            ref[h, tail - 16 :] = jnp.zeros((16, wide), F32)
        put_band((fr, fr4, cols), h, 0, wide_buf[h * cols : (h + 1) * cols])
        fl[h, 0:PAD] = jnp.zeros((PAD, wide), F32)
        fl[h, PAD + cols :] = jnp.zeros((PAD, wide), F32)
        fl[h, PAD : PAD + cols] = wide_buf[base + h * cols : base + (h + 1) * cols] * (1.0 / group_size)


def volume_kernel(ends, group_size, near, far, by_even, by_odd, _fl, _fr, _fr4, fl, fr, fr4, vbuf, *rest):
    pays, (mixed, wide_buf) = rest[: len(ends)], rest[len(ends) :]
    rows, cols, channels = near.shape
    disp = vbuf.shape[1]
    reach = fr.shape[1] - cols - PAD
    wide = group_size * SLOT
    half, at_far = cols // 2, rows * cols
    base = at_far + rows * half
    mixed[0:at_far] = near[...].reshape(at_far, channels)
    mixed[at_far:base] = far[:, half:].reshape(rows * half, channels)
    count = disp + 2 * rows
    for i, x in enumerate(end_columns(by_even, by_odd)):
        mixed[base + i * count : base + (i + 1) * count] = x.astype(BF16)
    wide_buf[...] = dot(mixed[...], channel_table(channels, group_size, False))
    for h in range(rows):
        put_band((fr, fr4, cols), h, -cols, wide_buf[h * cols : (h + 1) * cols])
        at = at_far + h * half
        put_band((fr, fr4, cols), h, -cols - half, wide_buf[at : at + half])
        at = base + disp + h
        fl[h, PAD - 1 : PAD] = wide_buf[at : at + 1] * (1.0 / group_size)
        at += count
        fl[h, PAD + cols : PAD + cols + 1] = wide_buf[at : at + 1] * (1.0 / group_size)
        put_band((fr, fr4, cols), h, cols, wide_buf[at + rows : at + rows + 1])
    total = cols + 2 * PAD
    low = lanes((8, 128)) < SLOT
    pairs, times, lots = rows // 2, disp // 2, wide // 128
    count = total // 16

    def products(i, _):
        p, at = lax.rem(i, pairs), pl.multiple_of(lax.div(i, pairs) * (8 * count), 8)
        lefts = [
            [
                [fl[2 * p + o, pl.ds(at + 8 * b, 8), 128 * j : 128 * (j + 1)] for j in range(lots)]
                for b in range(count)
            ]
            for o in range(2)
        ]
        for odd, band in enumerate((fr, fr4)):
            for r in range(1 - times, count):
                start = pl.multiple_of(at + reach - PAD + 8 * r, 8)
                here = [
                    [band[2 * p + o, pl.ds(start, 8), 128 * j : 128 * (j + 1)] for j in range(lots)]
                    for o in range(2)
                ]
                for t in range(max(0, -r), min(times, count - r)):
                    sums = []
                    for o in range(2):
                        acc = lefts[o][r + t][0] * here[o][0]
                        for j in range(1, lots):
                            acc = acc + lefts[o][r + t][j] * here[o][j]
                        sums.append(acc + pltpu.roll(acc, SLOT, 1))
                    vbuf[p, 2 * t + odd, pl.ds(at + 8 * (r + t), 8)] = jnp.where(low, *sums)
        return 0

    lax.fori_loop(0, 2 * pairs, products, 0)
    big = lanes((total, 128)) < SLOT

    for dd in range(disp // 2):
        for end, pay in zip(ends, pays):
            h = end()
            if isinstance(h, int):
                halves = [vbuf[h // 2, 2 * dd + o] for o in range(2)]
                if h % 2 == 0:
                    halves[1] = pltpu.roll(halves[1], SLOT, 1)
                else:
                    halves[0] = pltpu.roll(halves[0], SLOT, 1)
                out = jnp.where(big, halves[0], halves[1])
            else:
                last = pairs - 1
                first = jnp.where(big, vbuf[0, 2 * dd], pltpu.roll(vbuf[0, 2 * dd + 1], SLOT, 1))
                final = jnp.where(
                    big, pltpu.roll(vbuf[last, 2 * dd], SLOT, 1), vbuf[last, 2 * dd + 1]
                )
                out = jnp.where(h == 0, first, final)
            pay[dd * total : (dd + 1) * total] = out.astype(BF16)


def weight_kernel(
    masks, groups, feat, vbuf, ctl, by_even, by_odd, top, bot, tops, bots, *rest
):
    keep_out, give_out, ctsh, vt, buf, sums = rest
    disp, cols, width = ctl.shape
    pairs, per, half = vbuf.shape[0], 128 // feat, disp // 2
    mtop, mbot = masks()
    ctsh[0, 0] = jnp.zeros(ctsh.shape[2:], BF16)
    ctsh[half, 1] = jnp.zeros(ctsh.shape[2:], BF16)
    lane_in, lane_one = lanes((cols, 128)), lanes((1, 128))
    shifts = (feat, 128 - feat)
    edges = [x[0:disp, 0:128] for x in end_columns(by_even, by_odd)]
    turned = [[pltpu.roll(x, shift, 1) for shift in shifts] for x in edges]

    def aligned(t, z, i):
        return (
            t if i == 0 else pltpu.roll(t, 128 - feat * i, 1),
            z if i == per - 1 else pltpu.roll(z, feat * (per - 1 - i), 1),
        )

    corners = [aligned(tops[...].astype(F32) * mtop, bots[...].astype(F32) * mbot, i) for i in range(per)]

    def fill(q):
        t = top[q].astype(F32) * mtop
        z = bot[q].astype(F32) * mbot
        for i in range(per):
            d = q * per + i
            rims = aligned(t, z, i)
            inner = ctl[d].astype(F32)
            for p, (rim, shift) in enumerate(zip(rims, shifts)):

                def on_rim(x):
                    return x < feat if p == 0 else x >= 128 - feat

                at = slice(128 * p, 128 * (p + 1))
                buf[d, PAD : PAD + cols, at] = jnp.where(
                    on_rim(lane_in), rim, pltpu.roll(inner, shift, 1)
                )
                for side, row in enumerate((PAD - 1, PAD + cols)):
                    corner = corners[i][p][8 * side + q : 8 * side + q + 1]
                    buf[d, row : row + 1, at] = jnp.where(
                        on_rim(lane_one), corner, turned[side][p][d : d + 1]
                    )
            for e in range(3):
                ctsh[(d + 1) // 2, (d + 1) % 2, :, 256 * e : 256 * (e + 1)] = buf[
                    d, PAD - 1 + e : PAD - 1 + e + cols
                ].astype(BF16)

    none = jnp.zeros((cols, 128), F32)
    for p in range(pairs):
        for j in range(-1, half + 1):
            block = [
                vbuf[p, d, PAD : PAD + cols] if 0 <= d < disp and 0 <= j + half * o else none
                for o, d in enumerate((j, j + half))
            ]
            if j == half:
                block[1] = none
            x = jnp.concatenate(block, axis=0).astype(BF16)
            vt[p, :, 128 * (j + 1) : 128 * (j + 2)] = x.T
    full = None
    for q in range(half // per):
        fill(q)
        fill(q + half // per)
        first, size = q * per, per * 128
        for p in range(pairs):
            left = jnp.concatenate(
                [vt[p, :, 128 * (2 - a + first) : 128 * (2 - a + first) + size] for a in range(3)], axis=0
            )
            right = jnp.concatenate(
                [
                    jnp.concatenate(
                        [
                            ctsh[(d + 1) // 2, (d + 1) % 2, :, 256 * e + 128 * p : 256 * e + 128 * (p + 1)]
                            for e in range(3)
                        ],
                        axis=1,
                    )
                    for j in range(first, first + per)
                    for d in (j, j + half)
                ],
                axis=0,
            )
            part = dot(left, right)
            full = part if full is None else full + part
    keep = lanes((groups, 128)) < 3 * feat
    sums[...] = jnp.zeros(sums.shape, F32)
    for a in range(3):
        for e in range(3):
            block = full[128 * a : 128 * (a + 1), 128 * e : 128 * (e + 1)]
            out = block[0:groups] + pltpu.roll(block[SLOT : SLOT + groups], 128 - feat, 1)
            at = 128 * a + groups * e
            sums[at : at + groups] = jnp.where(keep, out, 0.0)
    half = sums.shape[0] // 2
    is_even = parity() == 0
    low, high = sums[0:half], sums[half:]
    keep_out[...] = jnp.where(is_even, low, high)
    give_out[...] = jnp.where(is_even, high, low)


def right_kernel(ctsh, w2, fl, *rest):
    *grads, rg0, rg1, rg2, acce, acco, both = rest
    rows, cols, channels = rg0.shape
    disp, wide = grads[0].shape[1], fl.shape[2]
    group_size = wide // SLOT
    step = disp // 8
    low = lanes((step * cols, 128)) < SLOT

    def conv(q, p, gv):
        slabs = [
            ctsh[q * step + s // 2 : q * step + s // 2 + step, s % 2, :, 256 * e + 128 * p : 256 * e + 128 * (p + 1)]
            for s in range(4)
            for e in range(3)
        ]
        slabs = [x.reshape(step * cols, 128) for x in slabs]
        acc = dot(jnp.concatenate(slabs, axis=1), w2[...]).astype(BF16).astype(F32)
        for o in range(2):
            x = acc[:, 128 * o : 128 * (o + 1)]
            r = pltpu.roll(x, SLOT, 1)
            for hh in range(2):
                y = jnp.where(low, r, x) if hh else jnp.where(low, x, r)
                for j in range(step):
                    gv[hh, 2 * (q * step + j) + o] = y[j * cols : (j + 1) * cols]

    count = cols // 8
    back = acce.shape[1] - cols
    lead = back // 8

    lots = wide // 128

    def right_row(gv, p, hh):
        h = 2 * p + hh
        here = [
            [fl[h, PAD + 8 * b : PAD + 8 * b + 8, 128 * j : 128 * (j + 1)] for j in range(lots)]
            for b in range(count)
        ]
        for odd, buf in enumerate((acce, acco)):
            for k in range(lead + count):
                accs = [None] * lots
                for t in range(disp // 2):
                    b = k + t - lead
                    if b < 0 or b >= count:
                        continue
                    g = gv[hh, 2 * t + odd, 8 * b : 8 * b + 8]
                    for j in range(lots):
                        term = g * here[b][j]
                        accs[j] = term if accs[j] is None else accs[j] + term
                for j in range(lots):
                    x = jnp.zeros((8, 128), F32) if accs[j] is None else accs[j]
                    buf[h, 8 * k : 8 * k + 8, 128 * j : 128 * (j + 1)] = x
        acco[h, 8 * (lead + count) :] = jnp.zeros((8, wide), F32)

    parts = disp // 2 // step
    for p, gv in enumerate(grads):
        for q in range(parts):
            conv(q, p, gv)
            if p and q % 2:
                right_row(grads[p - 1], p - 1, q // 2)
    for hh in range(2):
        right_row(grads[-1], len(grads) - 1, hh)
    size = back + cols
    for h in range(rows):
        both[h * size : (h + 1) * size] = (acce[h] + acco[h, STEP : STEP + size]).astype(BF16)
    whole = dot(both[...], channel_table(channels, group_size, True)).astype(BF16)
    half = cols // 2
    for h in range(rows):
        at = h * size + back
        rg2[h] = whole[at - cols - half : at - cols]
        rg1[h] = whole[at - cols : at]
        rg0[h] = whole[at : at + cols]


def left_kernel(fr, fr4, *rest):
    *grads, lg, accl = rest
    rows, cols, channels = lg.shape
    disp, wide = grads[0].shape[1], fr.shape[2]
    group_size = wide // SLOT
    reach = fr.shape[1] - cols - PAD
    count, times, lots = cols // 8, disp // 2, wide // 128

    def left_row(gv, p, hh):
        h = 2 * p + hh
        accs = [[None] * lots for _ in range(count)]
        for odd, band in enumerate((fr, fr4)):
            for r in range(1 - times, count):
                at = reach + 8 * r
                here = [band[h, at : at + 8, 128 * j : 128 * (j + 1)] for j in range(lots)]
                for t in range(max(0, -r), min(times, count - r)):
                    g = gv[hh, 2 * t + odd, 8 * (r + t) : 8 * (r + t) + 8]
                    for j in range(lots):
                        term, acc = g * here[j], accs[r + t][j]
                        accs[r + t][j] = term if acc is None else acc + term
        for b in range(count):
            for j in range(lots):
                accl[h, 8 * b : 8 * b + 8, 128 * j : 128 * (j + 1)] = accs[b][j] * (1.0 / group_size)

    for p, gv in enumerate(grads):
        for hh in range(2):
            left_row(gv, p, hh)
    whole = accl[...].reshape(rows * cols, wide).astype(BF16)
    out = dot(whole, channel_table(channels, group_size, True)).astype(BF16)
    lg[...] = out.reshape(rows, cols, channels)


def combine_kernel(got, rg2, out):
    cols = out.shape[1]
    half = cols // 2
    part = jnp.where(parity() == 0, 0.0, got[...].astype(F32))
    out[:, 0:half] = part[:, 0:half].astype(BF16)
    out[:, half:] = (part[:, half:] + rg2[...].astype(F32)).astype(BF16)


def halo_lanes(groups):
    first = SLOT - groups
    assert groups - first <= first
    return (groups, SLOT, groups), (SLOT + groups, SLOT + 2 * groups - first, SLOT + groups - first)


def place_halo(base, row, groups, offset, lane):
    for start, end, shift in halo_lanes(groups):
        moved = pltpu.roll(row, (shift - offset) % 128, 1)
        base = jnp.where((lane >= start) & (lane < end), moved, base)
    return base


def conv_kernel(masks, groups, vbuf, top, bot, wc, out, taps, buf, held, sems):
    disp, rows, feat, cols = out.shape
    total = buf.shape[2]
    lane = lanes((total, 128))
    zeros = jnp.zeros((cols, taps.shape[3]), BF16)
    taps[0, 0] = zeros
    taps[disp // 2, 1] = zeros
    halos_of = [(ref, mask) for ref, mask in zip((top, bot), masks())]

    def build(dd):
        for p, (ref, mask) in enumerate(halos_of):
            row = ref[dd * total : (dd + 1) * total].astype(F32) * mask
            for o in range(2):
                d = 2 * dd + o
                buf[p, d] = place_halo(vbuf[p, d], row, groups, SLOT * o, lane)
                for e in range(3):
                    at = 256 * e + 128 * p
                    taps[(d + 1) // 2, (d + 1) % 2, :, at : at + 128] = buf[
                        p, d, PAD - 1 + e : PAD - 1 + e + cols
                    ].astype(BF16)

    parts = sems.shape[0]
    step = disp // 2 // parts
    copies = []
    build(0)
    for q in range(parts):
        for dd in range(q * step + 1, min((q + 1) * step + 1, disp // 2)):
            build(dd)
        slabs = [
            taps[q * step + s // 2 : q * step + s // 2 + step, s % 2].reshape(step * cols, taps.shape[3])
            for s in range(4)
        ]
        acc = dot(jnp.concatenate(slabs, axis=1), wc[...])
        for j in range(step):
            both = acc[j * cols : (j + 1) * cols].astype(BF16).T
            for o in range(2):
                block = both[rows * feat * o : rows * feat * (o + 1)]
                held[2 * (q * step + j) + o] = block.reshape(rows, feat, cols)
        at = pl.ds(2 * q * step, 2 * step)
        copies.append(pltpu.make_async_copy(held.at[at], out.at[at], sems.at[q]))
        copies[-1].start()
    for copy in copies:
        copy.wait()


def finish_kernel(scale, mine, other, own, near, far, left, weight, right, left_out, held_w, held_r, sems):
    _, _, _, feat, groups = weight.shape
    copies = [pltpu.make_async_copy(left, left_out, sems.at[0])]
    copies[0].start()
    is_even = parity() == 0
    beside = jnp.where(is_even, near[...].astype(F32), 0.0)
    held_r[...] = (own[...].astype(F32) + beside + far[...].astype(F32)).astype(BF16)
    copies.append(pltpu.make_async_copy(held_r, right, sems.at[1]))
    copies[1].start()
    x, y = mine[...] * scale, other[...] * scale
    total = jnp.concatenate([jnp.where(is_even, x, y), jnp.where(is_even, y, x)], axis=0)
    for a in range(3):
        for e in range(3):
            at = 128 * a + groups * e
            block = total[at : at + groups].T
            for b in range(3):
                held_w[2 - a, 2 - b, 2 - e] = block[feat * b : feat * (b + 1)]
        copies.append(pltpu.make_async_copy(held_w.at[2 - a], weight.at[2 - a], sems.at[2 + a]))
        copies[-1].start()
    for copy in copies:
        copy.wait()


def copy_kernel(*refs):
    half = len(refs) // 2
    for src, dst in zip(refs[:half], refs[half:]):
        dst[...] = src[...]


def sum_kernel(*refs):
    *parts, out = refs
    out[...] = tree([ref[...].astype(F32) for ref in parts]).astype(out.dtype)


def tree(terms):
    while len(terms) > 1:
        terms = [terms[i] + terms[i + 1] for i in range(0, len(terms), 2)]
    return terms[0]


def taps_kernel(taps, w2, wc, turned):
    _, _, _, feat, groups = taps.shape
    rows = wc.shape[1] // 2 // feat
    lane_of = lanes((feat, 2 * SLOT))
    low = lanes((feat, 2 * SLOT)) < SLOT
    zero = jnp.zeros((feat, 2 * SLOT), F32)

    def wide(a, b, e):
        if not 0 <= b <= 2:
            return None
        return jnp.concatenate([taps[a, b, e].astype(F32), zero[:, groups:]], axis=1)

    def beside(x, y):
        if x is None and y is None:
            return zero
        x = zero if x is None else x
        y = zero if y is None else pltpu.roll(y, SLOT, 1)
        return jnp.where(low, x, y)

    def build(a, _):
        def at_row(h):
            return pl.multiple_of((a * rows + h) * feat, feat)

        for e in range(3):
            for h in range(rows):
                for p in range(rows // 2):
                    lane = SLOT * (rows * e + 2 * p)
                    block = beside(wide(a, 2 * p - h + 1, e), wide(a, 2 * p + 1 - h + 1, e))
                    if h == 0 and p == 0:
                        block = place_halo(block, wide(a, 0, e), groups, 0, lane_of)
                    if h == rows - 1 and p == rows // 2 - 1:
                        block = place_halo(block, wide(a, 2, e), groups, 0, lane_of)
                    turned[pl.ds(at_row(h), feat), lane : lane + 2 * SLOT] = block
        return 0

    lax.fori_loop(0, 3, build, 0)
    for s in range(4):
        for e in range(3):
            for r in range(4):
                for o in range(2):
                    taps_of = [None if not 0 <= s - o <= 2 else wide(2 - s + o, 2 - r + i, 2 - e) for i in range(2)]
                    at = 384 * s + 128 * e + feat * r
                    w2[at : at + feat, 128 * o : 128 * (o + 1)] = beside(*taps_of).astype(BF16)
    depth, size = turned.shape[1], rows * feat
    for a in range(3):
        for i in range(depth // 128):
            x = turned[size * a : size * (a + 1), 128 * i : 128 * (i + 1)].T.astype(BF16)
            for o in range(2):
                at = depth * (a + o) + 128 * i
                wc[at : at + 128, size * o : size * (o + 1)] = x
    for o in range(2):
        at = depth * 3 * (1 - o)
        wc[at : at + depth, size * o : size * (o + 1)] = jnp.zeros((depth, size), BF16)


TOKEN = ((8, 128), F32)


def with_token(kernel, inputs, outputs):
    def run(*refs):
        kernel(*refs[: inputs + outputs], *refs[inputs + outputs + 1 :])
        refs[inputs + outputs][...] = jnp.zeros(TOKEN[0], F32)

    return run


def call(kernel, outs, scratch, *args, after=(), token=False, us=0.0, alias=(), hbm=()):
    skip = len(after)
    if token:
        kernel = with_token(kernel, len(args), len(outs))
        outs = [*outs, TOKEN]
    return pl.pallas_call(
        lambda *refs: kernel(*refs[skip:]),
        out_shape=[jax.ShapeDtypeStruct(s, t) for s, t in outs],
        in_specs=[pl.BlockSpec(memory_space=pl.ANY)] * skip + [VMEM] * len(args),
        out_specs=[pl.BlockSpec(memory_space=pl.ANY) if i in hbm else VMEM for i in range(len(outs))],
        scratch_shapes=scratch,
        input_output_aliases={skip + i: o for i, o in alias},
        compiler_params=pltpu.CompilerParams(vmem_limit_bytes=LIMIT),
        cost_estimate=pl.CostEstimate(
            flops=int(us * 1.15e9), bytes_accessed=int(us * 3.7e6), transcendentals=0
        ),
    )(*after, *args)


def col_shift(block, distance):
    n = lax.axis_size("col")
    route = [(i - distance, i) for i in range(n) if 0 <= i - distance < n]
    return lax.ppermute(block, "col", route)


def row_shift(block, distance):
    n = lax.axis_size("row")
    route = [(i - distance, i) for i in range(n) if 0 <= i - distance < n]
    return lax.ppermute(block, "row", route)


def halos(pays):
    if lax.axis_size("row") == 2:
        got = lax.ppermute(pays[0], "row", [(0, 1), (1, 0)])
        return got, got
    return row_shift(pays[0], 1), row_shift(pays[1], -1)


def partners(n_row, n_col):
    col_bits = [1 << i for i in range(1, n_col.bit_length() - 1)]
    row_bits = [n_col << i for i in range(n_row.bit_length() - 1)]
    assert n_col == 2 << len(col_bits) and n_row == 1 << len(row_bits)
    return [*col_bits[:2], sum(col_bits[:2])], col_bits[2:], row_bits


def on_device(left_features, right_features, conv_weight, cotangent):
    rows, cols, channels = left_features.shape
    disp, feat = cotangent.shape[0], cotangent.shape[3]
    groups = conv_weight.shape[3]
    group_size = channels // groups
    wide = group_size * SLOT
    n_row, n_col = lax.axis_size("row"), lax.axis_size("col")
    per = 128 // feat

    if n_row == 2:
        ends = [lambda: (rows - 1) * (1 - lax.axis_index("row"))]
    else:
        ends = [lambda: rows - 1, lambda: 0]
    n = len(ends)

    def masks():
        at = lax.axis_index("row")
        return (
            jnp.where(at > 0, 1.0, 0.0).astype(F32),
            jnp.where(at < n_row - 1, 1.0, 0.0).astype(F32),
        )

    total = cols + 2 * PAD
    count = disp + 2 * rows
    ct = cotangent.transpose(0, 1, 3, 2)

    def swap(block, mask):
        route = [(i, i ^ mask) for i in range(n_row * n_col)]
        return lax.ppermute(block, ("row", "col"), route)

    far = col_shift(right_features, 2)
    (begun,) = call(begin_kernel, [TOKEN], [], us=3.0)
    by_even, by_odd, ctl, *rims = call(
        functools.partial(pack_kernel, ends),
        [
            ((count, channels), BF16),
            ((count, channels), BF16),
            ((disp, cols, rows * feat), BF16),
        ]
        + [((disp // per, cols, 128), BF16)] * n,
        [pltpu.VMEM((disp * cols, rows * feat), F32)],
        left_features,
        right_features,
        ct,
        after=[begun],
        us=0.4,
    )
    inner = range(1, n_col - 1, 2)
    by_even = swap(by_even, 1)
    by_odd = lax.ppermute(by_odd, "col", [(i, i + 1) for i in inner] + [(i + 1, i) for i in inner])
    band = 104 + cols + PAD
    banks = [((rows, total, wide), F32), ((rows, band, wide), F32), ((rows, band, wide), F32)]
    spread_rows = 2 * rows * cols
    fl, fr, fr4 = call(
        functools.partial(own_kernel, group_size),
        banks,
        [pltpu.VMEM((spread_rows, channels), BF16), pltpu.VMEM((spread_rows, wide), F32)],
        left_features,
        right_features,
        after=[ctl],
    )
    (passed,) = call(
        pass_kernel, [((rows, cols, channels), BF16)], [], right_features, far, after=[fl]
    )
    near = swap(passed, 1)
    top, bot = halos(rims)
    corner_pays = call(
        functools.partial(corner_kernel, ends, rows, disp),
        [((16, 128), BF16)] * n,
        [pltpu.VMEM((2, disp, 128), F32), pltpu.VMEM((16, 128), F32)],
        by_even,
        by_odd,
        after=[passed],
        us=5.0,
    )
    tops, bots = halos(corner_pays)
    spread_rows = rows * cols + rows * cols // 2 + 2 * count
    fl, fr, fr4, vbuf, *volume_rows = call(
        functools.partial(volume_kernel, ends, group_size),
        banks
        + [((rows // 2, disp, total, 2 * SLOT), F32)]
        + [((disp // 2 * total, 128), BF16)] * n,
        [pltpu.VMEM((spread_rows, channels), BF16), pltpu.VMEM((spread_rows, wide), F32)],
        near,
        far,
        by_even,
        by_odd,
        fl,
        fr,
        fr4,
        us=1.8,
        alias=[(4, 0), (5, 1), (6, 2)],
    )
    vtop, vbot = halos(volume_rows)
    keep, give, ctsh = call(
        functools.partial(weight_kernel, masks, groups, feat),
        [((3 * 64, 128), F32), ((3 * 64, 128), F32), ((disp // 2 + 1, 2, cols, 3 * 256), BF16)],
        [
            pltpu.VMEM((rows // 2, 128, (disp // 2 + 2) * 128), BF16),
            pltpu.VMEM((disp, total, 256), F32),
            pltpu.VMEM((3 * 128, 128), F32),
        ],
        vbuf, ctl, by_even, by_odd, top, bot, tops, bots,
        us=2.0,
    )

    got = swap(give, 1)
    w2, wc = call(
        taps_kernel,
        [((12 * 128, 2 * 128), BF16), ((4 * 3 * rows * SLOT, 2 * rows * feat), BF16)],
        [pltpu.VMEM((3 * rows * feat, 3 * rows * SLOT), F32)],
        conv_weight.transpose(0, 1, 2, 4, 3),
        after=[keep],
    )
    (part,) = call(sum_kernel, [(keep.shape, BF16)], [], keep, got, after=[w2])
    *grads, rg0, rg1, rg2 = call(
        right_kernel,
        [((2, disp, cols, 128), F32)] * (rows // 2)
        + [
            ((rows, cols, channels), BF16),
            ((rows, cols, channels), BF16),
            ((rows, cols // 2, channels), BF16),
        ],
        [
            pltpu.VMEM((rows, cols + cols + cols // 2, wide), F32),
            pltpu.VMEM((rows, cols + cols + cols // 2 + 8, wide), F32),
            pltpu.VMEM((rows * (cols + cols + cols // 2), wide), BF16),
        ],
        ctsh, w2, fl,
        after=[part],
        us=0.4,
    )
    rg1 = swap(rg1, 1)
    def join(part, mask, kind, after, us):
        terms = (part, swap(part, mask))
        return call(sum_kernel, [(part.shape, kind)], [], *terms, after=after, us=us)[0]

    three, along_cols, along_rows = partners(n_row, n_col)
    parts = [part] + [swap(part, m) for m in three]
    (part,) = call(sum_kernel, [(part.shape, BF16)], [], *parts, after=[rg0, vtop], us=4.0)
    (rg2,) = call(
        combine_kernel, [((rows, cols, channels), BF16)], [], rg1, rg2, after=[part]
    )
    order = [rg2]
    for mask in along_cols:
        part = join(part, mask, BF16, after=order, us=4.0)
        order = []
    output, conv_done = call(
        functools.partial(conv_kernel, masks, groups),
        [((disp, rows, feat, cols), BF16)],
        [
            pltpu.VMEM((disp // 2 + 1, 2, cols, 3 * rows * SLOT), BF16),
            pltpu.VMEM((rows // 2, disp, total, 128), F32),
            pltpu.VMEM((disp, rows, feat, cols), BF16),
            pltpu.SemaphoreType.DMA((4,)),
        ],
        vbuf, vtop, vbot, wc,
        after=[part],
        token=True,
        us=3.0,
        hbm=[0],
    )
    order = [conv_done]
    for mask in along_rows:
        part = join(part, mask, F32, after=order, us=4.0)
        order = []
    (lg,) = call(
        left_kernel,
        [((rows, cols, channels), BF16)],
        [pltpu.VMEM((rows, cols, wide), F32)],
        fr, fr4, *grads,
        after=[part],
        us=1.9,
    )
    rg2 = col_shift(rg2, -2)
    cells = disp * rows * n_row * cols * n_col
    weight_grad, right_grad, left_grad = call(
        functools.partial(finish_kernel, 1.0 / math.sqrt(cells)),
        [
            ((3, 3, 3, feat, groups), F32),
            ((rows, cols, channels), BF16),
            ((rows, cols, channels), BF16),
        ],
        [
            pltpu.VMEM((3, 3, 3, feat, groups), F32),
            pltpu.VMEM((rows, cols, channels), BF16),
            pltpu.SemaphoreType.DMA((5,)),
        ],
        part, swap(part, 1), rg0, rg1, rg2, lg,
        us=1.0,
        hbm=[0, 1, 2],
    )
    return (
        output.transpose(0, 1, 3, 2),
        weight_grad.transpose(0, 1, 2, 4, 3),
        left_grad,
        right_grad,
    )


def solution(mesh):
    in_specs = (P("row", "col", None), P("row", "col", None), P(), P(None, "row", "col", None))
    out_specs = (P(None, "row", "col", None), P(), P("row", "col", None), P("row", "col", None))
    return jax.shard_map(
        on_device, mesh=mesh, in_specs=in_specs, out_specs=out_specs, check_vma=False
    )
```

```python
import functools
import math

import jax
import jax.numpy as jnp
from jax import lax
from jax.experimental import pallas as pl
from jax.experimental.pallas import tpu as pltpu
from jax.sharding import PartitionSpec as P

DISP = 24
STEP = 4
SLOT = 64
PAD = 8
F32 = jnp.float32
BF16 = jnp.bfloat16
VMEM = pl.BlockSpec(memory_space=pltpu.VMEM)
LIMIT = 16 * 1024 * 1024


def lanes(shape):
    return lax.broadcasted_iota(jnp.int32, shape, len(shape) - 1)


def channel_table(channels, group_size, flip, value=1.0):
    shape = (group_size * SLOT, channels) if flip else (channels, group_size * SLOT)
    c = lax.broadcasted_iota(jnp.int32, shape, 1 if flip else 0)
    j = lax.broadcasted_iota(jnp.int32, shape, 0 if flip else 1)
    hit = c == (j & (SLOT - 1)) * group_size + (j >> (SLOT.bit_length() - 1))
    return jnp.where(hit, value, 0.0).astype(BF16)


def parity():
    return lax.rem(lax.axis_index("col"), 2)


def dot(a, b):
    return jnp.dot(a, b, preferred_element_type=F32)


def dot_nt(a, b):
    return lax.dot_general(a, b, (((1,), (1,)), ((), ())), preferred_element_type=F32)


def begin_kernel(out):
    out[...] = jnp.zeros(out.shape, F32)


def pack_kernel(ends, left, right, ct, even, odd, ctl, *rest):
    rims, ctf = rest[:-1], rest[-1]
    disp, rows, feat, cols = ct.shape
    per = 128 // feat
    for d in range(disp):
        block = ct[d].reshape(rows * feat, cols).astype(F32).T
        ctf[d * cols : (d + 1) * cols] = block
        ctl[d] = block.astype(BF16)
    columns = []
    for i, col in enumerate((cols - 1, 0)):
        block = ctf[pl.ds(col, disp, stride=cols), :]
        block = jnp.concatenate([block, jnp.zeros((disp, even.shape[1] - rows * feat), F32)], axis=1)
        edge = [x[h, col : col + 1].astype(F32) for x in (left, right) for h in range(rows)]
        columns.append(jnp.concatenate([block, *edge], axis=0))
    is_even = parity() == 0
    even[...] = jnp.where(is_even, columns[0], columns[1]).astype(BF16)
    odd[...] = jnp.where(is_even, columns[1], columns[0]).astype(BF16)
    for end, rim in zip(ends, rims):
        h = end()
        for q in range(disp // per):
            block = [ct[q * per + i, h].astype(F32) for i in range(per)]
            rim[q] = jnp.concatenate(block, axis=0).T.astype(BF16)


def pass_kernel(own, got, out):
    out[...] = jnp.where(parity() == 0, own[...].astype(F32), got[...].astype(F32)).astype(BF16)


def end_columns(by_even, by_odd):
    x, y = by_even[...].astype(F32), by_odd[...].astype(F32)
    is_even = parity() == 0
    return jnp.where(is_even, y, x), jnp.where(is_even, x, y)


def corner_kernel(ends, rows, disp, by_even, by_odd, *rest):
    pays, (edges, buf) = rest[: len(ends)], rest[len(ends) :]
    feat = 128 // rows
    per = 128 // feat
    count = disp // per
    lane = lanes((count, 128))
    for side, x in enumerate(end_columns(by_even, by_odd)):
        edges[side] = x[0:disp, 0:128]
    for end, pay in zip(ends, pays):
        h = end()
        buf[...] = jnp.zeros(buf.shape, F32)
        for side in range(2):
            out = jnp.zeros((count, 128), F32)
            for i in range(per):
                x = edges[side, pl.ds(i, count, stride=per)]
                first = pltpu.roll(x, feat * i, 1) if i else x
                last = pltpu.roll(x, (feat * (i - rows + 1)) % 128, 1) if i != rows - 1 else x
                x = jnp.where(h == 0, first, last)
                out = jnp.where((lane >= feat * i) & (lane < feat * (i + 1)), x, out)
            buf[8 * side : 8 * side + count] = out
        pay[...] = buf[...].astype(BF16)


def put_band(refs, h, column, block):
    fr, fr4, cols = refs
    at = fr.shape[1] - cols - PAD + column
    fr[h, at : at + block.shape[0]] = block
    fr4[h, at + STEP : at + STEP + block.shape[0]] = block


def own_kernel(group_size, left, right, fl, fr, fr4, mixed, wide_buf):
    rows, cols, channels = left.shape
    base, wide = rows * cols, group_size * SLOT
    mixed[0:base] = right[...].reshape(base, channels)
    mixed[base : 2 * base] = left[...].reshape(base, channels)
    wide_buf[...] = dot(mixed[...], channel_table(channels, group_size, False))
    tail = fr.shape[1]
    for h in range(rows):
        for ref in (fr, fr4):
            ref[h, 0:16] = jnp.zeros((16, wide), F32)
            ref[h, tail - 16 :] = jnp.zeros((16, wide), F32)
        put_band((fr, fr4, cols), h, 0, wide_buf[h * cols : (h + 1) * cols])
        fl[h, 0:PAD] = jnp.zeros((PAD, wide), F32)
        fl[h, PAD + cols :] = jnp.zeros((PAD, wide), F32)
        fl[h, PAD : PAD + cols] = wide_buf[base + h * cols : base + (h + 1) * cols] * (1.0 / group_size)


def volume_kernel(ends, group_size, near, far, by_even, by_odd, _fl, _fr, _fr4, fl, fr, fr4, vbuf, *rest):
    pays, (mixed, wide_buf) = rest[: len(ends)], rest[len(ends) :]
    rows, cols, channels = near.shape
    disp = vbuf.shape[1]
    reach = fr.shape[1] - cols - PAD
    wide = group_size * SLOT
    half, at_far = cols // 2, rows * cols
    base = at_far + rows * half
    mixed[0:at_far] = near[...].reshape(at_far, channels)
    mixed[at_far:base] = far[:, half:].reshape(rows * half, channels)
    count = disp + 2 * rows
    for i, x in enumerate(end_columns(by_even, by_odd)):
        mixed[base + i * count : base + (i + 1) * count] = x.astype(BF16)
    wide_buf[...] = dot(mixed[...], channel_table(channels, group_size, False))
    for h in range(rows):
        put_band((fr, fr4, cols), h, -cols, wide_buf[h * cols : (h + 1) * cols])
        at = at_far + h * half
        put_band((fr, fr4, cols), h, -cols - half, wide_buf[at : at + half])
        at = base + disp + h
        fl[h, PAD - 1 : PAD] = wide_buf[at : at + 1] * (1.0 / group_size)
        at += count
        fl[h, PAD + cols : PAD + cols + 1] = wide_buf[at : at + 1] * (1.0 / group_size)
        put_band((fr, fr4, cols), h, cols, wide_buf[at + rows : at + rows + 1])
    total = cols + 2 * PAD
    low = lanes((8, 128)) < SLOT
    pairs, times, lots = rows // 2, disp // 2, wide // 128
    count = total // 16

    def products(p, at):
        lefts = [
            [
                [fl[2 * p + o, at + 8 * b : at + 8 * b + 8, 128 * j : 128 * (j + 1)] for j in range(lots)]
                for b in range(count)
            ]
            for o in range(2)
        ]
        for odd, band in enumerate((fr, fr4)):
            for r in range(1 - times, count):
                start = at + reach - PAD + 8 * r
                here = [
                    [band[2 * p + o, start : start + 8, 128 * j : 128 * (j + 1)] for j in range(lots)]
                    for o in range(2)
                ]
                for t in range(max(0, -r), min(times, count - r)):
                    sums = []
                    for o in range(2):
                        acc = lefts[o][r + t][0] * here[o][0]
                        for j in range(1, lots):
                            acc = acc + lefts[o][r + t][j] * here[o][j]
                        sums.append(acc + pltpu.roll(acc, SLOT, 1))
                    row = at + 8 * (r + t)
                    vbuf[p, 2 * t + odd, row : row + 8] = jnp.where(low, *sums)

    for at in (8 * count, 0):
        for p in range(pairs):
            products(p, at)
    big = lanes((total, 128)) < SLOT

    for dd in range(disp // 2):
        for end, pay in zip(ends, pays):
            h = end()
            if isinstance(h, int):
                halves = [vbuf[h // 2, 2 * dd + o] for o in range(2)]
                if h % 2 == 0:
                    halves[1] = pltpu.roll(halves[1], SLOT, 1)
                else:
                    halves[0] = pltpu.roll(halves[0], SLOT, 1)
                out = jnp.where(big, halves[0], halves[1])
            else:
                last = pairs - 1
                first = jnp.where(big, vbuf[0, 2 * dd], pltpu.roll(vbuf[0, 2 * dd + 1], SLOT, 1))
                final = jnp.where(
                    big, pltpu.roll(vbuf[last, 2 * dd], SLOT, 1), vbuf[last, 2 * dd + 1]
                )
                out = jnp.where(h == 0, first, final)
            pay[dd * total : (dd + 1) * total] = out.astype(BF16)


def weight_kernel(
    masks, groups, feat, vbuf, ctl, by_even, by_odd, top, bot, tops, bots, *rest
):
    keep_out, give_out, ctsh, vt, buf, sums = rest
    disp, cols, width = ctl.shape
    pairs, per, half = vbuf.shape[0], 128 // feat, disp // 2
    mtop, mbot = masks()
    ctsh[0, 0] = jnp.zeros(ctsh.shape[2:], BF16)
    ctsh[half, 1] = jnp.zeros(ctsh.shape[2:], BF16)
    lane_in, lane_one = lanes((cols, 128)), lanes((1, 128))
    shifts = (feat, 128 - feat)
    edges = [x[0:disp, 0:128] for x in end_columns(by_even, by_odd)]
    turned = [[pltpu.roll(x, shift, 1) for shift in shifts] for x in edges]

    def aligned(t, z, i):
        return (
            t if i == 0 else pltpu.roll(t, 128 - feat * i, 1),
            z if i == per - 1 else pltpu.roll(z, feat * (per - 1 - i), 1),
        )

    corners = [aligned(tops[...].astype(F32) * mtop, bots[...].astype(F32) * mbot, i) for i in range(per)]

    def fill(q):
        t = top[q].astype(F32) * mtop
        z = bot[q].astype(F32) * mbot
        for i in range(per):
            d = q * per + i
            rims = aligned(t, z, i)
            inner = ctl[d].astype(F32)
            for p, (rim, shift) in enumerate(zip(rims, shifts)):

                def on_rim(x):
                    return x < feat if p == 0 else x >= 128 - feat

                at = slice(128 * p, 128 * (p + 1))
                buf[d, PAD : PAD + cols, at] = jnp.where(
                    on_rim(lane_in), rim, pltpu.roll(inner, shift, 1)
                )
                for side, row in enumerate((PAD - 1, PAD + cols)):
                    corner = corners[i][p][8 * side + q : 8 * side + q + 1]
                    buf[d, row : row + 1, at] = jnp.where(
                        on_rim(lane_one), corner, turned[side][p][d : d + 1]
                    )
            for e in range(3):
                ctsh[(d + 1) // 2, (d + 1) % 2, :, 256 * e : 256 * (e + 1)] = buf[
                    d, PAD - 1 + e : PAD - 1 + e + cols
                ].astype(BF16)

    none = jnp.zeros((cols, 128), F32)
    for p in range(pairs):
        for j in range(-1, half + 1):
            block = [
                vbuf[p, d, PAD : PAD + cols] if 0 <= d < disp and 0 <= j + half * o else none
                for o, d in enumerate((j, j + half))
            ]
            if j == half:
                block[1] = none
            x = jnp.concatenate(block, axis=0).astype(BF16)
            vt[p, :, 128 * (j + 1) : 128 * (j + 2)] = x.T
    full = None
    for q in range(half // per):
        fill(q)
        fill(q + half // per)
        first, size = q * per, per * 128
        for p in range(pairs):
            left = jnp.concatenate(
                [vt[p, :, 128 * (2 - a + first) : 128 * (2 - a + first) + size] for a in range(3)], axis=0
            )
            right = jnp.concatenate(
                [
                    jnp.concatenate(
                        [
                            ctsh[(d + 1) // 2, (d + 1) % 2, :, 256 * e + 128 * p : 256 * e + 128 * (p + 1)]
                            for e in range(3)
                        ],
                        axis=1,
                    )
                    for j in range(first, first + per)
                    for d in (j, j + half)
                ],
                axis=0,
            )
            part = dot(left, right)
            full = part if full is None else full + part
    keep = lanes((groups, 128)) < 3 * feat
    sums[...] = jnp.zeros(sums.shape, F32)
    for a in range(3):
        for e in range(3):
            block = full[128 * a : 128 * (a + 1), 128 * e : 128 * (e + 1)]
            out = block[0:groups] + pltpu.roll(block[SLOT : SLOT + groups], 128 - feat, 1)
            at = 128 * a + groups * e
            sums[at : at + groups] = jnp.where(keep, out, 0.0)
    half = sums.shape[0] // 2
    is_even = parity() == 0
    low, high = sums[0:half], sums[half:]
    keep_out[...] = jnp.where(is_even, low, high)
    give_out[...] = jnp.where(is_even, high, low)


def right_kernel(ctsh, w2, fl, *rest):
    *grads, rg0, rg1, rg2, acce, acco, both = rest
    rows, cols, channels = rg0.shape
    disp, wide = grads[0].shape[1], fl.shape[2]
    group_size = wide // SLOT
    step = disp // 4
    low = lanes((step * cols, 128)) < SLOT

    def conv(q, p, gv):
        slabs = [
            ctsh[q * step + s // 2 : q * step + s // 2 + step, s % 2, :, 256 * e + 128 * p : 256 * e + 128 * (p + 1)]
            for s in range(4)
            for e in range(3)
        ]
        slabs = [x.reshape(step * cols, 128) for x in slabs]
        acc = dot(jnp.concatenate(slabs, axis=1), w2[...]).astype(BF16).astype(F32)
        for o in range(2):
            x = acc[:, 128 * o : 128 * (o + 1)]
            r = pltpu.roll(x, SLOT, 1)
            for hh in range(2):
                y = jnp.where(low, r, x) if hh else jnp.where(low, x, r)
                for j in range(step):
                    gv[hh, 2 * (q * step + j) + o] = y[j * cols : (j + 1) * cols]

    count = cols // 8
    back = acce.shape[1] - cols
    lead = back // 8

    lots = wide // 128

    def right_row(gv, p, hh):
        h = 2 * p + hh
        here = [
            [fl[h, PAD + 8 * b : PAD + 8 * b + 8, 128 * j : 128 * (j + 1)] for j in range(lots)]
            for b in range(count)
        ]
        for odd, buf in enumerate((acce, acco)):
            for k in range(lead + count):
                accs = [None] * lots
                for t in range(disp // 2):
                    b = k + t - lead
                    if b < 0 or b >= count:
                        continue
                    g = gv[hh, 2 * t + odd, 8 * b : 8 * b + 8]
                    for j in range(lots):
                        term = g * here[b][j]
                        accs[j] = term if accs[j] is None else accs[j] + term
                for j in range(lots):
                    x = jnp.zeros((8, 128), F32) if accs[j] is None else accs[j]
                    buf[h, 8 * k : 8 * k + 8, 128 * j : 128 * (j + 1)] = x
        acco[h, 8 * (lead + count) :] = jnp.zeros((8, wide), F32)

    parts = disp // 2 // step
    for p, gv in enumerate(grads):
        for q in range(parts):
            conv(q, p, gv)
            if p:
                right_row(grads[p - 1], p - 1, q)
    for hh in range(2):
        right_row(grads[-1], len(grads) - 1, hh)
    size = back + cols
    for h in range(rows):
        both[h * size : (h + 1) * size] = (acce[h] + acco[h, STEP : STEP + size]).astype(BF16)
    whole = dot(both[...], channel_table(channels, group_size, True)).astype(BF16)
    half = cols // 2
    for h in range(rows):
        at = h * size + back
        rg2[h] = whole[at - cols - half : at - cols]
        rg1[h] = whole[at - cols : at]
        rg0[h] = whole[at : at + cols]


def left_kernel(fr, fr4, *rest):
    *grads, lg, accl = rest
    rows, cols, channels = lg.shape
    disp, wide = grads[0].shape[1], fr.shape[2]
    group_size = wide // SLOT
    reach = fr.shape[1] - cols - PAD
    count, times, lots = cols // 8, disp // 2, wide // 128

    def left_row(gv, p, hh):
        h = 2 * p + hh
        accs = [[None] * lots for _ in range(count)]
        for odd, band in enumerate((fr, fr4)):
            for r in range(1 - times, count):
                at = reach + 8 * r
                here = [band[h, at : at + 8, 128 * j : 128 * (j + 1)] for j in range(lots)]
                for t in range(max(0, -r), min(times, count - r)):
                    g = gv[hh, 2 * t + odd, 8 * (r + t) : 8 * (r + t) + 8]
                    for j in range(lots):
                        term, acc = g * here[j], accs[r + t][j]
                        accs[r + t][j] = term if acc is None else acc + term
        for b in range(count):
            for j in range(lots):
                accl[h, 8 * b : 8 * b + 8, 128 * j : 128 * (j + 1)] = accs[b][j] * (1.0 / group_size)

    for p, gv in enumerate(grads):
        for hh in range(2):
            left_row(gv, p, hh)
    whole = accl[...].reshape(rows * cols, wide).astype(BF16)
    out = dot(whole, channel_table(channels, group_size, True)).astype(BF16)
    lg[...] = out.reshape(rows, cols, channels)


def combine_kernel(got, rg2, out):
    cols = out.shape[1]
    half = cols // 2
    part = jnp.where(parity() == 0, 0.0, got[...].astype(F32))
    out[:, 0:half] = part[:, 0:half].astype(BF16)
    out[:, half:] = (part[:, half:] + rg2[...].astype(F32)).astype(BF16)


def halo_lanes(groups):
    first = SLOT - groups
    assert groups - first <= first
    return (groups, SLOT, groups), (SLOT + groups, SLOT + 2 * groups - first, SLOT + groups - first)


def place_halo(base, row, groups, offset, lane):
    for start, end, shift in halo_lanes(groups):
        moved = pltpu.roll(row, (shift - offset) % 128, 1)
        base = jnp.where((lane >= start) & (lane < end), moved, base)
    return base


def conv_kernel(masks, groups, vbuf, top, bot, wc, out, taps, buf, held, sems):
    disp, rows, feat, cols = out.shape
    total = buf.shape[2]
    lane = lanes((total, 128))
    zeros = jnp.zeros((cols, taps.shape[3]), BF16)
    taps[0, 0] = zeros
    taps[disp // 2, 1] = zeros
    halos_of = [(ref, mask) for ref, mask in zip((top, bot), masks())]

    def build(dd):
        for p, (ref, mask) in enumerate(halos_of):
            row = ref[dd * total : (dd + 1) * total].astype(F32) * mask
            for o in range(2):
                d = 2 * dd + o
                buf[p, d] = place_halo(vbuf[p, d], row, groups, SLOT * o, lane)
                for e in range(3):
                    at = 256 * e + 128 * p
                    taps[(d + 1) // 2, (d + 1) % 2, :, at : at + 128] = buf[
                        p, d, PAD - 1 + e : PAD - 1 + e + cols
                    ].astype(BF16)

    parts = sems.shape[0]
    step = disp // 2 // parts
    copies = []
    build(0)
    for q in range(parts):
        for dd in range(q * step + 1, min((q + 1) * step + 1, disp // 2)):
            build(dd)
        slabs = [
            taps[q * step + s // 2 : q * step + s // 2 + step, s % 2].reshape(step * cols, taps.shape[3])
            for s in range(4)
        ]
        acc = dot(jnp.concatenate(slabs, axis=1), wc[...])
        for j in range(step):
            both = acc[j * cols : (j + 1) * cols].astype(BF16).T
            for o in range(2):
                block = both[rows * feat * o : rows * feat * (o + 1)]
                held[2 * (q * step + j) + o] = block.reshape(rows, feat, cols)
        at = pl.ds(2 * q * step, 2 * step)
        copies.append(pltpu.make_async_copy(held.at[at], out.at[at], sems.at[q]))
        copies[-1].start()
    for copy in copies:
        copy.wait()


def finish_kernel(scale, mine, other, own, near, far, left, weight, right, left_out, held_w, held_r, sems):
    _, _, _, feat, groups = weight.shape
    copies = [pltpu.make_async_copy(left, left_out, sems.at[0])]
    copies[0].start()
    is_even = parity() == 0
    beside = jnp.where(is_even, near[...].astype(F32), 0.0)
    held_r[...] = (own[...].astype(F32) + beside + far[...].astype(F32)).astype(BF16)
    copies.append(pltpu.make_async_copy(held_r, right, sems.at[1]))
    copies[1].start()
    x, y = mine[...] * scale, other[...] * scale
    total = jnp.concatenate([jnp.where(is_even, x, y), jnp.where(is_even, y, x)], axis=0)
    for a in range(3):
        for e in range(3):
            at = 128 * a + groups * e
            block = total[at : at + groups].T
            for b in range(3):
                held_w[2 - a, 2 - b, 2 - e] = block[feat * b : feat * (b + 1)]
        copies.append(pltpu.make_async_copy(held_w.at[2 - a], weight.at[2 - a], sems.at[2 + a]))
        copies[-1].start()
    for copy in copies:
        copy.wait()


def copy_kernel(*refs):
    half = len(refs) // 2
    for src, dst in zip(refs[:half], refs[half:]):
        dst[...] = src[...]


def sum_kernel(*refs):
    *parts, out = refs
    out[...] = tree([ref[...].astype(F32) for ref in parts]).astype(out.dtype)


def tree(terms):
    while len(terms) > 1:
        terms = [terms[i] + terms[i + 1] for i in range(0, len(terms), 2)]
    return terms[0]


def taps_kernel(taps, w2, wc, turned):
    _, _, _, feat, groups = taps.shape
    rows = wc.shape[1] // 2 // feat
    lane_of = lanes((feat, 2 * SLOT))
    low = lanes((feat, 2 * SLOT)) < SLOT
    zero = jnp.zeros((feat, 2 * SLOT), F32)

    def wide(a, b, e):
        if not 0 <= b <= 2:
            return None
        return jnp.concatenate([taps[a, b, e].astype(F32), zero[:, groups:]], axis=1)

    def beside(x, y):
        if x is None and y is None:
            return zero
        x = zero if x is None else x
        y = zero if y is None else pltpu.roll(y, SLOT, 1)
        return jnp.where(low, x, y)

    def build(a, _):
        def at_row(h):
            return pl.multiple_of((a * rows + h) * feat, feat)

        for e in range(3):
            for h in range(rows):
                for p in range(rows // 2):
                    lane = SLOT * (rows * e + 2 * p)
                    block = beside(wide(a, 2 * p - h + 1, e), wide(a, 2 * p + 1 - h + 1, e))
                    if h == 0 and p == 0:
                        block = place_halo(block, wide(a, 0, e), groups, 0, lane_of)
                    if h == rows - 1 and p == rows // 2 - 1:
                        block = place_halo(block, wide(a, 2, e), groups, 0, lane_of)
                    turned[pl.ds(at_row(h), feat), lane : lane + 2 * SLOT] = block
        return 0

    lax.fori_loop(0, 3, build, 0)
    for s in range(4):
        for e in range(3):
            for r in range(4):
                for o in range(2):
                    taps_of = [None if not 0 <= s - o <= 2 else wide(2 - s + o, 2 - r + i, 2 - e) for i in range(2)]
                    at = 384 * s + 128 * e + feat * r
                    w2[at : at + feat, 128 * o : 128 * (o + 1)] = beside(*taps_of).astype(BF16)
    depth, size = turned.shape[1], rows * feat
    for a in range(3):
        for i in range(depth // 128):
            x = turned[size * a : size * (a + 1), 128 * i : 128 * (i + 1)].T.astype(BF16)
            for o in range(2):
                at = depth * (a + o) + 128 * i
                wc[at : at + 128, size * o : size * (o + 1)] = x
    for o in range(2):
        at = depth * 3 * (1 - o)
        wc[at : at + depth, size * o : size * (o + 1)] = jnp.zeros((depth, size), BF16)


TOKEN = ((8, 128), F32)


def with_token(kernel, inputs, outputs):
    def run(*refs):
        kernel(*refs[: inputs + outputs], *refs[inputs + outputs + 1 :])
        refs[inputs + outputs][...] = jnp.zeros(TOKEN[0], F32)

    return run


def call(kernel, outs, scratch, *args, after=(), token=False, us=0.0, alias=(), hbm=()):
    skip = len(after)
    if token:
        kernel = with_token(kernel, len(args), len(outs))
        outs = [*outs, TOKEN]
    return pl.pallas_call(
        lambda *refs: kernel(*refs[skip:]),
        out_shape=[jax.ShapeDtypeStruct(s, t) for s, t in outs],
        in_specs=[pl.BlockSpec(memory_space=pl.ANY)] * skip + [VMEM] * len(args),
        out_specs=[pl.BlockSpec(memory_space=pl.ANY) if i in hbm else VMEM for i in range(len(outs))],
        scratch_shapes=scratch,
        input_output_aliases={skip + i: o for i, o in alias},
        compiler_params=pltpu.CompilerParams(vmem_limit_bytes=LIMIT),
        cost_estimate=pl.CostEstimate(
            flops=int(us * 1.15e9), bytes_accessed=int(us * 3.7e6), transcendentals=0
        ),
    )(*after, *args)


def col_shift(block, distance):
    n = lax.axis_size("col")
    route = [(i - distance, i) for i in range(n) if 0 <= i - distance < n]
    return lax.ppermute(block, "col", route)


def row_shift(block, distance):
    n = lax.axis_size("row")
    route = [(i - distance, i) for i in range(n) if 0 <= i - distance < n]
    return lax.ppermute(block, "row", route)


def halos(pays):
    if lax.axis_size("row") == 2:
        got = lax.ppermute(pays[0], "row", [(0, 1), (1, 0)])
        return got, got
    return row_shift(pays[0], 1), row_shift(pays[1], -1)


def partners(n_row, n_col):
    col_bits = [1 << i for i in range(1, n_col.bit_length() - 1)]
    row_bits = [n_col << i for i in range(n_row.bit_length() - 1)]
    assert n_col == 2 << len(col_bits) and n_row == 1 << len(row_bits)
    return [*col_bits[:2], sum(col_bits[:2])], col_bits[2:], row_bits


def on_device(left_features, right_features, conv_weight, cotangent):
    rows, cols, channels = left_features.shape
    disp, feat = cotangent.shape[0], cotangent.shape[3]
    groups = conv_weight.shape[3]
    group_size = channels // groups
    wide = group_size * SLOT
    n_row, n_col = lax.axis_size("row"), lax.axis_size("col")
    per = 128 // feat

    if n_row == 2:
        ends = [lambda: (rows - 1) * (1 - lax.axis_index("row"))]
    else:
        ends = [lambda: rows - 1, lambda: 0]
    n = len(ends)

    def masks():
        at = lax.axis_index("row")
        return (
            jnp.where(at > 0, 1.0, 0.0).astype(F32),
            jnp.where(at < n_row - 1, 1.0, 0.0).astype(F32),
        )

    total = cols + 2 * PAD
    count = disp + 2 * rows
    ct = cotangent.transpose(0, 1, 3, 2)

    def swap(block, mask):
        route = [(i, i ^ mask) for i in range(n_row * n_col)]
        return lax.ppermute(block, ("row", "col"), route)

    far = col_shift(right_features, 2)
    (begun,) = call(begin_kernel, [TOKEN], [], us=3.0)
    by_even, by_odd, ctl, *rims = call(
        functools.partial(pack_kernel, ends),
        [
            ((count, channels), BF16),
            ((count, channels), BF16),
            ((disp, cols, rows * feat), BF16),
        ]
        + [((disp // per, cols, 128), BF16)] * n,
        [pltpu.VMEM((disp * cols, rows * feat), F32)],
        left_features,
        right_features,
        ct,
        after=[begun],
        us=0.4,
    )
    inner = range(1, n_col - 1, 2)
    by_even = swap(by_even, 1)
    by_odd = lax.ppermute(by_odd, "col", [(i, i + 1) for i in inner] + [(i + 1, i) for i in inner])
    band = 104 + cols + PAD
    banks = [((rows, total, wide), F32), ((rows, band, wide), F32), ((rows, band, wide), F32)]
    spread_rows = 2 * rows * cols
    fl, fr, fr4 = call(
        functools.partial(own_kernel, group_size),
        banks,
        [pltpu.VMEM((spread_rows, channels), BF16), pltpu.VMEM((spread_rows, wide), F32)],
        left_features,
        right_features,
        after=[ctl],
    )
    (passed,) = call(
        pass_kernel, [((rows, cols, channels), BF16)], [], right_features, far, after=[fl]
    )
    near = swap(passed, 1)
    top, bot = halos(rims)
    corner_pays = call(
        functools.partial(corner_kernel, ends, rows, disp),
        [((16, 128), BF16)] * n,
        [pltpu.VMEM((2, disp, 128), F32), pltpu.VMEM((16, 128), F32)],
        by_even,
        by_odd,
        after=[passed],
        us=5.0,
    )
    tops, bots = halos(corner_pays)
    spread_rows = rows * cols + rows * cols // 2 + 2 * count
    fl, fr, fr4, vbuf, *volume_rows = call(
        functools.partial(volume_kernel, ends, group_size),
        banks
        + [((rows // 2, disp, total, 2 * SLOT), F32)]
        + [((disp // 2 * total, 128), BF16)] * n,
        [pltpu.VMEM((spread_rows, channels), BF16), pltpu.VMEM((spread_rows, wide), F32)],
        near,
        far,
        by_even,
        by_odd,
        fl,
        fr,
        fr4,
        us=1.8,
        alias=[(4, 0), (5, 1), (6, 2)],
    )
    vtop, vbot = halos(volume_rows)
    keep, give, ctsh = call(
        functools.partial(weight_kernel, masks, groups, feat),
        [((3 * 64, 128), F32), ((3 * 64, 128), F32), ((disp // 2 + 1, 2, cols, 3 * 256), BF16)],
        [
            pltpu.VMEM((rows // 2, 128, (disp // 2 + 2) * 128), BF16),
            pltpu.VMEM((disp, total, 256), F32),
            pltpu.VMEM((3 * 128, 128), F32),
        ],
        vbuf, ctl, by_even, by_odd, top, bot, tops, bots,
        us=2.0,
    )

    got = swap(give, 1)
    w2, wc = call(
        taps_kernel,
        [((12 * 128, 2 * 128), BF16), ((4 * 3 * rows * SLOT, 2 * rows * feat), BF16)],
        [pltpu.VMEM((3 * rows * feat, 3 * rows * SLOT), F32)],
        conv_weight.transpose(0, 1, 2, 4, 3),
        after=[keep],
    )
    (part,) = call(sum_kernel, [(keep.shape, BF16)], [], keep, got, after=[w2])
    *grads, rg0, rg1, rg2 = call(
        right_kernel,
        [((2, disp, cols, 128), F32)] * (rows // 2)
        + [
            ((rows, cols, channels), BF16),
            ((rows, cols, channels), BF16),
            ((rows, cols // 2, channels), BF16),
        ],
        [
            pltpu.VMEM((rows, cols + cols + cols // 2, wide), F32),
            pltpu.VMEM((rows, cols + cols + cols // 2 + 8, wide), F32),
            pltpu.VMEM((rows * (cols + cols + cols // 2), wide), BF16),
        ],
        ctsh, w2, fl,
        after=[part],
        us=0.4,
    )
    rg1 = swap(rg1, 1)
    def join(part, mask, kind, after, us):
        terms = (part, swap(part, mask))
        return call(sum_kernel, [(part.shape, kind)], [], *terms, after=after, us=us)[0]

    three, along_cols, along_rows = partners(n_row, n_col)
    parts = [part] + [swap(part, m) for m in three]
    (part,) = call(sum_kernel, [(part.shape, BF16)], [], *parts, after=[rg0, vtop], us=4.0)
    (rg2,) = call(
        combine_kernel, [((rows, cols, channels), BF16)], [], rg1, rg2, after=[part]
    )
    order = [rg2]
    for mask in along_cols:
        part = join(part, mask, BF16, after=order, us=4.0)
        order = []
    output, conv_done = call(
        functools.partial(conv_kernel, masks, groups),
        [((disp, rows, feat, cols), BF16)],
        [
            pltpu.VMEM((disp // 2 + 1, 2, cols, 3 * rows * SLOT), BF16),
            pltpu.VMEM((rows // 2, disp, total, 128), F32),
            pltpu.VMEM((disp, rows, feat, cols), BF16),
            pltpu.SemaphoreType.DMA((4,)),
        ],
        vbuf, vtop, vbot, wc,
        after=[part],
        token=True,
        us=3.0,
        hbm=[0],
    )
    order = [conv_done]
    for mask in along_rows:
        part = join(part, mask, F32, after=order, us=4.0)
        order = []
    (lg,) = call(
        left_kernel,
        [((rows, cols, channels), BF16)],
        [pltpu.VMEM((rows, cols, wide), F32)],
        fr, fr4, *grads,
        after=[part],
        us=1.9,
    )
    rg2 = col_shift(rg2, -2)
    cells = disp * rows * n_row * cols * n_col
    weight_grad, right_grad, left_grad = call(
        functools.partial(finish_kernel, 1.0 / math.sqrt(cells)),
        [
            ((3, 3, 3, feat, groups), F32),
            ((rows, cols, channels), BF16),
            ((rows, cols, channels), BF16),
        ],
        [
            pltpu.VMEM((3, 3, 3, feat, groups), F32),
            pltpu.VMEM((rows, cols, channels), BF16),
            pltpu.SemaphoreType.DMA((5,)),
        ],
        part, swap(part, 1), rg0, rg1, rg2, lg,
        us=1.0,
        hbm=[0, 1, 2],
    )
    return (
        output.transpose(0, 1, 3, 2),
        weight_grad.transpose(0, 1, 2, 4, 3),
        left_grad,
        right_grad,
    )


def solution(mesh):
    in_specs = (P("row", "col", None), P("row", "col", None), P(), P(None, "row", "col", None))
    out_specs = (P(None, "row", "col", None), P(), P("row", "col", None), P("row", "col", None))
    return jax.shard_map(
        on_device, mesh=mesh, in_specs=in_specs, out_specs=out_specs, check_vma=False
    )
```

```python
import functools
import math

import jax
import jax.numpy as jnp
from jax import lax
from jax.experimental import pallas as pl
from jax.experimental.pallas import tpu as pltpu
from jax.sharding import PartitionSpec as P

DISP = 24
STEP = 4
SLOT = 64
PAD = 8
F32 = jnp.float32
BF16 = jnp.bfloat16
VMEM = pl.BlockSpec(memory_space=pltpu.VMEM)
LIMIT = 16 * 1024 * 1024


def lanes(shape):
    return lax.broadcasted_iota(jnp.int32, shape, len(shape) - 1)


def channel_table(channels, group_size, flip, value=1.0):
    shape = (group_size * SLOT, channels) if flip else (channels, group_size * SLOT)
    c = lax.broadcasted_iota(jnp.int32, shape, 1 if flip else 0)
    j = lax.broadcasted_iota(jnp.int32, shape, 0 if flip else 1)
    hit = c == (j & (SLOT - 1)) * group_size + (j >> (SLOT.bit_length() - 1))
    return jnp.where(hit, value, 0.0).astype(BF16)


def parity():
    return lax.rem(lax.axis_index("col"), 2)


def dot(a, b):
    return jnp.dot(a, b, preferred_element_type=F32)


def dot_nt(a, b):
    return lax.dot_general(a, b, (((1,), (1,)), ((), ())), preferred_element_type=F32)


def begin_kernel(out):
    out[...] = jnp.zeros(out.shape, F32)


def pack_kernel(ends, left, right, ct, even, odd, ctl, *rest):
    rims, ctf = rest[:-1], rest[-1]
    disp, rows, feat, cols = ct.shape
    per = 128 // feat
    for d in range(disp):
        block = ct[d].reshape(rows * feat, cols).astype(F32).T
        ctf[d * cols : (d + 1) * cols] = block
        ctl[d] = block.astype(BF16)
    columns = []
    for i, col in enumerate((cols - 1, 0)):
        block = ctf[pl.ds(col, disp, stride=cols), :]
        block = jnp.concatenate([block, jnp.zeros((disp, even.shape[1] - rows * feat), F32)], axis=1)
        edge = [x[h, col : col + 1].astype(F32) for x in (left, right) for h in range(rows)]
        columns.append(jnp.concatenate([block, *edge], axis=0))
    is_even = parity() == 0
    even[...] = jnp.where(is_even, columns[0], columns[1]).astype(BF16)
    odd[...] = jnp.where(is_even, columns[1], columns[0]).astype(BF16)
    for end, rim in zip(ends, rims):
        h = end()
        for q in range(disp // per):
            block = [ct[q * per + i, h].astype(F32) for i in range(per)]
            rim[q] = jnp.concatenate(block, axis=0).T.astype(BF16)


def pass_kernel(own, got, out):
    out[...] = jnp.where(parity() == 0, own[...].astype(F32), got[...].astype(F32)).astype(BF16)


def end_columns(by_even, by_odd):
    x, y = by_even[...].astype(F32), by_odd[...].astype(F32)
    is_even = parity() == 0
    return jnp.where(is_even, y, x), jnp.where(is_even, x, y)


def corner_kernel(ends, rows, disp, by_even, by_odd, *rest):
    pays, (edges, buf) = rest[: len(ends)], rest[len(ends) :]
    feat = 128 // rows
    per = 128 // feat
    count = disp // per
    lane = lanes((count, 128))
    for side, x in enumerate(end_columns(by_even, by_odd)):
        edges[side] = x[0:disp, 0:128]
    for end, pay in zip(ends, pays):
        h = end()
        buf[...] = jnp.zeros(buf.shape, F32)
        for side in range(2):
            out = jnp.zeros((count, 128), F32)
            for i in range(per):
                x = edges[side, pl.ds(i, count, stride=per)]
                first = pltpu.roll(x, feat * i, 1) if i else x
                last = pltpu.roll(x, (feat * (i - rows + 1)) % 128, 1) if i != rows - 1 else x
                x = jnp.where(h == 0, first, last)
                out = jnp.where((lane >= feat * i) & (lane < feat * (i + 1)), x, out)
            buf[8 * side : 8 * side + count] = out
        pay[...] = buf[...].astype(BF16)


def put_band(refs, h, column, block):
    fr, fr4, cols = refs
    at = fr.shape[1] - cols - PAD + column
    fr[h, at : at + block.shape[0]] = block
    fr4[h, at + STEP : at + STEP + block.shape[0]] = block


def own_kernel(group_size, left, right, fl, fr, fr4, mixed, wide_buf):
    rows, cols, channels = left.shape
    base, wide = rows * cols, group_size * SLOT
    mixed[0:base] = right[...].reshape(base, channels)
    mixed[base : 2 * base] = left[...].reshape(base, channels)
    wide_buf[...] = dot(mixed[...], channel_table(channels, group_size, False))
    tail = fr.shape[1]
    for h in range(rows):
        for ref in (fr, fr4):
            ref[h, 0:16] = jnp.zeros((16, wide), F32)
            ref[h, tail - 16 :] = jnp.zeros((16, wide), F32)
        put_band((fr, fr4, cols), h, 0, wide_buf[h * cols : (h + 1) * cols])
        fl[h, 0:PAD] = jnp.zeros((PAD, wide), F32)
        fl[h, PAD + cols :] = jnp.zeros((PAD, wide), F32)
        fl[h, PAD : PAD + cols] = wide_buf[base + h * cols : base + (h + 1) * cols] * (1.0 / group_size)


def volume_kernel(ends, group_size, near, far, by_even, by_odd, _fl, _fr, _fr4, fl, fr, fr4, vbuf, *rest):
    pays, (mixed, wide_buf) = rest[: len(ends)], rest[len(ends) :]
    rows, cols, channels = near.shape
    disp = vbuf.shape[1]
    reach = fr.shape[1] - cols - PAD
    wide = group_size * SLOT
    half, at_far = cols // 2, rows * cols
    base = at_far + rows * half
    mixed[0:at_far] = near[...].reshape(at_far, channels)
    mixed[at_far:base] = far[:, half:].reshape(rows * half, channels)
    count = disp + 2 * rows
    for i, x in enumerate(end_columns(by_even, by_odd)):
        mixed[base + i * count : base + (i + 1) * count] = x.astype(BF16)
    wide_buf[...] = dot(mixed[...], channel_table(channels, group_size, False))
    for h in range(rows):
        put_band((fr, fr4, cols), h, -cols, wide_buf[h * cols : (h + 1) * cols])
        at = at_far + h * half
        put_band((fr, fr4, cols), h, -cols - half, wide_buf[at : at + half])
        at = base + disp + h
        fl[h, PAD - 1 : PAD] = wide_buf[at : at + 1] * (1.0 / group_size)
        at += count
        fl[h, PAD + cols : PAD + cols + 1] = wide_buf[at : at + 1] * (1.0 / group_size)
        put_band((fr, fr4, cols), h, cols, wide_buf[at + rows : at + rows + 1])
    total = cols + 2 * PAD
    low = lanes((8, 128)) < SLOT
    pairs, times, lots = rows // 2, disp // 2, wide // 128
    count = total // 16

    def products(p, at):
        lefts = [
            [
                [fl[2 * p + o, at + 8 * b : at + 8 * b + 8, 128 * j : 128 * (j + 1)] for j in range(lots)]
                for b in range(count)
            ]
            for o in range(2)
        ]
        for odd, band in enumerate((fr, fr4)):
            for r in range(1 - times, count):
                start = at + reach - PAD + 8 * r
                here = [
                    [band[2 * p + o, start : start + 8, 128 * j : 128 * (j + 1)] for j in range(lots)]
                    for o in range(2)
                ]
                for t in range(max(0, -r), min(times, count - r)):
                    sums = []
                    for o in range(2):
                        acc = lefts[o][r + t][0] * here[o][0]
                        for j in range(1, lots):
                            acc = acc + lefts[o][r + t][j] * here[o][j]
                        sums.append(acc + pltpu.roll(acc, SLOT, 1))
                    row = at + 8 * (r + t)
                    vbuf[p, 2 * t + odd, row : row + 8] = jnp.where(low, *sums)

    for at in (8 * count, 0):
        for p in range(pairs):
            products(p, at)
    big = lanes((total, 128)) < SLOT

    for dd in range(disp // 2):
        for end, pay in zip(ends, pays):
            h = end()
            if isinstance(h, int):
                halves = [vbuf[h // 2, 2 * dd + o] for o in range(2)]
                if h % 2 == 0:
                    halves[1] = pltpu.roll(halves[1], SLOT, 1)
                else:
                    halves[0] = pltpu.roll(halves[0], SLOT, 1)
                out = jnp.where(big, halves[0], halves[1])
            else:
                last = pairs - 1
                first = jnp.where(big, vbuf[0, 2 * dd], pltpu.roll(vbuf[0, 2 * dd + 1], SLOT, 1))
                final = jnp.where(
                    big, pltpu.roll(vbuf[last, 2 * dd], SLOT, 1), vbuf[last, 2 * dd + 1]
                )
                out = jnp.where(h == 0, first, final)
            pay[dd * total : (dd + 1) * total] = out.astype(BF16)


def weight_kernel(
    masks, groups, feat, vbuf, ctl, by_even, by_odd, top, bot, tops, bots, *rest
):
    keep_out, give_out, ctsh, vt, buf, sums = rest
    disp, cols, width = ctl.shape
    pairs, per, half = vbuf.shape[0], 128 // feat, disp // 2
    mtop, mbot = masks()
    ctsh[0, 0] = jnp.zeros(ctsh.shape[2:], BF16)
    ctsh[half, 1] = jnp.zeros(ctsh.shape[2:], BF16)
    lane_in, lane_one = lanes((cols, 128)), lanes((1, 128))
    shifts = (feat, 128 - feat)
    edges = [x[0:disp, 0:128] for x in end_columns(by_even, by_odd)]
    turned = [[pltpu.roll(x, shift, 1) for shift in shifts] for x in edges]

    def aligned(t, z, i):
        return (
            t if i == 0 else pltpu.roll(t, 128 - feat * i, 1),
            z if i == per - 1 else pltpu.roll(z, feat * (per - 1 - i), 1),
        )

    corners = [aligned(tops[...].astype(F32) * mtop, bots[...].astype(F32) * mbot, i) for i in range(per)]

    def fill(q):
        t = top[q].astype(F32) * mtop
        z = bot[q].astype(F32) * mbot
        for i in range(per):
            d = q * per + i
            rims = aligned(t, z, i)
            inner = ctl[d].astype(F32)
            for p, (rim, shift) in enumerate(zip(rims, shifts)):

                def on_rim(x):
                    return x < feat if p == 0 else x >= 128 - feat

                at = slice(128 * p, 128 * (p + 1))
                buf[d, PAD : PAD + cols, at] = jnp.where(
                    on_rim(lane_in), rim, pltpu.roll(inner, shift, 1)
                )
                for side, row in enumerate((PAD - 1, PAD + cols)):
                    corner = corners[i][p][8 * side + q : 8 * side + q + 1]
                    buf[d, row : row + 1, at] = jnp.where(
                        on_rim(lane_one), corner, turned[side][p][d : d + 1]
                    )
            for e in range(3):
                ctsh[(d + 1) // 2, (d + 1) % 2, :, 256 * e : 256 * (e + 1)] = buf[
                    d, PAD - 1 + e : PAD - 1 + e + cols
                ].astype(BF16)

    none = jnp.zeros((cols, 128), F32)
    for p in range(pairs):
        for j in range(-1, half + 1):
            block = [
                vbuf[p, d, PAD : PAD + cols] if 0 <= d < disp and 0 <= j + half * o else none
                for o, d in enumerate((j, j + half))
            ]
            if j == half:
                block[1] = none
            x = jnp.concatenate(block, axis=0).astype(BF16)
            vt[p, :, 128 * (j + 1) : 128 * (j + 2)] = x.T
    full = None
    count = half // per
    fill(0)
    fill(count)
    for q in range(count):
        first, size = q * per, per * 128
        sums_of = []
        for p in range(pairs):
            left = jnp.concatenate(
                [vt[p, :, 128 * (2 - a + first) : 128 * (2 - a + first) + size] for a in range(3)], axis=0
            )
            right = jnp.concatenate(
                [
                    jnp.concatenate(
                        [
                            ctsh[(d + 1) // 2, (d + 1) % 2, :, 256 * e + 128 * p : 256 * e + 128 * (p + 1)]
                            for e in range(3)
                        ],
                        axis=1,
                    )
                    for j in range(first, first + per)
                    for d in (j, j + half)
                ],
                axis=0,
            )
            sums_of.append(dot(left, right))
        if q + 1 < count:
            fill(q + 1)
            fill(q + 1 + count)
        for part in sums_of:
            full = part if full is None else full + part
    keep = lanes((groups, 128)) < 3 * feat
    sums[...] = jnp.zeros(sums.shape, F32)
    for a in range(3):
        for e in range(3):
            block = full[128 * a : 128 * (a + 1), 128 * e : 128 * (e + 1)]
            out = block[0:groups] + pltpu.roll(block[SLOT : SLOT + groups], 128 - feat, 1)
            at = 128 * a + groups * e
            sums[at : at + groups] = jnp.where(keep, out, 0.0)
    half = sums.shape[0] // 2
    is_even = parity() == 0
    low, high = sums[0:half], sums[half:]
    keep_out[...] = jnp.where(is_even, low, high)
    give_out[...] = jnp.where(is_even, high, low)


def right_kernel(ctsh, w2, fl, *rest):
    *grads, rg0, rg1, rg2, acce, acco, both = rest
    rows, cols, channels = rg0.shape
    disp, wide = grads[0].shape[1], fl.shape[2]
    group_size = wide // SLOT
    step = disp // 4
    low = lanes((step * cols, 128)) < SLOT

    def conv(q, p, gv):
        slabs = [
            ctsh[q * step + s // 2 : q * step + s // 2 + step, s % 2, :, 256 * e + 128 * p : 256 * e + 128 * (p + 1)]
            for s in range(4)
            for e in range(3)
        ]
        slabs = [x.reshape(step * cols, 128) for x in slabs]
        acc = dot(jnp.concatenate(slabs, axis=1), w2[...]).astype(BF16).astype(F32)
        for o in range(2):
            x = acc[:, 128 * o : 128 * (o + 1)]
            r = pltpu.roll(x, SLOT, 1)
            for hh in range(2):
                y = jnp.where(low, r, x) if hh else jnp.where(low, x, r)
                for j in range(step):
                    gv[hh, 2 * (q * step + j) + o] = y[j * cols : (j + 1) * cols]

    count = cols // 8
    back = acce.shape[1] - cols
    lead = back // 8

    lots = wide // 128

    def right_row(gv, p, hh):
        h = 2 * p + hh
        here = [
            [fl[h, PAD + 8 * b : PAD + 8 * b + 8, 128 * j : 128 * (j + 1)] for j in range(lots)]
            for b in range(count)
        ]
        for odd, buf in enumerate((acce, acco)):
            for k in range(lead + count):
                accs = [None] * lots
                for t in range(disp // 2):
                    b = k + t - lead
                    if b < 0 or b >= count:
                        continue
                    g = gv[hh, 2 * t + odd, 8 * b : 8 * b + 8]
                    for j in range(lots):
                        term = g * here[b][j]
                        accs[j] = term if accs[j] is None else accs[j] + term
                for j in range(lots):
                    x = jnp.zeros((8, 128), F32) if accs[j] is None else accs[j]
                    buf[h, 8 * k : 8 * k + 8, 128 * j : 128 * (j + 1)] = x
        acco[h, 8 * (lead + count) :] = jnp.zeros((8, wide), F32)

    parts = disp // 2 // step
    for p, gv in enumerate(grads):
        for q in range(parts):
            conv(q, p, gv)
            if p:
                right_row(grads[p - 1], p - 1, q)
    for hh in range(2):
        right_row(grads[-1], len(grads) - 1, hh)
    size = back + cols
    for h in range(rows):
        both[h * size : (h + 1) * size] = (acce[h] + acco[h, STEP : STEP + size]).astype(BF16)
    whole = dot(both[...], channel_table(channels, group_size, True)).astype(BF16)
    half = cols // 2
    for h in range(rows):
        at = h * size + back
        rg2[h] = whole[at - cols - half : at - cols]
        rg1[h] = whole[at - cols : at]
        rg0[h] = whole[at : at + cols]


def left_kernel(fr, fr4, *rest):
    *grads, lg, accl = rest
    rows, cols, channels = lg.shape
    disp, wide = grads[0].shape[1], fr.shape[2]
    group_size = wide // SLOT
    reach = fr.shape[1] - cols - PAD
    count, times, lots = cols // 8, disp // 2, wide // 128

    def left_row(gv, p, hh):
        h = 2 * p + hh
        accs = [[None] * lots for _ in range(count)]
        for odd, band in enumerate((fr, fr4)):
            for r in range(1 - times, count):
                at = reach + 8 * r
                here = [band[h, at : at + 8, 128 * j : 128 * (j + 1)] for j in range(lots)]
                for t in range(max(0, -r), min(times, count - r)):
                    g = gv[hh, 2 * t + odd, 8 * (r + t) : 8 * (r + t) + 8]
                    for j in range(lots):
                        term, acc = g * here[j], accs[r + t][j]
                        accs[r + t][j] = term if acc is None else acc + term
        for b in range(count):
            for j in range(lots):
                accl[h, 8 * b : 8 * b + 8, 128 * j : 128 * (j + 1)] = accs[b][j] * (1.0 / group_size)

    for p, gv in enumerate(grads):
        for hh in range(2):
            left_row(gv, p, hh)
    whole = accl[...].reshape(rows * cols, wide).astype(BF16)
    out = dot(whole, channel_table(channels, group_size, True)).astype(BF16)
    lg[...] = out.reshape(rows, cols, channels)


def combine_kernel(got, rg2, out):
    cols = out.shape[1]
    half = cols // 2
    part = jnp.where(parity() == 0, 0.0, got[...].astype(F32))
    out[:, 0:half] = part[:, 0:half].astype(BF16)
    out[:, half:] = (part[:, half:] + rg2[...].astype(F32)).astype(BF16)


def halo_lanes(groups):
    first = SLOT - groups
    assert groups - first <= first
    return (groups, SLOT, groups), (SLOT + groups, SLOT + 2 * groups - first, SLOT + groups - first)


def place_halo(base, row, groups, offset, lane):
    for start, end, shift in halo_lanes(groups):
        moved = pltpu.roll(row, (shift - offset) % 128, 1)
        base = jnp.where((lane >= start) & (lane < end), moved, base)
    return base


def conv_kernel(masks, groups, vbuf, top, bot, wc, out, taps, buf, held, sems):
    disp, rows, feat, cols = out.shape
    total = buf.shape[2]
    lane = lanes((total, 128))
    zeros = jnp.zeros((cols, taps.shape[3]), BF16)
    taps[0, 0] = zeros
    taps[disp // 2, 1] = zeros
    halos_of = [(ref, mask) for ref, mask in zip((top, bot), masks())]

    def build(dd):
        for p, (ref, mask) in enumerate(halos_of):
            row = ref[dd * total : (dd + 1) * total].astype(F32) * mask
            for o in range(2):
                d = 2 * dd + o
                buf[p, d] = place_halo(vbuf[p, d], row, groups, SLOT * o, lane)
                for e in range(3):
                    at = 256 * e + 128 * p
                    taps[(d + 1) // 2, (d + 1) % 2, :, at : at + 128] = buf[
                        p, d, PAD - 1 + e : PAD - 1 + e + cols
                    ].astype(BF16)

    parts = sems.shape[0]
    step = disp // 2 // parts
    copies = []

    def build_part(q):
        for dd in range(q * step + 1, min((q + 1) * step + 1, disp // 2)):
            build(dd)

    build(0)
    build_part(0)
    for q in range(parts):
        slabs = [
            taps[q * step + s // 2 : q * step + s // 2 + step, s % 2].reshape(step * cols, taps.shape[3])
            for s in range(4)
        ]
        acc = dot(jnp.concatenate(slabs, axis=1), wc[...])
        if q + 1 < parts:
            build_part(q + 1)
        for j in range(step):
            both = acc[j * cols : (j + 1) * cols].astype(BF16).T
            for o in range(2):
                block = both[rows * feat * o : rows * feat * (o + 1)]
                held[2 * (q * step + j) + o] = block.reshape(rows, feat, cols)
        at = pl.ds(2 * q * step, 2 * step)
        copies.append(pltpu.make_async_copy(held.at[at], out.at[at], sems.at[q]))
        copies[-1].start()
    for copy in copies:
        copy.wait()


def finish_kernel(scale, mine, other, own, near, far, left, weight, right, left_out, held_w, held_r, sems):
    _, _, _, feat, groups = weight.shape
    copies = [pltpu.make_async_copy(left, left_out, sems.at[0])]
    copies[0].start()
    is_even = parity() == 0
    beside = jnp.where(is_even, near[...].astype(F32), 0.0)
    held_r[...] = (own[...].astype(F32) + beside + far[...].astype(F32)).astype(BF16)
    copies.append(pltpu.make_async_copy(held_r, right, sems.at[1]))
    copies[1].start()
    x, y = mine[...] * scale, other[...] * scale
    total = jnp.concatenate([jnp.where(is_even, x, y), jnp.where(is_even, y, x)], axis=0)
    for a in range(3):
        for e in range(3):
            at = 128 * a + groups * e
            block = total[at : at + groups].T
            for b in range(3):
                held_w[2 - a, 2 - b, 2 - e] = block[feat * b : feat * (b + 1)]
        copies.append(pltpu.make_async_copy(held_w.at[2 - a], weight.at[2 - a], sems.at[2 + a]))
        copies[-1].start()
    for copy in copies:
        copy.wait()


def copy_kernel(*refs):
    half = len(refs) // 2
    for src, dst in zip(refs[:half], refs[half:]):
        dst[...] = src[...]


def sum_kernel(*refs):
    *parts, out = refs
    out[...] = tree([ref[...].astype(F32) for ref in parts]).astype(out.dtype)


def tree(terms):
    while len(terms) > 1:
        terms = [terms[i] + terms[i + 1] for i in range(0, len(terms), 2)]
    return terms[0]


def taps_kernel(taps, w2, wc, turned):
    _, _, _, feat, groups = taps.shape
    rows = wc.shape[1] // 2 // feat
    lane_of = lanes((feat, 2 * SLOT))
    low = lanes((feat, 2 * SLOT)) < SLOT
    zero = jnp.zeros((feat, 2 * SLOT), F32)

    def wide(a, b, e):
        if not 0 <= b <= 2:
            return None
        return jnp.concatenate([taps[a, b, e].astype(F32), zero[:, groups:]], axis=1)

    def beside(x, y):
        if x is None and y is None:
            return zero
        x = zero if x is None else x
        y = zero if y is None else pltpu.roll(y, SLOT, 1)
        return jnp.where(low, x, y)

    def build(a, _):
        def at_row(h):
            return pl.multiple_of((a * rows + h) * feat, feat)

        for e in range(3):
            for h in range(rows):
                for p in range(rows // 2):
                    lane = SLOT * (rows * e + 2 * p)
                    block = beside(wide(a, 2 * p - h + 1, e), wide(a, 2 * p + 1 - h + 1, e))
                    if h == 0 and p == 0:
                        block = place_halo(block, wide(a, 0, e), groups, 0, lane_of)
                    if h == rows - 1 and p == rows // 2 - 1:
                        block = place_halo(block, wide(a, 2, e), groups, 0, lane_of)
                    turned[pl.ds(at_row(h), feat), lane : lane + 2 * SLOT] = block
        return 0

    lax.fori_loop(0, 3, build, 0)
    for s in range(4):
        for e in range(3):
            for r in range(4):
                for o in range(2):
                    taps_of = [None if not 0 <= s - o <= 2 else wide(2 - s + o, 2 - r + i, 2 - e) for i in range(2)]
                    at = 384 * s + 128 * e + feat * r
                    w2[at : at + feat, 128 * o : 128 * (o + 1)] = beside(*taps_of).astype(BF16)
    depth, size = turned.shape[1], rows * feat
    for a in range(3):
        for i in range(depth // 128):
            x = turned[size * a : size * (a + 1), 128 * i : 128 * (i + 1)].T.astype(BF16)
            for o in range(2):
                at = depth * (a + o) + 128 * i
                wc[at : at + 128, size * o : size * (o + 1)] = x
    for o in range(2):
        at = depth * 3 * (1 - o)
        wc[at : at + depth, size * o : size * (o + 1)] = jnp.zeros((depth, size), BF16)


TOKEN = ((8, 128), F32)


def with_token(kernel, inputs, outputs):
    def run(*refs):
        kernel(*refs[: inputs + outputs], *refs[inputs + outputs + 1 :])
        refs[inputs + outputs][...] = jnp.zeros(TOKEN[0], F32)

    return run


def call(kernel, outs, scratch, *args, after=(), token=False, us=0.0, alias=(), hbm=()):
    skip = len(after)
    if token:
        kernel = with_token(kernel, len(args), len(outs))
        outs = [*outs, TOKEN]
    return pl.pallas_call(
        lambda *refs: kernel(*refs[skip:]),
        out_shape=[jax.ShapeDtypeStruct(s, t) for s, t in outs],
        in_specs=[pl.BlockSpec(memory_space=pl.ANY)] * skip + [VMEM] * len(args),
        out_specs=[pl.BlockSpec(memory_space=pl.ANY) if i in hbm else VMEM for i in range(len(outs))],
        scratch_shapes=scratch,
        input_output_aliases={skip + i: o for i, o in alias},
        compiler_params=pltpu.CompilerParams(vmem_limit_bytes=LIMIT),
        cost_estimate=pl.CostEstimate(
            flops=int(us * 1.15e9), bytes_accessed=int(us * 3.7e6), transcendentals=0
        ),
    )(*after, *args)


def col_shift(block, distance):
    n = lax.axis_size("col")
    route = [(i - distance, i) for i in range(n) if 0 <= i - distance < n]
    return lax.ppermute(block, "col", route)


def row_shift(block, distance):
    n = lax.axis_size("row")
    route = [(i - distance, i) for i in range(n) if 0 <= i - distance < n]
    return lax.ppermute(block, "row", route)


def halos(pays):
    if lax.axis_size("row") == 2:
        got = lax.ppermute(pays[0], "row", [(0, 1), (1, 0)])
        return got, got
    return row_shift(pays[0], 1), row_shift(pays[1], -1)


def partners(n_row, n_col):
    col_bits = [1 << i for i in range(1, n_col.bit_length() - 1)]
    row_bits = [n_col << i for i in range(n_row.bit_length() - 1)]
    assert n_col == 2 << len(col_bits) and n_row == 1 << len(row_bits)
    return [*col_bits[:2], sum(col_bits[:2])], col_bits[2:], row_bits


def on_device(left_features, right_features, conv_weight, cotangent):
    rows, cols, channels = left_features.shape
    disp, feat = cotangent.shape[0], cotangent.shape[3]
    groups = conv_weight.shape[3]
    group_size = channels // groups
    wide = group_size * SLOT
    n_row, n_col = lax.axis_size("row"), lax.axis_size("col")
    per = 128 // feat

    if n_row == 2:
        ends = [lambda: (rows - 1) * (1 - lax.axis_index("row"))]
    else:
        ends = [lambda: rows - 1, lambda: 0]
    n = len(ends)

    def masks():
        at = lax.axis_index("row")
        return (
            jnp.where(at > 0, 1.0, 0.0).astype(F32),
            jnp.where(at < n_row - 1, 1.0, 0.0).astype(F32),
        )

    total = cols + 2 * PAD
    count = disp + 2 * rows
    ct = cotangent.transpose(0, 1, 3, 2)

    def swap(block, mask):
        route = [(i, i ^ mask) for i in range(n_row * n_col)]
        return lax.ppermute(block, ("row", "col"), route)

    far = col_shift(right_features, 2)
    (begun,) = call(begin_kernel, [TOKEN], [], us=3.0)
    by_even, by_odd, ctl, *rims = call(
        functools.partial(pack_kernel, ends),
        [
            ((count, channels), BF16),
            ((count, channels), BF16),
            ((disp, cols, rows * feat), BF16),
        ]
        + [((disp // per, cols, 128), BF16)] * n,
        [pltpu.VMEM((disp * cols, rows * feat), F32)],
        left_features,
        right_features,
        ct,
        after=[begun],
        us=0.4,
    )
    inner = range(1, n_col - 1, 2)
    by_even = swap(by_even, 1)
    by_odd = lax.ppermute(by_odd, "col", [(i, i + 1) for i in inner] + [(i + 1, i) for i in inner])
    band = 104 + cols + PAD
    banks = [((rows, total, wide), F32), ((rows, band, wide), F32), ((rows, band, wide), F32)]
    spread_rows = 2 * rows * cols
    fl, fr, fr4 = call(
        functools.partial(own_kernel, group_size),
        banks,
        [pltpu.VMEM((spread_rows, channels), BF16), pltpu.VMEM((spread_rows, wide), F32)],
        left_features,
        right_features,
        after=[ctl],
    )
    (passed,) = call(
        pass_kernel, [((rows, cols, channels), BF16)], [], right_features, far, after=[fl]
    )
    near = swap(passed, 1)
    top, bot = halos(rims)
    corner_pays = call(
        functools.partial(corner_kernel, ends, rows, disp),
        [((16, 128), BF16)] * n,
        [pltpu.VMEM((2, disp, 128), F32), pltpu.VMEM((16, 128), F32)],
        by_even,
        by_odd,
        after=[passed],
        us=5.0,
    )
    tops, bots = halos(corner_pays)
    spread_rows = rows * cols + rows * cols // 2 + 2 * count
    fl, fr, fr4, vbuf, *volume_rows = call(
        functools.partial(volume_kernel, ends, group_size),
        banks
        + [((rows // 2, disp, total, 2 * SLOT), F32)]
        + [((disp // 2 * total, 128), BF16)] * n,
        [pltpu.VMEM((spread_rows, channels), BF16), pltpu.VMEM((spread_rows, wide), F32)],
        near,
        far,
        by_even,
        by_odd,
        fl,
        fr,
        fr4,
        us=1.8,
        alias=[(4, 0), (5, 1), (6, 2)],
    )
    vtop, vbot = halos(volume_rows)
    keep, give, ctsh = call(
        functools.partial(weight_kernel, masks, groups, feat),
        [((3 * 64, 128), F32), ((3 * 64, 128), F32), ((disp // 2 + 1, 2, cols, 3 * 256), BF16)],
        [
            pltpu.VMEM((rows // 2, 128, (disp // 2 + 2) * 128), BF16),
            pltpu.VMEM((disp, total, 256), F32),
            pltpu.VMEM((3 * 128, 128), F32),
        ],
        vbuf, ctl, by_even, by_odd, top, bot, tops, bots,
        us=2.0,
    )

    got = swap(give, 1)
    w2, wc = call(
        taps_kernel,
        [((12 * 128, 2 * 128), BF16), ((4 * 3 * rows * SLOT, 2 * rows * feat), BF16)],
        [pltpu.VMEM((3 * rows * feat, 3 * rows * SLOT), F32)],
        conv_weight.transpose(0, 1, 2, 4, 3),
        after=[keep],
    )
    (part,) = call(sum_kernel, [(keep.shape, BF16)], [], keep, got, after=[w2])
    *grads, rg0, rg1, rg2 = call(
        right_kernel,
        [((2, disp, cols, 128), F32)] * (rows // 2)
        + [
            ((rows, cols, channels), BF16),
            ((rows, cols, channels), BF16),
            ((rows, cols // 2, channels), BF16),
        ],
        [
            pltpu.VMEM((rows, cols + cols + cols // 2, wide), F32),
            pltpu.VMEM((rows, cols + cols + cols // 2 + 8, wide), F32),
            pltpu.VMEM((rows * (cols + cols + cols // 2), wide), BF16),
        ],
        ctsh, w2, fl,
        after=[part],
        us=0.4,
    )
    rg1 = swap(rg1, 1)
    def join(part, mask, kind, after, us):
        terms = (part, swap(part, mask))
        return call(sum_kernel, [(part.shape, kind)], [], *terms, after=after, us=us)[0]

    three, along_cols, along_rows = partners(n_row, n_col)
    parts = [part] + [swap(part, m) for m in three]
    (part,) = call(sum_kernel, [(part.shape, BF16)], [], *parts, after=[rg0, vtop], us=4.0)
    (rg2,) = call(
        combine_kernel, [((rows, cols, channels), BF16)], [], rg1, rg2, after=[part]
    )
    order = [rg2]
    for mask in along_cols:
        part = join(part, mask, BF16, after=order, us=4.0)
        order = []
    output, conv_done = call(
        functools.partial(conv_kernel, masks, groups),
        [((disp, rows, feat, cols), BF16)],
        [
            pltpu.VMEM((disp // 2 + 1, 2, cols, 3 * rows * SLOT), BF16),
            pltpu.VMEM((rows // 2, disp, total, 128), F32),
            pltpu.VMEM((disp, rows, feat, cols), BF16),
            pltpu.SemaphoreType.DMA((4,)),
        ],
        vbuf, vtop, vbot, wc,
        after=[part],
        token=True,
        us=3.0,
        hbm=[0],
    )
    order = [conv_done]
    for mask in along_rows:
        part = join(part, mask, F32, after=order, us=4.0)
        order = []
    (lg,) = call(
        left_kernel,
        [((rows, cols, channels), BF16)],
        [pltpu.VMEM((rows, cols, wide), F32)],
        fr, fr4, *grads,
        after=[part],
        us=1.9,
    )
    rg2 = col_shift(rg2, -2)
    cells = disp * rows * n_row * cols * n_col
    weight_grad, right_grad, left_grad = call(
        functools.partial(finish_kernel, 1.0 / math.sqrt(cells)),
        [
            ((3, 3, 3, feat, groups), F32),
            ((rows, cols, channels), BF16),
            ((rows, cols, channels), BF16),
        ],
        [
            pltpu.VMEM((3, 3, 3, feat, groups), F32),
            pltpu.VMEM((rows, cols, channels), BF16),
            pltpu.SemaphoreType.DMA((5,)),
        ],
        part, swap(part, 1), rg0, rg1, rg2, lg,
        us=1.0,
        hbm=[0, 1, 2],
    )
    return (
        output.transpose(0, 1, 3, 2),
        weight_grad.transpose(0, 1, 2, 4, 3),
        left_grad,
        right_grad,
    )


def solution(mesh):
    in_specs = (P("row", "col", None), P("row", "col", None), P(), P(None, "row", "col", None))
    out_specs = (P(None, "row", "col", None), P(), P("row", "col", None), P("row", "col", None))
    return jax.shard_map(
        on_device, mesh=mesh, in_specs=in_specs, out_specs=out_specs, check_vma=False
    )
```
